32 devices in a mesh: tile: 8 (over z, y), mem: 4 (over x, core).
Axes of the slice: x: 2, y: 2, z: 4, core: 2. Of those that a mesh axis runs over, the one named last changes fastest.
Arguments:
- field: bfloat16 [61, 128, 1024], P(None, 'tile'), may hold values from -6 to 6
- vert_filter: bfloat16 [1, 60, 60], replicated, may hold values from -1 to 1.5
- loc_filter: bfloat16 [1, 60, 60], replicated, may hold values from -1 to 1.5
- alpha_table: float32 [16], replicated, may hold values from 0 to 1
- xscale_idx: int32 [2, 1024], replicated, may hold values from 0 to 15
- yscale_idx: int32 [2, 128], replicated, may hold values from 0 to 15
- members: bfloat16 [4, 61, 128, 1024], P('mem', None, 'tile'), may hold values from -6 to 6
Outputs:
- product: bfloat16 [61, 128, 1024], P(None, ('tile', 'mem'))
The draws below stay inside these ranges and needn't reach their ends.
All inputs are finite; a program needn't handle non-finite values.
Results may differ from the reference program's by a relative error of at most 0.0075.
Values may be sent and summed in bfloat16 or wider, within the bound.
No kernel may reach another device: no remote copies, remote signals or barrier semaphores. Data moves between devices by JAX's collectives and lax.ppermute only.
A program may use at most 128 MiB of HBM per device.

```python
import jax
import jax.numpy as jnp
from jax import lax

ROWS = 1024
VARS3 = 1
VARS2 = 1
LEV = 60
NSCALE = 16
COLS = 128
SLABS = 61
MEMBERS = 4


def banded(key):
    first, second = jax.random.split(key)
    rows = jnp.arange(LEV)[:, None]
    cols = jnp.arange(LEV)[None, :]
    shape = (VARS3, LEV, LEV)
    off_diag = jnp.clip(0.3 * jax.random.normal(first, shape, jnp.float32), -1.0, 1.0)
    diag = 1.0 + 0.5 * jax.random.uniform(second, shape, jnp.float32)
    inside = jnp.abs(rows - cols) <= 3
    result = jnp.where(rows == cols, diag, jnp.where(inside, off_diag, 0.0))
    return result.astype(jnp.bfloat16)


def draw_vert_filter(key, part):
    return banded(jax.random.fold_in(key, 11))


def draw_loc_filter(key, part):
    return banded(jax.random.fold_in(key, 23))


def draw_alpha_table(key, part):
    first, second = jax.random.split(jax.random.fold_in(key, 37))
    order = jax.random.permutation(first, NSCALE)
    slow_count = NSCALE // 2
    slow = order < slow_count
    frac = jax.random.uniform(second, (NSCALE,), jnp.float32)
    slow_low = jnp.log(jnp.float32(COLS) * 0.5)
    slow_len = jnp.exp(slow_low + frac * jnp.log(jnp.float32(6.0)))
    fast_len = jnp.exp(jnp.log(jnp.float32(3.0)) + frac * jnp.log(jnp.float32(20.0 / 3.0)))
    scale_len = jnp.where(slow, slow_len, fast_len)
    return (1.0 - 1.0 / scale_len).astype(jnp.float32)


def set_ends(values, own_key, smallest, largest):
    shape = values.shape
    index_at = [jax.random.randint(jax.random.fold_in(own_key, axis), (), 0, shape[axis]) for axis in range(len(shape))]
    values = values.at[tuple(index_at)].set(smallest)
    longest = shape.index(max(shape))
    index_at[longest] = (index_at[longest] + 1) % shape[longest]
    return values.at[tuple(index_at)].set(largest)


def level_of(rng, extent, pieces, smallest, top_value):
    gain, own = 1.0, jax.random.fold_in(rng, 6)
    for position, blocks in pieces:
        draws = jnp.exp(jax.random.uniform(jax.random.fold_in(own, position), (blocks,), jnp.float32, smallest / len(pieces), top_value / len(pieces)))
        gain = gain * jnp.repeat(draws, extent[position] // blocks).reshape([-1 if axis == position else 1 for axis in range(len(extent))])
    return gain


def scatter_about(rng, extent, deviation, limit, pieces=(), held_as=jnp.bfloat16):
    loudness = level_of(rng, extent, pieces, -0.22, 0.18) if pieces else 1.0
    array = jax.random.normal(rng, extent, jnp.float32) * deviation * loudness
    return jnp.minimum(jnp.maximum(array, -limit), limit).astype(held_as)


def setup_inputs(seed: int = 0) -> dict:
    key_list = jax.random.split(jax.random.key(seed), 8)
    field = scatter_about(key_list[0], (SLABS, COLS, ROWS), 1.0, 6.0, ((1, 8),))
    vert_filter = draw_vert_filter(jax.random.fold_in(key_list[7], 71), 0)
    loc_filter = draw_loc_filter(jax.random.fold_in(key_list[7], 71), 0)
    alpha_table = draw_alpha_table(jax.random.fold_in(key_list[7], 71), 0)
    xscale_idx = set_ends(jax.random.randint(key_list[4], (VARS3 + VARS2, ROWS), 0, NSCALE), jax.random.fold_in(key_list[4], 1), 0, NSCALE - 1).astype(jnp.int32)
    yscale_idx = set_ends(jax.random.randint(key_list[5], (VARS3 + VARS2, COLS), 0, NSCALE), jax.random.fold_in(key_list[5], 1), 0, NSCALE - 1).astype(jnp.int32)
    members = scatter_about(key_list[6], (MEMBERS, SLABS, COLS, ROWS), 1.0, 6.0, ((0, 4), (2, 8)))
    return dict(field=field, vert_filter=vert_filter, loc_filter=loc_filter, alpha_table=alpha_table, xscale_idx=xscale_idx, yscale_idx=yscale_idx, members=members)


def slab_vars():
    three_d = jnp.repeat(jnp.arange(VARS3, dtype=jnp.int32), LEV)
    two_d = VARS3 + jnp.arange(VARS2, dtype=jnp.int32)
    return jnp.concatenate([three_d, two_d])

def vertical(matrices, values):
    level_rows = VARS3 * LEV
    stacked = values[:level_rows].astype(jnp.float32).reshape(VARS3, LEV, COLS * ROWS)
    mixed = jnp.einsum('vij,vjp->vip', matrices.astype(jnp.float32), stacked)
    mixed = mixed.reshape(level_rows, COLS, ROWS)
    return jnp.concatenate([mixed, values[level_rows:].astype(jnp.float32)], 0)

def recursive(values, alpha, axis):
    moved = jnp.moveaxis(values, axis, 0)
    gain_fwd = jnp.sqrt(1.0 - alpha * alpha)
    gain_back = (1.0 - alpha * alpha) / jnp.sqrt(1.0 + alpha * alpha)

    def forward_step(carry, column):
        carry = alpha * carry + gain_fwd * column
        return (carry, carry)
    start = jnp.zeros(moved.shape[1:], jnp.float32)
    _, forward = lax.scan(forward_step, start, moved)

    def backward_step(carry, column):
        carry = alpha * carry + gain_back * column
        return (carry, carry)
    _, backward = lax.scan(backward_step, start, forward, reverse=True)
    return jnp.moveaxis(backward, 0, axis)

def reference(field, vert_filter, loc_filter, alpha_table, xscale_idx, yscale_idx, members):
    filtered = vertical(vert_filter, field).astype(jnp.bfloat16)
    var_index = slab_vars()
    alpha_x = alpha_table[xscale_idx[var_index]]
    alpha_y = alpha_table[yscale_idx[var_index]]
    smooth_x = recursive(filtered.astype(jnp.float32), alpha_x, 1)
    static_term = recursive(smooth_x, alpha_y, 2)

    def member_step(running, member):
        scaled = (member.astype(jnp.float32) * field.astype(jnp.float32)).astype(jnp.bfloat16)
        localized = vertical(loc_filter, scaled)
        return (running + member.astype(jnp.float32) * localized, None)
    start = jnp.zeros((SLABS, COLS, ROWS), jnp.float32)
    total, _ = lax.scan(member_step, start, members)
    ens_term = total / (MEMBERS - 1)
    return (static_term + ens_term).astype(jnp.bfloat16)
```

```python
import functools

import jax
import jax.numpy as jnp
from jax import lax
from jax.experimental import pallas as pl
from jax.experimental.pallas import tpu as pltpu
from jax.sharding import PartitionSpec as P

F32, BF16 = jnp.float32, jnp.bfloat16
SUB = 16
LANES = 256
BLOCK = 256
MIB = 1 << 20


def iota(shape, dim):
    return lax.broadcasted_iota(jnp.int32, shape, dim)


def dot(left, right):
    return jnp.dot(left, right, preferred_element_type=F32)


def gain_of(alpha):
    rest = (1.0 - alpha) * (1.0 + alpha)
    return jnp.sqrt(rest) * rest / jnp.sqrt(1.0 + alpha * alpha)


def lookup(table_ref, entries):
    found = jnp.zeros(entries.shape, F32)
    for entry in range(table_ref.shape[0]):
        found = jnp.where(entries == entry, table_ref[entry], found)
    return found


def padded(slab_count):
    return -(-slab_count // (4 * SUB)) * 4 * SUB


def to_columns(perm, flat_ref, out_ref, cols):
    total = flat_ref.shape[0]
    wanted = out_ref.shape[0]
    step = SUB * cols
    for chunk in range(out_ref.shape[1] // SUB):
        depth = min(step, total - chunk * step)
        part = flat_ref[chunk * step : chunk * step + depth, :]
        moved = dot(perm[:, :depth], part)
        out_ref[:, chunk * SUB : (chunk + 1) * SUB, :] = moved.reshape(wanted, SUB, -1)


def columns_kernel(levels, table_ref, entries_ref, field_ref, ends_ref, own_ref, coef_ref, work, tail):
    cols, slabs, lanes = work.shape
    own_cols = own_ref.shape[0]
    mem = lax.axis_index("mem")
    shape = (SUB * cols, SUB * cols)
    out_row, in_row = iota(shape, 0), iota(shape, 1)
    hit = (out_row % SUB == in_row // cols) & (out_row // SUB == in_row % cols)
    to_columns(hit.astype(BF16), field_ref, work, cols)
    pair = lookup(table_ref, entries_ref[...])
    alpha = jnp.where(iota((slabs, lanes), 0) < levels, pair[0:1], pair[1:2])
    state = work[0]
    for col in range(1, cols):
        state = alpha * state + work[col]
        work[col] = state
    for col in range(cols - 2, -1, -1):
        state = alpha * state + work[col]
        work[col] = state
    gain = gain_of(alpha)
    tail[0] = gain * work[cols - 1]
    tail[1] = gain * state
    share = pl.ds(pl.multiple_of(mem * SUB, SUB), SUB)
    ends_ref[...] = tail[:, share, :].astype(BF16)
    own_ref[...] = work[pl.ds(mem * own_cols, own_cols)] * gain[None]
    square = pair * pair
    power, sums = jnp.ones_like(pair), jnp.zeros_like(pair)
    rights, geometric = [], []
    for _ in range(cols):
        power, sums = power * pair, sums * square + 1.0
        rights.append(power)
        geometric.append(sums)
    for col in range(cols):
        coef_ref[0, col] = rights[col] * geometric[cols - 1 - col]
        coef_ref[1, col] = rights[cols - 1 - col]


def columns_call(table, entries, flat_field, levels, cols, own_cols):
    total, rows = flat_field.shape
    slabs = padded(total // cols)
    return pl.pallas_call(
        functools.partial(columns_kernel, levels),
        name="columns",
        grid=(rows // LANES,),
        in_specs=[
            pl.BlockSpec(memory_space=pltpu.SMEM),
            pl.BlockSpec((2, LANES), lambda i: (0, i)),
            pl.BlockSpec((total, LANES), lambda i: (0, i)),
        ],
        out_specs=[
            pl.BlockSpec((2, SUB, LANES), lambda i: (0, 0, i)),
            pl.BlockSpec((own_cols, slabs, LANES), lambda i: (0, 0, i)),
            pl.BlockSpec((2, cols, 2, LANES), lambda i: (0, 0, 0, i)),
        ],
        out_shape=[
            jax.ShapeDtypeStruct((2, SUB, rows), BF16),
            jax.ShapeDtypeStruct((own_cols, slabs, rows), F32),
            jax.ShapeDtypeStruct((2, cols, 2, rows), F32),
        ],
        scratch_shapes=[
            pltpu.VMEM((cols, slabs, LANES), F32),
            pltpu.VMEM((2, slabs, LANES), F32),
        ],
        compiler_params=pltpu.CompilerParams(vmem_limit_bytes=32 * MIB),
        cost_estimate=pl.CostEstimate(flops=5 * 10**8, bytes_accessed=4 * MIB, transcendentals=0),
    )(table, entries, flat_field)


def spread(matrix, levels, slabs, row_slab, row_col, col_slab, col_col):
    rows, cols = row_slab.shape
    size = matrix.shape[0]
    left = (iota((rows, size), 1) == row_slab[:, :size]).astype(BF16)
    right = (iota((size, cols), 0) == col_slab[:size, :]).astype(BF16)
    inner = dot(left, matrix).astype(BF16)
    full = dot(inner, right)
    full = jnp.where((row_slab >= levels) & (row_slab == col_slab), 1.0, full)
    return jnp.where(row_col == col_col, full, 0.0).astype(BF16)


def ensemble_kernel(levels, cols, loc_ref, field_ref, mine_ref, other_ref, send_ref, keep_ref, field_w, mine_w, other_w):
    own_cols, slabs, lanes = keep_ref.shape
    mem = lax.axis_index("mem")
    core, chip = mem % 2, mem // 2
    shape = (2 * own_cols * SUB, cols * SUB)
    out_row, in_row = iota(shape, 0), iota(shape, 1)
    slot = out_row // SUB
    first = jnp.where(slot < own_cols, (2 * (1 - chip) + core) * own_cols, (2 * chip + core) * own_cols)
    hit = (out_row % SUB == in_row // cols) & (first + slot % own_cols == in_row % cols)
    perm = hit.astype(BF16)
    to_columns(perm, field_ref, field_w, cols)
    to_columns(perm, mine_ref, mine_w, cols)
    to_columns(perm, other_ref, other_w, cols)
    side = own_cols * slabs
    row, col = iota((side, side), 0), iota((side, side), 1)
    local = spread(loc_ref[...], levels, slabs, row % slabs, row // slabs, col % slabs, col // slabs)
    for half in range(2):
        part = slice(half * own_cols, (half + 1) * own_cols)
        field = field_w[part]
        total = None
        for member_w in (mine_w, other_w):
            member = member_w[part]
            scaled = (member * field).astype(BF16).reshape(side, lanes)
            term = member * dot(local, scaled).reshape(own_cols, slabs, lanes)
            total = term if total is None else total + term
        if half == 0:
            send_ref[...] = total.astype(BF16)
        else:
            keep_ref[...] = total


def ensemble_call(loc, flat_field, mine, other, levels, cols, own_cols):
    total, rows = flat_field.shape
    slabs = padded(total // cols)
    wide = pl.BlockSpec((total, LANES), lambda i: (0, i))
    out = pl.BlockSpec((own_cols, slabs, LANES), lambda i: (0, 0, i))
    return pl.pallas_call(
        functools.partial(ensemble_kernel, levels, cols),
        name="ensemble",
        grid=(rows // LANES,),
        in_specs=[pl.BlockSpec(loc.shape, lambda i: (0, 0)), wide, wide, wide],
        out_specs=[out, out],
        out_shape=[
            jax.ShapeDtypeStruct((own_cols, slabs, rows), BF16),
            jax.ShapeDtypeStruct((own_cols, slabs, rows), F32),
        ],
        scratch_shapes=[pltpu.VMEM((2 * own_cols, slabs, LANES), F32)] * 3,
        compiler_params=pltpu.CompilerParams(vmem_limit_bytes=32 * MIB),
        cost_estimate=pl.CostEstimate(flops=5 * 10**8, bytes_accessed=8 * MIB, transcendentals=0),
    )(loc, flat_field, mine, other)


def tables_kernel(levels, own_cols, col_dev, slabs, table_ref, entries_ref, vert_ref, mat_ref, coef_ref, vert_out):
    first = lax.axis_index("tile") * col_dev + lax.axis_index("mem") * own_cols
    count = 2 * own_cols
    alphas = [table_ref[entries_ref[var, first + col]] for var in range(2) for col in range(own_cols)]
    by_lane = jnp.zeros((1, 128), F32)
    by_row = jnp.zeros((count, 1), F32)
    for k, alpha in enumerate(alphas):
        by_lane = jnp.where(iota((1, 128), 1) == k, alpha, by_lane)
        by_row = jnp.where(iota((count, 1), 0) == k, alpha, by_row)

    def series(alpha, number):
        alpha = jnp.broadcast_to(alpha, number.shape)
        total, unit = jnp.zeros(number.shape, F32), jnp.ones(number.shape, F32)
        single, power, both = alpha, alpha * alpha, jnp.ones(number.shape, F32)
        for bit in range(BLOCK.bit_length()):
            here = (number >> bit) % 2 == 1
            total = jnp.where(here, unit + power * total, total)
            both = jnp.where(here, both * single, both)
            unit, single, power = unit * (1.0 + power), single * single, power * power
        return total, both

    down, _ = series(by_lane, BLOCK - iota((BLOCK, 128), 0))
    place = iota((count, BLOCK), 1)
    across, right = series(by_row, BLOCK - place)
    _, left = series(by_row, place + 1)
    coef_ref[0] = left * across
    coef_ref[1] = right
    coef_ref[2] = jnp.broadcast_to(right[:, 0:1], right.shape)
    coef_ref[3] = jnp.broadcast_to(left[:, 0:1] * across[:, 0:1], right.shape)
    far = jnp.abs(iota((BLOCK, BLOCK), 0) - iota((BLOCK, BLOCK), 1)).astype(F32)
    for k in range(count):
        alpha = by_row[k : k + 1]
        decay = jnp.exp(far * jnp.log(jnp.maximum(alpha, 1e-30)))
        reach = jnp.minimum(down[:, k : k + 1], across[k : k + 1])
        mat_ref[k] = (gain_of(alpha) * decay * reach).astype(BF16)
    shape = vert_out.shape
    row, col = iota(shape, 0), iota(shape, 1)
    vert_out[...] = spread(vert_ref[...], levels, slabs, row // 8, row % 8, col % slabs, col // slabs)


def tables_call(table, entries, vert, levels, own_cols, col_dev, slabs):
    count = 2 * own_cols
    smem = pl.BlockSpec(memory_space=pltpu.SMEM)
    return pl.pallas_call(
        functools.partial(tables_kernel, levels, own_cols, col_dev, slabs),
        name="tables",
        in_specs=[smem, smem, pl.BlockSpec(memory_space=pltpu.VMEM)],
        out_specs=[pl.BlockSpec(memory_space=pltpu.VMEM)] * 3,
        out_shape=[
            jax.ShapeDtypeStruct((count, BLOCK, BLOCK), BF16),
            jax.ShapeDtypeStruct((4, count, BLOCK), F32),
            jax.ShapeDtypeStruct((8 * slabs, own_cols * slabs), BF16),
        ],
        compiler_params=pltpu.CompilerParams(vmem_limit_bytes=32 * MIB),
        cost_estimate=pl.CostEstimate(flops=10**8, bytes_accessed=2 * MIB, transcendentals=0),
    )(table, entries, vert)


def along_rows(lines, matrix, coef):
    count, rows = lines.shape
    blocks = rows // BLOCK
    parts = jnp.concatenate([lines[:, b * BLOCK : (b + 1) * BLOCK] for b in range(blocks)], 0)
    local = dot(parts.astype(BF16), matrix)
    local = [local[b * count : (b + 1) * count] for b in range(blocks)]
    into, right, decay, turn = coef[0:1], coef[1:2], coef[2:3, 0:1], coef[3:4, 0:1]
    forward, state = [None], None
    for b in range(blocks - 1):
        end = local[b][:, BLOCK - 1 : BLOCK]
        state = end if state is None else decay * state + end
        forward.append(state)
    out, state = [None] * blocks, None
    for b in range(blocks - 1, -1, -1):
        piece = local[b]
        if forward[b] is not None:
            piece = piece + into * forward[b]
        if state is not None:
            piece = piece + right * state
        out[b] = piece
        if b:
            start = local[b][:, 0:1] + turn * forward[b]
            state = start if state is None else decay * state + start
    return out


def final_kernel(
    levels, scale, own_ref, coef_ref, mine_ref, core_ref, chip_ref, far_ref, mat_ref, row_coef_ref, vert_ref,
    keep_ref, came_ref, out_ref, carry, smooth, filt
):
    own_cols, slabs, rows = own_ref.shape
    mem = lax.axis_index("mem")
    for flip, ref in ((0, mine_ref), (1, core_ref), (2, chip_ref), (3, far_ref)):
        share = pl.ds(pl.multiple_of((mem ^ flip) * SUB, SUB), SUB)
        carry[:, share, :] = ref[...].astype(F32)
    top = levels // 8 * 8
    for col in range(own_cols):
        pair = coef_ref[:, mem * own_cols + col]
        is_level = iota((slabs, rows), 0) < levels
        from_left = jnp.where(is_level, pair[0, 0:1], pair[0, 1:2])
        from_right = jnp.where(is_level, pair[1, 0:1], pair[1, 1:2])
        smooth[col] = own_ref[col] + from_left * carry[0] + from_right * carry[1]
    for col in range(own_cols):
        lines = smooth[col]
        main = along_rows(lines, mat_ref[col], row_coef_ref[:, col])
        last = along_rows(lines[top : top + 8], mat_ref[own_cols + col], row_coef_ref[:, own_cols + col])
        for b, (piece, extra) in enumerate(zip(main, last)):
            place = slice(b * BLOCK, (b + 1) * BLOCK)
            filt[col * slabs : col * slabs + slabs, place] = piece
            filt[col * slabs + top : col * slabs + top + 8, place] = jnp.where(
                iota((8, BLOCK), 0) < levels - top, piece[top : top + 8], extra
            )
    shape = vert_ref.shape
    row, place = iota(shape, 0), iota(shape, 1)
    order = ((row // 8 == place % slabs) & (row % 8 == place // slabs)).astype(BF16)
    count = out_ref.shape[0]
    side = own_cols * slabs
    for start in range(0, rows, BLOCK):
        part = slice(start, start + BLOCK)
        static = filt[:, part]
        ens = (keep_ref[:, :, part] + came_ref[:, :, part].astype(F32)).reshape(side, BLOCK) * scale
        static_hi, ens_hi = static.astype(BF16), ens.astype(BF16)
        static_lo = (static - static_hi.astype(F32)).astype(BF16)
        ens_lo = (ens - ens_hi.astype(F32)).astype(BF16)
        total = dot(vert_ref[...], static_hi) + dot(vert_ref[...], static_lo) + dot(order, ens_hi) + dot(order, ens_lo)
        total = total.reshape(slabs, 8, BLOCK)
        out_ref[:, :, part] = total[:count, :own_cols].astype(BF16)


def final_call(slab_count, levels, scale, args):
    own_cols, slabs, rows = args[0].shape
    vmem = pl.BlockSpec(memory_space=pltpu.VMEM)
    return pl.pallas_call(
        functools.partial(final_kernel, levels, scale),
        name="final",
        in_specs=[vmem] * len(args),
        out_specs=vmem,
        out_shape=jax.ShapeDtypeStruct((slab_count, own_cols, rows), BF16),
        scratch_shapes=[
            pltpu.VMEM((2, slabs, rows), F32),
            pltpu.VMEM((own_cols, slabs, rows), F32),
            pltpu.VMEM((own_cols * slabs, rows), F32),
        ],
        compiler_params=pltpu.CompilerParams(vmem_limit_bytes=32 * MIB),
        cost_estimate=pl.CostEstimate(flops=10**9, bytes_accessed=6 * MIB, transcendentals=0),
    )(*args)


def tile_carries(ends, coef, levels, tile_count):
    tile, mem = lax.axis_index("tile"), lax.axis_index("mem")
    slab = mem * SUB + jnp.arange(SUB)[:, None]
    decay = jnp.where(slab < levels, coef[1, 0, 0], coef[1, 0, 1])
    turn = jnp.where(slab < levels, coef[0, 0, 0], coef[0, 0, 1])
    one, none = jnp.ones_like(decay), jnp.zeros_like(decay)
    from_left, from_right, turned = one, one, none
    left, right = none, none
    block = ends.astype(F32)
    span = 1
    while span < tile_count:
        sent = block.astype(BF16)
        came = lax.ppermute(sent, "tile", [(i, i ^ span) for i in range(tile_count)]).astype(F32)
        second = (tile // span) % 2 == 1
        lower = jnp.where(second, came, block)
        upper = jnp.where(second, block, came)
        bent = turn * lower[0] + upper[1]
        left = left + jnp.where(second, from_left * lower[0], 0.0)
        right = right + jnp.where(second, turned * lower[0], from_right * bent)
        block = jnp.stack([decay * lower[0] + upper[0], lower[1] + decay * bent])
        turned = jnp.where(second, turned * decay, turned + from_right * turn * decay)
        from_left = jnp.where(second, from_left * decay, from_left)
        from_right = jnp.where(second, from_right, from_right * decay)
        turn = turn * (1.0 + decay * decay)
        decay = decay * decay
        span *= 2
    return jnp.stack([left, right]).astype(BF16)


def body(field, vert_filter, loc_filter, alpha_table, xscale_idx, yscale_idx, members):
    tile_count, mem_count = lax.axis_size("tile"), lax.axis_size("mem")
    slab_count, cols, rows = field.shape
    levels = vert_filter.shape[1]
    own_cols = cols // mem_count
    slabs = padded(slab_count)

    def swap(array, flip):
        return lax.ppermute(array, "mem", [(i, i ^ flip) for i in range(mem_count)])

    flat_field = field.reshape(slab_count * cols, rows)
    mine = members.reshape(slab_count * cols, rows)
    other = swap(mine, 1)
    ends, own, coef = columns_call(alpha_table, xscale_idx, flat_field, levels, cols, own_cols)
    mats, row_coef, vert = tables_call(alpha_table, yscale_idx, vert_filter[0], levels, own_cols, cols, slabs)
    send, keep = ensemble_call(loc_filter[0], flat_field, mine, other, levels, cols, own_cols)
    came = swap(send, 2)
    carried = tile_carries(ends, coef, levels, tile_count)
    shares = [carried] + [swap(carried, flip) for flip in range(1, mem_count)]
    scale = 1.0 / (mem_count * members.shape[0] - 1)
    return final_call(slab_count, levels, scale, [own, coef, *shares, mats, row_coef, vert, keep, came])


def solution(mesh):
    return jax.shard_map(
        body,
        mesh=mesh,
        in_specs=(P(None, "tile", None), P(), P(), P(), P(), P(), P("mem", None, "tile", None)),
        out_specs=P(None, ("tile", "mem"), None),
        check_vma=False,
    )
```

```python
import functools

import jax
import jax.numpy as jnp
from jax import lax
from jax.experimental import pallas as pl
from jax.experimental.pallas import tpu as pltpu
from jax.sharding import PartitionSpec as P

F32, BF16 = jnp.float32, jnp.bfloat16
COL_BITS = 4
SUB = 16
LANES = 256
BLOCK = 256
MIB = 1 << 20
VMEM = 32 * MIB


def iota(shape, dim):
    return lax.broadcasted_iota(jnp.int32, shape, dim)


def dot(left, right):
    return jnp.dot(left, right, preferred_element_type=F32)


def gain_of(alpha):
    rest = (1.0 - alpha) * (1.0 + alpha)
    return jnp.sqrt(rest) * rest / jnp.sqrt(1.0 + alpha * alpha)


def lookup(table_ref, entries):
    found = jnp.zeros(entries.shape, F32)
    for entry in range(table_ref.shape[0]):
        found = jnp.where(entries == entry, table_ref[entry], found)
    return found


def padded(slab_count):
    return -(-slab_count // (4 * SUB)) * 4 * SUB


def to_columns(perm, flat_ref, out_ref, cols):
    total = flat_ref.shape[0]
    wanted = out_ref.shape[0]
    step = SUB * cols
    for chunk in range(out_ref.shape[1] // SUB):
        depth = min(step, total - chunk * step)
        part = flat_ref[chunk * step : chunk * step + depth, :]
        moved = dot(perm[:, :depth], part)
        out_ref[:, chunk * SUB : (chunk + 1) * SUB, :] = moved.reshape(wanted, SUB, -1)


def sweep(work, alpha):
    cols = work.shape[0]
    state = work[0]
    for col in range(1, cols):
        state = alpha * state + work[col]
        work[col] = state
    for col in range(cols - 2, -1, -1):
        state = alpha * state + work[col]
        work[col] = state


def transposer(cols):
    shape = (SUB * cols, SUB * cols)
    out_row, in_row = iota(shape, 0), iota(shape, 1)
    hit = (out_row % SUB == in_row // cols) & (out_row // SUB == in_row % cols)
    return hit.astype(BF16)


def ends_kernel(levels, slab_count, mem_ref, table_ref, entries_ref, field_ref, ends_ref, work):
    cols, _, lanes = work.shape
    first = mem_ref[0] * SUB
    shape = field_ref.shape
    held = jnp.where(iota(shape, 0) // cols + first < slab_count, field_ref[...], 0)
    work[...] = dot(transposer(cols), held).reshape(work.shape)
    pair = lookup(table_ref, entries_ref[...])
    alpha = jnp.where(iota((SUB, lanes), 0) + first < levels, pair[0:1], pair[1:2])
    sweep(work, alpha)
    gain = gain_of(alpha)
    ends_ref[0] = (gain * work[cols - 1]).astype(BF16)
    ends_ref[1] = (gain * work[0]).astype(BF16)


def ends_call(mem, table, entries, flat_field, levels, cols):
    total, rows = flat_field.shape
    return pl.pallas_call(
        functools.partial(ends_kernel, levels, total // cols),
        name="ends",
        grid_spec=pltpu.PrefetchScalarGridSpec(
            num_scalar_prefetch=1,
            grid=(rows // LANES,),
            in_specs=[
                pl.BlockSpec(memory_space=pltpu.SMEM),
                pl.BlockSpec((2, LANES), lambda i, mem: (0, i)),
                pl.BlockSpec((SUB * cols, LANES), lambda i, mem: (mem[0], i)),
            ],
            out_specs=pl.BlockSpec((2, SUB, LANES), lambda i, mem: (0, 0, i)),
            scratch_shapes=[pltpu.VMEM((cols, SUB, LANES), F32)],
        ),
        out_shape=jax.ShapeDtypeStruct((2, SUB, rows), BF16),
        compiler_params=pltpu.CompilerParams(vmem_limit_bytes=VMEM),
        cost_estimate=pl.CostEstimate(flops=10**8, bytes_accessed=MIB, transcendentals=0),
    )(mem, table, entries, flat_field)


def local_kernel(levels, table_ref, entries_ref, field_ref, after_ref, own_ref, coef_ref, work):
    cols, slabs, lanes = work.shape
    own_cols = own_ref.shape[0]
    mem = lax.axis_index("mem")
    to_columns(transposer(cols), field_ref, work, cols)
    pair = lookup(table_ref, entries_ref[...])
    alpha = jnp.where(iota((slabs, lanes), 0) < levels, pair[0:1], pair[1:2])
    sweep(work, alpha)
    own_ref[...] = work[pl.ds(mem * own_cols, own_cols)] * gain_of(alpha)[None]
    square = pair * pair
    power, sums = jnp.ones_like(pair), jnp.zeros_like(pair)
    rights, geometric = [], []
    for _ in range(cols):
        power, sums = power * pair, sums * square + 1.0
        rights.append(power)
        geometric.append(sums)
    for col in range(cols):
        coef_ref[0, col] = rights[col] * geometric[cols - 1 - col]
        coef_ref[1, col] = rights[cols - 1 - col]


def local_call(table, entries, flat_field, after, levels, cols, own_cols):
    total, rows = flat_field.shape
    slabs = padded(total // cols)
    return pl.pallas_call(
        functools.partial(local_kernel, levels),
        name="local",
        grid=(rows // LANES,),
        in_specs=[
            pl.BlockSpec(memory_space=pltpu.SMEM),
            pl.BlockSpec((2, LANES), lambda i: (0, i)),
            pl.BlockSpec((total, LANES), lambda i: (0, i)),
            pl.BlockSpec(memory_space=pl.ANY),
        ],
        out_specs=[
            pl.BlockSpec((own_cols, slabs, LANES), lambda i: (0, 0, i)),
            pl.BlockSpec((2, cols, 2, LANES), lambda i: (0, 0, 0, i)),
        ],
        out_shape=[
            jax.ShapeDtypeStruct((own_cols, slabs, rows), F32),
            jax.ShapeDtypeStruct((2, cols, 2, rows), F32),
        ],
        scratch_shapes=[pltpu.VMEM((cols, slabs, LANES), F32)],
        compiler_params=pltpu.CompilerParams(vmem_limit_bytes=VMEM),
        cost_estimate=pl.CostEstimate(flops=5 * 10**8, bytes_accessed=4 * MIB, transcendentals=0),
    )(table, entries, flat_field, after)


def spread(matrix, levels, slabs, row_slab, row_col, col_slab, col_col):
    rows, cols = row_slab.shape
    size = matrix.shape[0]
    left = (iota((rows, size), 1) == row_slab[:, :size]).astype(BF16)
    right = (iota((size, cols), 0) == col_slab[:size, :]).astype(BF16)
    inner = dot(left, matrix).astype(BF16)
    full = dot(inner, right)
    full = jnp.where((row_slab >= levels) & (row_slab == col_slab), 1.0, full)
    return jnp.where(row_col == col_col, full, 0.0).astype(BF16)


def ensemble_kernel(levels, cols, loc_ref, field_ref, mine_ref, other_ref, after_ref, send_ref, keep_ref, field_w, mine_w, other_w):
    own_cols, slabs, lanes = keep_ref.shape
    mem = lax.axis_index("mem")
    core, chip = mem % 2, mem // 2
    shape = (2 * own_cols * SUB, cols * SUB)
    out_row, in_row = iota(shape, 0), iota(shape, 1)
    slot = out_row // SUB
    first = jnp.where(slot < own_cols, (2 * (1 - chip) + core) * own_cols, (2 * chip + core) * own_cols)
    hit = (out_row % SUB == in_row // cols) & (first + slot % own_cols == in_row % cols)
    perm = hit.astype(BF16)
    to_columns(perm, field_ref, field_w, cols)
    to_columns(perm, mine_ref, mine_w, cols)
    to_columns(perm, other_ref, other_w, cols)
    side = own_cols * slabs
    row, col = iota((side, side), 0), iota((side, side), 1)
    local = spread(loc_ref[...], levels, slabs, row % slabs, row // slabs, col % slabs, col // slabs)
    for half in range(2):
        part = slice(half * own_cols, (half + 1) * own_cols)
        field = field_w[part]
        total = None
        for member_w in (mine_w, other_w):
            member = member_w[part]
            scaled = (member * field).astype(BF16).reshape(side, lanes)
            term = member * dot(local, scaled).reshape(own_cols, slabs, lanes)
            total = term if total is None else total + term
        if half == 0:
            send_ref[...] = total.astype(BF16)
        else:
            keep_ref[...] = total


def ensemble_call(loc, flat_field, mine, other, after, levels, cols, own_cols):
    total, rows = flat_field.shape
    slabs = padded(total // cols)
    wide = pl.BlockSpec((total, LANES), lambda i: (0, i))
    out = pl.BlockSpec((own_cols, slabs, LANES), lambda i: (0, 0, i))
    return pl.pallas_call(
        functools.partial(ensemble_kernel, levels, cols),
        name="ensemble",
        grid=(rows // LANES,),
        in_specs=[pl.BlockSpec(loc.shape, lambda i: (0, 0)), wide, wide, wide, pl.BlockSpec(memory_space=pl.ANY)],
        out_specs=[out, out],
        out_shape=[
            jax.ShapeDtypeStruct((own_cols, slabs, rows), BF16),
            jax.ShapeDtypeStruct((own_cols, slabs, rows), F32),
        ],
        scratch_shapes=[pltpu.VMEM((2 * own_cols, slabs, LANES), F32)] * 3,
        compiler_params=pltpu.CompilerParams(vmem_limit_bytes=VMEM),
        cost_estimate=pl.CostEstimate(flops=5 * 10**8, bytes_accessed=8 * MIB, transcendentals=0),
    )(loc, flat_field, mine, other, after)


def tables_kernel(levels, own_cols, col_dev, slabs, table_ref, entries_ref, vert_ref, after_ref, mat_ref, coef_ref, vert_out):
    first = lax.axis_index("tile") * col_dev + lax.axis_index("mem") * own_cols
    count = 2 * own_cols
    alphas = [table_ref[entries_ref[var, first + col]] for var in range(2) for col in range(own_cols)]
    by_lane = jnp.zeros((1, 128), F32)
    by_row = jnp.zeros((count, 1), F32)
    for k, alpha in enumerate(alphas):
        by_lane = jnp.where(iota((1, 128), 1) == k, alpha, by_lane)
        by_row = jnp.where(iota((count, 1), 0) == k, alpha, by_row)

    def series(alpha, number):
        alpha = jnp.broadcast_to(alpha, number.shape)
        total, unit = jnp.zeros(number.shape, F32), jnp.ones(number.shape, F32)
        single, power, both = alpha, alpha * alpha, jnp.ones(number.shape, F32)
        for bit in range(BLOCK.bit_length()):
            here = (number >> bit) % 2 == 1
            total = jnp.where(here, unit + power * total, total)
            both = jnp.where(here, both * single, both)
            unit, single, power = unit * (1.0 + power), single * single, power * power
        return total, both

    down, _ = series(by_lane, BLOCK - iota((BLOCK, 128), 0))
    place = iota((count, BLOCK), 1)
    across, right = series(by_row, BLOCK - place)
    _, left = series(by_row, place + 1)
    coef_ref[0] = left * across
    coef_ref[1] = right
    coef_ref[2] = jnp.broadcast_to(right[:, 0:1], right.shape)
    coef_ref[3] = jnp.broadcast_to(left[:, 0:1] * across[:, 0:1], right.shape)
    far = jnp.abs(iota((BLOCK, BLOCK), 0) - iota((BLOCK, BLOCK), 1)).astype(F32)
    for k in range(count):
        alpha = by_row[k : k + 1]
        decay = jnp.exp(far * jnp.log(jnp.maximum(alpha, 1e-30)))
        reach = jnp.minimum(down[:, k : k + 1], across[k : k + 1])
        mat_ref[k] = (gain_of(alpha) * decay * reach).astype(BF16)
    shape = vert_out.shape
    row, col = iota(shape, 0), iota(shape, 1)
    vert_out[...] = spread(vert_ref[...], levels, slabs, row // 8, row % 8, col % slabs, col // slabs)


def tables_call(table, entries, vert, after, levels, own_cols, col_dev, slabs):
    count = 2 * own_cols
    smem = pl.BlockSpec(memory_space=pltpu.SMEM)
    return pl.pallas_call(
        functools.partial(tables_kernel, levels, own_cols, col_dev, slabs),
        name="tables",
        in_specs=[smem, smem, pl.BlockSpec(memory_space=pltpu.VMEM), pl.BlockSpec(memory_space=pl.ANY)],
        out_specs=[pl.BlockSpec(memory_space=pltpu.VMEM)] * 3,
        out_shape=[
            jax.ShapeDtypeStruct((count, BLOCK, BLOCK), BF16),
            jax.ShapeDtypeStruct((4, count, BLOCK), F32),
            jax.ShapeDtypeStruct((8 * slabs, own_cols * slabs), BF16),
        ],
        compiler_params=pltpu.CompilerParams(vmem_limit_bytes=VMEM),
        cost_estimate=pl.CostEstimate(flops=10**8, bytes_accessed=2 * MIB, transcendentals=0),
    )(table, entries, vert, after)


def along_rows(lines, matrix, coef):
    count, rows = lines.shape
    blocks = rows // BLOCK
    parts = jnp.concatenate([lines[:, b * BLOCK : (b + 1) * BLOCK] for b in range(blocks)], 0)
    local = dot(parts.astype(BF16), matrix)
    local = [local[b * count : (b + 1) * count] for b in range(blocks)]
    into, right, decay, turn = coef[0:1], coef[1:2], coef[2:3, 0:1], coef[3:4, 0:1]
    forward, state = [None], None
    for b in range(blocks - 1):
        end = local[b][:, BLOCK - 1 : BLOCK]
        state = end if state is None else decay * state + end
        forward.append(state)
    out, state = [None] * blocks, None
    for b in range(blocks - 1, -1, -1):
        piece = local[b]
        if forward[b] is not None:
            piece = piece + into * forward[b]
        if state is not None:
            piece = piece + right * state
        out[b] = piece
        if b:
            start = local[b][:, 0:1] + turn * forward[b]
            state = start if state is None else decay * state + start
    return out


def final_kernel(
    levels, scale, own_ref, coef_ref, mine_ref, core_ref, chip_ref, far_ref, mat_ref, row_coef_ref, vert_ref,
    keep_ref, came_ref, out_ref, carry, smooth, filt
):
    own_cols, slabs, rows = own_ref.shape
    mem = lax.axis_index("mem")
    for flip, ref in ((0, mine_ref), (1, core_ref), (2, chip_ref), (3, far_ref)):
        share = pl.ds(pl.multiple_of((mem ^ flip) * SUB, SUB), SUB)
        carry[:, share, :] = ref[...].astype(F32)
    top = levels // 8 * 8
    for col in range(own_cols):
        pair = coef_ref[:, mem * own_cols + col]
        is_level = iota((slabs, rows), 0) < levels
        from_left = jnp.where(is_level, pair[0, 0:1], pair[0, 1:2])
        from_right = jnp.where(is_level, pair[1, 0:1], pair[1, 1:2])
        smooth[col] = own_ref[col] + from_left * carry[0] + from_right * carry[1]
    for col in range(own_cols):
        lines = smooth[col]
        main = along_rows(lines, mat_ref[col], row_coef_ref[:, col])
        last = along_rows(lines[top : top + 8], mat_ref[own_cols + col], row_coef_ref[:, own_cols + col])
        for b, (piece, extra) in enumerate(zip(main, last)):
            place = slice(b * BLOCK, (b + 1) * BLOCK)
            filt[col * slabs : col * slabs + slabs, place] = piece
            filt[col * slabs + top : col * slabs + top + 8, place] = jnp.where(
                iota((8, BLOCK), 0) < levels - top, piece[top : top + 8], extra
            )
    shape = vert_ref.shape
    row, place = iota(shape, 0), iota(shape, 1)
    order = ((row // 8 == place % slabs) & (row % 8 == place // slabs)).astype(BF16)
    count = out_ref.shape[0]
    side = own_cols * slabs
    for start in range(0, rows, BLOCK):
        part = slice(start, start + BLOCK)
        static = filt[:, part]
        ens = (keep_ref[:, :, part] + came_ref[:, :, part].astype(F32)).reshape(side, BLOCK) * scale
        static_hi, ens_hi = static.astype(BF16), ens.astype(BF16)
        static_lo = (static - static_hi.astype(F32)).astype(BF16)
        ens_lo = (ens - ens_hi.astype(F32)).astype(BF16)
        total = dot(vert_ref[...], static_hi) + dot(vert_ref[...], static_lo) + dot(order, ens_hi) + dot(order, ens_lo)
        total = total.reshape(slabs, 8, BLOCK)
        out_ref[:, :, part] = total[:count, :own_cols].astype(BF16)


def final_call(slab_count, levels, scale, args):
    own_cols, slabs, rows = args[0].shape
    vmem = pl.BlockSpec(memory_space=pltpu.VMEM)
    return pl.pallas_call(
        functools.partial(final_kernel, levels, scale),
        name="final",
        in_specs=[vmem] * len(args),
        out_specs=vmem,
        out_shape=jax.ShapeDtypeStruct((slab_count, own_cols, rows), BF16),
        scratch_shapes=[
            pltpu.VMEM((2, slabs, rows), F32),
            pltpu.VMEM((own_cols, slabs, rows), F32),
            pltpu.VMEM((own_cols * slabs, rows), F32),
        ],
        compiler_params=pltpu.CompilerParams(vmem_limit_bytes=VMEM),
        cost_estimate=pl.CostEstimate(flops=10**9, bytes_accessed=6 * MIB, transcendentals=0),
    )(*args)


def merge_kernel(levels, last, step, after_count, *refs):
    table_ref, entries_ref = refs[:2]
    pairs = refs[2 : 4 + 2 * step]
    out_ref = refs[4 + 2 * step + after_count]
    _, subs, rows = out_ref.shape
    tile, mem = lax.axis_index("tile"), lax.axis_index("mem")
    pair = lookup(table_ref, entries_ref[...])
    decay, turn = pair, jnp.ones_like(pair)
    for _ in range(COL_BITS):
        turn = turn * (1.0 + decay * decay)
        decay = decay * decay
    turn = pair * turn
    is_level = iota((subs, rows), 0) + mem * SUB < levels
    decay = jnp.where(is_level, decay[0:1], decay[1:2])
    turn = jnp.where(is_level, turn[0:1], turn[1:2])
    one, none = jnp.ones_like(decay), jnp.zeros_like(decay)
    from_left, from_right, turned, left, right = one, one, none, none, none
    for level in range(step + 1):
        second = (tile >> level) % 2 == 1
        if last or level == step:
            mine, came = (pairs[2 * level + k][...].astype(F32) for k in range(2))
            lower = jnp.where(second, came, mine)
            upper = jnp.where(second, mine, came)
            bent = turn * lower[0] + upper[1]
        if last:
            left = left + jnp.where(second, from_left * lower[0], 0.0)
            right = right + jnp.where(second, turned * lower[0], from_right * bent)
            turned = jnp.where(second, turned * decay, turned + from_right * turn * decay)
            from_left = jnp.where(second, from_left * decay, from_left)
            from_right = jnp.where(second, from_right, from_right * decay)
        elif level == step:
            left = decay * lower[0] + upper[0]
            right = lower[1] + decay * bent
        turn = turn * (1.0 + decay * decay)
        decay = decay * decay
    out_ref[0] = left.astype(BF16)
    out_ref[1] = right.astype(BF16)


def merge_call(table, entries, pairs, after, levels, last):
    step = len(pairs) // 2 - 1
    vmem, smem = pl.BlockSpec(memory_space=pltpu.VMEM), pl.BlockSpec(memory_space=pltpu.SMEM)
    held = [pl.BlockSpec(memory_space=pl.ANY)] * len(after)
    return pl.pallas_call(
        functools.partial(merge_kernel, levels, last, step, len(after)),
        name="merge",
        in_specs=[smem] + [vmem] * (1 + len(pairs)) + held,
        out_specs=[vmem] + held,
        out_shape=[jax.ShapeDtypeStruct(array.shape, array.dtype) for array in [pairs[0], *after]],
        input_output_aliases={2 + len(pairs) + k: 1 + k for k in range(len(after))},
        compiler_params=pltpu.CompilerParams(vmem_limit_bytes=VMEM),
        cost_estimate=pl.CostEstimate(flops=10**6, bytes_accessed=MIB // 4, transcendentals=0),
    )(table, entries, *pairs, *after)


def body(field, vert_filter, loc_filter, alpha_table, xscale_idx, yscale_idx, members):
    tile_count, mem_count = lax.axis_size("tile"), lax.axis_size("mem")
    slab_count, cols, rows = field.shape
    levels = vert_filter.shape[1]
    own_cols = cols // mem_count
    slabs = padded(slab_count)

    def swap(array, flip, axis="mem"):
        return lax.ppermute(array, axis, [(i, i ^ flip) for i in range(lax.axis_size(axis))])

    flat_field = pltpu.with_memory_space_constraint(field.reshape(slab_count * cols, rows), pltpu.HBM)
    mine = members.reshape(slab_count * cols, rows)
    other = swap(mine, 1)
    mem = lax.axis_index("mem").astype(jnp.int32).reshape(1)
    alpha_table = pltpu.with_memory_space_constraint(alpha_table, pltpu.HBM)
    xscale_idx = pltpu.with_memory_space_constraint(xscale_idx, pltpu.HBM)
    block = ends_call(mem, alpha_table, xscale_idx, flat_field, levels, cols)

    pairs, span, step = [], 1, 0
    while span < tile_count:
        pairs += [block, swap(block, span, "tile")]
        span, last = 2 * span, 2 * span >= tile_count
        if step == 0:
            own, coef = local_call(alpha_table, xscale_idx, flat_field, block, levels, cols, own_cols)
            block, own = merge_call(alpha_table, xscale_idx, pairs, [own], levels, last)
        elif step == 1:
            send, keep = ensemble_call(loc_filter[0], field.reshape(slab_count * cols, rows), mine, other, block, levels, cols, own_cols)
            block, send = merge_call(alpha_table, xscale_idx, pairs, [send], levels, last)
            came = swap(send, 2)
        elif step == 2:
            mats, row_coef, vert = tables_call(
                alpha_table, yscale_idx, vert_filter[0], block, levels, own_cols, cols, slabs
            )
            block, mats = merge_call(alpha_table, xscale_idx, pairs, [mats], levels, last)
        else:
            (block,) = merge_call(alpha_table, xscale_idx, pairs, [], levels, last)
        step += 1
    shares = [block] + [swap(block, flip) for flip in range(1, mem_count)]
    scale = 1.0 / (mem_count * members.shape[0] - 1)
    return final_call(slab_count, levels, scale, [own, coef, *shares, mats, row_coef, vert, keep, came])


def solution(mesh):
    return jax.shard_map(
        body,
        mesh=mesh,
        in_specs=(P(None, "tile", None), P(), P(), P(), P(), P(), P("mem", None, "tile", None)),
        out_specs=P(None, ("tile", "mem"), None),
        check_vma=False,
    )
```

```python
import functools

import jax
import jax.numpy as jnp
from jax import lax
from jax.experimental import pallas as pl
from jax.experimental.pallas import tpu as pltpu
from jax.sharding import PartitionSpec as P

F32, BF16 = jnp.float32, jnp.bfloat16
COL_BITS = 4
SUB = 16
SWEEP_LANES = 512
BLOCK = 256
MIB = 1 << 20
VMEM = 32 * MIB


def iota(shape, dim):
    return lax.broadcasted_iota(jnp.int32, shape, dim)


def dot(left, right):
    return jnp.dot(left, right, preferred_element_type=F32)


def gain_of(alpha):
    rest = (1.0 - alpha) * (1.0 + alpha)
    return jnp.sqrt(rest) * rest / jnp.sqrt(1.0 + alpha * alpha)


def lookup(table_ref, entries):
    found = jnp.zeros(entries.shape, F32)
    for entry in range(table_ref.shape[0]):
        found = jnp.where(entries == entry, table_ref[entry], found)
    return found


def padded(slab_count):
    return -(-slab_count // (4 * SUB)) * 4 * SUB


def to_columns(perm, flat_ref, out_ref, cols):
    total = flat_ref.shape[0]
    wanted = out_ref.shape[0]
    step = SUB * cols
    for chunk in range(out_ref.shape[1] // SUB):
        depth = min(step, total - chunk * step)
        part = flat_ref[chunk * step : chunk * step + depth, :]
        moved = dot(perm[:, :depth], part)
        out_ref[:, chunk * SUB : (chunk + 1) * SUB, :] = moved.reshape(wanted, SUB, -1)


def sweep(work, alpha):
    cols = work.shape[0]
    state = work[0]
    for col in range(1, cols):
        state = alpha * state + work[col]
        work[col] = state
    for col in range(cols - 2, -1, -1):
        state = alpha * state + work[col]
        work[col] = state


def transposer(cols):
    shape = (SUB * cols, SUB * cols)
    out_row, in_row = iota(shape, 0), iota(shape, 1)
    hit = (out_row % SUB == in_row // cols) & (out_row // SUB == in_row % cols)
    return hit.astype(BF16)


def ends_kernel(levels, slab_count, mem_ref, table_ref, entries_ref, field_ref, ends_ref, work):
    cols, _, lanes = work.shape
    first = mem_ref[0] * SUB
    shape = field_ref.shape
    held = jnp.where(iota(shape, 0) // cols + first < slab_count, field_ref[...], 0)
    work[...] = dot(transposer(cols), held).reshape(work.shape)
    pair = lookup(table_ref, entries_ref[...])
    alpha = jnp.where(iota((SUB, lanes), 0) + first < levels, pair[0:1], pair[1:2])
    sweep(work, alpha)
    gain = gain_of(alpha)
    ends_ref[0] = (gain * work[cols - 1]).astype(BF16)
    ends_ref[1] = (gain * work[0]).astype(BF16)


def ends_call(mem, table, entries, flat_field, levels, cols):
    total, rows = flat_field.shape
    return pl.pallas_call(
        functools.partial(ends_kernel, levels, total // cols),
        name="ends",
        grid_spec=pltpu.PrefetchScalarGridSpec(
            num_scalar_prefetch=1,
            grid=(1,),
            in_specs=[
                pl.BlockSpec(memory_space=pltpu.SMEM),
                pl.BlockSpec((2, rows), lambda i, mem: (0, i)),
                pl.BlockSpec((SUB * cols, rows), lambda i, mem: (mem[0], i)),
            ],
            out_specs=pl.BlockSpec((2, SUB, rows), lambda i, mem: (0, 0, i)),
            scratch_shapes=[pltpu.VMEM((cols, SUB, rows), F32)],
        ),
        out_shape=jax.ShapeDtypeStruct((2, SUB, rows), BF16),
        compiler_params=pltpu.CompilerParams(vmem_limit_bytes=VMEM),
        cost_estimate=pl.CostEstimate(flops=10**8, bytes_accessed=MIB, transcendentals=0),
    )(mem, table, entries, flat_field)


def local_kernel(levels, table_ref, entries_ref, field_ref, after_ref, own_ref, coef_ref, work):
    cols, slabs, lanes = work.shape
    own_cols = own_ref.shape[0]
    mem = lax.axis_index("mem")
    to_columns(transposer(cols), field_ref, work, cols)
    pair = lookup(table_ref, entries_ref[...])
    alpha = jnp.where(iota((slabs, lanes), 0) < levels, pair[0:1], pair[1:2])
    sweep(work, alpha)
    own_ref[...] = work[pl.ds(mem * own_cols, own_cols)] * gain_of(alpha)[None]
    square = pair * pair
    power, sums = jnp.ones_like(pair), jnp.zeros_like(pair)
    rights, geometric = [], []
    for _ in range(cols):
        power, sums = power * pair, sums * square + 1.0
        rights.append(power)
        geometric.append(sums)
    for col in range(cols):
        coef_ref[0, col] = rights[col] * geometric[cols - 1 - col]
        coef_ref[1, col] = rights[cols - 1 - col]


def local_call(table, entries, flat_field, after, levels, cols, own_cols):
    total, rows = flat_field.shape
    slabs = padded(total // cols)
    return pl.pallas_call(
        functools.partial(local_kernel, levels),
        name="local",
        grid=(rows // SWEEP_LANES,),
        in_specs=[
            pl.BlockSpec(memory_space=pltpu.SMEM),
            pl.BlockSpec((2, SWEEP_LANES), lambda i: (0, i)),
            pl.BlockSpec((total, SWEEP_LANES), lambda i: (0, i)),
            pl.BlockSpec(memory_space=pl.ANY),
        ],
        out_specs=[
            pl.BlockSpec((own_cols, slabs, SWEEP_LANES), lambda i: (0, 0, i)),
            pl.BlockSpec((2, cols, 2, SWEEP_LANES), lambda i: (0, 0, 0, i)),
        ],
        out_shape=[
            jax.ShapeDtypeStruct((own_cols, slabs, rows), F32),
            jax.ShapeDtypeStruct((2, cols, 2, rows), F32),
        ],
        scratch_shapes=[pltpu.VMEM((cols, slabs, SWEEP_LANES), F32)],
        compiler_params=pltpu.CompilerParams(vmem_limit_bytes=VMEM),
        cost_estimate=pl.CostEstimate(flops=5 * 10**8, bytes_accessed=4 * MIB, transcendentals=0),
    )(table, entries, flat_field, after)


def spread(matrix, levels, slabs, row_slab, row_col, col_slab, col_col):
    rows, cols = row_slab.shape
    size = matrix.shape[0]
    left = (iota((rows, size), 1) == row_slab[:, :size]).astype(BF16)
    right = (iota((size, cols), 0) == col_slab[:size, :]).astype(BF16)
    inner = dot(left, matrix).astype(BF16)
    full = dot(inner, right)
    full = jnp.where((row_slab >= levels) & (row_slab == col_slab), 1.0, full)
    return jnp.where(row_col == col_col, full, 0.0).astype(BF16)


def ensemble_kernel(levels, cols, loc_ref, field_ref, mine_ref, other_ref, after_ref, send_ref, keep_ref, *work):
    own_cols, count = work[0].shape[0] // 2, keep_ref.shape[0]
    _, slabs, lanes = work[0].shape
    mem = lax.axis_index("mem")
    core, chip = mem % 2, mem // 2
    shape = (2 * own_cols * SUB, cols * SUB)
    out_row, in_row = iota(shape, 0), iota(shape, 1)
    slot = out_row // SUB
    first = jnp.where(slot < own_cols, (2 * (1 - chip) + core) * own_cols, (2 * chip + core) * own_cols)
    hit = (out_row % SUB == in_row // cols) & (first + slot % own_cols == in_row % cols)
    perm = hit.astype(BF16)
    for ref, out in zip((field_ref, mine_ref, other_ref), work):
        to_columns(perm, ref, out, cols)
    side = own_cols * slabs
    row, col = iota((side, side), 0), iota((side, side), 1)
    local = spread(loc_ref[...], levels, slabs, row % slabs, row // slabs, col % slabs, col // slabs)
    order = ((row // own_cols == col % slabs) & (row % own_cols == col // slabs)).astype(BF16)
    for half, out_ref in enumerate((send_ref, keep_ref)):
        part = slice(half * own_cols, (half + 1) * own_cols)
        field = work[0][part]
        total = None
        for member_w in work[1:]:
            member = member_w[part]
            scaled = (member * field).astype(BF16).reshape(side, lanes)
            term = member * dot(local, scaled).reshape(own_cols, slabs, lanes)
            total = term if total is None else total + term
        total = total.reshape(side, lanes)
        high = total.astype(BF16)
        ordered = dot(order, high)
        if out_ref is keep_ref:
            ordered = ordered + dot(order, (total - high.astype(F32)).astype(BF16))
        out_ref[...] = ordered[:count].astype(out_ref.dtype)


def ensemble_call(half, loc, flat_field, mine, other, after, levels, cols, own_cols):
    total, rows = flat_field.shape
    slab_count, lanes = total // cols, rows // 2
    wide = pl.BlockSpec((total, lanes), lambda i: (0, half))
    out_shape = (slab_count * own_cols, lanes)
    out = pl.BlockSpec(out_shape, lambda i: (0, 0))
    return pl.pallas_call(
        functools.partial(ensemble_kernel, levels, cols),
        name="ensemble",
        grid=(1,),
        in_specs=[pl.BlockSpec(loc.shape, lambda i: (0, 0)), wide, wide, wide, pl.BlockSpec(memory_space=pl.ANY)],
        out_specs=[out, out],
        out_shape=[jax.ShapeDtypeStruct(out_shape, BF16), jax.ShapeDtypeStruct(out_shape, F32)],
        scratch_shapes=[pltpu.VMEM((2 * own_cols, padded(slab_count), lanes), F32)] * 3,
        compiler_params=pltpu.CompilerParams(vmem_limit_bytes=VMEM),
        cost_estimate=pl.CostEstimate(flops=5 * 10**8, bytes_accessed=4 * MIB, transcendentals=0),
    )(loc, flat_field, mine, other, after)


def tables_kernel(levels, own_cols, col_dev, slabs, table_ref, entries_ref, vert_ref, after_ref, mat_ref, coef_ref, vert_out):
    first = lax.axis_index("tile") * col_dev + lax.axis_index("mem") * own_cols
    count = 2 * own_cols
    alphas = [table_ref[entries_ref[var, first + col]] for var in range(2) for col in range(own_cols)]
    by_lane = jnp.zeros((1, 128), F32)
    by_row = jnp.zeros((count, 1), F32)
    for k, alpha in enumerate(alphas):
        by_lane = jnp.where(iota((1, 128), 1) == k, alpha, by_lane)
        by_row = jnp.where(iota((count, 1), 0) == k, alpha, by_row)

    def series(alpha, number):
        alpha = jnp.broadcast_to(alpha, number.shape)
        total, unit = jnp.zeros(number.shape, F32), jnp.ones(number.shape, F32)
        single, power, both = alpha, alpha * alpha, jnp.ones(number.shape, F32)
        for bit in range(BLOCK.bit_length()):
            here = (number >> bit) % 2 == 1
            total = jnp.where(here, unit + power * total, total)
            both = jnp.where(here, both * single, both)
            unit, single, power = unit * (1.0 + power), single * single, power * power
        return total, both

    down, _ = series(by_lane, BLOCK - iota((BLOCK, 128), 0))
    place = iota((count, BLOCK), 1)
    across, right = series(by_row, BLOCK - place)
    _, left = series(by_row, place + 1)
    coef_ref[0] = left * across
    coef_ref[1] = right
    coef_ref[2] = jnp.broadcast_to(right[:, 0:1], right.shape)
    coef_ref[3] = jnp.broadcast_to(left[:, 0:1] * across[:, 0:1], right.shape)
    far = jnp.abs(iota((BLOCK, BLOCK), 0) - iota((BLOCK, BLOCK), 1)).astype(F32)
    for k in range(count):
        alpha = by_row[k : k + 1]
        decay = jnp.exp(far * jnp.log(jnp.maximum(alpha, 1e-30)))
        reach = jnp.minimum(down[:, k : k + 1], across[k : k + 1])
        mat_ref[k] = (gain_of(alpha) * decay * reach).astype(BF16)
    shape = vert_out.shape
    row, col = iota(shape, 0), iota(shape, 1)
    vert_out[...] = spread(vert_ref[...], levels, slabs, row // own_cols, row % own_cols, col % slabs, col // slabs)


def tables_call(table, entries, vert, after, levels, own_cols, col_dev, slabs):
    count = 2 * own_cols
    smem = pl.BlockSpec(memory_space=pltpu.SMEM)
    return pl.pallas_call(
        functools.partial(tables_kernel, levels, own_cols, col_dev, slabs),
        name="tables",
        in_specs=[smem, smem, pl.BlockSpec(memory_space=pltpu.VMEM), pl.BlockSpec(memory_space=pl.ANY)],
        out_specs=[pl.BlockSpec(memory_space=pltpu.VMEM)] * 3,
        out_shape=[
            jax.ShapeDtypeStruct((count, BLOCK, BLOCK), BF16),
            jax.ShapeDtypeStruct((4, count, BLOCK), F32),
            jax.ShapeDtypeStruct((own_cols * slabs, own_cols * slabs), BF16),
        ],
        compiler_params=pltpu.CompilerParams(vmem_limit_bytes=VMEM),
        cost_estimate=pl.CostEstimate(flops=10**8, bytes_accessed=2 * MIB, transcendentals=0),
    )(table, entries, vert, after)


def along_rows(lines, matrix, coef):
    count, rows = lines.shape
    blocks = rows // BLOCK
    parts = jnp.concatenate([lines[:, b * BLOCK : (b + 1) * BLOCK] for b in range(blocks)], 0)
    local = dot(parts.astype(BF16), matrix)
    local = [local[b * count : (b + 1) * count] for b in range(blocks)]
    into, right, decay, turn = coef[0:1], coef[1:2], coef[2:3, 0:1], coef[3:4, 0:1]
    forward, state = [None], None
    for b in range(blocks - 1):
        end = local[b][:, BLOCK - 1 : BLOCK]
        state = end if state is None else decay * state + end
        forward.append(state)
    out, state = [None] * blocks, None
    for b in range(blocks - 1, -1, -1):
        piece = local[b]
        if forward[b] is not None:
            piece = piece + into * forward[b]
        if state is not None:
            piece = piece + right * state
        out[b] = piece
        if b:
            start = local[b][:, 0:1] + turn * forward[b]
            state = start if state is None else decay * state + start
    return out


def final_kernel(
    levels, scale, own_ref, coef_ref, mine_ref, core_ref, chip_ref, far_ref, mat_ref, row_coef_ref, vert_ref,
    keep_0_ref, keep_1_ref, came_0_ref, came_1_ref, out_ref, carry, smooth, filt
):
    own_cols, slabs, rows = own_ref.shape
    mem = lax.axis_index("mem")
    for flip, ref in ((0, mine_ref), (1, core_ref), (2, chip_ref), (3, far_ref)):
        share = pl.ds(pl.multiple_of((mem ^ flip) * SUB, SUB), SUB)
        carry[:, share, :] = ref[...].astype(F32)
    top = levels // 8 * 8
    for col in range(own_cols):
        pair = coef_ref[:, mem * own_cols + col]
        is_level = iota((slabs, rows), 0) < levels
        from_left = jnp.where(is_level, pair[0, 0:1], pair[0, 1:2])
        from_right = jnp.where(is_level, pair[1, 0:1], pair[1, 1:2])
        smooth[col] = own_ref[col] + from_left * carry[0] + from_right * carry[1]
    for col in range(own_cols):
        lines = smooth[col]
        main = along_rows(lines, mat_ref[col], row_coef_ref[:, col])
        last = along_rows(lines[top : top + 8], mat_ref[own_cols + col], row_coef_ref[:, own_cols + col])
        for b, (piece, extra) in enumerate(zip(main, last)):
            place = slice(b * BLOCK, (b + 1) * BLOCK)
            filt[col * slabs : col * slabs + slabs, place] = piece
            filt[col * slabs + top : col * slabs + top + 8, place] = jnp.where(
                iota((8, BLOCK), 0) < levels - top, piece[top : top + 8], extra
            )
    count = out_ref.shape[0]
    half = rows // 2
    for start in range(0, rows, BLOCK):
        part = slice(start, start + BLOCK)
        static = filt[:, part]
        high = static.astype(BF16)
        low = (static - high.astype(F32)).astype(BF16)
        total = dot(vert_ref[...], high) + dot(vert_ref[...], low)
        keep_ref, came_ref = ((keep_0_ref, came_0_ref), (keep_1_ref, came_1_ref))[start // half]
        inside = slice(start % half, start % half + BLOCK)
        ens = keep_ref[:, inside] + came_ref[:, inside].astype(F32)
        total = total[: count * own_cols] + ens * scale
        out_ref[:, :, part] = total.reshape(count, own_cols, BLOCK).astype(BF16)


def final_call(slab_count, levels, scale, args):
    own_cols, slabs, rows = args[0].shape
    vmem = pl.BlockSpec(memory_space=pltpu.VMEM)
    return pl.pallas_call(
        functools.partial(final_kernel, levels, scale),
        name="final",
        in_specs=[vmem] * len(args),
        out_specs=vmem,
        out_shape=jax.ShapeDtypeStruct((slab_count, own_cols, rows), BF16),
        scratch_shapes=[
            pltpu.VMEM((2, slabs, rows), F32),
            pltpu.VMEM((own_cols, slabs, rows), F32),
            pltpu.VMEM((own_cols * slabs, rows), F32),
        ],
        compiler_params=pltpu.CompilerParams(vmem_limit_bytes=VMEM),
        cost_estimate=pl.CostEstimate(flops=10**9, bytes_accessed=6 * MIB, transcendentals=0),
    )(*args)


def merge_kernel(levels, last, step, after_count, *refs):
    table_ref, entries_ref = refs[:2]
    pairs = refs[2 : 4 + 2 * step]
    out_ref = refs[4 + 2 * step + after_count]
    subs, rows = out_ref.shape[-2:]
    tile, mem = lax.axis_index("tile"), lax.axis_index("mem")
    pair = lookup(table_ref, entries_ref[...])
    decay, turn = pair, jnp.ones_like(pair)
    for _ in range(COL_BITS):
        turn = turn * (1.0 + decay * decay)
        decay = decay * decay
    turn = pair * turn
    is_level = iota((subs, rows), 0) + mem * SUB < levels
    decay = jnp.where(is_level, decay[0:1], decay[1:2])
    turn = jnp.where(is_level, turn[0:1], turn[1:2])
    one, none = jnp.ones_like(decay), jnp.zeros_like(decay)
    from_left, from_right, turned, left, right = one, one, none, none, none
    for level in range(step + 1):
        second = (tile >> level) % 2 == 1
        if last or level == step:
            mine, came = (pairs[2 * level + k][...].astype(F32) for k in range(2))
            if last and level == step:
                lower, upper = [jnp.where(second, came, mine)], [None, came]
            else:
                lower = jnp.where(second, came, mine)
                upper = jnp.where(second, mine, came)
            bent = turn * lower[0] + upper[1]
        if last:
            left = left + jnp.where(second, from_left * lower[0], 0.0)
            right = right + jnp.where(second, turned * lower[0], from_right * bent)
            turned = jnp.where(second, turned * decay, turned + from_right * turn * decay)
            from_left = jnp.where(second, from_left * decay, from_left)
            from_right = jnp.where(second, from_right, from_right * decay)
        elif level == step:
            left = decay * lower[0] + upper[0]
            right = lower[1] + decay * bent
        turn = turn * (1.0 + decay * decay)
        decay = decay * decay
    if len(out_ref.shape) == 2:
        second = (tile >> (step + 1)) % 2 == 1
        out_ref[...] = jnp.where(second, right, left).astype(BF16)
    else:
        out_ref[0] = left.astype(BF16)
        out_ref[1] = right.astype(BF16)


def merge_call(table, entries, pairs, after, levels, remaining):
    step = len(pairs) // 2 - 1
    out_shape = pairs[0].shape[1:] if remaining == 1 else pairs[0].shape
    vmem, smem = pl.BlockSpec(memory_space=pltpu.VMEM), pl.BlockSpec(memory_space=pltpu.SMEM)
    held = [pl.BlockSpec(memory_space=pl.ANY)] * len(after)
    return pl.pallas_call(
        functools.partial(merge_kernel, levels, remaining == 0, step, len(after)),
        name="merge",
        in_specs=[smem] + [vmem] * (1 + len(pairs)) + held,
        out_specs=[vmem] + held,
        out_shape=[jax.ShapeDtypeStruct(out_shape, BF16)]
        + [jax.ShapeDtypeStruct(array.shape, array.dtype) for array in after],
        input_output_aliases={2 + len(pairs) + k: 1 + k for k in range(len(after))},
        compiler_params=pltpu.CompilerParams(vmem_limit_bytes=VMEM),
        cost_estimate=pl.CostEstimate(flops=10**6, bytes_accessed=MIB // 4, transcendentals=0),
    )(table, entries, *pairs, *after)


def body(field, vert_filter, loc_filter, alpha_table, xscale_idx, yscale_idx, members):
    tile_count, mem_count = lax.axis_size("tile"), lax.axis_size("mem")
    slab_count, cols, rows = field.shape
    levels = vert_filter.shape[1]
    own_cols = cols // mem_count
    slabs = padded(slab_count)

    def swap(array, flip, axis="mem"):
        return lax.ppermute(array, axis, [(i, i ^ flip) for i in range(lax.axis_size(axis))])

    full_field = field.reshape(slab_count * cols, rows)
    flat_field = pltpu.with_memory_space_constraint(full_field, pltpu.HBM)
    mine = members.reshape(slab_count * cols, rows)
    held = pltpu.with_memory_space_constraint(mine, pltpu.HBM)
    other = swap(mine, 1)
    mem = lax.axis_index("mem").astype(jnp.int32).reshape(1)
    alpha_table = pltpu.with_memory_space_constraint(alpha_table, pltpu.HBM)
    xscale_idx = pltpu.with_memory_space_constraint(xscale_idx, pltpu.HBM)
    block = ends_call(mem, alpha_table, xscale_idx, flat_field, levels, cols)

    def ensemble(half, after):
        return ensemble_call(half, loc_filter[0], full_field, held, other, after, levels, cols, own_cols)

    def merge(pairs, after):
        return merge_call(alpha_table, xscale_idx, pairs, after, levels, steps - len(pairs) // 2)

    steps = tile_count.bit_length() - 1
    pairs = []
    for step in range(steps):
        pairs += [block, swap(block, 1 << step, "tile")]
        if step == 0:
            own, coef = local_call(alpha_table, xscale_idx, full_field, block, levels, cols, own_cols)
            send_0, keep_0 = ensemble(0, own)
            block, send_0 = merge(pairs, [send_0])
            came_0 = swap(send_0, 2)
        elif step == 1:
            send_1, keep_1 = ensemble(1, block)
            block, send_1 = merge(pairs, [send_1])
            came_1 = swap(send_1, 2)
        elif step == 2:
            mats, row_coef, vert = tables_call(
                alpha_table, yscale_idx, vert_filter[0], block, levels, own_cols, cols, slabs
            )
            block, mats = merge(pairs, [mats])
        else:
            (block,) = merge(pairs, [])
    shares = [block] + [swap(block, flip) for flip in range(1, mem_count)]
    scale = 1.0 / (mem_count * members.shape[0] - 1)
    ens = [keep_0, keep_1, came_0, came_1]
    return final_call(slab_count, levels, scale, [own, coef, *shares, mats, row_coef, vert, *ens])


def solution(mesh):
    return jax.shard_map(
        body,
        mesh=mesh,
        in_specs=(P(None, "tile", None), P(), P(), P(), P(), P(), P("mem", None, "tile", None)),
        out_specs=P(None, ("tile", "mem"), None),
        check_vma=False,
    )
```

```python
import functools

import jax
import jax.numpy as jnp
from jax import lax
from jax.experimental import pallas as pl
from jax.experimental.pallas import tpu as pltpu
from jax.sharding import PartitionSpec as P

F32, BF16 = jnp.float32, jnp.bfloat16
SUB = 16
CORES = 2
LANES = 256
BLOCK = 256
MIB = 1 << 20
VMEM = 32 * MIB


def iota(shape, dim):
    return lax.broadcasted_iota(jnp.int32, shape, dim)


def split(number, size):
    assert size & (size - 1) == 0
    return number >> (size.bit_length() - 1), number & (size - 1)


def dot(left, right):
    return jnp.dot(left, right, preferred_element_type=F32)


def gain_of(alpha):
    rest = (1.0 - alpha) * (1.0 + alpha)
    return jnp.sqrt(rest) * rest / jnp.sqrt(1.0 + alpha * alpha)


def lookup(table_ref, entries):
    found = jnp.zeros(entries.shape, F32)
    for entry in range(table_ref.shape[0]):
        found = jnp.where(entries == entry, table_ref[entry], found)
    return found


def padded(slab_count):
    return -(-slab_count // (4 * SUB)) * 4 * SUB


def to_columns(perm, flat, out_ref, cols):
    total = flat.shape[0]
    wanted = out_ref.shape[0]
    step = SUB * cols
    for chunk in range(out_ref.shape[1] // SUB):
        depth = min(step, total - chunk * step)
        moved = dot(perm[:, :depth], flat[chunk * step : chunk * step + depth])
        out_ref[:, chunk * SUB : (chunk + 1) * SUB, :] = moved.reshape(wanted, SUB, -1)


def sweep(work, alpha):
    cols = work.shape[0]
    state = work[0]
    for col in range(1, cols):
        state = alpha * state + work[col]
        work[col] = state
    for col in range(cols - 2, -1, -1):
        state = alpha * state + work[col]
        work[col] = state


def transposer(cols):
    shape = (SUB * cols, SUB * cols)
    (out_col, out_slab), (in_slab, in_col) = split(iota(shape, 0), SUB), split(iota(shape, 1), cols)
    return ((out_slab == in_slab) & (out_col == in_col)).astype(BF16)


def ends_kernel(levels, slab_count, core_ref, table_ref, entries_ref, field_ref, ends_ref, work):
    _, cols, subs, lanes = work.shape
    first = core_ref[0] * subs
    perm = transposer(cols)
    for chunk in range(work.shape[0]):
        part = slice(chunk * lanes, (chunk + 1) * lanes)
        held = jnp.where(iota((cols * subs, lanes), 0) < (slab_count - first) * cols, field_ref[:, part], 0)
        to_columns(perm, held, work.at[chunk], cols)
        pair = lookup(table_ref, entries_ref[:, part])
        alpha = jnp.where(iota((subs, lanes), 0) + first < levels, pair[0:1], pair[1:2])
        sweep(work.at[chunk], alpha)
        gain = gain_of(alpha)
        ends_ref[0, :, part] = (gain * work[chunk, cols - 1]).astype(BF16)
        ends_ref[1, :, part] = (gain * work[chunk, 0]).astype(BF16)


def ends_call(core, table, entries, flat_field, levels, cols):
    total, rows = flat_field.shape
    subs = padded(total // cols) // CORES
    return pl.pallas_call(
        functools.partial(ends_kernel, levels, total // cols),
        name="ends",
        grid_spec=pltpu.PrefetchScalarGridSpec(
            num_scalar_prefetch=1,
            grid=(1,),
            in_specs=[
                pl.BlockSpec(memory_space=pltpu.SMEM),
                pl.BlockSpec(entries.shape, lambda i, core: (0, 0)),
                pl.BlockSpec((subs * cols, rows), lambda i, core: (core[0], 0)),
            ],
            out_specs=pl.BlockSpec((2, subs, rows), lambda i, core: (0, 0, 0)),
            scratch_shapes=[pltpu.VMEM((rows // LANES, cols, subs, LANES), F32)],
        ),
        out_shape=jax.ShapeDtypeStruct((2, subs, rows), BF16),
        compiler_params=pltpu.CompilerParams(vmem_limit_bytes=VMEM),
        cost_estimate=pl.CostEstimate(flops=10**8, bytes_accessed=2 * MIB, transcendentals=0),
    )(core, table, entries, flat_field)


def line_coefs(pair, cols):
    decay, turn = pair, pair
    while cols > 1:
        turn = turn * (1.0 + decay * decay)
        decay = decay * decay
        cols //= 2
    return decay, turn


def local_kernel(levels, steps, table_ref, entries_ref, field_ref, after_ref, own_ref, coef_ref, work):
    _, cols, slabs, lanes = work.shape
    own_cols = own_ref.shape[0]
    tile, mem = lax.axis_index("tile"), lax.axis_index("mem")
    perm = transposer(cols)
    for chunk in range(work.shape[0]):
        part = slice(chunk * lanes, (chunk + 1) * lanes)
        to_columns(perm, field_ref.at[:, part], work.at[chunk], cols)
        pair = lookup(table_ref, entries_ref[:, part])
        alpha = jnp.where(iota((slabs, lanes), 0) < levels, pair[0:1], pair[1:2])
        sweep(work.at[chunk], alpha)
        own_ref[:, :, part] = work[chunk, pl.ds(mem * own_cols, own_cols)] * gain_of(alpha)[None]
    pair = lookup(table_ref, entries_ref[...])
    square = pair * pair
    power, sums = jnp.ones_like(pair), jnp.zeros_like(pair)
    rights, geometric = [], []
    for _ in range(cols):
        power, sums = power * pair, sums * square + 1.0
        rights.append(power)
        geometric.append(sums)
    for col in range(cols):
        coef_ref[0, col] = rights[col] * geometric[cols - 1 - col]
        coef_ref[1, col] = rights[cols - 1 - col]
    decay, turn = line_coefs(pair, cols)
    from_left, from_right, turned = jnp.ones_like(pair), jnp.ones_like(pair), jnp.zeros_like(pair)
    for level in range(steps - 1):
        second = ((tile >> level) & 1) == 1
        turned = jnp.where(second, turned * decay, turned + from_right * turn * decay)
        from_left = jnp.where(second, from_left * decay, from_left)
        from_right = jnp.where(second, from_right, from_right * decay)
        turn = turn * (1.0 + decay * decay)
        decay = decay * decay
    second = ((tile >> (steps - 1)) & 1) == 1
    coef_ref[0, cols] = jnp.where(second, from_left, 0.0)
    coef_ref[1, cols] = jnp.where(second, turned, from_right)


def local_call(table, entries, flat_field, after, levels, steps, cols, own_cols):
    total, rows = flat_field.shape
    slabs = padded(total // cols)
    vmem, smem = pl.BlockSpec(memory_space=pltpu.VMEM), pl.BlockSpec(memory_space=pltpu.SMEM)
    return pl.pallas_call(
        functools.partial(local_kernel, levels, steps),
        name="local",
        in_specs=[smem, vmem, vmem, pl.BlockSpec(memory_space=pl.ANY)],
        out_specs=[vmem, vmem],
        out_shape=[
            jax.ShapeDtypeStruct((own_cols, slabs, rows), F32),
            jax.ShapeDtypeStruct((2, cols + 1, 2, rows), F32),
        ],
        scratch_shapes=[pltpu.VMEM((rows // LANES, cols, slabs, LANES), F32)],
        compiler_params=pltpu.CompilerParams(vmem_limit_bytes=VMEM),
        cost_estimate=pl.CostEstimate(flops=5 * 10**8, bytes_accessed=4 * MIB, transcendentals=0),
    )(table, entries, flat_field, after)


def spread(matrix, levels, row_slab, row_col, col_slab, col_col):
    rows, cols = row_slab.shape
    size = matrix.shape[0]
    left = (iota((rows, size), 1) == row_slab[:, :size]).astype(BF16)
    right = (iota((size, cols), 0) == col_slab[:size, :]).astype(BF16)
    inner = dot(left, matrix).astype(BF16)
    full = dot(inner, right)
    full = jnp.where((row_slab >= levels) & (row_slab == col_slab), 1.0, full)
    return jnp.where(row_col == col_col, full, 0.0).astype(BF16)


def ensemble_kernel(levels, cols, loc_ref, field_ref, mine_ref, other_ref, after_ref, send_ref, keep_ref, *work):
    own_cols, count = work[0].shape[0] // 2, keep_ref.shape[0]
    _, slabs, lanes = work[0].shape
    mem = lax.axis_index("mem")
    chip, core = split(mem, 2)
    shape = (2 * own_cols * SUB, cols * SUB)
    (slot, out_slab), (in_slab, in_col) = split(iota(shape, 0), SUB), split(iota(shape, 1), cols)
    first = jnp.where(slot < own_cols, (2 * (1 - chip) + core) * own_cols, (2 * chip + core) * own_cols)
    hit = (out_slab == in_slab) & (first + (slot & (own_cols - 1)) == in_col)
    perm = hit.astype(BF16)
    for ref, out in zip((field_ref, mine_ref, other_ref), work):
        to_columns(perm, ref, out, cols)
    side = own_cols * slabs
    row, col = iota((side, side), 0), iota((side, side), 1)
    (row_col, row_slab), (col_col, col_slab) = split(row, slabs), split(col, slabs)
    local = spread(loc_ref[...], levels, row_slab, row_col, col_slab, col_col)
    row_slab, row_col = split(row, own_cols)
    order = ((row_slab == col_slab) & (row_col == col_col)).astype(BF16)
    for half, out_ref in enumerate((send_ref, keep_ref)):
        part = slice(half * own_cols, (half + 1) * own_cols)
        field = work[0][part]
        total = None
        for member_w in work[1:]:
            member = member_w[part]
            scaled = (member * field).astype(BF16).reshape(side, lanes)
            term = member * dot(local, scaled).reshape(own_cols, slabs, lanes)
            total = term if total is None else total + term
        total = total.reshape(side, lanes)
        high = total.astype(BF16)
        ordered = dot(order, high)
        if out_ref is keep_ref:
            ordered = ordered + dot(order, (total - high.astype(F32)).astype(BF16))
        out_ref[...] = ordered[:count].astype(out_ref.dtype)


def ensemble_call(loc, flat_field, mine, other, after, levels, cols, own_cols):
    total, rows = flat_field.shape
    slab_count = total // cols
    vmem = pl.BlockSpec(memory_space=pltpu.VMEM)
    out_shape = (slab_count * own_cols, rows)
    return pl.pallas_call(
        functools.partial(ensemble_kernel, levels, cols),
        name="ensemble",
        in_specs=[vmem] * 4 + [pl.BlockSpec(memory_space=pl.ANY)],
        out_specs=[vmem, vmem],
        out_shape=[jax.ShapeDtypeStruct(out_shape, BF16), jax.ShapeDtypeStruct(out_shape, F32)],
        scratch_shapes=[pltpu.VMEM((2 * own_cols, padded(slab_count), rows), F32)] * 3,
        compiler_params=pltpu.CompilerParams(vmem_limit_bytes=VMEM),
        cost_estimate=pl.CostEstimate(flops=5 * 10**8, bytes_accessed=8 * MIB, transcendentals=0),
    )(loc, flat_field, mine, other, after)


def tables_kernel(levels, own_cols, col_dev, slabs, table_ref, entries_ref, vert_ref, after_ref, mat_ref, coef_ref, vert_out):
    first = lax.axis_index("tile") * col_dev + lax.axis_index("mem") * own_cols
    count = 2 * own_cols
    alphas = [table_ref[entries_ref[var, first + col]] for var in range(2) for col in range(own_cols)]
    by_lane = jnp.zeros((1, 128), F32)
    by_row = jnp.zeros((count, 1), F32)
    for k, alpha in enumerate(alphas):
        by_lane = jnp.where(iota((1, 128), 1) == k, alpha, by_lane)
        by_row = jnp.where(iota((count, 1), 0) == k, alpha, by_row)

    def series(alpha, number):
        alpha = jnp.broadcast_to(alpha, number.shape)
        total, unit = jnp.zeros(number.shape, F32), jnp.ones(number.shape, F32)
        single, power, both = alpha, alpha * alpha, jnp.ones(number.shape, F32)
        for bit in range(BLOCK.bit_length()):
            here = ((number >> bit) & 1) == 1
            total = jnp.where(here, unit + power * total, total)
            both = jnp.where(here, both * single, both)
            unit, single, power = unit * (1.0 + power), single * single, power * power
        return total, both

    down, _ = series(by_lane, BLOCK - iota((BLOCK, 128), 0))
    place = iota((count, BLOCK), 1)
    across, right = series(by_row, BLOCK - place)
    _, left = series(by_row, place + 1)
    coef_ref[0] = left * across
    coef_ref[1] = right
    coef_ref[2] = jnp.broadcast_to(right[:, 0:1], right.shape)
    coef_ref[3] = jnp.broadcast_to(left[:, 0:1] * across[:, 0:1], right.shape)
    far = jnp.abs(iota((BLOCK, BLOCK), 0) - iota((BLOCK, BLOCK), 1)).astype(F32)
    for k in range(count):
        alpha = by_row[k : k + 1]
        decay = jnp.exp(far * jnp.log(jnp.maximum(alpha, 1e-30)))
        reach = jnp.minimum(down[:, k : k + 1], across[k : k + 1])
        mat_ref[k] = (gain_of(alpha) * decay * reach).astype(BF16)
    shape = vert_out.shape
    (row_slab, row_col), (col_col, col_slab) = split(iota(shape, 0), own_cols), split(iota(shape, 1), slabs)
    vert_out[...] = spread(vert_ref[...], levels, row_slab, row_col, col_slab, col_col)


def tables_call(table, entries, vert, after, levels, own_cols, col_dev, slabs):
    count = 2 * own_cols
    smem = pl.BlockSpec(memory_space=pltpu.SMEM)
    return pl.pallas_call(
        functools.partial(tables_kernel, levels, own_cols, col_dev, slabs),
        name="tables",
        in_specs=[smem, smem, pl.BlockSpec(memory_space=pltpu.VMEM), pl.BlockSpec(memory_space=pl.ANY)],
        out_specs=[pl.BlockSpec(memory_space=pltpu.VMEM)] * 3,
        out_shape=[
            jax.ShapeDtypeStruct((count, BLOCK, BLOCK), BF16),
            jax.ShapeDtypeStruct((4, count, BLOCK), F32),
            jax.ShapeDtypeStruct((own_cols * slabs, own_cols * slabs), BF16),
        ],
        compiler_params=pltpu.CompilerParams(vmem_limit_bytes=VMEM),
        cost_estimate=pl.CostEstimate(flops=10**8, bytes_accessed=2 * MIB, transcendentals=0),
    )(table, entries, vert, after)


def along_rows(lines, matrix, coef):
    count, rows = lines.shape
    blocks = rows // BLOCK
    parts = jnp.concatenate([lines[:, b * BLOCK : (b + 1) * BLOCK] for b in range(blocks)], 0)
    local = dot(parts.astype(BF16), matrix)
    local = [local[b * count : (b + 1) * count] for b in range(blocks)]
    into, right, decay, turn = coef[0:1], coef[1:2], coef[2:3, 0:1], coef[3:4, 0:1]
    forward, state = [None], None
    for b in range(blocks - 1):
        end = local[b][:, BLOCK - 1 : BLOCK]
        state = end if state is None else decay * state + end
        forward.append(state)
    out, state = [None] * blocks, None
    for b in range(blocks - 1, -1, -1):
        piece = local[b]
        if forward[b] is not None:
            piece = piece + into * forward[b]
        if state is not None:
            piece = piece + right * state
        out[b] = piece
        if b:
            start = local[b][:, 0:1] + turn * forward[b]
            state = start if state is None else decay * state + start
    return out


def final_kernel(
    levels, scale, own_ref, coef_ref, part_0_ref, part_1_ref, last_0_ref, last_1_ref, mat_ref, row_coef_ref, vert_ref,
    keep_ref, came_ref, out_ref, carry, last, smooth, filt
):
    own_cols, slabs, rows = own_ref.shape
    cols = coef_ref.shape[1] - 1
    mem = lax.axis_index("mem")
    subs = slabs // CORES
    core = mem & (CORES - 1)
    for flip, part_ref, last_ref in ((0, part_0_ref, last_0_ref), (1, part_1_ref, last_1_ref)):
        share = pl.ds(pl.multiple_of((core ^ flip) * subs, subs), subs)
        carry[:, share, :] = part_ref[...].astype(F32)
        last[share, :] = last_ref[...].astype(F32)
    top = levels // 8 * 8
    is_level = iota((8, rows), 0) < levels - top
    for side in range(2):
        old = carry[side, top : top + 8]
        carry[side] = carry[side] + coef_ref[side, cols, 0:1] * last[...]
        other = old + coef_ref[side, cols, 1:2] * last[top : top + 8]
        carry[side, top : top + 8] = jnp.where(is_level, carry[side, top : top + 8], other)
    for col in range(own_cols):
        pair = coef_ref[:, mem * own_cols + col]
        smooth[col] = own_ref[col] + pair[0, 0:1] * carry[0] + pair[1, 0:1] * carry[1]
        end = slice(top, top + 8)
        other = own_ref[col, end] + pair[0, 1:2] * carry[0, end] + pair[1, 1:2] * carry[1, end]
        smooth[col, end] = jnp.where(is_level, smooth[col, end], other)
    for col in range(own_cols):
        lines = smooth[col]
        main = along_rows(lines, mat_ref[col], row_coef_ref[:, col])
        last = along_rows(lines[top : top + 8], mat_ref[own_cols + col], row_coef_ref[:, own_cols + col])
        for b, (piece, extra) in enumerate(zip(main, last)):
            place = slice(b * BLOCK, (b + 1) * BLOCK)
            filt[col * slabs : col * slabs + slabs, place] = piece
            filt[col * slabs + top : col * slabs + top + 8, place] = jnp.where(
                iota((8, BLOCK), 0) < levels - top, piece[top : top + 8], extra
            )
    count = out_ref.shape[0]
    for start in range(0, rows, BLOCK):
        part = slice(start, start + BLOCK)
        static = filt[:, part]
        high = static.astype(BF16)
        low = (static - high.astype(F32)).astype(BF16)
        total = dot(vert_ref[...], high) + dot(vert_ref[...], low)
        ens = keep_ref[:, part] + came_ref[:, part].astype(F32)
        total = total[: count * own_cols] + ens * scale
        out_ref[:, :, part] = total.reshape(count, own_cols, BLOCK).astype(BF16)


def final_call(slab_count, levels, scale, args):
    own_cols, slabs, rows = args[0].shape
    vmem = pl.BlockSpec(memory_space=pltpu.VMEM)
    return pl.pallas_call(
        functools.partial(final_kernel, levels, scale),
        name="final",
        in_specs=[vmem] * len(args),
        out_specs=vmem,
        out_shape=jax.ShapeDtypeStruct((slab_count, own_cols, rows), BF16),
        scratch_shapes=[
            pltpu.VMEM((2, slabs, rows), F32),
            pltpu.VMEM((slabs, rows), F32),
            pltpu.VMEM((own_cols, slabs, rows), F32),
            pltpu.VMEM((own_cols * slabs, rows), F32),
        ],
        compiler_params=pltpu.CompilerParams(vmem_limit_bytes=VMEM),
        cost_estimate=pl.CostEstimate(flops=10**9, bytes_accessed=6 * MIB, transcendentals=0),
    )(*args)


def merge_kernel(levels, cols, step, last, after_count, *refs):
    table_ref, entries_ref = refs[:2]
    pairs = refs[2 : 4 + 2 * step]
    out_ref, *part_ref = refs[4 + 2 * step + after_count :]
    _, subs, rows = pairs[0].shape
    tile, mem = lax.axis_index("tile"), lax.axis_index("mem")
    decay, turn = line_coefs(lookup(table_ref, entries_ref[...]), cols)
    is_level = iota((subs, rows), 0) + (mem & (CORES - 1)) * subs < levels
    decay = jnp.where(is_level, decay[0:1], decay[1:2])
    turn = jnp.where(is_level, turn[0:1], turn[1:2])
    from_left, from_right, turned, left, right = 1.0, 1.0, 0.0, 0.0, 0.0
    for level in range(step + 1):
        second = ((tile >> level) & 1) == 1
        if last or level == step:
            mine, came = (pairs[2 * level + k][...].astype(F32) for k in range(2))
            lower = jnp.where(second, came, mine)
            upper = jnp.where(second, mine, came)
            bent = turn * lower[0] + upper[1]
        if last:
            left = left + jnp.where(second, from_left * lower[0], 0.0)
            right = right + jnp.where(second, turned * lower[0], from_right * bent)
            turned = jnp.where(second, turned * decay, turned + from_right * turn * decay)
            from_left = jnp.where(second, from_left * decay, from_left)
            from_right = jnp.where(second, from_right, from_right * decay)
        if level == step:
            block = decay * lower[0] + upper[0], lower[1] + decay * bent
        turn = turn * (1.0 + decay * decay)
        decay = decay * decay
    if last:
        second = ((tile >> (step + 1)) & 1) == 1
        out_ref[...] = jnp.where(second, block[1], block[0]).astype(BF16)
        part_ref[0][0] = left.astype(BF16)
        part_ref[0][1] = jnp.where(second, right, right + from_right * turn * block[0]).astype(BF16)
    else:
        out_ref[0] = block[0].astype(BF16)
        out_ref[1] = block[1].astype(BF16)


def merge_call(table, entries, pairs, after, levels, cols, last):
    step = len(pairs) // 2 - 1
    whole = jax.ShapeDtypeStruct(pairs[0].shape, BF16)
    outs = [jax.ShapeDtypeStruct(whole.shape[1:], BF16), whole] if last else [whole]
    vmem, smem = pl.BlockSpec(memory_space=pltpu.VMEM), pl.BlockSpec(memory_space=pltpu.SMEM)
    held = [pl.BlockSpec(memory_space=pl.ANY)] * len(after)
    return pl.pallas_call(
        functools.partial(merge_kernel, levels, cols, step, last, len(after)),
        name="merge",
        in_specs=[smem] + [vmem] * (1 + len(pairs)) + held,
        out_specs=[vmem] * len(outs) + held,
        out_shape=outs + [jax.ShapeDtypeStruct(array.shape, array.dtype) for array in after],
        input_output_aliases={2 + len(pairs) + k: len(outs) + k for k in range(len(after))},
        compiler_params=pltpu.CompilerParams(vmem_limit_bytes=VMEM),
        cost_estimate=pl.CostEstimate(flops=10**6, bytes_accessed=MIB // 4, transcendentals=0),
    )(table, entries, *pairs, *after)


def body(field, vert_filter, loc_filter, alpha_table, xscale_idx, yscale_idx, members):
    tile_count, mem_count = lax.axis_size("tile"), lax.axis_size("mem")
    slab_count, cols, rows = field.shape
    levels = vert_filter.shape[1]
    own_cols = cols // mem_count
    slabs = padded(slab_count)
    steps = tile_count.bit_length() - 1

    def swap(array, flip, axis="mem"):
        return lax.ppermute(array, axis, [(i, i ^ flip) for i in range(lax.axis_size(axis))])

    def merge(pairs, after):
        last = len(pairs) == 2 * (steps - 1)
        return merge_call(alpha_table, xscale_idx, pairs, after, levels, cols, last)

    full_field = field.reshape(slab_count * cols, rows)
    flat_field = pltpu.with_memory_space_constraint(full_field, pltpu.HBM)
    mine = members.reshape(slab_count * cols, rows)
    other = swap(mine, 1)
    core = (lax.axis_index("mem") & (CORES - 1)).astype(jnp.int32).reshape(1)
    alpha_table = pltpu.with_memory_space_constraint(alpha_table, pltpu.HBM)
    xscale_idx = pltpu.with_memory_space_constraint(xscale_idx, pltpu.HBM)
    block = ends_call(core, alpha_table, xscale_idx, flat_field, levels, cols)

    pairs = [block, swap(block, 1, "tile")]
    own, coef = local_call(alpha_table, xscale_idx, full_field, block, levels, steps, cols, own_cols)
    send, keep = ensemble_call(loc_filter[0], full_field, mine, other, own, levels, cols, own_cols)
    block, send = merge(pairs, [send])
    came = swap(send, 2)
    pairs += [block, swap(block, 2, "tile")]
    mats, row_coef, vert = tables_call(alpha_table, yscale_idx, vert_filter[0], block, levels, own_cols, cols, slabs)
    held = [mats]
    for step in range(2, steps):
        block, *rest = merge(pairs, held)
        if held:
            mats, held = rest.pop(), []
        if step < steps - 1:
            pairs += [block, swap(block, 1 << step, "tile")]
    last = swap(block, tile_count // 2, "tile")
    shares = [rest[0], swap(rest[0], 1), last, swap(last, 1)]
    scale = 1.0 / (mem_count * members.shape[0] - 1)
    return final_call(slab_count, levels, scale, [own, coef, *shares, mats, row_coef, vert, keep, came])


def solution(mesh):
    return jax.shard_map(
        body,
        mesh=mesh,
        in_specs=(P(None, "tile", None), P(), P(), P(), P(), P(), P("mem", None, "tile", None)),
        out_specs=P(None, ("tile", "mem"), None),
        check_vma=False,
    )
```

```python
import functools

import jax
import jax.numpy as jnp
from jax import lax
from jax.experimental import pallas as pl
from jax.experimental.pallas import tpu as pltpu
from jax.sharding import PartitionSpec as P

F32, BF16 = jnp.float32, jnp.bfloat16
SUB = 16
CORES = 2
LANES = 256
BLOCK = 256
MIB = 1 << 20
VMEM = 32 * MIB


def iota(shape, dim):
    return lax.broadcasted_iota(jnp.int32, shape, dim)


def taking(microseconds):
    return pl.CostEstimate(flops=int(microseconds * 1.15e9), bytes_accessed=MIB // 4, transcendentals=0)


def split(number, size):
    assert size & (size - 1) == 0
    return number >> (size.bit_length() - 1), number & (size - 1)


def dot(left, right):
    return jnp.dot(left, right, preferred_element_type=F32)


def gain_of(alpha):
    rest = (1.0 - alpha) * (1.0 + alpha)
    return jnp.sqrt(rest) * rest / jnp.sqrt(1.0 + alpha * alpha)


def lookup(table_ref, entries):
    found = jnp.zeros(entries.shape, F32)
    for entry in range(table_ref.shape[0]):
        found = jnp.where(entries == entry, table_ref[entry], found)
    return found


def padded(slab_count):
    return -(-slab_count // (4 * SUB)) * 4 * SUB


def to_columns(perm, flat, out_ref, cols):
    total = flat.shape[0]
    wanted = out_ref.shape[0]
    step = SUB * cols
    for chunk in range(out_ref.shape[1] // SUB):
        depth = min(step, total - chunk * step)
        moved = dot(perm[:, :depth], flat[chunk * step : chunk * step + depth])
        out_ref[:, chunk * SUB : (chunk + 1) * SUB, :] = moved.reshape(wanted, SUB, -1).astype(out_ref.dtype)


def sweep(work, alpha):
    cols = work.shape[0]
    state = work[0]
    for col in range(1, cols):
        state = alpha * state + work[col]
        work[col] = state
    for col in range(cols - 2, -1, -1):
        state = alpha * state + work[col]
        work[col] = state


def transposer(cols):
    shape = (SUB * cols, SUB * cols)
    (out_col, out_slab), (in_slab, in_col) = split(iota(shape, 0), SUB), split(iota(shape, 1), cols)
    return ((out_slab == in_slab) & (out_col == in_col)).astype(BF16)


def line_coefs(pair, cols):
    decay, turn = pair, pair
    while cols > 1:
        turn = turn * (1.0 + decay * decay)
        decay = decay * decay
        cols //= 2
    return decay, turn


def reflected(decay, turn, tile, steps):
    behind = (1 << steps) - 1 - tile
    total, power = jnp.zeros_like(turn), jnp.ones_like(turn)
    for level in range(steps):
        here = ((behind >> level) & 1) == 1
        total = jnp.where(here, total + power * power * turn, total)
        power = jnp.where(here, power * decay, power)
        turn = turn * (1.0 + decay * decay)
        decay = decay * decay
    return total


def ends_kernel(levels, steps, slab_count, core_ref, table_ref, entries_ref, field_ref, ends_ref, work):
    _, cols, subs, lanes = work.shape
    first = core_ref[0] * subs
    tile = lax.axis_index("tile")
    perm = transposer(cols)
    for chunk in range(work.shape[0]):
        part = slice(chunk * lanes, (chunk + 1) * lanes)
        held = jnp.where(iota((cols * subs, lanes), 0) < (slab_count - first) * cols, field_ref[:, part], 0)
        to_columns(perm, held, work.at[chunk], cols)
        pair = lookup(table_ref, entries_ref[:, part])
        is_level = iota((subs, lanes), 0) + first < levels
        alpha = jnp.where(is_level, pair[0:1], pair[1:2])
        sweep(work.at[chunk], alpha)
        gain = gain_of(alpha)
        decay, turn = line_coefs(pair, cols)
        behind = decay * reflected(decay, turn, tile, steps)
        behind = jnp.where(is_level, behind[0:1], behind[1:2])
        forward = gain * work[chunk, cols - 1]
        ends_ref[0, :, part] = forward.astype(BF16)
        ends_ref[1, :, part] = (gain * work[chunk, 0] + behind * forward).astype(BF16)


def ends_call(core, table, entries, flat_field, levels, steps, cols):
    total, rows = flat_field.shape
    subs = padded(total // cols) // CORES
    return pl.pallas_call(
        functools.partial(ends_kernel, levels, steps, total // cols),
        name="ends",
        grid_spec=pltpu.PrefetchScalarGridSpec(
            num_scalar_prefetch=1,
            grid=(1,),
            in_specs=[
                pl.BlockSpec(memory_space=pltpu.SMEM),
                pl.BlockSpec(entries.shape, lambda i, core: (0, 0)),
                pl.BlockSpec((subs * cols, rows), lambda i, core: (core[0], 0)),
            ],
            out_specs=pl.BlockSpec((2, subs, rows), lambda i, core: (0, 0, 0)),
            scratch_shapes=[pltpu.VMEM((rows // LANES, cols, subs, LANES), F32)],
        ),
        out_shape=jax.ShapeDtypeStruct((2, subs, rows), BF16),
        compiler_params=pltpu.CompilerParams(vmem_limit_bytes=VMEM),
        cost_estimate=taking(2.1),
    )(core, table, entries, flat_field)


def local_kernel(levels, steps, table_ref, entries_ref, field_ref, after_ref, own_ref, coef_ref, work):
    _, cols, slabs, lanes = work.shape
    own_cols = own_ref.shape[0]
    tile, mem = lax.axis_index("tile"), lax.axis_index("mem")
    perm = transposer(cols)
    for chunk in range(work.shape[0]):
        part = slice(chunk * lanes, (chunk + 1) * lanes)
        to_columns(perm, field_ref.at[:, part], work.at[chunk], cols)
        pair = lookup(table_ref, entries_ref[:, part])
        alpha = jnp.where(iota((slabs, lanes), 0) < levels, pair[0:1], pair[1:2])
        sweep(work.at[chunk], alpha)
        own_ref[:, :, part] = work[chunk, pl.ds(mem * own_cols, own_cols)] * gain_of(alpha)[None]
    pair = lookup(table_ref, entries_ref[...])
    square = pair * pair
    power, sums = jnp.ones_like(pair), jnp.zeros_like(pair)
    rights, geometric = [], []
    for _ in range(cols):
        power, sums = power * pair, sums * square + 1.0
        rights.append(power)
        geometric.append(sums)
    for col in range(cols):
        coef_ref[0, col] = rights[col] * geometric[cols - 1 - col]
        coef_ref[1, col] = rights[cols - 1 - col]
    decay, turn = line_coefs(pair, cols)
    behind = decay * reflected(decay, turn, tile, steps)
    from_left, from_right = jnp.ones_like(pair), jnp.ones_like(pair)
    for level in range(steps - 2):
        second = ((tile >> level) & 1) == 1
        from_left = jnp.where(second, from_left * decay, from_left)
        from_right = jnp.where(second, from_right, from_right * decay)
        decay = decay * decay
    quarter = tile >> (steps - 2)
    outer = (quarter == 0) | (quarter == 3)
    for flip, weight in ((1, 1.0), (2, decay), (3, jnp.where(outer, decay * decay, 1.0))):
        upper = (quarter ^ flip) < quarter
        coef_ref[0, cols + flip - 1] = jnp.where(upper, from_left * weight, 0.0)
        coef_ref[1, cols + flip - 1] = weight * jnp.where(upper, behind * from_left, from_right)


def local_call(table, entries, flat_field, after, levels, steps, cols, own_cols):
    total, rows = flat_field.shape
    slabs = padded(total // cols)
    vmem, smem = pl.BlockSpec(memory_space=pltpu.VMEM), pl.BlockSpec(memory_space=pltpu.SMEM)
    return pl.pallas_call(
        functools.partial(local_kernel, levels, steps),
        name="local",
        in_specs=[smem, vmem, vmem, pl.BlockSpec(memory_space=pl.ANY)],
        out_specs=[vmem, vmem],
        out_shape=[
            jax.ShapeDtypeStruct((own_cols, slabs, rows), F32),
            jax.ShapeDtypeStruct((2, cols + 3, 2, rows), F32),
        ],
        scratch_shapes=[pltpu.VMEM((rows // LANES, cols, slabs, LANES), F32)],
        compiler_params=pltpu.CompilerParams(vmem_limit_bytes=VMEM),
        cost_estimate=taking(2.1),
    )(table, entries, flat_field, after)


def spread(matrix, levels, row_slab, row_col, col_slab, col_col):
    rows, cols = row_slab.shape
    size = matrix.shape[0]
    left = (iota((rows, size), 1) == row_slab[:, :size]).astype(BF16)
    right = (iota((size, cols), 0) == col_slab[:size, :]).astype(BF16)
    inner = dot(left, matrix).astype(BF16)
    full = dot(inner, right)
    full = jnp.where((row_slab >= levels) & (row_slab == col_slab), 1.0, full)
    return jnp.where(row_col == col_col, full, 0.0).astype(BF16)


def member_term(local, member_w, field_w, part):
    cols, slabs, rows = field_w[part].shape
    member = member_w[part]
    scaled = (member * field_w[part].astype(F32)).astype(BF16).reshape(cols * slabs, rows)
    return member * dot(local, scaled).reshape(cols, slabs, rows)


def mine_kernel(
    levels, cols, loc_ref, field_ref, mine_ref, after_ref, perm_ref, local_ref, order_ref, field_out, total_out, member_w
):
    own_cols = field_out.shape[0] // 2
    slabs = field_out.shape[1]
    chip, core = split(lax.axis_index("mem"), 2)
    (slot, out_slab), (in_slab, in_col) = split(iota(perm_ref.shape, 0), SUB), split(iota(perm_ref.shape, 1), cols)
    first = jnp.where(slot < own_cols, (2 * (1 - chip) + core) * own_cols, (2 * chip + core) * own_cols)
    hit = (out_slab == in_slab) & (first + (slot & (own_cols - 1)) == in_col)
    perm = hit.astype(BF16)
    perm_ref[...] = perm
    row, col = iota(local_ref.shape, 0), iota(local_ref.shape, 1)
    (row_col, row_slab), (col_col, col_slab) = split(row, slabs), split(col, slabs)
    local = spread(loc_ref[...], levels, row_slab, row_col, col_slab, col_col)
    local_ref[...] = local
    row_slab, row_col = split(row, own_cols)
    order_ref[...] = ((row_slab == col_slab) & (row_col == col_col)).astype(BF16)
    to_columns(perm, field_ref, field_out, cols)
    to_columns(perm, mine_ref, member_w, cols)
    for part in (slice(0, own_cols), slice(own_cols, 2 * own_cols)):
        total_out[part] = member_term(local, member_w, field_out, part)


def other_kernel(cols, perm_ref, local_ref, order_ref, field_w, total_ref, other_ref, send_ref, keep_ref, member_w):
    own_cols, count = field_w.shape[0] // 2, keep_ref.shape[0]
    to_columns(perm_ref[...], other_ref, member_w, cols)
    for part, out_ref in ((slice(0, own_cols), send_ref), (slice(own_cols, 2 * own_cols), keep_ref)):
        total = total_ref[part] + member_term(local_ref[...], member_w, field_w, part)
        total = total.reshape(order_ref.shape[0], -1)
        high = total.astype(BF16)
        ordered = dot(order_ref[...], high)
        if out_ref is keep_ref:
            ordered = ordered + dot(order_ref[...], (total - high.astype(F32)).astype(BF16))
        out_ref[...] = ordered[:count].astype(out_ref.dtype)


def ensemble_calls(loc, flat_field, mine, other, after, levels, cols, own_cols):
    total, rows = flat_field.shape
    slab_count = total // cols
    slabs, side = padded(slab_count), own_cols * padded(slab_count)
    vmem = pl.BlockSpec(memory_space=pltpu.VMEM)
    work = (2 * own_cols, slabs, rows)
    held = pl.pallas_call(
        functools.partial(mine_kernel, levels, cols),
        name="mine",
        in_specs=[vmem] * 3 + [pl.BlockSpec(memory_space=pl.ANY)],
        out_specs=[vmem] * 5,
        out_shape=[
            jax.ShapeDtypeStruct((2 * own_cols * SUB, cols * SUB), BF16),
            jax.ShapeDtypeStruct((side, side), BF16),
            jax.ShapeDtypeStruct((side, side), BF16),
            jax.ShapeDtypeStruct(work, BF16),
            jax.ShapeDtypeStruct(work, F32),
        ],
        scratch_shapes=[pltpu.VMEM(work, F32)],
        compiler_params=pltpu.CompilerParams(vmem_limit_bytes=VMEM),
        cost_estimate=taking(1.8),
    )(loc, flat_field, mine, after)
    out_shape = (slab_count * own_cols, rows)
    return pl.pallas_call(
        functools.partial(other_kernel, cols),
        name="other",
        in_specs=[vmem] * 6,
        out_specs=[vmem, vmem],
        out_shape=[jax.ShapeDtypeStruct(out_shape, BF16), jax.ShapeDtypeStruct(out_shape, F32)],
        scratch_shapes=[pltpu.VMEM(work, F32)],
        compiler_params=pltpu.CompilerParams(vmem_limit_bytes=VMEM),
        cost_estimate=taking(2.0),
    )(*held, other)


def tables_kernel(levels, own_cols, col_dev, slabs, table_ref, entries_ref, vert_ref, after_ref, mat_ref, coef_ref, vert_out):
    first = lax.axis_index("tile") * col_dev + lax.axis_index("mem") * own_cols
    count = 2 * own_cols
    alphas = [table_ref[entries_ref[var, first + col]] for var in range(2) for col in range(own_cols)]
    by_lane = jnp.zeros((1, 128), F32)
    by_row = jnp.zeros((count, 1), F32)
    for k, alpha in enumerate(alphas):
        by_lane = jnp.where(iota((1, 128), 1) == k, alpha, by_lane)
        by_row = jnp.where(iota((count, 1), 0) == k, alpha, by_row)

    def series(alpha, number):
        alpha = jnp.broadcast_to(alpha, number.shape)
        total, unit = jnp.zeros(number.shape, F32), jnp.ones(number.shape, F32)
        single, power, both = alpha, alpha * alpha, jnp.ones(number.shape, F32)
        for bit in range(BLOCK.bit_length()):
            here = ((number >> bit) & 1) == 1
            total = jnp.where(here, unit + power * total, total)
            both = jnp.where(here, both * single, both)
            unit, single, power = unit * (1.0 + power), single * single, power * power
        return total, both

    down, _ = series(by_lane, BLOCK - iota((BLOCK, 128), 0))
    place = iota((count, BLOCK), 1)
    across, right = series(by_row, BLOCK - place)
    _, left = series(by_row, place + 1)
    coef_ref[0] = left * across
    coef_ref[1] = right
    coef_ref[2] = jnp.broadcast_to(right[:, 0:1], right.shape)
    coef_ref[3] = jnp.broadcast_to(left[:, 0:1] * across[:, 0:1], right.shape)
    far = jnp.abs(iota((BLOCK, BLOCK), 0) - iota((BLOCK, BLOCK), 1)).astype(F32)
    for k in range(count):
        alpha = by_row[k : k + 1]
        decay = jnp.exp(far * jnp.log(jnp.maximum(alpha, 1e-30)))
        reach = jnp.minimum(down[:, k : k + 1], across[k : k + 1])
        mat_ref[k] = (gain_of(alpha) * decay * reach).astype(BF16)
    shape = vert_out.shape
    (row_slab, row_col), (col_col, col_slab) = split(iota(shape, 0), own_cols), split(iota(shape, 1), slabs)
    vert_out[...] = spread(vert_ref[...], levels, row_slab, row_col, col_slab, col_col)


def tables_call(table, entries, vert, after, levels, own_cols, col_dev, slabs):
    count = 2 * own_cols
    smem = pl.BlockSpec(memory_space=pltpu.SMEM)
    return pl.pallas_call(
        functools.partial(tables_kernel, levels, own_cols, col_dev, slabs),
        name="tables",
        in_specs=[smem, smem, pl.BlockSpec(memory_space=pltpu.VMEM), pl.BlockSpec(memory_space=pl.ANY)],
        out_specs=[pl.BlockSpec(memory_space=pltpu.VMEM)] * 3,
        out_shape=[
            jax.ShapeDtypeStruct((count, BLOCK, BLOCK), BF16),
            jax.ShapeDtypeStruct((4, count, BLOCK), F32),
            jax.ShapeDtypeStruct((own_cols * slabs, own_cols * slabs), BF16),
        ],
        compiler_params=pltpu.CompilerParams(vmem_limit_bytes=VMEM),
        cost_estimate=taking(1.5),
    )(table, entries, vert, after)


def along_rows(lines, matrix, coef):
    count, rows = lines.shape
    blocks = rows // BLOCK
    parts = jnp.concatenate([lines[:, b * BLOCK : (b + 1) * BLOCK] for b in range(blocks)], 0)
    local = dot(parts.astype(BF16), matrix)
    local = [local[b * count : (b + 1) * count] for b in range(blocks)]
    into, right, decay, turn = coef[0:1], coef[1:2], coef[2:3, 0:1], coef[3:4, 0:1]
    forward, state = [None], None
    for b in range(blocks - 1):
        end = local[b][:, BLOCK - 1 : BLOCK]
        state = end if state is None else decay * state + end
        forward.append(state)
    out, state = [None] * blocks, None
    for b in range(blocks - 1, -1, -1):
        piece = local[b]
        if forward[b] is not None:
            piece = piece + into * forward[b]
        if state is not None:
            piece = piece + right * state
        out[b] = piece
        if b:
            start = local[b][:, 0:1] + turn * forward[b]
            state = start if state is None else decay * state + start
    return out


def final_kernel(
    levels, scale, own_ref, coef_ref, mat_ref, row_coef_ref, vert_ref, keep_ref, came_ref, *refs
):
    own_cols, slabs, rows = own_ref.shape
    cols = coef_ref.shape[1] - 3
    mine, others, (out_ref, carry, last, smooth, filt) = refs[:4], refs[4:8], refs[8:]
    mem = lax.axis_index("mem")
    subs = slabs // CORES
    core = mem & (CORES - 1)
    for flip, (part_ref, *last_refs) in enumerate((mine, others)):
        share = pl.ds(pl.multiple_of((core ^ flip) * subs, subs), subs)
        carry[:, share, :] = part_ref[...].astype(F32)
        for k, last_ref in enumerate(last_refs):
            last[k, share, :] = last_ref[...].astype(F32)
    top = levels // 8 * 8
    is_level = iota((8, rows), 0) < levels - top
    for side in range(2):
        value, end = carry[side], carry[side, top : top + 8]
        for k in range(3):
            value = value + coef_ref[side, cols + k, 0:1] * last[k]
            end = end + coef_ref[side, cols + k, 1:2] * last[k, top : top + 8]
        carry[side] = value
        carry[side, top : top + 8] = jnp.where(is_level, carry[side, top : top + 8], end)
    for col in range(own_cols):
        pair = coef_ref[:, mem * own_cols + col]
        smooth[col] = own_ref[col] + pair[0, 0:1] * carry[0] + pair[1, 0:1] * carry[1]
        end = slice(top, top + 8)
        other = own_ref[col, end] + pair[0, 1:2] * carry[0, end] + pair[1, 1:2] * carry[1, end]
        smooth[col, end] = jnp.where(is_level, smooth[col, end], other)
    for col in range(own_cols):
        lines = smooth[col]
        main = along_rows(lines, mat_ref[col], row_coef_ref[:, col])
        last = along_rows(lines[top : top + 8], mat_ref[own_cols + col], row_coef_ref[:, own_cols + col])
        for b, (piece, extra) in enumerate(zip(main, last)):
            place = slice(b * BLOCK, (b + 1) * BLOCK)
            filt[col * slabs : col * slabs + slabs, place] = piece
            filt[col * slabs + top : col * slabs + top + 8, place] = jnp.where(
                iota((8, BLOCK), 0) < levels - top, piece[top : top + 8], extra
            )
    count = out_ref.shape[0]
    for start in range(0, rows, BLOCK):
        part = slice(start, start + BLOCK)
        static = filt[:, part]
        high = static.astype(BF16)
        low = (static - high.astype(F32)).astype(BF16)
        total = dot(vert_ref[...], high) + dot(vert_ref[...], low)
        ens = keep_ref[:, part] + came_ref[:, part].astype(F32)
        total = total[: count * own_cols] + ens * scale
        out_ref[:, :, part] = total.reshape(count, own_cols, BLOCK).astype(BF16)


def final_call(slab_count, levels, scale, args):
    own_cols, slabs, rows = args[0].shape
    vmem = pl.BlockSpec(memory_space=pltpu.VMEM)
    return pl.pallas_call(
        functools.partial(final_kernel, levels, scale),
        name="final",
        in_specs=[vmem] * len(args),
        out_specs=vmem,
        out_shape=jax.ShapeDtypeStruct((slab_count, own_cols, rows), BF16),
        scratch_shapes=[
            pltpu.VMEM((2, slabs, rows), F32),
            pltpu.VMEM((3, slabs, rows), F32),
            pltpu.VMEM((own_cols, slabs, rows), F32),
            pltpu.VMEM((own_cols * slabs, rows), F32),
        ],
        compiler_params=pltpu.CompilerParams(vmem_limit_bytes=VMEM),
        cost_estimate=taking(2.0),
    )(*args)


def merge_kernel(levels, cols, steps, step, last, after_count, *refs):
    table_ref, entries_ref, ends_ref = refs[:3]
    came_refs, outs = refs[3 : 3 + step], refs[3 + step + after_count :]
    _, subs, rows = ends_ref.shape
    tile, mem = lax.axis_index("tile"), lax.axis_index("mem")
    decay, turn = line_coefs(lookup(table_ref, entries_ref[...]), cols)
    is_level = iota((subs, rows), 0) + (mem & (CORES - 1)) * subs < levels
    behind = reflected(decay, turn, tile, steps)
    decay = jnp.where(is_level, decay[0:1], decay[1:2])
    behind = jnp.where(is_level, behind[0:1], behind[1:2])
    turned = behind * decay
    right, left = ends_ref[0].astype(F32), ends_ref[1].astype(F32)
    into_right, into_left, from_left, from_right = 0.0, behind * right, 1.0, 1.0
    for level, came_ref in enumerate(came_refs):
        second = ((tile >> level) & 1) == 1
        came_right, came_left = came_ref[0].astype(F32), came_ref[1].astype(F32)
        into_right = into_right + jnp.where(second, from_left * came_right, 0.0)
        into_left = into_left + jnp.where(second, 0.0, from_right * came_left)
        right = jnp.where(second, decay * came_right + right, decay * right + came_right)
        left = jnp.where(second, came_left + decay * left, left + decay * came_left)
        from_left = jnp.where(second, from_left * decay, from_left)
        from_right = jnp.where(second, from_right, from_right * decay)
        decay = decay * decay
    if last:
        quarter = tile >> (steps - 2)
        outs[0][...] = jnp.where((quarter & 1) == 1, left, right).astype(BF16)
        outs[1][...] = jnp.where(quarter >= 2, left, right).astype(BF16)
        outs[2][0] = into_right.astype(BF16)
        outs[2][1] = (into_left + turned * into_right).astype(BF16)
    else:
        outs[0][0] = right.astype(BF16)
        outs[0][1] = left.astype(BF16)


def merge_call(table, entries, ends, came, after, levels, cols, steps):
    last = len(came) == steps - 2
    whole = jax.ShapeDtypeStruct(ends.shape, BF16)
    one = jax.ShapeDtypeStruct(ends.shape[1:], BF16)
    outs = [one, one, whole] if last else [whole]
    vmem, smem = pl.BlockSpec(memory_space=pltpu.VMEM), pl.BlockSpec(memory_space=pltpu.SMEM)
    held = [pl.BlockSpec(memory_space=pl.ANY)] * len(after)
    return pl.pallas_call(
        functools.partial(merge_kernel, levels, cols, steps, len(came), last, len(after)),
        name="merge",
        in_specs=[smem] + [vmem] * (2 + len(came)) + held,
        out_specs=[vmem] * len(outs) + held,
        out_shape=outs + [jax.ShapeDtypeStruct(array.shape, array.dtype) for array in after],
        input_output_aliases={3 + len(came) + k: len(outs) + k for k in range(len(after))},
        compiler_params=pltpu.CompilerParams(vmem_limit_bytes=VMEM),
        cost_estimate=taking(0.8),
    )(table, entries, ends, *came, *after)


def body(field, vert_filter, loc_filter, alpha_table, xscale_idx, yscale_idx, members):
    tile_count, mem_count = lax.axis_size("tile"), lax.axis_size("mem")
    slab_count, cols, rows = field.shape
    levels = vert_filter.shape[1]
    own_cols = cols // mem_count
    slabs = padded(slab_count)
    steps = tile_count.bit_length() - 1

    def swap(array, flip, axis="mem"):
        return lax.ppermute(array, axis, [(i, i ^ flip) for i in range(lax.axis_size(axis))])

    full_field = field.reshape(slab_count * cols, rows)
    flat_field = pltpu.with_memory_space_constraint(full_field, pltpu.HBM)
    mine = members.reshape(slab_count * cols, rows)
    other = swap(mine, 1)
    core = (lax.axis_index("mem") & (CORES - 1)).astype(jnp.int32).reshape(1)
    alpha_table = pltpu.with_memory_space_constraint(alpha_table, pltpu.HBM)
    xscale_idx = pltpu.with_memory_space_constraint(xscale_idx, pltpu.HBM)
    ends = ends_call(core, alpha_table, xscale_idx, flat_field, levels, steps, cols)
    blocks, came = [ends], []
    send, keep = ensemble_calls(loc_filter[0], full_field, mine, other, ends, levels, cols, own_cols)
    over = swap(send, 2)
    own, coef = local_call(alpha_table, xscale_idx, full_field, send, levels, steps, cols, own_cols)
    for level in range(steps - 2):
        came.append(swap(blocks[0], 1 << level, "tile"))
        *blocks, own = merge_call(alpha_table, xscale_idx, ends, came, [own], levels, cols, steps)
    near, far, part = blocks
    last = {flip: swap(near if flip == 1 else far, flip << (steps - 2), "tile") for flip in (2, 3, 1)}
    mats, row_coef, vert = tables_call(alpha_table, yscale_idx, vert_filter[0], part, levels, own_cols, cols, slabs)
    shares = [part, last[1], last[2], last[3]]
    shares += [swap(share, 1) for share in shares]
    scale = 1.0 / (mem_count * members.shape[0] - 1)
    return final_call(slab_count, levels, scale, [own, coef, mats, row_coef, vert, keep, over, *shares])


def solution(mesh):
    return jax.shard_map(
        body,
        mesh=mesh,
        in_specs=(P(None, "tile", None), P(), P(), P(), P(), P(), P("mem", None, "tile", None)),
        out_specs=P(None, ("tile", "mem"), None),
        check_vma=False,
    )
```

```python
import functools

import jax
import jax.numpy as jnp
from jax import lax
from jax.experimental import pallas as pl
from jax.experimental.pallas import tpu as pltpu
from jax.sharding import PartitionSpec as P

F32, BF16 = jnp.float32, jnp.bfloat16
SUB = 16
CORES = 2
LANES = 256
BLOCK = 256
MIB = 1 << 20
VMEM = 32 * MIB


def iota(shape, dim):
    return lax.broadcasted_iota(jnp.int32, shape, dim)


def taking(microseconds):
    return pl.CostEstimate(flops=int(microseconds * 1.15e9), bytes_accessed=MIB // 4, transcendentals=0)


def split(number, size):
    assert size & (size - 1) == 0
    return number >> (size.bit_length() - 1), number & (size - 1)


def dot(left, right):
    return jnp.dot(left, right, preferred_element_type=F32)


def gain_of(alpha):
    rest = (1.0 - alpha) * (1.0 + alpha)
    return jnp.sqrt(rest) * rest / jnp.sqrt(1.0 + alpha * alpha)


def lookup(table_ref, entries):
    found = jnp.zeros(entries.shape, F32)
    for entry in range(table_ref.shape[0]):
        found = jnp.where(entries == entry, table_ref[entry], found)
    return found


def padded(slab_count):
    return -(-slab_count // (4 * SUB)) * 4 * SUB


def to_columns(perm, flat, out_ref, cols):
    total = flat.shape[0]
    wanted = out_ref.shape[0]
    step = SUB * cols
    for chunk in range(out_ref.shape[1] // SUB):
        depth = min(step, total - chunk * step)
        moved = dot(perm[:, :depth], flat[chunk * step : chunk * step + depth])
        out_ref[:, chunk * SUB : (chunk + 1) * SUB, :] = moved.reshape(wanted, SUB, -1).astype(out_ref.dtype)


def sweep(work, alpha):
    cols = work.shape[0]
    state = work[0]
    for col in range(1, cols):
        state = alpha * state + work[col]
        work[col] = state
    for col in range(cols - 2, -1, -1):
        state = alpha * state + work[col]
        work[col] = state


def transposer(cols):
    shape = (SUB * cols, SUB * cols)
    (out_col, out_slab), (in_slab, in_col) = split(iota(shape, 0), SUB), split(iota(shape, 1), cols)
    return ((out_slab == in_slab) & (out_col == in_col)).astype(BF16)


def share_rows(total, cols, subs, share):
    return slice(share * subs * cols, min((share + 1) * subs * cols, total))


def sweep_share(levels, slab_count, share, alpha, held, work):
    cols, subs, lanes = work.shape
    first = share * subs
    held = jnp.where(iota(held.shape, 0) < (slab_count - first) * cols, held, 0)
    to_columns(transposer(cols), held, work, cols)
    is_level = iota((subs, lanes), 0) + first < levels
    alpha = jnp.where(is_level, alpha[0:1], alpha[1:2])
    sweep(work, alpha)
    return gain_of(alpha), is_level


def ends_kernel(
    levels, steps, slab_count, share_ref, table_ref, entries_ref, field_ref, ends_ref, own_ref, lines_ref, work
):
    pieces, cols, subs, lanes = work.shape
    own_cols = own_ref.shape[0]
    tile, mem = lax.axis_index("tile"), lax.axis_index("mem")
    share = share_ref[0]
    pair = lookup(table_ref, entries_ref[...])
    decay, turn = line_coefs(pair, cols)
    behind = reflected(decay, turn, tile, steps)
    lines_ref[0], lines_ref[1], lines_ref[2] = pair, decay, behind
    for piece in range(pieces):
        part = slice(piece * lanes, (piece + 1) * lanes)
        gain, is_level = sweep_share(levels, slab_count, share, pair[:, part], field_ref[:, part], work.at[piece])
        turned = (decay * behind)[:, part]
        turned = jnp.where(is_level, turned[0:1], turned[1:2])
        forward = gain * work[piece, cols - 1]
        ends_ref[0, :, part] = forward.astype(BF16)
        ends_ref[1, :, part] = (gain * work[piece, 0] + turned * forward).astype(BF16)
        own_ref[:, :, part] = work[piece, pl.ds(mem * own_cols, own_cols)] * gain[None]


def ends_call(share, table, entries, flat_field, levels, steps, cols, own_cols):
    total, rows = flat_field.shape
    subs = padded(total // cols) // CORES
    vmem, smem = pl.BlockSpec(memory_space=pltpu.VMEM), pl.BlockSpec(memory_space=pltpu.SMEM)
    return pl.pallas_call(
        functools.partial(ends_kernel, levels, steps, total // cols),
        name="ends",
        grid_spec=pltpu.PrefetchScalarGridSpec(
            num_scalar_prefetch=1,
            grid=(1,),
            in_specs=[
                smem,
                pl.BlockSpec(entries.shape, lambda i, share: (0, 0)),
                pl.BlockSpec((subs * cols, rows), lambda i, share: (share[0], 0)),
            ],
            out_specs=[vmem] * 3,
            scratch_shapes=[pltpu.VMEM((rows // LANES, cols, subs, LANES), F32)],
        ),
        out_shape=[
            jax.ShapeDtypeStruct((2, subs, rows), BF16),
            jax.ShapeDtypeStruct((own_cols, subs, rows), F32),
            jax.ShapeDtypeStruct((3, 2, rows), F32),
        ],
        compiler_params=pltpu.CompilerParams(vmem_limit_bytes=VMEM),
        cost_estimate=taking(2.1),
    )(share, table, entries, flat_field)


def line_coefs(pair, cols):
    decay, turn = pair, pair
    while cols > 1:
        turn = turn * (1.0 + decay * decay)
        decay = decay * decay
        cols //= 2
    return decay, turn


def reflected(decay, turn, tile, steps):
    behind = (1 << steps) - 1 - tile
    total, power = jnp.zeros_like(turn), jnp.ones_like(turn)
    for level in range(steps):
        here = ((behind >> level) & 1) == 1
        total = jnp.where(here, total + power * power * turn, total)
        power = jnp.where(here, power * decay, power)
        turn = turn * (1.0 + decay * decay)
        decay = decay * decay
    return total


def local_kernel(levels, steps, slab_count, lines_ref, field_ref, after_ref, own_ref, coef_ref, held_ref, work):
    pieces, cols, subs, lanes = work.shape
    own_cols = own_ref.shape[0]
    tile, mem = lax.axis_index("tile"), lax.axis_index("mem")
    share = (mem & (CORES - 1)) ^ 1
    for core in range(CORES):
        rows = share_rows(slab_count * cols, cols, subs, core)

        @pl.when(share == core)
        def _():
            held_ref[0 : rows.stop - rows.start, :] = field_ref[rows, :]

    pair, decay, behind = lines_ref[0], lines_ref[1], lines_ref[2]
    for piece in range(pieces):
        part = slice(piece * lanes, (piece + 1) * lanes)
        gain, _ = sweep_share(levels, slab_count, share, pair[:, part], held_ref[:, part], work.at[piece])
        own_ref[:, :, part] = work[piece, pl.ds(mem * own_cols, own_cols)] * gain[None]
    square = pair * pair
    power, sums = jnp.ones_like(pair), jnp.zeros_like(pair)
    rights, geometric = [], []
    for _ in range(cols):
        power, sums = power * pair, sums * square + 1.0
        rights.append(power)
        geometric.append(sums)
    for col in range(cols):
        coef_ref[0, col] = rights[col] * geometric[cols - 1 - col]
        coef_ref[1, col] = rights[cols - 1 - col]
    turned = decay * behind
    from_left, from_right = jnp.ones_like(pair), jnp.ones_like(pair)
    for level in range(steps - 2):
        second = ((tile >> level) & 1) == 1
        from_left = jnp.where(second, from_left * decay, from_left)
        from_right = jnp.where(second, from_right, from_right * decay)
        decay = decay * decay
    quarter = tile >> (steps - 2)
    outer = (quarter == 0) | (quarter == 3)
    for flip, weight in ((1, 1.0), (2, decay), (3, jnp.where(outer, decay * decay, 1.0))):
        upper = (quarter ^ flip) < quarter
        coef_ref[0, cols + flip - 1] = jnp.where(upper, from_left * weight, 0.0)
        coef_ref[1, cols + flip - 1] = weight * jnp.where(upper, turned * from_left, from_right)


def local_call(lines, flat_field, after, levels, steps, cols, own_cols):
    total, rows = flat_field.shape
    subs = padded(total // cols) // CORES
    vmem = pl.BlockSpec(memory_space=pltpu.VMEM)
    return pl.pallas_call(
        functools.partial(local_kernel, levels, steps, total // cols),
        name="local",
        in_specs=[vmem, vmem, pl.BlockSpec(memory_space=pl.ANY)],
        out_specs=[vmem, vmem],
        out_shape=[
            jax.ShapeDtypeStruct((own_cols, subs, rows), F32),
            jax.ShapeDtypeStruct((2, cols + 3, 2, rows), F32),
        ],
        scratch_shapes=[
            pltpu.VMEM((subs * cols, rows), BF16),
            pltpu.VMEM((rows // LANES, cols, subs, LANES), F32),
        ],
        compiler_params=pltpu.CompilerParams(vmem_limit_bytes=VMEM),
        cost_estimate=taking(3.0),
    )(lines, flat_field, after)


def spread(matrix, levels, row_slab, row_col, col_slab, col_col):
    rows, cols = row_slab.shape
    size = matrix.shape[0]
    left = (iota((rows, size), 1) == row_slab[:, :size]).astype(BF16)
    right = (iota((size, cols), 0) == col_slab[:size, :]).astype(BF16)
    inner = dot(left, matrix).astype(BF16)
    full = dot(inner, right)
    full = jnp.where((row_slab >= levels) & (row_slab == col_slab), 1.0, full)
    return jnp.where(row_col == col_col, full, 0.0).astype(BF16)


def member_term(local, member_w, field_w, part):
    cols, slabs, rows = field_w[part].shape
    member = member_w[part]
    scaled = (member * field_w[part].astype(F32)).astype(BF16).reshape(cols * slabs, rows)
    return member * dot(local, scaled).reshape(cols, slabs, rows)


def mine_kernel(
    levels, cols, loc_ref, field_ref, mine_ref, after_ref, perm_ref, local_ref, order_ref, field_out, total_out, member_w
):
    own_cols = field_out.shape[0] // 2
    slabs = field_out.shape[1]
    chip, core = split(lax.axis_index("mem"), 2)
    (slot, out_slab), (in_slab, in_col) = split(iota(perm_ref.shape, 0), SUB), split(iota(perm_ref.shape, 1), cols)
    first = jnp.where(slot < own_cols, (2 * (1 - chip) + core) * own_cols, (2 * chip + core) * own_cols)
    hit = (out_slab == in_slab) & (first + (slot & (own_cols - 1)) == in_col)
    perm = hit.astype(BF16)
    perm_ref[...] = perm
    row, col = iota(local_ref.shape, 0), iota(local_ref.shape, 1)
    (row_col, row_slab), (col_col, col_slab) = split(row, slabs), split(col, slabs)
    local = spread(loc_ref[...], levels, row_slab, row_col, col_slab, col_col)
    local_ref[...] = local
    row_slab, row_col = split(row, own_cols)
    order_ref[...] = ((row_slab == col_slab) & (row_col == col_col)).astype(BF16)
    to_columns(perm, field_ref, field_out, cols)
    to_columns(perm, mine_ref, member_w, cols)
    for part in (slice(0, own_cols), slice(own_cols, 2 * own_cols)):
        total_out[part] = member_term(local, member_w, field_out, part)


def other_kernel(cols, perm_ref, local_ref, order_ref, field_w, total_ref, other_ref, send_ref, keep_ref, member_w):
    own_cols, count = field_w.shape[0] // 2, keep_ref.shape[0]
    to_columns(perm_ref[...], other_ref, member_w, cols)
    for part, out_ref in ((slice(0, own_cols), send_ref), (slice(own_cols, 2 * own_cols), keep_ref)):
        total = total_ref[part] + member_term(local_ref[...], member_w, field_w, part)
        total = total.reshape(order_ref.shape[0], -1)
        high = total.astype(BF16)
        ordered = dot(order_ref[...], high)
        if out_ref is keep_ref:
            ordered = ordered + dot(order_ref[...], (total - high.astype(F32)).astype(BF16))
        out_ref[...] = ordered[:count].astype(out_ref.dtype)


def ensemble_calls(loc, flat_field, mine, other, after, levels, cols, own_cols):
    total, rows = flat_field.shape
    slab_count = total // cols
    slabs, side = padded(slab_count), own_cols * padded(slab_count)
    vmem = pl.BlockSpec(memory_space=pltpu.VMEM)
    work = (2 * own_cols, slabs, rows)
    held = pl.pallas_call(
        functools.partial(mine_kernel, levels, cols),
        name="mine",
        in_specs=[vmem] * 3 + [pl.BlockSpec(memory_space=pl.ANY)],
        out_specs=[vmem] * 5,
        out_shape=[
            jax.ShapeDtypeStruct((2 * own_cols * SUB, cols * SUB), BF16),
            jax.ShapeDtypeStruct((side, side), BF16),
            jax.ShapeDtypeStruct((side, side), BF16),
            jax.ShapeDtypeStruct(work, BF16),
            jax.ShapeDtypeStruct(work, F32),
        ],
        scratch_shapes=[pltpu.VMEM(work, F32)],
        compiler_params=pltpu.CompilerParams(vmem_limit_bytes=VMEM),
        cost_estimate=taking(1.8),
    )(loc, flat_field, mine, after)
    out_shape = (slab_count * own_cols, rows)
    return pl.pallas_call(
        functools.partial(other_kernel, cols),
        name="other",
        in_specs=[vmem] * 6,
        out_specs=[vmem, vmem],
        out_shape=[jax.ShapeDtypeStruct(out_shape, BF16), jax.ShapeDtypeStruct(out_shape, F32)],
        scratch_shapes=[pltpu.VMEM(work, F32)],
        compiler_params=pltpu.CompilerParams(vmem_limit_bytes=VMEM),
        cost_estimate=taking(2.0),
    )(*held, other)


def tables_kernel(levels, own_cols, col_dev, slabs, table_ref, entries_ref, vert_ref, after_ref, mat_ref, coef_ref, vert_out):
    first = lax.axis_index("tile") * col_dev + lax.axis_index("mem") * own_cols
    count = 2 * own_cols
    by_row = jnp.zeros((count, 1), F32)
    every, found = entries_ref[...], jnp.zeros(entries_ref.shape, F32)
    for entry in range(table_ref.shape[1]):
        found = jnp.where(every == entry, table_ref[0:1, entry : entry + 1], found)
    for col in range(own_cols):
        here = iota(found.shape, 1) == first + col
        alphas = jnp.sum(jnp.where(here, found, 0.0), axis=1, keepdims=True)
        for var in range(2):
            by_row = jnp.where(iota((count, 1), 0) == var * own_cols + col, alphas[var : var + 1], by_row)

    def series(alpha, number):
        alpha = jnp.broadcast_to(alpha, number.shape)
        total, unit = jnp.zeros(number.shape, F32), jnp.ones(number.shape, F32)
        single, power, both = alpha, alpha * alpha, jnp.ones(number.shape, F32)
        for bit in range(BLOCK.bit_length()):
            here = ((number >> bit) & 1) == 1
            total = jnp.where(here, unit + power * total, total)
            both = jnp.where(here, both * single, both)
            unit, single, power = unit * (1.0 + power), single * single, power * power
        return total, both

    place = iota((count, BLOCK), 1)
    across, right = series(by_row, BLOCK - place)
    down = jnp.concatenate([across, jnp.zeros((128 - count, BLOCK), F32)], 0).T
    _, left = series(by_row, place + 1)
    coef_ref[0] = left * across
    coef_ref[1] = right
    coef_ref[2] = jnp.broadcast_to(right[:, 0:1], right.shape)
    coef_ref[3] = jnp.broadcast_to(left[:, 0:1] * across[:, 0:1], right.shape)
    far = jnp.abs(iota((BLOCK, BLOCK), 0) - iota((BLOCK, BLOCK), 1)).astype(F32)
    for k in range(count):
        alpha = by_row[k : k + 1]
        decay = jnp.exp(far * jnp.log(jnp.maximum(alpha, 1e-30)))
        reach = jnp.minimum(down[:, k : k + 1], across[k : k + 1])
        mat_ref[k] = (gain_of(alpha) * decay * reach).astype(BF16)
    shape = vert_out.shape
    (row_slab, row_col), (col_col, col_slab) = split(iota(shape, 0), own_cols), split(iota(shape, 1), slabs)
    vert_out[...] = spread(vert_ref[...], levels, row_slab, row_col, col_slab, col_col)


def tables_call(table, entries, vert, after, levels, own_cols, col_dev, slabs):
    count = 2 * own_cols
    return pl.pallas_call(
        functools.partial(tables_kernel, levels, own_cols, col_dev, slabs),
        name="tables",
        in_specs=[pl.BlockSpec(memory_space=pltpu.VMEM)] * 3 + [pl.BlockSpec(memory_space=pl.ANY)],
        out_specs=[pl.BlockSpec(memory_space=pltpu.VMEM)] * 3,
        out_shape=[
            jax.ShapeDtypeStruct((count, BLOCK, BLOCK), BF16),
            jax.ShapeDtypeStruct((4, count, BLOCK), F32),
            jax.ShapeDtypeStruct((own_cols * slabs, own_cols * slabs), BF16),
        ],
        compiler_params=pltpu.CompilerParams(vmem_limit_bytes=VMEM),
        cost_estimate=taking(1.0),
    )(table[None], entries, vert, after)


def along_rows(lines, matrix, coef):
    count, rows = lines.shape
    blocks = rows // BLOCK
    parts = jnp.concatenate([lines[:, b * BLOCK : (b + 1) * BLOCK] for b in range(blocks)], 0)
    local = dot(parts.astype(BF16), matrix)
    local = [local[b * count : (b + 1) * count] for b in range(blocks)]
    into, right, decay, turn = coef[0:1], coef[1:2], coef[2:3, 0:1], coef[3:4, 0:1]
    forward, state = [None], None
    for b in range(blocks - 1):
        end = local[b][:, BLOCK - 1 : BLOCK]
        state = end if state is None else decay * state + end
        forward.append(state)
    out, state = [None] * blocks, None
    for b in range(blocks - 1, -1, -1):
        piece = local[b]
        if forward[b] is not None:
            piece = piece + into * forward[b]
        if state is not None:
            piece = piece + right * state
        out[b] = piece
        if b:
            start = local[b][:, 0:1] + turn * forward[b]
            state = start if state is None else decay * state + start
    return out


def filter_share(levels, share, own_ref, coef_ref, mat_ref, row_coef_ref, part_ref, last_refs, out_ref):
    own_cols, subs, rows = own_ref.shape
    cols = coef_ref.shape[1] - 3
    mem = lax.axis_index("mem")
    end = slice(subs - 8, subs)
    is_level = iota((8, rows), 0) + share * subs + subs - 8 < levels
    lasts = [ref[...].astype(F32) for ref in last_refs]
    carry, carry_end = [], []
    for side in range(2):
        value = part_ref[side].astype(F32)
        other = value[end]
        for k, last in enumerate(lasts):
            value = value + coef_ref[side, cols + k, 0:1] * last
            other = other + coef_ref[side, cols + k, 1:2] * last[end]
        carry.append(value)
        carry_end.append(other)
    for col in range(own_cols):
        pair = coef_ref[:, mem * own_cols + col]
        own = own_ref[col]
        lines = own + pair[0, 0:1] * carry[0] + pair[1, 0:1] * carry[1]
        last_lines = own[end] + pair[0, 1:2] * carry_end[0] + pair[1, 1:2] * carry_end[1]
        main = along_rows(lines, mat_ref[col], row_coef_ref[:, col])
        last = along_rows(last_lines, mat_ref[own_cols + col], row_coef_ref[:, own_cols + col])
        for b, (piece, extra) in enumerate(zip(main, last)):
            place = slice(b * BLOCK, (b + 1) * BLOCK)
            out_ref[col, 0 : subs - 8, place] = piece[0 : subs - 8]
            out_ref[col, end, place] = jnp.where(is_level[:, place], piece[end], extra)


def rows_kernel(levels, own_ref, coef_ref, mat_ref, row_coef_ref, part_ref, *refs):
    share = lax.axis_index("mem") & (CORES - 1)
    filter_share(levels, share, own_ref, coef_ref, mat_ref, row_coef_ref, part_ref, refs[:3], refs[3])


def rows_call(levels, own, coef, mats, row_coef, shares):
    vmem = pl.BlockSpec(memory_space=pltpu.VMEM)
    args = [own, coef, mats, row_coef, *shares]
    return pl.pallas_call(
        functools.partial(rows_kernel, levels),
        name="rows",
        in_specs=[vmem] * len(args),
        out_specs=vmem,
        out_shape=jax.ShapeDtypeStruct(own.shape, F32),
        compiler_params=pltpu.CompilerParams(vmem_limit_bytes=VMEM),
        cost_estimate=taking(0.7),
    )(*args)


def final_kernel(
    levels, scale, done_ref, own_ref, coef_ref, mat_ref, row_coef_ref, part_ref, last_1_ref, last_2_ref, last_3_ref,
    vert_ref, keep_ref, came_ref, out_hbm, filt, out_ref, sent
):
    own_cols, subs, rows = own_ref.shape
    share = lax.axis_index("mem") & (CORES - 1)
    filt[:, pl.ds(pl.multiple_of(share * subs, subs), subs), :] = done_ref[...]
    other = 1 - share
    place = pl.ds(pl.multiple_of(other * subs, subs), subs)
    last_refs = last_1_ref, last_2_ref, last_3_ref
    filter_share(
        levels, other, own_ref, coef_ref, mat_ref, row_coef_ref, part_ref, last_refs, filt.at[:, place, :]
    )
    count = out_ref.shape[0]
    copies = []
    for start in range(0, rows, BLOCK):
        part = slice(start, start + BLOCK)
        static = filt[:, :, part].reshape(vert_ref.shape[1], BLOCK)
        high = static.astype(BF16)
        low = (static - high.astype(F32)).astype(BF16)
        total = dot(vert_ref[...], high) + dot(vert_ref[...], low)
        ens = keep_ref[:, part] + came_ref[:, part].astype(F32)
        total = total[: count * own_cols] + ens * scale
        out_ref[:, :, part] = total.reshape(count, own_cols, BLOCK).astype(BF16)
        copy = pltpu.make_async_copy(out_ref.at[:, :, part], out_hbm.at[:, :, part], sent.at[start // BLOCK])
        copy.start()
        copies.append(copy)
    for copy in copies:
        copy.wait()


def final_call(slab_count, levels, scale, done, own, coef, mats, row_coef, shares, vert, keep, came):
    own_cols, subs, rows = own.shape
    vmem = pl.BlockSpec(memory_space=pltpu.VMEM)
    args = [done, own, coef, mats, row_coef, *shares, vert, keep, came]
    out_shape = (slab_count, own_cols, rows)
    return pl.pallas_call(
        functools.partial(final_kernel, levels, scale),
        name="final",
        in_specs=[vmem] * len(args),
        out_specs=pl.BlockSpec(memory_space=pl.ANY),
        out_shape=jax.ShapeDtypeStruct(out_shape, BF16),
        scratch_shapes=[
            pltpu.VMEM((own_cols, CORES * subs, rows), F32),
            pltpu.VMEM(out_shape, BF16),
            pltpu.SemaphoreType.DMA((rows // BLOCK,)),
        ],
        compiler_params=pltpu.CompilerParams(vmem_limit_bytes=VMEM),
        cost_estimate=taking(1.5),
    )(*args)


def merge_kernel(levels, steps, step, last, after_count, *refs):
    lines_ref, ends_ref = refs[:2]
    came_refs, outs = refs[2 : 2 + step], refs[2 + step + after_count :]
    _, subs, rows = ends_ref.shape
    tile, mem = lax.axis_index("tile"), lax.axis_index("mem")
    is_level = iota((subs, rows), 0) + (mem & (CORES - 1)) * subs < levels
    decay = jnp.where(is_level, lines_ref[1, 0:1], lines_ref[1, 1:2])
    behind = jnp.where(is_level, lines_ref[2, 0:1], lines_ref[2, 1:2])
    turned = behind * decay
    right, left = ends_ref[0].astype(F32), ends_ref[1].astype(F32)
    into_right, into_left, from_left, from_right = 0.0, behind * right, 1.0, 1.0
    for level, came_ref in enumerate(came_refs):
        second = ((tile >> level) & 1) == 1
        came_right, came_left = came_ref[0].astype(F32), came_ref[1].astype(F32)
        into_right = into_right + jnp.where(second, from_left * came_right, 0.0)
        into_left = into_left + jnp.where(second, 0.0, from_right * came_left)
        right = jnp.where(second, decay * came_right + right, decay * right + came_right)
        left = jnp.where(second, came_left + decay * left, left + decay * came_left)
        from_left = jnp.where(second, from_left * decay, from_left)
        from_right = jnp.where(second, from_right, from_right * decay)
        decay = decay * decay
    if last:
        quarter = tile >> (steps - 2)
        outs[0][...] = jnp.where((quarter & 1) == 1, left, right).astype(BF16)
        outs[1][...] = jnp.where(quarter >= 2, left, right).astype(BF16)
        outs[2][0] = into_right.astype(BF16)
        outs[2][1] = (into_left + turned * into_right).astype(BF16)
    else:
        outs[0][0] = right.astype(BF16)
        outs[0][1] = left.astype(BF16)


def merge_call(lines, ends, came, after, levels, steps):
    last = len(came) == steps - 2
    whole = jax.ShapeDtypeStruct(ends.shape, BF16)
    one = jax.ShapeDtypeStruct(ends.shape[1:], BF16)
    outs = [one, one, whole] if last else [whole]
    vmem = pl.BlockSpec(memory_space=pltpu.VMEM)
    held = [pl.BlockSpec(memory_space=pl.ANY)] * len(after)
    return pl.pallas_call(
        functools.partial(merge_kernel, levels, steps, len(came), last, len(after)),
        name="merge",
        in_specs=[vmem] * (2 + len(came)) + held,
        out_specs=[vmem] * len(outs) + held,
        out_shape=outs + [jax.ShapeDtypeStruct(array.shape, array.dtype) for array in after],
        input_output_aliases={2 + len(came) + k: len(outs) + k for k in range(len(after))},
        compiler_params=pltpu.CompilerParams(vmem_limit_bytes=VMEM),
        cost_estimate=taking(0.8),
    )(lines, ends, *came, *after)


def body(field, vert_filter, loc_filter, alpha_table, xscale_idx, yscale_idx, members):
    tile_count, mem_count = lax.axis_size("tile"), lax.axis_size("mem")
    slab_count, cols, rows = field.shape
    levels = vert_filter.shape[1]
    own_cols = cols // mem_count
    slabs = padded(slab_count)
    steps = tile_count.bit_length() - 1

    def swap(array, flip, axis="mem"):
        return lax.ppermute(array, axis, [(i, i ^ flip) for i in range(lax.axis_size(axis))])

    full_field = field.reshape(slab_count * cols, rows)
    flat_field = pltpu.with_memory_space_constraint(full_field, pltpu.HBM)
    mine = members.reshape(slab_count * cols, rows)
    other = swap(mine, 1)
    line_table = pltpu.with_memory_space_constraint(alpha_table, pltpu.HBM)
    line_entries = pltpu.with_memory_space_constraint(xscale_idx, pltpu.HBM)
    share = (lax.axis_index("mem") & (CORES - 1)).astype(jnp.int32).reshape(1)
    ends, own_0, lines = ends_call(share, line_table, line_entries, flat_field, levels, steps, cols, own_cols)
    blocks, came = [ends], []
    send, keep = ensemble_calls(loc_filter[0], full_field, mine, other, ends, levels, cols, own_cols)
    over = swap(send, 2)
    own_1, coef = local_call(lines, full_field, send, levels, steps, cols, own_cols)
    mats, row_coef, vert = tables_call(alpha_table, yscale_idx, vert_filter[0], own_1, levels, own_cols, cols, slabs)
    for level in range(steps - 2):
        came.append(swap(blocks[0], 1 << level, "tile"))
        *blocks, mats = merge_call(lines, ends, came, [mats], levels, steps)
    near, far, part = blocks
    last = {flip: swap(near if flip == 1 else far, flip << (steps - 2), "tile") for flip in (2, 3, 1)}
    shares = [part, last[1], last[2], last[3]]
    others = [swap(share, 1) for share in shares]
    done = rows_call(levels, own_0, coef, mats, row_coef, shares)
    scale = 1.0 / (mem_count * members.shape[0] - 1)
    return final_call(slab_count, levels, scale, done, own_1, coef, mats, row_coef, others, vert, keep, over)


def solution(mesh):
    return jax.shard_map(
        body,
        mesh=mesh,
        in_specs=(P(None, "tile", None), P(), P(), P(), P(), P(), P("mem", None, "tile", None)),
        out_specs=P(None, ("tile", "mem"), None),
        check_vma=False,
    )
```

```python
import functools

import jax
import jax.numpy as jnp
from jax import lax
from jax.experimental import pallas as pl
from jax.experimental.pallas import tpu as pltpu
from jax.sharding import PartitionSpec as P

F32, BF16 = jnp.float32, jnp.bfloat16
SUB = 16
CORES = 2
LANES = 256
BLOCK = 256
MIB = 1 << 20
VMEM = 32 * MIB


def iota(shape, dim):
    return lax.broadcasted_iota(jnp.int32, shape, dim)


def taking(microseconds):
    return pl.CostEstimate(flops=int(microseconds * 1.15e9), bytes_accessed=MIB // 4, transcendentals=0)


def split(number, size):
    assert size & (size - 1) == 0
    return number >> (size.bit_length() - 1), number & (size - 1)


def dot(left, right):
    return jnp.dot(left, right, preferred_element_type=F32)


def gain_of(alpha):
    rest = (1.0 - alpha) * (1.0 + alpha)
    return jnp.sqrt(rest) * rest / jnp.sqrt(1.0 + alpha * alpha)


def lookup(table_ref, entries):
    found = jnp.zeros(entries.shape, F32)
    for entry in range(table_ref.shape[0]):
        found = jnp.where(entries == entry, table_ref[entry], found)
    return found


def padded(slab_count):
    return -(-slab_count // (4 * SUB)) * 4 * SUB


def to_columns(perm, flat, out_ref, cols):
    total = flat.shape[0]
    wanted = out_ref.shape[0]
    step = SUB * cols
    for chunk in range(out_ref.shape[1] // SUB):
        depth = min(step, total - chunk * step)
        moved = dot(perm[:, :depth], flat[chunk * step : chunk * step + depth])
        out_ref[:, chunk * SUB : (chunk + 1) * SUB, :] = moved.reshape(wanted, SUB, -1).astype(out_ref.dtype)


def sweep(work, alpha):
    cols = work.shape[0]
    state = work[0]
    for col in range(1, cols):
        state = alpha * state + work[col]
        work[col] = state
    for col in range(cols - 2, -1, -1):
        state = alpha * state + work[col]
        work[col] = state


def transposer(cols):
    shape = (SUB * cols, SUB * cols)
    (out_col, out_slab), (in_slab, in_col) = split(iota(shape, 0), SUB), split(iota(shape, 1), cols)
    return ((out_slab == in_slab) & (out_col == in_col)).astype(BF16)


def share_rows(total, cols, subs, share):
    return slice(share * subs * cols, min((share + 1) * subs * cols, total))


def sweep_share(levels, slab_count, share, perm, alpha, held, work):
    cols, subs, lanes = work.shape
    first = share * subs
    held = jnp.where(iota(held.shape, 0) < (slab_count - first) * cols, held, 0)
    to_columns(perm, held, work, cols)
    is_level = iota((subs, lanes), 0) + first < levels
    alpha = jnp.where(is_level, alpha[0:1], alpha[1:2])
    sweep(work, alpha)
    return gain_of(alpha), is_level


def ends_kernel(
    levels, steps, slab_count, share_ref, table_ref, entries_ref, field_ref, ends_ref, own_ref, lines_ref, work
):
    pieces, cols, subs, lanes = work.shape
    own_cols = own_ref.shape[0]
    tile, mem = lax.axis_index("tile"), lax.axis_index("mem")
    share, perm = share_ref[0], transposer(cols)
    pair = lookup(table_ref, entries_ref[...])
    decay, turn = line_coefs(pair, cols)
    behind = reflected(decay, turn, tile, steps)
    lines_ref[0], lines_ref[1], lines_ref[2] = pair, decay, behind
    for piece in range(pieces):
        part = slice(piece * lanes, (piece + 1) * lanes)
        gain, is_level = sweep_share(levels, slab_count, share, perm, pair[:, part], field_ref[:, part], work.at[piece])
        turned = (decay * behind)[:, part]
        turned = jnp.where(is_level, turned[0:1], turned[1:2])
        forward = gain * work[piece, cols - 1]
        ends_ref[0, :, part] = forward.astype(BF16)
        ends_ref[1, :, part] = (gain * work[piece, 0] + turned * forward).astype(BF16)
        own_ref[:, :, part] = work[piece, pl.ds(mem * own_cols, own_cols)] * gain[None]


def ends_call(share, table, entries, flat_field, levels, steps, cols, own_cols):
    total, rows = flat_field.shape
    subs = padded(total // cols) // CORES
    vmem, smem = pl.BlockSpec(memory_space=pltpu.VMEM), pl.BlockSpec(memory_space=pltpu.SMEM)
    return pl.pallas_call(
        functools.partial(ends_kernel, levels, steps, total // cols),
        name="ends",
        grid_spec=pltpu.PrefetchScalarGridSpec(
            num_scalar_prefetch=1,
            grid=(1,),
            in_specs=[
                smem,
                pl.BlockSpec(entries.shape, lambda i, share: (0, 0)),
                pl.BlockSpec((subs * cols, rows), lambda i, share: (share[0], 0)),
            ],
            out_specs=[vmem] * 3,
            scratch_shapes=[pltpu.VMEM((rows // LANES, cols, subs, LANES), F32)],
        ),
        out_shape=[
            jax.ShapeDtypeStruct((2, subs, rows), BF16),
            jax.ShapeDtypeStruct((own_cols, subs, rows), F32),
            jax.ShapeDtypeStruct((3, 2, rows), F32),
        ],
        compiler_params=pltpu.CompilerParams(vmem_limit_bytes=VMEM),
        cost_estimate=taking(2.1),
    )(share, table, entries, flat_field)


def line_coefs(pair, cols):
    decay, turn = pair, pair
    while cols > 1:
        turn = turn * (1.0 + decay * decay)
        decay = decay * decay
        cols //= 2
    return decay, turn


def reflected(decay, turn, tile, steps):
    behind = (1 << steps) - 1 - tile
    total, power = jnp.zeros_like(turn), jnp.ones_like(turn)
    for level in range(steps):
        here = ((behind >> level) & 1) == 1
        total = jnp.where(here, total + power * power * turn, total)
        power = jnp.where(here, power * decay, power)
        turn = turn * (1.0 + decay * decay)
        decay = decay * decay
    return total


def local_kernel(levels, steps, slab_count, lines_ref, field_ref, after_ref, own_ref, coef_ref, held_ref, work):
    pieces, cols, subs, lanes = work.shape
    own_cols = own_ref.shape[0]
    tile, mem = lax.axis_index("tile"), lax.axis_index("mem")
    share = (mem & (CORES - 1)) ^ 1
    for core in range(CORES):
        rows = share_rows(slab_count * cols, cols, subs, core)

        @pl.when(share == core)
        def _():
            held_ref[0 : rows.stop - rows.start, :] = field_ref[rows, :]

    pair, decay, behind = lines_ref[0], lines_ref[1], lines_ref[2]
    perm = transposer(cols)
    for piece in range(pieces):
        part = slice(piece * lanes, (piece + 1) * lanes)
        gain, _ = sweep_share(levels, slab_count, share, perm, pair[:, part], held_ref[:, part], work.at[piece])
        own_ref[:, :, part] = work[piece, pl.ds(mem * own_cols, own_cols)] * gain[None]
    square = pair * pair
    power, sums = jnp.ones_like(pair), jnp.zeros_like(pair)
    rights, geometric = [], []
    for _ in range(cols):
        power, sums = power * pair, sums * square + 1.0
        rights.append(power)
        geometric.append(sums)
    for col in range(cols):
        coef_ref[0, col] = rights[col] * geometric[cols - 1 - col]
        coef_ref[1, col] = rights[cols - 1 - col]
    turned = decay * behind
    from_left, from_right = jnp.ones_like(pair), jnp.ones_like(pair)
    for level in range(steps - 2):
        second = ((tile >> level) & 1) == 1
        from_left = jnp.where(second, from_left * decay, from_left)
        from_right = jnp.where(second, from_right, from_right * decay)
        decay = decay * decay
    quarter = tile >> (steps - 2)
    outer = (quarter == 0) | (quarter == 3)
    for flip, weight in ((1, 1.0), (2, decay), (3, jnp.where(outer, decay * decay, 1.0))):
        upper = (quarter ^ flip) < quarter
        coef_ref[0, cols + flip - 1] = jnp.where(upper, from_left * weight, 0.0)
        coef_ref[1, cols + flip - 1] = weight * jnp.where(upper, turned * from_left, from_right)


def local_call(lines, flat_field, after, levels, steps, cols, own_cols):
    total, rows = flat_field.shape
    subs = padded(total // cols) // CORES
    vmem = pl.BlockSpec(memory_space=pltpu.VMEM)
    return pl.pallas_call(
        functools.partial(local_kernel, levels, steps, total // cols),
        name="local",
        in_specs=[vmem, vmem, pl.BlockSpec(memory_space=pl.ANY)],
        out_specs=[vmem, vmem],
        out_shape=[
            jax.ShapeDtypeStruct((own_cols, subs, rows), F32),
            jax.ShapeDtypeStruct((2, cols + 3, 2, rows), F32),
        ],
        scratch_shapes=[
            pltpu.VMEM((subs * cols, rows), BF16),
            pltpu.VMEM((rows // LANES, cols, subs, LANES), F32),
        ],
        compiler_params=pltpu.CompilerParams(vmem_limit_bytes=VMEM),
        cost_estimate=taking(0.5),
    )(lines, flat_field, after)


def spread(matrix, levels, row_slab, row_col, col_slab, col_col):
    rows, cols = row_slab.shape
    size = matrix.shape[0]
    left = (iota((rows, size), 1) == row_slab[:, :size]).astype(BF16)
    right = (iota((size, cols), 0) == col_slab[:size, :]).astype(BF16)
    inner = dot(left, matrix).astype(BF16)
    full = dot(inner, right)
    full = jnp.where((row_slab >= levels) & (row_slab == col_slab), 1.0, full)
    return jnp.where(row_col == col_col, full, 0.0).astype(BF16)


def member_term(local, member_w, field_w, part):
    member = member_w[part]
    cols, slabs, rows = member.shape
    scaled = (member * field_w[part].astype(F32)).astype(BF16).reshape(cols * slabs, rows)
    return member * dot(local, scaled).reshape(cols, slabs, rows)


def mine_kernel(
    levels, cols, loc_ref, field_ref, mine_ref, after_ref, perm_ref, local_ref, order_ref, field_out, total_out, member_w
):
    own_cols = field_out.shape[0] // 2
    slabs = field_out.shape[1]
    chip, core = split(lax.axis_index("mem"), 2)
    (slot, out_slab), (in_slab, in_col) = split(iota(perm_ref.shape, 0), SUB), split(iota(perm_ref.shape, 1), cols)
    first = jnp.where(slot < own_cols, (2 * (1 - chip) + core) * own_cols, (2 * chip + core) * own_cols)
    hit = (out_slab == in_slab) & (first + (slot & (own_cols - 1)) == in_col)
    perm = hit.astype(BF16)
    perm_ref[...] = perm
    row, col = iota(local_ref.shape, 0), iota(local_ref.shape, 1)
    (row_col, row_slab), (col_col, col_slab) = split(row, slabs), split(col, slabs)
    local = spread(loc_ref[...], levels, row_slab, row_col, col_slab, col_col)
    local_ref[...] = local
    row_slab, row_col = split(row, own_cols)
    order_ref[...] = ((row_slab == col_slab) & (row_col == col_col)).astype(BF16)
    to_columns(perm, field_ref, field_out, cols)
    to_columns(perm, mine_ref, member_w, cols)
    for part in (slice(0, own_cols), slice(own_cols, 2 * own_cols)):
        total_out[part] = member_term(local, member_w, field_out, part)


def other_kernel(half, cols, perm_ref, local_ref, order_ref, field_w, total_ref, other_ref, after_ref, out_ref, member_w):
    own_cols, count = member_w.shape[0], out_ref.shape[0]
    part = slice(half * own_cols, (half + 1) * own_cols)
    to_columns(perm_ref[half * own_cols * SUB : (half + 1) * own_cols * SUB, :], other_ref, member_w, cols)
    total = total_ref[part] + member_term(local_ref[...], member_w, field_w.at[part], slice(0, own_cols))
    total = total.reshape(order_ref.shape[0], -1)
    high = total.astype(BF16)
    ordered = dot(order_ref[...], high)
    if out_ref.dtype == F32:
        ordered = ordered + dot(order_ref[...], (total - high.astype(F32)).astype(BF16))
    out_ref[...] = ordered[:count].astype(out_ref.dtype)


def ensemble_calls(loc, flat_field, mine, other, after, levels, cols, own_cols):
    total, rows = flat_field.shape
    slab_count = total // cols
    slabs, side = padded(slab_count), own_cols * padded(slab_count)
    vmem = pl.BlockSpec(memory_space=pltpu.VMEM)
    work = (2 * own_cols, slabs, rows)
    held = pl.pallas_call(
        functools.partial(mine_kernel, levels, cols),
        name="mine",
        in_specs=[vmem] * 3 + [pl.BlockSpec(memory_space=pl.ANY)],
        out_specs=[vmem] * 5,
        out_shape=[
            jax.ShapeDtypeStruct((2 * own_cols * SUB, cols * SUB), BF16),
            jax.ShapeDtypeStruct((side, side), BF16),
            jax.ShapeDtypeStruct((side, side), BF16),
            jax.ShapeDtypeStruct(work, BF16),
            jax.ShapeDtypeStruct(work, F32),
        ],
        scratch_shapes=[pltpu.VMEM(work, F32)],
        compiler_params=pltpu.CompilerParams(vmem_limit_bytes=VMEM),
        cost_estimate=taking(1.8),
    )(loc, flat_field, mine, after)
    after, outs = other, []
    for half, dtype in enumerate((BF16, F32)):
        after = pl.pallas_call(
            functools.partial(other_kernel, half, cols),
            name=("send", "keep")[half],
            in_specs=[vmem] * 6 + [pl.BlockSpec(memory_space=pl.ANY)],
            out_specs=vmem,
            out_shape=jax.ShapeDtypeStruct((slab_count * own_cols, rows), dtype),
            scratch_shapes=[pltpu.VMEM((own_cols, slabs, rows), F32)],
            compiler_params=pltpu.CompilerParams(vmem_limit_bytes=VMEM),
            cost_estimate=taking((0.8, 4.0)[half]),
        )(*held, other, after)
        outs.append(after)
    return outs


def tables_kernel(levels, own_cols, col_dev, slabs, table_ref, entries_ref, vert_ref, after_ref, mat_ref, coef_ref, vert_out):
    first = lax.axis_index("tile") * col_dev + lax.axis_index("mem") * own_cols
    count = 2 * own_cols
    by_row = jnp.zeros((count, 1), F32)
    every, found = entries_ref[...], jnp.zeros(entries_ref.shape, F32)
    for entry in range(table_ref.shape[1]):
        found = jnp.where(every == entry, table_ref[0:1, entry : entry + 1], found)
    for col in range(own_cols):
        here = iota(found.shape, 1) == first + col
        alphas = jnp.sum(jnp.where(here, found, 0.0), axis=1, keepdims=True)
        for var in range(2):
            by_row = jnp.where(iota((count, 1), 0) == var * own_cols + col, alphas[var : var + 1], by_row)

    def series(alpha, number):
        alpha = jnp.broadcast_to(alpha, number.shape)
        total, unit = jnp.zeros(number.shape, F32), jnp.ones(number.shape, F32)
        single, power, both = alpha, alpha * alpha, jnp.ones(number.shape, F32)
        for bit in range(BLOCK.bit_length()):
            here = ((number >> bit) & 1) == 1
            total = jnp.where(here, unit + power * total, total)
            both = jnp.where(here, both * single, both)
            unit, single, power = unit * (1.0 + power), single * single, power * power
        return total, both

    place = iota((count, BLOCK), 1)
    across, right = series(by_row, BLOCK - place)
    down = jnp.concatenate([across, jnp.zeros((128 - count, BLOCK), F32)], 0).T
    _, left = series(by_row, place + 1)
    coef_ref[0] = left * across
    coef_ref[1] = right
    coef_ref[2] = jnp.broadcast_to(right[:, 0:1], right.shape)
    coef_ref[3] = jnp.broadcast_to(left[:, 0:1] * across[:, 0:1], right.shape)
    far = jnp.abs(iota((BLOCK, BLOCK), 0) - iota((BLOCK, BLOCK), 1)).astype(F32)
    for k in range(count):
        alpha = by_row[k : k + 1]
        decay = jnp.exp(far * jnp.log(jnp.maximum(alpha, 1e-30)))
        reach = jnp.minimum(down[:, k : k + 1], across[k : k + 1])
        mat_ref[k] = (gain_of(alpha) * decay * reach).astype(BF16)
    shape = vert_out.shape
    (row_slab, row_col), (col_col, col_slab) = split(iota(shape, 0), own_cols), split(iota(shape, 1), slabs)
    vert_out[...] = spread(vert_ref[...], levels, row_slab, row_col, col_slab, col_col)


def tables_call(table, entries, vert, after, levels, own_cols, col_dev, slabs):
    count = 2 * own_cols
    return pl.pallas_call(
        functools.partial(tables_kernel, levels, own_cols, col_dev, slabs),
        name="tables",
        in_specs=[pl.BlockSpec(memory_space=pltpu.VMEM)] * 3 + [pl.BlockSpec(memory_space=pl.ANY)],
        out_specs=[pl.BlockSpec(memory_space=pltpu.VMEM)] * 3,
        out_shape=[
            jax.ShapeDtypeStruct((count, BLOCK, BLOCK), BF16),
            jax.ShapeDtypeStruct((4, count, BLOCK), F32),
            jax.ShapeDtypeStruct((own_cols * slabs, own_cols * slabs), BF16),
        ],
        compiler_params=pltpu.CompilerParams(vmem_limit_bytes=VMEM),
        cost_estimate=taking(0.4),
    )(table[None], entries, vert, after)


def along_rows(lines, matrix, coef):
    count, rows = lines.shape
    blocks = rows // BLOCK
    parts = jnp.concatenate([lines[:, b * BLOCK : (b + 1) * BLOCK] for b in range(blocks)], 0)
    local = dot(parts.astype(BF16), matrix)
    local = [local[b * count : (b + 1) * count] for b in range(blocks)]
    into, right, decay, turn = coef[0:1], coef[1:2], coef[2:3, 0:1], coef[3:4, 0:1]
    forward, state = [None], None
    for b in range(blocks - 1):
        end = local[b][:, BLOCK - 1 : BLOCK]
        state = end if state is None else decay * state + end
        forward.append(state)
    out, state = [None] * blocks, None
    for b in range(blocks - 1, -1, -1):
        piece = local[b]
        if forward[b] is not None:
            piece = piece + into * forward[b]
        if state is not None:
            piece = piece + right * state
        out[b] = piece
        if b:
            start = local[b][:, 0:1] + turn * forward[b]
            state = start if state is None else decay * state + start
    return out


def filter_share(levels, share, own_ref, coef_ref, mat_ref, row_coef_ref, part_ref, last_refs, out_ref):
    own_cols, subs, rows = own_ref.shape
    cols = coef_ref.shape[1] - 3
    mem = lax.axis_index("mem")
    end = slice(subs - 8, subs)
    is_level = iota((8, rows), 0) + share * subs + subs - 8 < levels
    lasts = [ref[...].astype(F32) for ref in last_refs]
    carry, carry_end = [], []
    for side in range(2):
        value = part_ref[side].astype(F32)
        other = value[end]
        for k, last in enumerate(lasts):
            value = value + coef_ref[side, cols + k, 0:1] * last
            other = other + coef_ref[side, cols + k, 1:2] * last[end]
        carry.append(value)
        carry_end.append(other)
    for col in range(own_cols):
        pair = coef_ref[:, mem * own_cols + col]
        own = own_ref[col]
        lines = own + pair[0, 0:1] * carry[0] + pair[1, 0:1] * carry[1]
        last_lines = own[end] + pair[0, 1:2] * carry_end[0] + pair[1, 1:2] * carry_end[1]
        main = along_rows(lines, mat_ref[col], row_coef_ref[:, col])
        last = along_rows(last_lines, mat_ref[own_cols + col], row_coef_ref[:, own_cols + col])
        for b, (piece, extra) in enumerate(zip(main, last)):
            place = slice(b * BLOCK, (b + 1) * BLOCK)
            out_ref[col, 0 : subs - 8, place] = piece[0 : subs - 8]
            out_ref[col, end, place] = jnp.where(is_level[:, place], piece[end], extra)


def rows_kernel(levels, own_ref, coef_ref, mat_ref, row_coef_ref, part_ref, *refs):
    share = lax.axis_index("mem") & (CORES - 1)
    filter_share(levels, share, own_ref, coef_ref, mat_ref, row_coef_ref, part_ref, refs[:3], refs[3])


def rows_call(levels, own, coef, mats, row_coef, shares):
    vmem = pl.BlockSpec(memory_space=pltpu.VMEM)
    args = [own, coef, mats, row_coef, *shares]
    return pl.pallas_call(
        functools.partial(rows_kernel, levels),
        name="rows",
        in_specs=[vmem] * len(args),
        out_specs=vmem,
        out_shape=jax.ShapeDtypeStruct(own.shape, F32),
        compiler_params=pltpu.CompilerParams(vmem_limit_bytes=VMEM),
        cost_estimate=taking(0.9),
    )(*args)


def final_kernel(
    levels, scale, done_ref, own_ref, coef_ref, mat_ref, row_coef_ref, part_ref, last_1_ref, last_2_ref, last_3_ref,
    vert_ref, keep_ref, came_ref, out_hbm, filt, out_ref, sent
):
    own_cols, subs, rows = own_ref.shape
    share = lax.axis_index("mem") & (CORES - 1)
    filt[:, pl.ds(pl.multiple_of(share * subs, subs), subs), :] = done_ref[...]
    other = 1 - share
    place = pl.ds(pl.multiple_of(other * subs, subs), subs)
    last_refs = last_1_ref, last_2_ref, last_3_ref
    filter_share(
        levels, other, own_ref, coef_ref, mat_ref, row_coef_ref, part_ref, last_refs, filt.at[:, place, :]
    )
    count = out_ref.shape[0]
    copies = []
    for start in range(0, rows, BLOCK):
        part = slice(start, start + BLOCK)
        static = filt[:, :, part].reshape(vert_ref.shape[1], BLOCK)
        high = static.astype(BF16)
        low = (static - high.astype(F32)).astype(BF16)
        total = dot(vert_ref[...], high) + dot(vert_ref[...], low)
        ens = keep_ref[:, part] + came_ref[:, part].astype(F32)
        total = total[: count * own_cols] + ens * scale
        out_ref[:, :, part] = total.reshape(count, own_cols, BLOCK).astype(BF16)
        copy = pltpu.make_async_copy(out_ref.at[:, :, part], out_hbm.at[:, :, part], sent.at[start // BLOCK])
        copy.start()
        copies.append(copy)
    for copy in copies:
        copy.wait()


def final_call(slab_count, levels, scale, done, own, coef, mats, row_coef, shares, vert, keep, came):
    own_cols, subs, rows = own.shape
    vmem = pl.BlockSpec(memory_space=pltpu.VMEM)
    args = [done, own, coef, mats, row_coef, *shares, vert, keep, came]
    out_shape = (slab_count, own_cols, rows)
    return pl.pallas_call(
        functools.partial(final_kernel, levels, scale),
        name="final",
        in_specs=[vmem] * len(args),
        out_specs=pl.BlockSpec(memory_space=pl.ANY),
        out_shape=jax.ShapeDtypeStruct(out_shape, BF16),
        scratch_shapes=[
            pltpu.VMEM((own_cols, CORES * subs, rows), F32),
            pltpu.VMEM(out_shape, BF16),
            pltpu.SemaphoreType.DMA((rows // BLOCK,)),
        ],
        compiler_params=pltpu.CompilerParams(vmem_limit_bytes=VMEM),
        cost_estimate=taking(1.5),
    )(*args)


def merge_kernel(levels, steps, step, last, after_count, *refs):
    lines_ref, ends_ref = refs[:2]
    came_refs, outs = refs[2 : 2 + step], refs[2 + step + after_count :]
    _, subs, rows = ends_ref.shape
    tile, mem = lax.axis_index("tile"), lax.axis_index("mem")
    is_level = iota((subs, rows), 0) + (mem & (CORES - 1)) * subs < levels
    decay = jnp.where(is_level, lines_ref[1, 0:1], lines_ref[1, 1:2])
    behind = jnp.where(is_level, lines_ref[2, 0:1], lines_ref[2, 1:2])
    turned = behind * decay
    right, left = ends_ref[0].astype(F32), ends_ref[1].astype(F32)
    into_right, into_left, from_left, from_right = 0.0, behind * right, 1.0, 1.0
    for level, came_ref in enumerate(came_refs):
        second = ((tile >> level) & 1) == 1
        came_right, came_left = came_ref[0].astype(F32), came_ref[1].astype(F32)
        into_right = into_right + jnp.where(second, from_left * came_right, 0.0)
        into_left = into_left + jnp.where(second, 0.0, from_right * came_left)
        right = jnp.where(second, decay * came_right + right, decay * right + came_right)
        left = jnp.where(second, came_left + decay * left, left + decay * came_left)
        from_left = jnp.where(second, from_left * decay, from_left)
        from_right = jnp.where(second, from_right, from_right * decay)
        decay = decay * decay
    if last:
        quarter = tile >> (steps - 2)
        outs[0][...] = jnp.where((quarter & 1) == 1, left, right).astype(BF16)
        outs[1][...] = jnp.where(quarter >= 2, left, right).astype(BF16)
        outs[2][0] = into_right.astype(BF16)
        outs[2][1] = (into_left + turned * into_right).astype(BF16)
    else:
        outs[0][0] = right.astype(BF16)
        outs[0][1] = left.astype(BF16)


def merge_call(lines, ends, came, after, levels, steps):
    last = len(came) == steps - 2
    whole = jax.ShapeDtypeStruct(ends.shape, BF16)
    one = jax.ShapeDtypeStruct(ends.shape[1:], BF16)
    outs = [one, one, whole] if last else [whole]
    vmem = pl.BlockSpec(memory_space=pltpu.VMEM)
    held = [pl.BlockSpec(memory_space=pl.ANY)] * len(after)
    return pl.pallas_call(
        functools.partial(merge_kernel, levels, steps, len(came), last, len(after)),
        name="merge",
        in_specs=[vmem] * (2 + len(came)) + held,
        out_specs=[vmem] * len(outs) + held,
        out_shape=outs + [jax.ShapeDtypeStruct(array.shape, array.dtype) for array in after],
        input_output_aliases={2 + len(came) + k: len(outs) + k for k in range(len(after))},
        compiler_params=pltpu.CompilerParams(vmem_limit_bytes=VMEM),
        cost_estimate=taking(0.8),
    )(lines, ends, *came, *after)


def body(field, vert_filter, loc_filter, alpha_table, xscale_idx, yscale_idx, members):
    tile_count, mem_count = lax.axis_size("tile"), lax.axis_size("mem")
    slab_count, cols, rows = field.shape
    levels = vert_filter.shape[1]
    own_cols = cols // mem_count
    slabs = padded(slab_count)
    steps = tile_count.bit_length() - 1

    def swap(array, flip, axis="mem"):
        return lax.ppermute(array, axis, [(i, i ^ flip) for i in range(lax.axis_size(axis))])

    full_field = field.reshape(slab_count * cols, rows)
    flat_field = pltpu.with_memory_space_constraint(full_field, pltpu.HBM)
    mine = members.reshape(slab_count * cols, rows)
    other = swap(mine, 1)
    line_table = pltpu.with_memory_space_constraint(alpha_table, pltpu.HBM)
    line_entries = pltpu.with_memory_space_constraint(xscale_idx, pltpu.HBM)
    share = (lax.axis_index("mem") & (CORES - 1)).astype(jnp.int32).reshape(1)
    ends, own_0, lines = ends_call(share, line_table, line_entries, flat_field, levels, steps, cols, own_cols)
    blocks, came = [ends], []
    send, keep = ensemble_calls(loc_filter[0], full_field, mine, other, ends, levels, cols, own_cols)
    over = swap(send, 2)
    for level in range(steps - 2):
        came.append(swap(blocks[0], 1 << level, "tile"))
        *blocks, keep = merge_call(lines, ends, came, [keep], levels, steps)
    near, far, part = blocks
    last = {flip: swap(near if flip == 1 else far, flip << (steps - 2), "tile") for flip in (2, 3, 1)}
    own_1, coef = local_call(lines, full_field, near, levels, steps, cols, own_cols)
    mats, row_coef, vert = tables_call(alpha_table, yscale_idx, vert_filter[0], own_1, levels, own_cols, cols, slabs)
    shares = [part, last[1], last[2], last[3]]
    others = [swap(share, 1) for share in shares]
    done = rows_call(levels, own_0, coef, mats, row_coef, shares)
    scale = 1.0 / (mem_count * members.shape[0] - 1)
    return final_call(slab_count, levels, scale, done, own_1, coef, mats, row_coef, others, vert, keep, over)


def solution(mesh):
    return jax.shard_map(
        body,
        mesh=mesh,
        in_specs=(P(None, "tile", None), P(), P(), P(), P(), P(), P("mem", None, "tile", None)),
        out_specs=P(None, ("tile", "mem"), None),
        check_vma=False,
    )
```

```python
import functools

import jax
import jax.numpy as jnp
from jax import lax
from jax.experimental import pallas as pl
from jax.experimental.pallas import tpu as pltpu
from jax.sharding import PartitionSpec as P

F32, BF16 = jnp.float32, jnp.bfloat16
SUB = 16
CORES = 2
LANES = 256
BLOCK = 256
MIB = 1 << 20
VMEM = 32 * MIB


def iota(shape, dim):
    return lax.broadcasted_iota(jnp.int32, shape, dim)


def taking(microseconds):
    return pl.CostEstimate(flops=int(microseconds * 1.15e9), bytes_accessed=MIB // 4, transcendentals=0)


def split(number, size):
    assert size & (size - 1) == 0
    return number >> (size.bit_length() - 1), number & (size - 1)


def dot(left, right):
    return jnp.dot(left, right, preferred_element_type=F32)


def gain_of(alpha):
    rest = (1.0 - alpha) * (1.0 + alpha)
    return jnp.sqrt(rest) * rest / jnp.sqrt(1.0 + alpha * alpha)


def lookup(table_ref, entries):
    found = jnp.zeros(entries.shape, F32)
    for entry in range(table_ref.shape[0]):
        found = jnp.where(entries == entry, table_ref[entry], found)
    return found


def padded(slab_count):
    return -(-slab_count // (4 * SUB)) * 4 * SUB


def to_columns(perm, flat, out_ref, cols):
    total = flat.shape[0]
    wanted = out_ref.shape[0]
    step = SUB * cols
    for chunk in range(out_ref.shape[1] // SUB):
        depth = min(step, total - chunk * step)
        moved = dot(perm[:, :depth], flat[chunk * step : chunk * step + depth])
        out_ref[:, chunk * SUB : (chunk + 1) * SUB, :] = moved.reshape(wanted, SUB, -1).astype(out_ref.dtype)


def sweep(work, alpha):
    cols = work.shape[0]
    state = work[0]
    for col in range(1, cols):
        state = alpha * state + work[col]
        work[col] = state
    for col in range(cols - 2, -1, -1):
        state = alpha * state + work[col]
        work[col] = state


def transposer(cols):
    shape = (SUB * cols, SUB * cols)
    (out_col, out_slab), (in_slab, in_col) = split(iota(shape, 0), SUB), split(iota(shape, 1), cols)
    return ((out_slab == in_slab) & (out_col == in_col)).astype(BF16)


def share_rows(total, cols, subs, share):
    return slice(share * subs * cols, min((share + 1) * subs * cols, total))


def sweep_share(levels, slab_count, share, perm, alpha, held, work):
    cols, subs, lanes = work.shape
    first = share * subs
    held = jnp.where(iota(held.shape, 0) < (slab_count - first) * cols, held, 0)
    to_columns(perm, held, work, cols)
    is_level = iota((subs, lanes), 0) + first < levels
    alpha = jnp.where(is_level, alpha[0:1], alpha[1:2])
    sweep(work, alpha)
    return gain_of(alpha), is_level


def ends_kernel(
    levels, steps, slab_count, share_ref, table_ref, entries_ref, field_ref, ends_ref, own_ref, lines_ref, work
):
    pieces, cols, subs, lanes = work.shape
    own_cols = own_ref.shape[0]
    tile, mem = lax.axis_index("tile"), lax.axis_index("mem")
    share, perm = share_ref[0], transposer(cols)
    pair = lookup(table_ref, entries_ref[...])
    decay, turn = line_coefs(pair, cols)
    behind = reflected(decay, turn, tile, steps)
    lines_ref[0], lines_ref[1], lines_ref[2] = pair, decay, behind
    for piece in range(pieces):
        part = slice(piece * lanes, (piece + 1) * lanes)
        gain, is_level = sweep_share(levels, slab_count, share, perm, pair[:, part], field_ref[:, part], work.at[piece])
        turned = (decay * behind)[:, part]
        turned = jnp.where(is_level, turned[0:1], turned[1:2])
        forward = gain * work[piece, cols - 1]
        ends_ref[0, :, part] = forward.astype(BF16)
        ends_ref[1, :, part] = (gain * work[piece, 0] + turned * forward).astype(BF16)
        own_ref[:, :, part] = work[piece, pl.ds(mem * own_cols, own_cols)] * gain[None]


def ends_call(share, table, entries, flat_field, levels, steps, cols, own_cols):
    total, rows = flat_field.shape
    subs = padded(total // cols) // CORES
    vmem, smem = pl.BlockSpec(memory_space=pltpu.VMEM), pl.BlockSpec(memory_space=pltpu.SMEM)
    return pl.pallas_call(
        functools.partial(ends_kernel, levels, steps, total // cols),
        name="ends",
        grid_spec=pltpu.PrefetchScalarGridSpec(
            num_scalar_prefetch=1,
            grid=(1,),
            in_specs=[
                smem,
                pl.BlockSpec(entries.shape, lambda i, share: (0, 0)),
                pl.BlockSpec((subs * cols, rows), lambda i, share: (share[0], 0)),
            ],
            out_specs=[vmem] * 3,
            scratch_shapes=[pltpu.VMEM((rows // LANES, cols, subs, LANES), F32)],
        ),
        out_shape=[
            jax.ShapeDtypeStruct((2, subs, rows), BF16),
            jax.ShapeDtypeStruct((own_cols, subs, rows), F32),
            jax.ShapeDtypeStruct((3, 2, rows), F32),
        ],
        compiler_params=pltpu.CompilerParams(vmem_limit_bytes=VMEM),
        cost_estimate=taking(2.1),
    )(share, table, entries, flat_field)


def line_coefs(pair, cols):
    decay, turn = pair, pair
    while cols > 1:
        turn = turn * (1.0 + decay * decay)
        decay = decay * decay
        cols //= 2
    return decay, turn


def reflected(decay, turn, tile, steps):
    behind = (1 << steps) - 1 - tile
    total, power = jnp.zeros_like(turn), jnp.ones_like(turn)
    for level in range(steps):
        here = ((behind >> level) & 1) == 1
        total = jnp.where(here, total + power * power * turn, total)
        power = jnp.where(here, power * decay, power)
        turn = turn * (1.0 + decay * decay)
        decay = decay * decay
    return total


def local_kernel(levels, slab_count, lines_ref, field_ref, after_ref, own_ref, held_ref, work):
    pieces, cols, subs, lanes = work.shape
    own_cols = own_ref.shape[0]
    mem = lax.axis_index("mem")
    share = (mem & (CORES - 1)) ^ 1
    for core in range(CORES):
        rows = share_rows(slab_count * cols, cols, subs, core)

        @pl.when(share == core)
        def _():
            held_ref[0 : rows.stop - rows.start, :] = field_ref[rows, :]

    pair, perm = lines_ref[0], transposer(cols)
    for piece in range(pieces):
        part = slice(piece * lanes, (piece + 1) * lanes)
        gain, _ = sweep_share(levels, slab_count, share, perm, pair[:, part], held_ref[:, part], work.at[piece])
        own_ref[:, :, part] = work[piece, pl.ds(mem * own_cols, own_cols)] * gain[None]


def local_call(lines, flat_field, after, levels, cols, own_cols):
    total, rows = flat_field.shape
    subs = padded(total // cols) // CORES
    vmem = pl.BlockSpec(memory_space=pltpu.VMEM)
    return pl.pallas_call(
        functools.partial(local_kernel, levels, total // cols),
        name="local",
        in_specs=[vmem, vmem, pl.BlockSpec(memory_space=pl.ANY)],
        out_specs=vmem,
        out_shape=jax.ShapeDtypeStruct((own_cols, subs, rows), F32),
        scratch_shapes=[
            pltpu.VMEM((subs * cols, rows), BF16),
            pltpu.VMEM((rows // LANES, cols, subs, LANES), F32),
        ],
        compiler_params=pltpu.CompilerParams(vmem_limit_bytes=VMEM),
        cost_estimate=taking(0.5),
    )(lines, flat_field, after)


def coefs_kernel(steps, lines_ref, after_ref, coef_ref):
    cols = coef_ref.shape[1] - 3
    tile = lax.axis_index("tile")
    pair, decay, behind = lines_ref[0], lines_ref[1], lines_ref[2]
    square = pair * pair
    power, sums = jnp.ones_like(pair), jnp.zeros_like(pair)
    rights, geometric = [], []
    for _ in range(cols):
        power, sums = power * pair, sums * square + 1.0
        rights.append(power)
        geometric.append(sums)
    for col in range(cols):
        coef_ref[0, col] = rights[col] * geometric[cols - 1 - col]
        coef_ref[1, col] = rights[cols - 1 - col]
    turned = decay * behind
    from_left, from_right = jnp.ones_like(pair), jnp.ones_like(pair)
    for level in range(steps - 2):
        second = ((tile >> level) & 1) == 1
        from_left = jnp.where(second, from_left * decay, from_left)
        from_right = jnp.where(second, from_right, from_right * decay)
        decay = decay * decay
    quarter = tile >> (steps - 2)
    outer = (quarter == 0) | (quarter == 3)
    for flip, weight in ((1, 1.0), (2, decay), (3, jnp.where(outer, decay * decay, 1.0))):
        upper = (quarter ^ flip) < quarter
        coef_ref[0, cols + flip - 1] = jnp.where(upper, from_left * weight, 0.0)
        coef_ref[1, cols + flip - 1] = weight * jnp.where(upper, turned * from_left, from_right)


def coefs_call(lines, after, steps, cols):
    vmem = pl.BlockSpec(memory_space=pltpu.VMEM)
    return pl.pallas_call(
        functools.partial(coefs_kernel, steps),
        name="coefs",
        in_specs=[vmem, pl.BlockSpec(memory_space=pl.ANY)],
        out_specs=vmem,
        out_shape=jax.ShapeDtypeStruct((2, cols + 3, *lines.shape[1:]), F32),
        compiler_params=pltpu.CompilerParams(vmem_limit_bytes=VMEM),
        cost_estimate=taking(4.0),
    )(lines, after)


def spread(matrix, levels, row_slab, row_col, col_slab, col_col):
    rows, cols = row_slab.shape
    size = matrix.shape[0]
    left = (iota((rows, size), 1) == row_slab[:, :size]).astype(BF16)
    right = (iota((size, cols), 0) == col_slab[:size, :]).astype(BF16)
    inner = dot(left, matrix).astype(BF16)
    full = dot(inner, right)
    full = jnp.where((row_slab >= levels) & (row_slab == col_slab), 1.0, full)
    return jnp.where(row_col == col_col, full, 0.0).astype(BF16)


def selection(block, shape, own_cols, cols):
    (slot, out_slab), (in_slab, in_col) = split(iota(shape, 0), SUB), split(iota(shape, 1), cols)
    return ((out_slab == in_slab) & (block * own_cols + slot == in_col)).astype(BF16)


def member_term(local, member, field):
    scaled = (member * field.astype(F32)).astype(BF16).reshape(local.shape[0], -1)
    return member * dot(local, scaled).reshape(member.shape)


def mine_kernel(
    levels, cols, loc_ref, field_ref, mine_ref, after_ref, perm_ref, local_ref, order_ref, field_out, total_out, member_w
):
    own_cols, slabs, _ = field_out.shape
    chip, core = split(lax.axis_index("mem"), 2)
    perm = selection(2 * (1 - chip) + core, perm_ref.shape, own_cols, cols)
    perm_ref[...] = perm
    to_columns(perm, field_ref, field_out, cols)
    to_columns(perm, mine_ref, member_w, cols)
    row, col = iota(local_ref.shape, 0), iota(local_ref.shape, 1)
    (row_col, row_slab), (col_col, col_slab) = split(row, slabs), split(col, slabs)
    local = spread(loc_ref[...], levels, row_slab, row_col, col_slab, col_col)
    local_ref[...] = local
    row_slab, row_col = split(row, own_cols)
    order_ref[...] = ((row_slab == col_slab) & (row_col == col_col)).astype(BF16)
    total_out[...] = member_term(local, member_w[...], field_out[...])


def send_kernel(cols, perm_ref, local_ref, order_ref, field_w, total_ref, other_ref, send_ref, member_w):
    to_columns(perm_ref[...], other_ref, member_w, cols)
    total = total_ref[...] + member_term(local_ref[...], member_w[...], field_w[...])
    total = total.reshape(order_ref.shape[0], -1).astype(BF16)
    send_ref[...] = dot(order_ref[...], total)[: send_ref.shape[0]].astype(BF16)


def keep_kernel(cols, local_ref, order_ref, field_ref, mine_ref, other_ref, after_ref, keep_ref, field_w, mine_w, other_w):
    own_cols = field_w.shape[0]
    perm = selection(lax.axis_index("mem"), (own_cols * SUB, cols * SUB), own_cols, cols)
    for ref, out in ((field_ref, field_w), (mine_ref, mine_w), (other_ref, other_w)):
        to_columns(perm, ref, out, cols)
    field, local = field_w[...], local_ref[...]
    total = member_term(local, mine_w[...], field) + member_term(local, other_w[...], field)
    total = total.reshape(order_ref.shape[0], -1)
    high = total.astype(BF16)
    ordered = dot(order_ref[...], high) + dot(order_ref[...], (total - high.astype(F32)).astype(BF16))
    keep_ref[...] = ordered[: keep_ref.shape[0]]


def mine_call(loc, flat_field, mine, after, levels, cols, own_cols):
    total, rows = flat_field.shape
    slabs = padded(total // cols)
    vmem = pl.BlockSpec(memory_space=pltpu.VMEM)
    work, side = (own_cols, slabs, rows), own_cols * slabs
    return pl.pallas_call(
        functools.partial(mine_kernel, levels, cols),
        name="mine",
        in_specs=[vmem] * 3 + [pl.BlockSpec(memory_space=pl.ANY)],
        out_specs=[vmem] * 5,
        out_shape=[
            jax.ShapeDtypeStruct((own_cols * SUB, cols * SUB), BF16),
            jax.ShapeDtypeStruct((side, side), BF16),
            jax.ShapeDtypeStruct((side, side), BF16),
            jax.ShapeDtypeStruct(work, BF16),
            jax.ShapeDtypeStruct(work, F32),
        ],
        scratch_shapes=[pltpu.VMEM(work, F32)],
        compiler_params=pltpu.CompilerParams(vmem_limit_bytes=VMEM),
        cost_estimate=taking(1.8),
    )(loc, flat_field, mine, after)


def send_call(held, other, cols):
    own_cols, _, rows = held[3].shape
    vmem = pl.BlockSpec(memory_space=pltpu.VMEM)
    return pl.pallas_call(
        functools.partial(send_kernel, cols),
        name="send",
        in_specs=[vmem] * 6,
        out_specs=vmem,
        out_shape=jax.ShapeDtypeStruct((other.shape[0] // cols * own_cols, rows), BF16),
        scratch_shapes=[pltpu.VMEM(held[4].shape, F32)],
        compiler_params=pltpu.CompilerParams(vmem_limit_bytes=VMEM),
        cost_estimate=taking(0.8),
    )(*held, other)


def keep_call(held, flat_field, mine, other, after, cols):
    own_cols, _, rows = held[3].shape
    vmem = pl.BlockSpec(memory_space=pltpu.VMEM)
    return pl.pallas_call(
        functools.partial(keep_kernel, cols),
        name="keep",
        in_specs=[vmem] * 5 + [pl.BlockSpec(memory_space=pl.ANY)],
        out_specs=vmem,
        out_shape=jax.ShapeDtypeStruct((other.shape[0] // cols * own_cols, rows), F32),
        scratch_shapes=[pltpu.VMEM(held[4].shape, F32)] * 3,
        compiler_params=pltpu.CompilerParams(vmem_limit_bytes=VMEM),
        cost_estimate=taking(0.6),
    )(held[1], held[2], flat_field, mine, other, after)


def tables_kernel(levels, own_cols, col_dev, slabs, table_ref, entries_ref, vert_ref, after_ref, mat_ref, coef_ref, vert_out):
    first = lax.axis_index("tile") * col_dev + lax.axis_index("mem") * own_cols
    count = 2 * own_cols
    by_row = jnp.zeros((count, 1), F32)
    every, found = entries_ref[...], jnp.zeros(entries_ref.shape, F32)
    for entry in range(table_ref.shape[1]):
        found = jnp.where(every == entry, table_ref[0:1, entry : entry + 1], found)
    for col in range(own_cols):
        here = iota(found.shape, 1) == first + col
        alphas = jnp.sum(jnp.where(here, found, 0.0), axis=1, keepdims=True)
        for var in range(2):
            by_row = jnp.where(iota((count, 1), 0) == var * own_cols + col, alphas[var : var + 1], by_row)

    def series(alpha, number):
        alpha = jnp.broadcast_to(alpha, number.shape)
        total, unit = jnp.zeros(number.shape, F32), jnp.ones(number.shape, F32)
        single, power, both = alpha, alpha * alpha, jnp.ones(number.shape, F32)
        for bit in range(BLOCK.bit_length()):
            here = ((number >> bit) & 1) == 1
            total = jnp.where(here, unit + power * total, total)
            both = jnp.where(here, both * single, both)
            unit, single, power = unit * (1.0 + power), single * single, power * power
        return total, both

    place = iota((count, BLOCK), 1)
    across, right = series(by_row, BLOCK - place)
    down = jnp.concatenate([across, jnp.zeros((128 - count, BLOCK), F32)], 0).T
    _, left = series(by_row, place + 1)
    coef_ref[0] = left * across
    coef_ref[1] = right
    coef_ref[2] = jnp.broadcast_to(right[:, 0:1], right.shape)
    coef_ref[3] = jnp.broadcast_to(left[:, 0:1] * across[:, 0:1], right.shape)
    far = jnp.abs(iota((BLOCK, BLOCK), 0) - iota((BLOCK, BLOCK), 1)).astype(F32)
    for k in range(count):
        alpha = by_row[k : k + 1]
        decay = jnp.exp(far * jnp.log(jnp.maximum(alpha, 1e-30)))
        reach = jnp.minimum(down[:, k : k + 1], across[k : k + 1])
        mat_ref[k] = (gain_of(alpha) * decay * reach).astype(BF16)
    shape = vert_out.shape[1:]
    (row_slab, row_col), (col_col, col_slab) = split(iota(shape, 0), own_cols), split(iota(shape, 1), slabs // CORES)
    for share in range(CORES):
        first = share * (slabs // CORES)
        vert_out[share] = spread(vert_ref[...], levels, row_slab, row_col, col_slab + first, col_col)


def tables_call(table, entries, vert, after, levels, own_cols, col_dev, slabs):
    count = 2 * own_cols
    return pl.pallas_call(
        functools.partial(tables_kernel, levels, own_cols, col_dev, slabs),
        name="tables",
        in_specs=[pl.BlockSpec(memory_space=pltpu.VMEM)] * 3 + [pl.BlockSpec(memory_space=pl.ANY)],
        out_specs=[pl.BlockSpec(memory_space=pltpu.VMEM)] * 3,
        out_shape=[
            jax.ShapeDtypeStruct((count, BLOCK, BLOCK), BF16),
            jax.ShapeDtypeStruct((4, count, BLOCK), F32),
            jax.ShapeDtypeStruct((CORES, own_cols * slabs, own_cols * slabs // CORES), BF16),
        ],
        compiler_params=pltpu.CompilerParams(vmem_limit_bytes=VMEM),
        cost_estimate=taking(0.4),
    )(table[None], entries, vert, after)


def along_rows(lines, matrix, coef):
    count, rows = lines.shape
    blocks = rows // BLOCK
    parts = jnp.concatenate([lines[:, b * BLOCK : (b + 1) * BLOCK] for b in range(blocks)], 0)
    local = dot(parts.astype(BF16), matrix)
    local = [local[b * count : (b + 1) * count] for b in range(blocks)]
    into, right, decay, turn = coef[0:1], coef[1:2], coef[2:3, 0:1], coef[3:4, 0:1]
    forward, state = [None], None
    for b in range(blocks - 1):
        end = local[b][:, BLOCK - 1 : BLOCK]
        state = end if state is None else decay * state + end
        forward.append(state)
    out, state = [None] * blocks, None
    for b in range(blocks - 1, -1, -1):
        piece = local[b]
        if forward[b] is not None:
            piece = piece + into * forward[b]
        if state is not None:
            piece = piece + right * state
        out[b] = piece
        if b:
            start = local[b][:, 0:1] + turn * forward[b]
            state = start if state is None else decay * state + start
    return out


def filter_share(levels, share, own_ref, coef_ref, mat_ref, row_coef_ref, part_ref, last_refs, out_ref):
    own_cols, subs, rows = own_ref.shape
    cols = coef_ref.shape[1] - 3
    mem = lax.axis_index("mem")
    end = slice(subs - 8, subs)
    is_level = iota((8, rows), 0) + share * subs + subs - 8 < levels
    lasts = [ref[...].astype(F32) for ref in last_refs]
    carry, carry_end = [], []
    for side in range(2):
        value = part_ref[side].astype(F32)
        other = value[end]
        for k, last in enumerate(lasts):
            value = value + coef_ref[side, cols + k, 0:1] * last
            other = other + coef_ref[side, cols + k, 1:2] * last[end]
        carry.append(value)
        carry_end.append(other)
    for col in range(own_cols):
        pair = coef_ref[:, mem * own_cols + col]
        own = own_ref[col]
        lines = own + pair[0, 0:1] * carry[0] + pair[1, 0:1] * carry[1]
        last_lines = own[end] + pair[0, 1:2] * carry_end[0] + pair[1, 1:2] * carry_end[1]
        main = along_rows(lines, mat_ref[col], row_coef_ref[:, col])
        last = along_rows(last_lines, mat_ref[own_cols + col], row_coef_ref[:, own_cols + col])
        for b, (piece, extra) in enumerate(zip(main, last)):
            place = slice(b * BLOCK, (b + 1) * BLOCK)
            out_ref[col, 0 : subs - 8, place] = piece[0 : subs - 8]
            out_ref[col, end, place] = jnp.where(is_level[:, place], piece[end], extra)


def mixed(vert, static):
    high = static.astype(BF16)
    return dot(vert, high) + dot(vert, (static - high.astype(F32)).astype(BF16))


def rows_kernel(levels, scale, own_ref, coef_ref, mat_ref, row_coef_ref, part_ref, *refs):
    *last_refs, vert_ref, keep_ref, base_ref, filt = refs
    share = lax.axis_index("mem") & (CORES - 1)
    filter_share(levels, share, own_ref, coef_ref, mat_ref, row_coef_ref, part_ref, last_refs, filt)
    total = mixed(vert_ref[share], filt[...].reshape(vert_ref.shape[2], -1))
    base_ref[...] = total[: base_ref.shape[0]] + keep_ref[...] * scale


def rows_call(levels, scale, own, coef, mats, row_coef, shares, vert, keep):
    vmem = pl.BlockSpec(memory_space=pltpu.VMEM)
    args = [own, coef, mats, row_coef, *shares, vert, keep]
    return pl.pallas_call(
        functools.partial(rows_kernel, levels, scale),
        name="rows",
        in_specs=[vmem] * len(args),
        out_specs=vmem,
        out_shape=jax.ShapeDtypeStruct(keep.shape, F32),
        scratch_shapes=[pltpu.VMEM(own.shape, F32)],
        compiler_params=pltpu.CompilerParams(vmem_limit_bytes=VMEM),
        cost_estimate=taking(1.2),
    )(*args)


def join_kernel(
    levels, own_ref, coef_ref, mat_ref, row_coef_ref, part_ref, last_1_ref, last_2_ref, last_3_ref, vert_ref, base_ref,
    total_ref, filt
):
    other = 1 - (lax.axis_index("mem") & (CORES - 1))
    last_refs = last_1_ref, last_2_ref, last_3_ref
    filter_share(levels, other, own_ref, coef_ref, mat_ref, row_coef_ref, part_ref, last_refs, filt)
    total = mixed(vert_ref[other], filt[...].reshape(vert_ref.shape[2], -1))
    total_ref[...] = total[: base_ref.shape[0]] + base_ref[...]


def join_call(levels, own, coef, mats, row_coef, shares, vert, base):
    vmem = pl.BlockSpec(memory_space=pltpu.VMEM)
    args = [own, coef, mats, row_coef, *shares, vert, base]
    return pl.pallas_call(
        functools.partial(join_kernel, levels),
        name="join",
        in_specs=[vmem] * len(args),
        out_specs=vmem,
        out_shape=jax.ShapeDtypeStruct(base.shape, F32),
        scratch_shapes=[pltpu.VMEM(own.shape, F32)],
        compiler_params=pltpu.CompilerParams(vmem_limit_bytes=VMEM),
        cost_estimate=taking(0.8),
    )(*args)


def final_kernel(scale, total_ref, came_ref, out_hbm, out_ref, sent):
    count, own_cols, rows = out_ref.shape
    copies = []
    for piece, first in enumerate(range(0, count, SUB)):
        place = slice(first, min(first + SUB, count))
        wide = slice(place.start * own_cols, place.stop * own_cols)
        total = total_ref[wide] + came_ref[wide].astype(F32) * scale
        out_ref[place] = total.reshape(place.stop - place.start, own_cols, rows).astype(BF16)
        copies.append(pltpu.make_async_copy(out_ref.at[place], out_hbm.at[place], sent.at[piece]))
        copies[-1].start()
    for copy in copies:
        copy.wait()


def final_call(slab_count, own_cols, scale, total, came):
    rows = total.shape[1]
    vmem = pl.BlockSpec(memory_space=pltpu.VMEM)
    out_shape = (slab_count, own_cols, rows)
    return pl.pallas_call(
        functools.partial(final_kernel, scale),
        name="final",
        in_specs=[vmem] * 2,
        out_specs=pl.BlockSpec(memory_space=pl.ANY),
        out_shape=jax.ShapeDtypeStruct(out_shape, BF16),
        scratch_shapes=[pltpu.VMEM(out_shape, BF16), pltpu.SemaphoreType.DMA((-(-slab_count // SUB),))],
        compiler_params=pltpu.CompilerParams(vmem_limit_bytes=VMEM),
        cost_estimate=taking(0.8),
    )(total, came)


def merge_kernel(levels, steps, step, last, after_count, *refs):
    lines_ref, ends_ref = refs[:2]
    came_refs, outs = refs[2 : 2 + step], refs[2 + step + after_count :]
    _, subs, rows = ends_ref.shape
    tile, mem = lax.axis_index("tile"), lax.axis_index("mem")
    is_level = iota((subs, rows), 0) + (mem & (CORES - 1)) * subs < levels
    decay = jnp.where(is_level, lines_ref[1, 0:1], lines_ref[1, 1:2])
    behind = jnp.where(is_level, lines_ref[2, 0:1], lines_ref[2, 1:2])
    turned = behind * decay
    right, left = ends_ref[0].astype(F32), ends_ref[1].astype(F32)
    into_right, into_left, from_left, from_right = 0.0, behind * right, 1.0, 1.0
    for level, came_ref in enumerate(came_refs):
        second = ((tile >> level) & 1) == 1
        came_right, came_left = came_ref[0].astype(F32), came_ref[1].astype(F32)
        into_right = into_right + jnp.where(second, from_left * came_right, 0.0)
        into_left = into_left + jnp.where(second, 0.0, from_right * came_left)
        right = jnp.where(second, decay * came_right + right, decay * right + came_right)
        left = jnp.where(second, came_left + decay * left, left + decay * came_left)
        from_left = jnp.where(second, from_left * decay, from_left)
        from_right = jnp.where(second, from_right, from_right * decay)
        decay = decay * decay
    if last:
        quarter = tile >> (steps - 2)
        outs[0][...] = jnp.where((quarter & 1) == 1, left, right).astype(BF16)
        outs[1][...] = jnp.where(quarter >= 2, left, right).astype(BF16)
        outs[2][0] = into_right.astype(BF16)
        outs[2][1] = (into_left + turned * into_right).astype(BF16)
    else:
        outs[0][0] = right.astype(BF16)
        outs[0][1] = left.astype(BF16)


def merge_call(lines, ends, came, after, levels, steps):
    last = len(came) == steps - 2
    whole = jax.ShapeDtypeStruct(ends.shape, BF16)
    one = jax.ShapeDtypeStruct(ends.shape[1:], BF16)
    outs = [one, one, whole] if last else [whole]
    vmem = pl.BlockSpec(memory_space=pltpu.VMEM)
    held = [pl.BlockSpec(memory_space=pl.ANY)] * len(after)
    return pl.pallas_call(
        functools.partial(merge_kernel, levels, steps, len(came), last, len(after)),
        name="merge",
        in_specs=[vmem] * (2 + len(came)) + held,
        out_specs=[vmem] * len(outs) + held,
        out_shape=outs + [jax.ShapeDtypeStruct(array.shape, array.dtype) for array in after],
        input_output_aliases={2 + len(came) + k: len(outs) + k for k in range(len(after))},
        compiler_params=pltpu.CompilerParams(vmem_limit_bytes=VMEM),
        cost_estimate=taking(0.8),
    )(lines, ends, *came, *after)


def body(field, vert_filter, loc_filter, alpha_table, xscale_idx, yscale_idx, members):
    tile_count, mem_count = lax.axis_size("tile"), lax.axis_size("mem")
    slab_count, cols, rows = field.shape
    levels = vert_filter.shape[1]
    own_cols = cols // mem_count
    slabs = padded(slab_count)
    steps = tile_count.bit_length() - 1

    def swap(array, flip, axis="mem"):
        return lax.ppermute(array, axis, [(i, i ^ flip) for i in range(lax.axis_size(axis))])

    full_field = field.reshape(slab_count * cols, rows)
    flat_field = pltpu.with_memory_space_constraint(full_field, pltpu.HBM)
    mine = members.reshape(slab_count * cols, rows)
    other = swap(mine, 1)
    line_table = pltpu.with_memory_space_constraint(alpha_table, pltpu.HBM)
    line_entries = pltpu.with_memory_space_constraint(xscale_idx, pltpu.HBM)
    share = (lax.axis_index("mem") & (CORES - 1)).astype(jnp.int32).reshape(1)
    ends, own_0, lines = ends_call(share, line_table, line_entries, flat_field, levels, steps, cols, own_cols)
    blocks, came = [ends], []
    held = mine_call(loc_filter[0], full_field, mine, ends, levels, cols, own_cols)
    send = send_call(held, other, cols)
    over = swap(send, 2)
    coef = coefs_call(lines, send, steps, cols)
    for level in range(steps - 2):
        came.append(swap(blocks[0], 1 << level, "tile"))
        *blocks, coef = merge_call(lines, ends, came, [coef], levels, steps)
    near, far, part = blocks
    last = {flip: swap(near if flip == 1 else far, flip << (steps - 2), "tile") for flip in (2, 3, 1)}
    keep = keep_call(held, full_field, mine, other, near, cols)
    own_1 = local_call(lines, full_field, near, levels, cols, own_cols)
    mats, row_coef, vert = tables_call(alpha_table, yscale_idx, vert_filter[0], own_1, levels, own_cols, cols, slabs)
    shares = [part, last[1], last[2], last[3]]
    others = [swap(share, 1) for share in shares]
    scale = 1.0 / (mem_count * members.shape[0] - 1)
    base = rows_call(levels, scale, own_0, coef, mats, row_coef, shares, vert, keep)
    total = join_call(levels, own_1, coef, mats, row_coef, others, vert, base)
    return final_call(slab_count, own_cols, scale, total, over)


def solution(mesh):
    return jax.shard_map(
        body,
        mesh=mesh,
        in_specs=(P(None, "tile", None), P(), P(), P(), P(), P(), P("mem", None, "tile", None)),
        out_specs=P(None, ("tile", "mem"), None),
        check_vma=False,
    )
```

```python
import functools

import jax
import jax.numpy as jnp
from jax import lax
from jax.experimental import pallas as pl
from jax.experimental.pallas import tpu as pltpu
from jax.sharding import PartitionSpec as P

F32, BF16 = jnp.float32, jnp.bfloat16
SUB = 16
CORES = 2
LANES = 256
ORDER = (2, 3, 1)
FETCHES = 1
BLOCK = 256
MIB = 1 << 20
VMEM = 32 * MIB


def iota(shape, dim):
    return lax.broadcasted_iota(jnp.int32, shape, dim)


def taking(microseconds):
    return pl.CostEstimate(flops=int(microseconds * 1.15e9), bytes_accessed=MIB // 4, transcendentals=0)


def split(number, size):
    assert size & (size - 1) == 0
    return number >> (size.bit_length() - 1), number & (size - 1)


def dot(left, right):
    return jnp.dot(left, right, preferred_element_type=F32)


def gain_of(alpha):
    rest = (1.0 - alpha) * (1.0 + alpha)
    return jnp.sqrt(rest) * rest / jnp.sqrt(1.0 + alpha * alpha)


def lookup(table_ref, entries):
    found = jnp.zeros(entries.shape, F32)
    for entry in range(table_ref.shape[0]):
        found = jnp.where(entries == entry, table_ref[entry], found)
    return found


def padded(slab_count):
    return -(-slab_count // (4 * SUB)) * 4 * SUB


def to_columns(perm, flat, out_ref, cols):
    total = flat.shape[0]
    wanted = out_ref.shape[0]
    step = SUB * cols
    for chunk in range(out_ref.shape[1] // SUB):
        depth = min(step, total - chunk * step)
        moved = dot(perm[:, :depth], flat[chunk * step : chunk * step + depth])
        out_ref[:, chunk * SUB : (chunk + 1) * SUB, :] = moved.reshape(wanted, SUB, -1).astype(out_ref.dtype)


def sweep(work, alpha):
    cols = work.shape[0]
    state = work[0]
    for col in range(1, cols):
        state = alpha * state + work[col]
        work[col] = state
    for col in range(cols - 2, -1, -1):
        state = alpha * state + work[col]
        work[col] = state


def transposer(cols):
    shape = (SUB * cols, SUB * cols)
    (out_col, out_slab), (in_slab, in_col) = split(iota(shape, 0), SUB), split(iota(shape, 1), cols)
    return ((out_slab == in_slab) & (out_col == in_col)).astype(BF16)


def share_rows(total, cols, subs, share):
    return slice(share * subs * cols, min((share + 1) * subs * cols, total))


def clear_rest(held_ref, rows):
    first = rows.stop - rows.start
    if first < held_ref.shape[0]:
        held_ref[first:, :] = jnp.zeros((held_ref.shape[0] - first, held_ref.shape[1]), BF16)


def sweep_share(levels, share, perm, alpha, held, work):
    cols, subs, lanes = work.shape
    to_columns(perm, held, work, cols)
    is_level = iota((subs, lanes), 0) + share * subs < levels
    alpha = jnp.where(is_level, alpha[0:1], alpha[1:2])
    sweep(work, alpha)
    return gain_of(alpha), is_level


def ends_kernel(
    levels, steps, slab_count, table_hbm, entries_hbm, loc_hbm, field_hbm, ends_ref, own_ref, lines_ref, perm_ref,
    local_ref, order_ref, table_ref, entries_ref, loc_ref, held_ref, work, small, arrived
):
    pieces, cols, subs, lanes = work.shape
    own_cols = own_ref.shape[0]
    slabs, rows = CORES * subs, held_ref.shape[1]
    tile, mem = lax.axis_index("tile"), lax.axis_index("mem")
    chip, share = split(mem, CORES)
    parts = arrived.shape[0]

    def fetch(part, begin):
        width = rows // parts
        place = pl.ds(part * width, width)
        for core in range(CORES):
            held = share_rows(slab_count * cols, cols, subs, core)

            @pl.when(share == core)
            def _():
                copy = pltpu.make_async_copy(
                    field_hbm.at[held, place], held_ref.at[0 : held.stop - held.start, place], arrived.at[part]
                )
                if begin:
                    copy.start()
                    clear_rest(held_ref, held)
                else:
                    copy.wait()

    for part in range(parts):
        fetch(part, True)
    given = [
        pltpu.make_async_copy(source, target, small.at[k])
        for k, (source, target) in enumerate(
            ((table_hbm, table_ref), (entries_hbm, entries_ref), (loc_hbm, loc_ref))
        )
    ]
    for copy in given:
        copy.start()
    perm_ref[...] = selection(2 * (1 - chip) + share, perm_ref.shape, own_cols, cols)
    row, col = iota(local_ref.shape, 0), iota(local_ref.shape, 1)
    (row_col, row_slab), (col_col, col_slab) = split(row, slabs), split(col, slabs)
    order_slab, order_col = split(row, own_cols)
    order_ref[...] = ((order_slab == col_slab) & (order_col == col_col)).astype(BF16)
    perm = transposer(cols)
    for copy in given:
        copy.wait()
    local_ref[...] = spread(loc_ref[...], levels, row_slab, row_col, col_slab, col_col)
    pair = lookup(table_ref, entries_ref[...])
    decay, turn = line_coefs(pair, cols)
    behind = reflected(decay, turn, tile, steps)
    lines_ref[0], lines_ref[1], lines_ref[2] = pair, decay, behind
    for piece in range(pieces):
        if piece % (pieces // parts) == 0:
            fetch(piece // (pieces // parts), False)
        part = slice(piece * lanes, (piece + 1) * lanes)
        gain, is_level = sweep_share(levels, share, perm, pair[:, part], held_ref[:, part], work.at[piece])
        turned = (decay * behind)[:, part]
        turned = jnp.where(is_level, turned[0:1], turned[1:2])
        forward = gain * work[piece, cols - 1]
        ends_ref[0, :, part] = forward.astype(BF16)
        ends_ref[1, :, part] = (gain * work[piece, 0] + turned * forward).astype(BF16)
        own_ref[:, :, part] = work[piece, pl.ds(mem * own_cols, own_cols)] * gain[None]


def ends_call(table, entries, loc, flat_field, levels, steps, cols, own_cols):
    total, rows = flat_field.shape
    subs = padded(total // cols) // CORES
    side = own_cols * CORES * subs
    vmem = pl.BlockSpec(memory_space=pltpu.VMEM)
    return pl.pallas_call(
        functools.partial(ends_kernel, levels, steps, total // cols),
        name="ends",
        in_specs=[pl.BlockSpec(memory_space=pl.ANY)] * 4,
        out_specs=[vmem] * 6,
        out_shape=[
            jax.ShapeDtypeStruct((2, subs, rows), BF16),
            jax.ShapeDtypeStruct((own_cols, subs, rows), F32),
            jax.ShapeDtypeStruct((3, 2, rows), F32),
            jax.ShapeDtypeStruct((own_cols * SUB, cols * SUB), BF16),
            jax.ShapeDtypeStruct((side, side), BF16),
            jax.ShapeDtypeStruct((side, side), BF16),
        ],
        scratch_shapes=[
            pltpu.SMEM(table.shape, F32),
            pltpu.VMEM(entries.shape, jnp.int32),
            pltpu.VMEM(loc.shape, BF16),
            pltpu.VMEM((subs * cols, rows), BF16),
            pltpu.VMEM((rows // LANES, cols, subs, LANES), F32),
            pltpu.SemaphoreType.DMA((3,)),
            pltpu.SemaphoreType.DMA((FETCHES,)),
        ],
        compiler_params=pltpu.CompilerParams(vmem_limit_bytes=VMEM),
        cost_estimate=taking(2.1),
    )(table, entries, loc, flat_field)


def line_coefs(pair, cols):
    decay, turn = pair, pair
    while cols > 1:
        turn = turn * (1.0 + decay * decay)
        decay = decay * decay
        cols //= 2
    return decay, turn


def reflected(decay, turn, tile, steps):
    behind = (1 << steps) - 1 - tile
    total, power = jnp.zeros_like(turn), jnp.ones_like(turn)
    for level in range(steps):
        here = ((behind >> level) & 1) == 1
        total = jnp.where(here, total + power * power * turn, total)
        power = jnp.where(here, power * decay, power)
        turn = turn * (1.0 + decay * decay)
        decay = decay * decay
    return total


def local_kernel(levels, slab_count, lines_ref, field_ref, after_ref, own_ref, held_ref, work):
    pieces, cols, subs, lanes = work.shape
    own_cols = own_ref.shape[0]
    mem = lax.axis_index("mem")
    share = (mem & (CORES - 1)) ^ 1
    for core in range(CORES):
        rows = share_rows(slab_count * cols, cols, subs, core)

        @pl.when(share == core)
        def _():
            held_ref[0 : rows.stop - rows.start, :] = field_ref[rows, :]
            clear_rest(held_ref, rows)

    pair, perm = lines_ref[0], transposer(cols)
    for piece in range(pieces):
        part = slice(piece * lanes, (piece + 1) * lanes)
        gain, _ = sweep_share(levels, share, perm, pair[:, part], held_ref[:, part], work.at[piece])
        own_ref[:, :, part] = work[piece, pl.ds(mem * own_cols, own_cols)] * gain[None]


def local_call(lines, flat_field, after, levels, cols, own_cols):
    total, rows = flat_field.shape
    subs = padded(total // cols) // CORES
    vmem = pl.BlockSpec(memory_space=pltpu.VMEM)
    return pl.pallas_call(
        functools.partial(local_kernel, levels, total // cols),
        name="local",
        in_specs=[vmem, vmem, pl.BlockSpec(memory_space=pl.ANY)],
        out_specs=vmem,
        out_shape=jax.ShapeDtypeStruct((own_cols, subs, rows), F32),
        scratch_shapes=[
            pltpu.VMEM((subs * cols, rows), BF16),
            pltpu.VMEM((rows // LANES, cols, subs, LANES), F32),
        ],
        compiler_params=pltpu.CompilerParams(vmem_limit_bytes=VMEM),
        cost_estimate=taking(0.5),
    )(lines, flat_field, after)


def coefs_kernel(steps, lines_ref, after_ref, coef_ref):
    cols = coef_ref.shape[1] - 3
    tile = lax.axis_index("tile")
    pair, decay, behind = lines_ref[0], lines_ref[1], lines_ref[2]
    square = pair * pair
    power, sums = jnp.ones_like(pair), jnp.zeros_like(pair)
    rights, geometric = [], []
    for _ in range(cols):
        power, sums = power * pair, sums * square + 1.0
        rights.append(power)
        geometric.append(sums)
    for col in range(cols):
        coef_ref[0, col] = rights[col] * geometric[cols - 1 - col]
        coef_ref[1, col] = rights[cols - 1 - col]
    turned = decay * behind
    from_left, from_right = jnp.ones_like(pair), jnp.ones_like(pair)
    for level in range(steps - 2):
        second = ((tile >> level) & 1) == 1
        from_left = jnp.where(second, from_left * decay, from_left)
        from_right = jnp.where(second, from_right, from_right * decay)
        decay = decay * decay
    quarter = tile >> (steps - 2)
    outer = (quarter == 0) | (quarter == 3)
    for flip, weight in ((1, 1.0), (2, decay), (3, jnp.where(outer, decay * decay, 1.0))):
        upper = (quarter ^ flip) < quarter
        coef_ref[0, cols + ORDER.index(flip)] = jnp.where(upper, from_left * weight, 0.0)
        coef_ref[1, cols + ORDER.index(flip)] = weight * jnp.where(upper, turned * from_left, from_right)


def coefs_call(lines, after, steps, cols):
    vmem = pl.BlockSpec(memory_space=pltpu.VMEM)
    return pl.pallas_call(
        functools.partial(coefs_kernel, steps),
        name="coefs",
        in_specs=[vmem, pl.BlockSpec(memory_space=pl.ANY)],
        out_specs=vmem,
        out_shape=jax.ShapeDtypeStruct((2, cols + 3, *lines.shape[1:]), F32),
        compiler_params=pltpu.CompilerParams(vmem_limit_bytes=VMEM),
        cost_estimate=taking(4.0),
    )(lines, after)


def spread(matrix, levels, row_slab, row_col, col_slab, col_col):
    rows, cols = row_slab.shape
    size = matrix.shape[0]
    left = (iota((rows, size), 1) == row_slab[:, :size]).astype(BF16)
    right = (iota((size, cols), 0) == col_slab[:size, :]).astype(BF16)
    inner = dot(left, matrix).astype(BF16)
    full = dot(inner, right)
    full = jnp.where((row_slab >= levels) & (row_slab == col_slab), 1.0, full)
    return jnp.where(row_col == col_col, full, 0.0).astype(BF16)


def selection(block, shape, own_cols, cols):
    (slot, out_slab), (in_slab, in_col) = split(iota(shape, 0), SUB), split(iota(shape, 1), cols)
    return ((out_slab == in_slab) & (block * own_cols + slot == in_col)).astype(BF16)


def member_term(local, member, field):
    scaled = (member * field.astype(F32)).astype(BF16).reshape(local.shape[0], -1)
    return member * dot(local, scaled).reshape(member.shape)


def mine_kernel(cols, perm_ref, local_ref, field_ref, mine_ref, after_ref, field_out, total_out, member_w):
    to_columns(perm_ref[...], field_ref, field_out, cols)
    to_columns(perm_ref[...], mine_ref, member_w, cols)
    total_out[...] = member_term(local_ref[...], member_w[...], field_out[...])


def send_kernel(cols, perm_ref, local_ref, order_ref, field_w, total_ref, other_ref, send_ref, member_w):
    to_columns(perm_ref[...], other_ref, member_w, cols)
    total = total_ref[...] + member_term(local_ref[...], member_w[...], field_w[...])
    total = total.reshape(order_ref.shape[0], -1).astype(BF16)
    send_ref[...] = dot(order_ref[...], total)[: send_ref.shape[0]].astype(BF16)


def keep_kernel(cols, local_ref, order_ref, field_ref, mine_ref, other_ref, after_ref, keep_ref, field_w, mine_w, other_w):
    own_cols = field_w.shape[0]
    perm = selection(lax.axis_index("mem"), (own_cols * SUB, cols * SUB), own_cols, cols)
    for ref, out in ((field_ref, field_w), (mine_ref, mine_w), (other_ref, other_w)):
        to_columns(perm, ref, out, cols)
    field, local = field_w[...], local_ref[...]
    total = member_term(local, mine_w[...], field) + member_term(local, other_w[...], field)
    total = total.reshape(order_ref.shape[0], -1)
    high = total.astype(BF16)
    ordered = dot(order_ref[...], high) + dot(order_ref[...], (total - high.astype(F32)).astype(BF16))
    keep_ref[...] = ordered[: keep_ref.shape[0]]


def mine_call(perm, local, flat_field, mine, after, cols, own_cols):
    total, rows = flat_field.shape
    work = (own_cols, padded(total // cols), rows)
    vmem = pl.BlockSpec(memory_space=pltpu.VMEM)
    return pl.pallas_call(
        functools.partial(mine_kernel, cols),
        name="mine",
        in_specs=[vmem] * 4 + [pl.BlockSpec(memory_space=pl.ANY)],
        out_specs=[vmem] * 2,
        out_shape=[jax.ShapeDtypeStruct(work, BF16), jax.ShapeDtypeStruct(work, F32)],
        scratch_shapes=[pltpu.VMEM(work, F32)],
        compiler_params=pltpu.CompilerParams(vmem_limit_bytes=VMEM),
        cost_estimate=taking(1.8),
    )(perm, local, flat_field, mine, after)


def send_call(held, other, cols):
    own_cols, _, rows = held[3].shape
    vmem = pl.BlockSpec(memory_space=pltpu.VMEM)
    return pl.pallas_call(
        functools.partial(send_kernel, cols),
        name="send",
        in_specs=[vmem] * 6,
        out_specs=vmem,
        out_shape=jax.ShapeDtypeStruct((other.shape[0] // cols * own_cols, rows), BF16),
        scratch_shapes=[pltpu.VMEM(held[4].shape, F32)],
        compiler_params=pltpu.CompilerParams(vmem_limit_bytes=VMEM),
        cost_estimate=taking(0.8),
    )(*held, other)


def keep_call(held, flat_field, mine, other, after, cols):
    own_cols, _, rows = held[3].shape
    vmem = pl.BlockSpec(memory_space=pltpu.VMEM)
    return pl.pallas_call(
        functools.partial(keep_kernel, cols),
        name="keep",
        in_specs=[vmem] * 5 + [pl.BlockSpec(memory_space=pl.ANY)],
        out_specs=vmem,
        out_shape=jax.ShapeDtypeStruct((other.shape[0] // cols * own_cols, rows), F32),
        scratch_shapes=[pltpu.VMEM(held[4].shape, F32)] * 3,
        compiler_params=pltpu.CompilerParams(vmem_limit_bytes=VMEM),
        cost_estimate=taking(0.6),
    )(held[1], held[2], flat_field, mine, other, after)


def tables_kernel(levels, own_cols, col_dev, slabs, table_ref, entries_ref, vert_ref, after_ref, mat_ref, coef_ref, vert_out):
    first = lax.axis_index("tile") * col_dev + lax.axis_index("mem") * own_cols
    count = 2 * own_cols
    by_row = jnp.zeros((count, 1), F32)
    every, found = entries_ref[...], jnp.zeros(entries_ref.shape, F32)
    for entry in range(table_ref.shape[1]):
        found = jnp.where(every == entry, table_ref[0:1, entry : entry + 1], found)
    for col in range(own_cols):
        here = iota(found.shape, 1) == first + col
        alphas = jnp.sum(jnp.where(here, found, 0.0), axis=1, keepdims=True)
        for var in range(2):
            by_row = jnp.where(iota((count, 1), 0) == var * own_cols + col, alphas[var : var + 1], by_row)

    def series(alpha, number):
        alpha = jnp.broadcast_to(alpha, number.shape)
        total, unit = jnp.zeros(number.shape, F32), jnp.ones(number.shape, F32)
        single, power, both = alpha, alpha * alpha, jnp.ones(number.shape, F32)
        for bit in range(BLOCK.bit_length()):
            here = ((number >> bit) & 1) == 1
            total = jnp.where(here, unit + power * total, total)
            both = jnp.where(here, both * single, both)
            unit, single, power = unit * (1.0 + power), single * single, power * power
        return total, both

    place = iota((count, BLOCK), 1)
    across, right = series(by_row, BLOCK - place)
    down = jnp.concatenate([across, jnp.zeros((128 - count, BLOCK), F32)], 0).T
    _, left = series(by_row, place + 1)
    coef_ref[0] = left * across
    coef_ref[1] = right
    coef_ref[2] = jnp.broadcast_to(right[:, 0:1], right.shape)
    coef_ref[3] = jnp.broadcast_to(left[:, 0:1] * across[:, 0:1], right.shape)
    far = jnp.abs(iota((BLOCK, BLOCK), 0) - iota((BLOCK, BLOCK), 1)).astype(F32)
    for k in range(count):
        alpha = by_row[k : k + 1]
        decay = jnp.exp(far * jnp.log(jnp.maximum(alpha, 1e-30)))
        reach = jnp.minimum(down[:, k : k + 1], across[k : k + 1])
        mat_ref[k] = (gain_of(alpha) * decay * reach).astype(BF16)
    shape = vert_out.shape[1:]
    (row_slab, row_col), (col_col, col_slab) = split(iota(shape, 0), own_cols), split(iota(shape, 1), slabs // CORES)
    for share in range(CORES):
        first = share * (slabs // CORES)
        vert_out[share] = spread(vert_ref[...], levels, row_slab, row_col, col_slab + first, col_col)


def tables_call(table, entries, vert, after, levels, own_cols, col_dev, slabs):
    count = 2 * own_cols
    return pl.pallas_call(
        functools.partial(tables_kernel, levels, own_cols, col_dev, slabs),
        name="tables",
        in_specs=[pl.BlockSpec(memory_space=pltpu.VMEM)] * 3 + [pl.BlockSpec(memory_space=pl.ANY)],
        out_specs=[pl.BlockSpec(memory_space=pltpu.VMEM)] * 3,
        out_shape=[
            jax.ShapeDtypeStruct((count, BLOCK, BLOCK), BF16),
            jax.ShapeDtypeStruct((4, count, BLOCK), F32),
            jax.ShapeDtypeStruct((CORES, own_cols * slabs, own_cols * slabs // CORES), BF16),
        ],
        compiler_params=pltpu.CompilerParams(vmem_limit_bytes=VMEM),
        cost_estimate=taking(0.4),
    )(table[None], entries, vert, after)


def along_rows(lines, matrix, coef):
    count, rows = lines.shape
    blocks = rows // BLOCK
    parts = jnp.concatenate([lines[:, b * BLOCK : (b + 1) * BLOCK] for b in range(blocks)], 0)
    local = dot(parts.astype(BF16), matrix)
    local = [local[b * count : (b + 1) * count] for b in range(blocks)]
    into, right, decay, turn = coef[0:1], coef[1:2], coef[2:3, 0:1], coef[3:4, 0:1]
    forward, state = [None], None
    for b in range(blocks - 1):
        end = local[b][:, BLOCK - 1 : BLOCK]
        state = end if state is None else decay * state + end
        forward.append(state)
    out, state = [None] * blocks, None
    for b in range(blocks - 1, -1, -1):
        piece = local[b]
        if forward[b] is not None:
            piece = piece + into * forward[b]
        if state is not None:
            piece = piece + right * state
        out[b] = piece
        if b:
            start = local[b][:, 0:1] + turn * forward[b]
            state = start if state is None else decay * state + start
    return out


def filter_share(levels, share, own_ref, coef_ref, mat_ref, row_coef_ref, part_ref, last_refs, out_ref):
    own_cols, subs, rows = own_ref.shape
    cols = coef_ref.shape[1] - 3
    mem = lax.axis_index("mem")
    end = slice(subs - 8, subs)
    is_level = iota((8, rows), 0) + share * subs + subs - 8 < levels
    lasts = [ref[...].astype(F32) for ref in last_refs]
    carry, carry_end = [], []
    for side in range(2):
        value = part_ref[side].astype(F32)
        other = value[end]
        for k, last in enumerate(lasts):
            value = value + coef_ref[side, cols + k, 0:1] * last
            other = other + coef_ref[side, cols + k, 1:2] * last[end]
        carry.append(value)
        carry_end.append(other)
    for col in range(own_cols):
        pair = coef_ref[:, mem * own_cols + col]
        own = own_ref[col]
        lines = own + pair[0, 0:1] * carry[0] + pair[1, 0:1] * carry[1]
        last_lines = own[end] + pair[0, 1:2] * carry_end[0] + pair[1, 1:2] * carry_end[1]
        main = along_rows(lines, mat_ref[col], row_coef_ref[:, col])
        last = along_rows(last_lines, mat_ref[own_cols + col], row_coef_ref[:, own_cols + col])
        for b, (piece, extra) in enumerate(zip(main, last)):
            place = slice(b * BLOCK, (b + 1) * BLOCK)
            out_ref[col, 0 : subs - 8, place] = piece[0 : subs - 8]
            out_ref[col, end, place] = jnp.where(is_level[:, place], piece[end], extra)


def mixed(vert, static):
    return dot(vert, static.astype(BF16))


def rows_kernel(levels, scale, own_ref, coef_ref, mat_ref, row_coef_ref, part_ref, *refs):
    *last_refs, vert_ref, keep_ref, base_ref, filt = refs
    share = lax.axis_index("mem") & (CORES - 1)
    filter_share(levels, share, own_ref, coef_ref, mat_ref, row_coef_ref, part_ref, last_refs, filt)
    total = mixed(vert_ref[share], filt[...].reshape(vert_ref.shape[2], -1))
    base_ref[...] = total[: base_ref.shape[0]] + keep_ref[...] * scale


def rows_call(levels, scale, own, coef, mats, row_coef, shares, vert, keep):
    vmem = pl.BlockSpec(memory_space=pltpu.VMEM)
    args = [own, coef, mats, row_coef, *shares, vert, keep]
    return pl.pallas_call(
        functools.partial(rows_kernel, levels, scale),
        name="rows",
        in_specs=[vmem] * len(args),
        out_specs=vmem,
        out_shape=jax.ShapeDtypeStruct(keep.shape, F32),
        scratch_shapes=[pltpu.VMEM(own.shape, F32)],
        compiler_params=pltpu.CompilerParams(vmem_limit_bytes=VMEM),
        cost_estimate=taking(1.2),
    )(*args)


def join_kernel(
    levels, own_ref, coef_ref, mat_ref, row_coef_ref, part_ref, last_1_ref, last_2_ref, last_3_ref, vert_ref, base_ref,
    total_ref, filt
):
    other = 1 - (lax.axis_index("mem") & (CORES - 1))
    last_refs = last_1_ref, last_2_ref, last_3_ref
    filter_share(levels, other, own_ref, coef_ref, mat_ref, row_coef_ref, part_ref, last_refs, filt)
    total = mixed(vert_ref[other], filt[...].reshape(vert_ref.shape[2], -1))
    total_ref[...] = total[: base_ref.shape[0]] + base_ref[...]


def join_call(levels, own, coef, mats, row_coef, shares, vert, base):
    vmem = pl.BlockSpec(memory_space=pltpu.VMEM)
    args = [own, coef, mats, row_coef, *shares, vert, base]
    return pl.pallas_call(
        functools.partial(join_kernel, levels),
        name="join",
        in_specs=[vmem] * len(args),
        out_specs=vmem,
        out_shape=jax.ShapeDtypeStruct(base.shape, F32),
        scratch_shapes=[pltpu.VMEM(own.shape, F32)],
        compiler_params=pltpu.CompilerParams(vmem_limit_bytes=VMEM),
        cost_estimate=taking(0.8),
    )(*args)


def final_kernel(scale, total_ref, came_ref, out_hbm, out_ref, sent):
    count, own_cols, rows = out_ref.shape
    copies = []
    for piece, first in enumerate(range(0, count, SUB)):
        place = slice(first, min(first + SUB, count))
        wide = slice(place.start * own_cols, place.stop * own_cols)
        total = total_ref[wide] + came_ref[wide].astype(F32) * scale
        out_ref[place] = total.reshape(place.stop - place.start, own_cols, rows).astype(BF16)
        copies.append(pltpu.make_async_copy(out_ref.at[place], out_hbm.at[place], sent.at[piece]))
        copies[-1].start()
    for copy in copies:
        copy.wait()


def final_call(slab_count, own_cols, scale, total, came):
    rows = total.shape[1]
    vmem = pl.BlockSpec(memory_space=pltpu.VMEM)
    out_shape = (slab_count, own_cols, rows)
    return pl.pallas_call(
        functools.partial(final_kernel, scale),
        name="final",
        in_specs=[vmem] * 2,
        out_specs=pl.BlockSpec(memory_space=pl.ANY),
        out_shape=jax.ShapeDtypeStruct(out_shape, BF16),
        scratch_shapes=[pltpu.VMEM(out_shape, BF16), pltpu.SemaphoreType.DMA((-(-slab_count // SUB),))],
        compiler_params=pltpu.CompilerParams(vmem_limit_bytes=VMEM),
        cost_estimate=taking(0.8),
    )(total, came)


def merge_kernel(levels, steps, step, last, after_count, *refs):
    lines_ref, ends_ref = refs[:2]
    came_refs, outs = refs[2 : 2 + step], refs[2 + step + after_count :]
    _, subs, rows = ends_ref.shape
    tile, mem = lax.axis_index("tile"), lax.axis_index("mem")
    is_level = iota((subs, rows), 0) + (mem & (CORES - 1)) * subs < levels
    decay = jnp.where(is_level, lines_ref[1, 0:1], lines_ref[1, 1:2])
    behind = jnp.where(is_level, lines_ref[2, 0:1], lines_ref[2, 1:2])
    turned = behind * decay
    right, left = ends_ref[0].astype(F32), ends_ref[1].astype(F32)
    into_right, into_left, from_left, from_right = 0.0, behind * right, 1.0, 1.0
    for level, came_ref in enumerate(came_refs):
        second = ((tile >> level) & 1) == 1
        came_right, came_left = came_ref[0].astype(F32), came_ref[1].astype(F32)
        into_right = into_right + jnp.where(second, from_left * came_right, 0.0)
        into_left = into_left + jnp.where(second, 0.0, from_right * came_left)
        right = jnp.where(second, decay * came_right + right, decay * right + came_right)
        left = jnp.where(second, came_left + decay * left, left + decay * came_left)
        from_left = jnp.where(second, from_left * decay, from_left)
        from_right = jnp.where(second, from_right, from_right * decay)
        decay = decay * decay
    if last:
        quarter = tile >> (steps - 2)
        outs[0][...] = jnp.where((quarter & 1) == 1, left, right).astype(BF16)
        outs[1][...] = jnp.where(quarter >= 2, left, right).astype(BF16)
        outs[2][0] = into_right.astype(BF16)
        outs[2][1] = (into_left + turned * into_right).astype(BF16)
    else:
        outs[0][0] = right.astype(BF16)
        outs[0][1] = left.astype(BF16)


def merge_call(lines, ends, came, after, levels, steps):
    last = len(came) == steps - 2
    whole = jax.ShapeDtypeStruct(ends.shape, BF16)
    one = jax.ShapeDtypeStruct(ends.shape[1:], BF16)
    outs = [one, one, whole] if last else [whole]
    vmem = pl.BlockSpec(memory_space=pltpu.VMEM)
    held = [pl.BlockSpec(memory_space=pl.ANY)] * len(after)
    return pl.pallas_call(
        functools.partial(merge_kernel, levels, steps, len(came), last, len(after)),
        name="merge",
        in_specs=[vmem] * (2 + len(came)) + held,
        out_specs=[vmem] * len(outs) + held,
        out_shape=outs + [jax.ShapeDtypeStruct(array.shape, array.dtype) for array in after],
        input_output_aliases={2 + len(came) + k: len(outs) + k for k in range(len(after))},
        compiler_params=pltpu.CompilerParams(vmem_limit_bytes=VMEM),
        cost_estimate=taking(0.8),
    )(lines, ends, *came, *after)


def body(field, vert_filter, loc_filter, alpha_table, xscale_idx, yscale_idx, members):
    tile_count, mem_count = lax.axis_size("tile"), lax.axis_size("mem")
    slab_count, cols, rows = field.shape
    levels = vert_filter.shape[1]
    own_cols = cols // mem_count
    slabs = padded(slab_count)
    steps = tile_count.bit_length() - 1

    def swap(array, flip, axis="mem"):
        return lax.ppermute(array, axis, [(i, i ^ flip) for i in range(lax.axis_size(axis))])

    full_field = field.reshape(slab_count * cols, rows)
    flat_field = pltpu.with_memory_space_constraint(full_field, pltpu.HBM)
    mine = members.reshape(slab_count * cols, rows)
    other = swap(mine, 1)
    line_table = pltpu.with_memory_space_constraint(alpha_table, pltpu.HBM)
    line_entries = pltpu.with_memory_space_constraint(xscale_idx, pltpu.HBM)
    line_loc = pltpu.with_memory_space_constraint(loc_filter[0], pltpu.HBM)
    ends, own_0, lines, *matrices = ends_call(
        line_table, line_entries, line_loc, flat_field, levels, steps, cols, own_cols
    )
    blocks, came = [ends], []
    held = [*matrices, *mine_call(*matrices[:2], full_field, mine, ends, cols, own_cols)]
    send = send_call(held, other, cols)
    over = swap(send, 2)
    coef = coefs_call(lines, send, steps, cols)
    for level in range(steps - 2):
        came.append(swap(blocks[0], 1 << level, "tile"))
        *blocks, coef = merge_call(lines, ends, came, [coef], levels, steps)
    near, far, part = blocks
    last = {flip: swap(near if flip == 1 else far, flip << (steps - 2), "tile") for flip in ORDER}
    keep = keep_call(held, full_field, mine, other, near, cols)
    own_1 = local_call(lines, full_field, near, levels, cols, own_cols)
    mats, row_coef, vert = tables_call(alpha_table, yscale_idx, vert_filter[0], own_1, levels, own_cols, cols, slabs)
    shares = [part] + [last[flip] for flip in ORDER]
    others = [swap(share, 1) for share in shares]
    scale = 1.0 / (mem_count * members.shape[0] - 1)
    base = rows_call(levels, scale, own_0, coef, mats, row_coef, shares, vert, keep)
    total = join_call(levels, own_1, coef, mats, row_coef, others, vert, base)
    return final_call(slab_count, own_cols, scale, total, over)


def solution(mesh):
    return jax.shard_map(
        body,
        mesh=mesh,
        in_specs=(P(None, "tile", None), P(), P(), P(), P(), P(), P("mem", None, "tile", None)),
        out_specs=P(None, ("tile", "mem"), None),
        check_vma=False,
    )
```

```python
import functools

import jax
import jax.numpy as jnp
from jax import lax
from jax.experimental import pallas as pl
from jax.experimental.pallas import tpu as pltpu
from jax.sharding import PartitionSpec as P

F32, BF16 = jnp.float32, jnp.bfloat16
SUB = 16
CORES = 2
LANES = 256
ORDER = (2, 3, 1)
FETCHES = 1
BLOCK = 256
MIB = 1 << 20
VMEM = 32 * MIB


def iota(shape, dim):
    return lax.broadcasted_iota(jnp.int32, shape, dim)


def taking(microseconds):
    return pl.CostEstimate(flops=int(microseconds * 1.15e9), bytes_accessed=MIB // 4, transcendentals=0)


def split(number, size):
    assert size & (size - 1) == 0
    return number >> (size.bit_length() - 1), number & (size - 1)


def dot(left, right):
    return jnp.dot(left, right, preferred_element_type=F32)


def gain_of(alpha):
    rest = (1.0 - alpha) * (1.0 + alpha)
    return jnp.sqrt(rest) * rest / jnp.sqrt(1.0 + alpha * alpha)


def lookup(table_ref, entries):
    found = jnp.zeros(entries.shape, F32)
    for entry in range(table_ref.shape[0]):
        found = jnp.where(entries == entry, table_ref[entry], found)
    return found


def padded(slab_count):
    return -(-slab_count // (4 * SUB)) * 4 * SUB


def to_columns(perm, flat, out_ref, cols):
    total = flat.shape[0]
    wanted = out_ref.shape[0]
    step = SUB * cols
    for chunk in range(out_ref.shape[1] // SUB):
        depth = min(step, total - chunk * step)
        moved = dot(perm[:, :depth], flat[chunk * step : chunk * step + depth])
        out_ref[:, chunk * SUB : (chunk + 1) * SUB, :] = moved.reshape(wanted, SUB, -1).astype(out_ref.dtype)


def sweep(work, alpha):
    cols = work.shape[0]
    state = work[0]
    for col in range(1, cols):
        state = alpha * state + work[col]
        work[col] = state
    for col in range(cols - 2, -1, -1):
        state = alpha * state + work[col]
        work[col] = state


def transposer(cols):
    shape = (SUB * cols, SUB * cols)
    (out_col, out_slab), (in_slab, in_col) = split(iota(shape, 0), SUB), split(iota(shape, 1), cols)
    return ((out_slab == in_slab) & (out_col == in_col)).astype(BF16)


def share_rows(total, cols, subs, share):
    return slice(share * subs * cols, min((share + 1) * subs * cols, total))


def clear_rest(held_ref, rows):
    first = rows.stop - rows.start
    if first < held_ref.shape[0]:
        held_ref[first:, :] = jnp.zeros((held_ref.shape[0] - first, held_ref.shape[1]), BF16)


def sweep_share(levels, share, perm, alpha, held, work):
    cols, subs, lanes = work.shape
    to_columns(perm, held, work, cols)
    is_level = iota((subs, lanes), 0) + share * subs < levels
    alpha = jnp.where(is_level, alpha[0:1], alpha[1:2])
    sweep(work, alpha)
    return gain_of(alpha), is_level


def ends_kernel(
    levels, steps, slab_count, own_cols, table_hbm, entries_hbm, loc_hbm, field_hbm, ends_ref, work, lines_ref, perm_ref,
    local_ref, order_ref, table_ref, entries_ref, loc_ref, held_ref, small, arrived
):
    pieces, cols, subs, lanes = work.shape
    slabs, rows = CORES * subs, held_ref.shape[1]
    tile, mem = lax.axis_index("tile"), lax.axis_index("mem")
    chip, share = split(mem, CORES)
    parts = arrived.shape[0]

    def fetch(part, begin):
        width = rows // parts
        place = pl.ds(part * width, width)
        for core in range(CORES):
            held = share_rows(slab_count * cols, cols, subs, core)

            @pl.when(share == core)
            def _():
                copy = pltpu.make_async_copy(
                    field_hbm.at[held, place], held_ref.at[0 : held.stop - held.start, place], arrived.at[part]
                )
                if begin:
                    copy.start()
                    clear_rest(held_ref, held)
                else:
                    copy.wait()

    for part in range(parts):
        fetch(part, True)
    given = [
        pltpu.make_async_copy(source, target, small.at[k])
        for k, (source, target) in enumerate(
            ((table_hbm, table_ref), (entries_hbm, entries_ref), (loc_hbm, loc_ref))
        )
    ]
    for copy in given:
        copy.start()
    perm_ref[...] = selection(2 * (1 - chip) + share, perm_ref.shape, own_cols, cols)
    row, col = iota(local_ref.shape, 0), iota(local_ref.shape, 1)
    (row_col, row_slab), (col_col, col_slab) = split(row, slabs), split(col, slabs)
    order_slab, order_col = split(row, own_cols)
    order_ref[...] = ((order_slab == col_slab) & (order_col == col_col)).astype(BF16)
    perm = transposer(cols)
    for copy in given:
        copy.wait()
    local_ref[...] = spread(loc_ref[...], levels, row_slab, row_col, col_slab, col_col)
    pair = lookup(table_ref, entries_ref[...])
    decay, turn = line_coefs(pair, cols)
    behind = reflected(decay, turn, tile, steps)
    lines_ref[0], lines_ref[1], lines_ref[2] = pair, decay, behind
    for piece in range(pieces):
        if piece % (pieces // parts) == 0:
            fetch(piece // (pieces // parts), False)
        part = slice(piece * lanes, (piece + 1) * lanes)
        gain, is_level = sweep_share(levels, share, perm, pair[:, part], held_ref[:, part], work.at[piece])
        turned = (decay * behind)[:, part]
        turned = jnp.where(is_level, turned[0:1], turned[1:2])
        forward = gain * work[piece, cols - 1]
        ends_ref[0, :, part] = forward.astype(BF16)
        ends_ref[1, :, part] = (gain * work[piece, 0] + turned * forward).astype(BF16)


def ends_call(table, entries, loc, flat_field, levels, steps, cols, own_cols):
    total, rows = flat_field.shape
    subs = padded(total // cols) // CORES
    side = own_cols * CORES * subs
    vmem = pl.BlockSpec(memory_space=pltpu.VMEM)
    return pl.pallas_call(
        functools.partial(ends_kernel, levels, steps, total // cols, own_cols),
        name="ends",
        in_specs=[pl.BlockSpec(memory_space=pl.ANY)] * 4,
        out_specs=[vmem] * 6,
        out_shape=[
            jax.ShapeDtypeStruct((2, subs, rows), BF16),
            jax.ShapeDtypeStruct((rows // LANES, cols, subs, LANES), F32),
            jax.ShapeDtypeStruct((3, 2, rows), F32),
            jax.ShapeDtypeStruct((own_cols * SUB, cols * SUB), BF16),
            jax.ShapeDtypeStruct((side, side), BF16),
            jax.ShapeDtypeStruct((side, side), BF16),
        ],
        scratch_shapes=[
            pltpu.SMEM(table.shape, F32),
            pltpu.VMEM(entries.shape, jnp.int32),
            pltpu.VMEM(loc.shape, BF16),
            pltpu.VMEM((subs * cols, rows), BF16),
            pltpu.SemaphoreType.DMA((3,)),
            pltpu.SemaphoreType.DMA((FETCHES,)),
        ],
        compiler_params=pltpu.CompilerParams(vmem_limit_bytes=VMEM),
        cost_estimate=taking(2.1),
    )(table, entries, loc, flat_field)


def line_coefs(pair, cols):
    decay, turn = pair, pair
    while cols > 1:
        turn = turn * (1.0 + decay * decay)
        decay = decay * decay
        cols //= 2
    return decay, turn


def reflected(decay, turn, tile, steps):
    behind = (1 << steps) - 1 - tile
    total, power = jnp.zeros_like(turn), jnp.ones_like(turn)
    for level in range(steps):
        here = ((behind >> level) & 1) == 1
        total = jnp.where(here, total + power * power * turn, total)
        power = jnp.where(here, power * decay, power)
        turn = turn * (1.0 + decay * decay)
        decay = decay * decay
    return total


def local_kernel(levels, slab_count, lines_ref, states_ref, field_ref, after_ref, mine_ref, own_ref, held_ref, work):
    pieces, cols, subs, lanes = work.shape
    own_cols = own_ref.shape[0]
    mem = lax.axis_index("mem")
    share = (mem & (CORES - 1)) ^ 1
    for core in range(CORES):
        rows = share_rows(slab_count * cols, cols, subs, core)

        @pl.when(share == core)
        def _():
            held_ref[0 : rows.stop - rows.start, :] = field_ref[rows, :]
            clear_rest(held_ref, rows)

    pair, perm = lines_ref[0], transposer(cols)
    for piece in range(pieces):
        part = slice(piece * lanes, (piece + 1) * lanes)
        gain, _ = sweep_share(levels, share, perm, pair[:, part], held_ref[:, part], work.at[piece])
        wanted = pl.ds(mem * own_cols, own_cols)
        own_ref[:, :, part] = work[piece, wanted] * gain[None]
        is_level = iota((subs, lanes), 0) + (1 - share) * subs < levels
        gain = gain_of(jnp.where(is_level, pair[0:1, part], pair[1:2, part]))
        mine_ref[:, :, part] = states_ref[piece, wanted] * gain[None]


def local_call(lines, states, flat_field, after, levels, cols, own_cols):
    total, rows = flat_field.shape
    subs = padded(total // cols) // CORES
    vmem = pl.BlockSpec(memory_space=pltpu.VMEM)
    return pl.pallas_call(
        functools.partial(local_kernel, levels, total // cols),
        name="local",
        in_specs=[vmem] * 3 + [pl.BlockSpec(memory_space=pl.ANY)],
        out_specs=[vmem] * 2,
        out_shape=[jax.ShapeDtypeStruct((own_cols, subs, rows), F32)] * 2,
        scratch_shapes=[
            pltpu.VMEM((subs * cols, rows), BF16),
            pltpu.VMEM((rows // LANES, cols, subs, LANES), F32),
        ],
        compiler_params=pltpu.CompilerParams(vmem_limit_bytes=VMEM),
        cost_estimate=taking(0.5),
    )(lines, states, flat_field, after)


def coefs_kernel(steps, lines_ref, after_ref, coef_ref):
    cols = coef_ref.shape[1] - 3
    tile = lax.axis_index("tile")
    pair, decay, behind = lines_ref[0], lines_ref[1], lines_ref[2]
    square = pair * pair
    power, sums = jnp.ones_like(pair), jnp.zeros_like(pair)
    rights, geometric = [], []
    for _ in range(cols):
        power, sums = power * pair, sums * square + 1.0
        rights.append(power)
        geometric.append(sums)
    for col in range(cols):
        coef_ref[0, col] = rights[col] * geometric[cols - 1 - col]
        coef_ref[1, col] = rights[cols - 1 - col]
    turned = decay * behind
    from_left, from_right = jnp.ones_like(pair), jnp.ones_like(pair)
    for level in range(steps - 2):
        second = ((tile >> level) & 1) == 1
        from_left = jnp.where(second, from_left * decay, from_left)
        from_right = jnp.where(second, from_right, from_right * decay)
        decay = decay * decay
    quarter = tile >> (steps - 2)
    outer = (quarter == 0) | (quarter == 3)
    for flip, weight in ((1, 1.0), (2, decay), (3, jnp.where(outer, decay * decay, 1.0))):
        upper = (quarter ^ flip) < quarter
        coef_ref[0, cols + ORDER.index(flip)] = jnp.where(upper, from_left * weight, 0.0)
        coef_ref[1, cols + ORDER.index(flip)] = weight * jnp.where(upper, turned * from_left, from_right)


def coefs_call(lines, after, steps, cols):
    vmem = pl.BlockSpec(memory_space=pltpu.VMEM)
    return pl.pallas_call(
        functools.partial(coefs_kernel, steps),
        name="coefs",
        in_specs=[vmem, pl.BlockSpec(memory_space=pl.ANY)],
        out_specs=vmem,
        out_shape=jax.ShapeDtypeStruct((2, cols + 3, *lines.shape[1:]), F32),
        compiler_params=pltpu.CompilerParams(vmem_limit_bytes=VMEM),
        cost_estimate=taking(4.0),
    )(lines, after)


def spread(matrix, levels, row_slab, row_col, col_slab, col_col):
    rows, cols = row_slab.shape
    size = matrix.shape[0]
    left = (iota((rows, size), 1) == row_slab[:, :size]).astype(BF16)
    right = (iota((size, cols), 0) == col_slab[:size, :]).astype(BF16)
    inner = dot(left, matrix).astype(BF16)
    full = dot(inner, right)
    full = jnp.where((row_slab >= levels) & (row_slab == col_slab), 1.0, full)
    return jnp.where(row_col == col_col, full, 0.0).astype(BF16)


def selection(block, shape, own_cols, cols):
    (slot, out_slab), (in_slab, in_col) = split(iota(shape, 0), SUB), split(iota(shape, 1), cols)
    return ((out_slab == in_slab) & (block * own_cols + slot == in_col)).astype(BF16)


def member_term(local, member, field):
    scaled = (member * field.astype(F32)).astype(BF16).reshape(local.shape[0], -1)
    return member * dot(local, scaled).reshape(member.shape)


def mine_kernel(cols, perm_ref, local_ref, field_ref, mine_ref, after_ref, field_out, total_out, member_w):
    to_columns(perm_ref[...], field_ref, field_out, cols)
    to_columns(perm_ref[...], mine_ref, member_w, cols)
    total_out[...] = member_term(local_ref[...], member_w[...], field_out[...])


def send_kernel(cols, perm_ref, local_ref, order_ref, field_w, total_ref, other_ref, send_ref, member_w):
    to_columns(perm_ref[...], other_ref, member_w, cols)
    total = total_ref[...] + member_term(local_ref[...], member_w[...], field_w[...])
    total = total.reshape(order_ref.shape[0], -1).astype(BF16)
    send_ref[...] = dot(order_ref[...], total)[: send_ref.shape[0]].astype(BF16)


def keep_kernel(cols, local_ref, order_ref, field_ref, mine_ref, other_ref, after_ref, keep_ref, field_w, mine_w, other_w):
    own_cols = field_w.shape[0]
    perm = selection(lax.axis_index("mem"), (own_cols * SUB, cols * SUB), own_cols, cols)
    for ref, out in ((field_ref, field_w), (mine_ref, mine_w), (other_ref, other_w)):
        to_columns(perm, ref, out, cols)
    field, local = field_w[...], local_ref[...]
    total = member_term(local, mine_w[...], field) + member_term(local, other_w[...], field)
    total = total.reshape(order_ref.shape[0], -1)
    high = total.astype(BF16)
    ordered = dot(order_ref[...], high) + dot(order_ref[...], (total - high.astype(F32)).astype(BF16))
    keep_ref[...] = ordered[: keep_ref.shape[0]]


def mine_call(perm, local, flat_field, mine, after, cols, own_cols):
    total, rows = flat_field.shape
    work = (own_cols, padded(total // cols), rows)
    vmem = pl.BlockSpec(memory_space=pltpu.VMEM)
    return pl.pallas_call(
        functools.partial(mine_kernel, cols),
        name="mine",
        in_specs=[vmem] * 4 + [pl.BlockSpec(memory_space=pl.ANY)],
        out_specs=[vmem] * 2,
        out_shape=[jax.ShapeDtypeStruct(work, BF16), jax.ShapeDtypeStruct(work, F32)],
        scratch_shapes=[pltpu.VMEM(work, F32)],
        compiler_params=pltpu.CompilerParams(vmem_limit_bytes=VMEM),
        cost_estimate=taking(1.8),
    )(perm, local, flat_field, mine, after)


def send_call(held, other, cols):
    own_cols, _, rows = held[3].shape
    vmem = pl.BlockSpec(memory_space=pltpu.VMEM)
    return pl.pallas_call(
        functools.partial(send_kernel, cols),
        name="send",
        in_specs=[vmem] * 6,
        out_specs=vmem,
        out_shape=jax.ShapeDtypeStruct((other.shape[0] // cols * own_cols, rows), BF16),
        scratch_shapes=[pltpu.VMEM(held[4].shape, F32)],
        compiler_params=pltpu.CompilerParams(vmem_limit_bytes=VMEM),
        cost_estimate=taking(0.8),
    )(*held, other)


def keep_call(held, flat_field, mine, other, after, cols):
    own_cols, _, rows = held[3].shape
    vmem = pl.BlockSpec(memory_space=pltpu.VMEM)
    return pl.pallas_call(
        functools.partial(keep_kernel, cols),
        name="keep",
        in_specs=[vmem] * 5 + [pl.BlockSpec(memory_space=pl.ANY)],
        out_specs=vmem,
        out_shape=jax.ShapeDtypeStruct((other.shape[0] // cols * own_cols, rows), F32),
        scratch_shapes=[pltpu.VMEM(held[4].shape, F32)] * 3,
        compiler_params=pltpu.CompilerParams(vmem_limit_bytes=VMEM),
        cost_estimate=taking(0.6),
    )(held[1], held[2], flat_field, mine, other, after)


def tables_kernel(levels, own_cols, col_dev, slabs, table_ref, entries_ref, vert_ref, after_ref, mat_ref, coef_ref, vert_out):
    first = lax.axis_index("tile") * col_dev + lax.axis_index("mem") * own_cols
    count = 2 * own_cols
    by_row = jnp.zeros((count, 1), F32)
    every, found = entries_ref[...], jnp.zeros(entries_ref.shape, F32)
    for entry in range(table_ref.shape[1]):
        found = jnp.where(every == entry, table_ref[0:1, entry : entry + 1], found)
    for col in range(own_cols):
        here = iota(found.shape, 1) == first + col
        alphas = jnp.sum(jnp.where(here, found, 0.0), axis=1, keepdims=True)
        for var in range(2):
            by_row = jnp.where(iota((count, 1), 0) == var * own_cols + col, alphas[var : var + 1], by_row)

    def series(alpha, number):
        alpha = jnp.broadcast_to(alpha, number.shape)
        total, unit = jnp.zeros(number.shape, F32), jnp.ones(number.shape, F32)
        single, power, both = alpha, alpha * alpha, jnp.ones(number.shape, F32)
        for bit in range(BLOCK.bit_length()):
            here = ((number >> bit) & 1) == 1
            total = jnp.where(here, unit + power * total, total)
            both = jnp.where(here, both * single, both)
            unit, single, power = unit * (1.0 + power), single * single, power * power
        return total, both

    place = iota((count, BLOCK), 1)
    across, right = series(by_row, BLOCK - place)
    down = jnp.concatenate([across, jnp.zeros((128 - count, BLOCK), F32)], 0).T
    _, left = series(by_row, place + 1)
    coef_ref[0] = left * across
    coef_ref[1] = right
    coef_ref[2] = jnp.broadcast_to(right[:, 0:1], right.shape)
    coef_ref[3] = jnp.broadcast_to(left[:, 0:1] * across[:, 0:1], right.shape)
    far = jnp.abs(iota((BLOCK, BLOCK), 0) - iota((BLOCK, BLOCK), 1)).astype(F32)
    for k in range(count):
        alpha = by_row[k : k + 1]
        decay = jnp.exp(far * jnp.log(jnp.maximum(alpha, 1e-30)))
        reach = jnp.minimum(down[:, k : k + 1], across[k : k + 1])
        mat_ref[k] = (gain_of(alpha) * decay * reach).astype(BF16)
    shape = vert_out.shape[1:]
    (row_slab, row_col), (col_col, col_slab) = split(iota(shape, 0), own_cols), split(iota(shape, 1), slabs // CORES)
    for share in range(CORES):
        first = share * (slabs // CORES)
        vert_out[share] = spread(vert_ref[...], levels, row_slab, row_col, col_slab + first, col_col)


def tables_call(table, entries, vert, after, levels, own_cols, col_dev, slabs):
    count = 2 * own_cols
    return pl.pallas_call(
        functools.partial(tables_kernel, levels, own_cols, col_dev, slabs),
        name="tables",
        in_specs=[pl.BlockSpec(memory_space=pltpu.VMEM)] * 3 + [pl.BlockSpec(memory_space=pl.ANY)],
        out_specs=[pl.BlockSpec(memory_space=pltpu.VMEM)] * 3,
        out_shape=[
            jax.ShapeDtypeStruct((count, BLOCK, BLOCK), BF16),
            jax.ShapeDtypeStruct((4, count, BLOCK), F32),
            jax.ShapeDtypeStruct((CORES, own_cols * slabs, own_cols * slabs // CORES), BF16),
        ],
        compiler_params=pltpu.CompilerParams(vmem_limit_bytes=VMEM),
        cost_estimate=taking(0.4),
    )(table[None], entries, vert, after)


def along_rows(lines, matrix, coef):
    count, rows = lines.shape
    blocks = rows // BLOCK
    parts = jnp.concatenate([lines[:, b * BLOCK : (b + 1) * BLOCK] for b in range(blocks)], 0)
    local = dot(parts.astype(BF16), matrix)
    local = [local[b * count : (b + 1) * count] for b in range(blocks)]
    into, right, decay, turn = coef[0:1], coef[1:2], coef[2:3, 0:1], coef[3:4, 0:1]
    forward, state = [None], None
    for b in range(blocks - 1):
        end = local[b][:, BLOCK - 1 : BLOCK]
        state = end if state is None else decay * state + end
        forward.append(state)
    out, state = [None] * blocks, None
    for b in range(blocks - 1, -1, -1):
        piece = local[b]
        if forward[b] is not None:
            piece = piece + into * forward[b]
        if state is not None:
            piece = piece + right * state
        out[b] = piece
        if b:
            start = local[b][:, 0:1] + turn * forward[b]
            state = start if state is None else decay * state + start
    return out


def filter_share(levels, share, own_ref, coef_ref, mat_ref, row_coef_ref, part_ref, last_refs, out_ref):
    own_cols, subs, rows = own_ref.shape
    cols = coef_ref.shape[1] - 3
    mem = lax.axis_index("mem")
    end = slice(subs - 8, subs)
    is_level = iota((8, rows), 0) + share * subs + subs - 8 < levels
    lasts = [ref[...].astype(F32) for ref in last_refs]
    carry, carry_end = [], []
    for side in range(2):
        value = part_ref[side].astype(F32)
        other = value[end]
        for k, last in enumerate(lasts):
            value = value + coef_ref[side, cols + k, 0:1] * last
            other = other + coef_ref[side, cols + k, 1:2] * last[end]
        carry.append(value)
        carry_end.append(other)
    for col in range(own_cols):
        pair = coef_ref[:, mem * own_cols + col]
        own = own_ref[col]
        lines = own + pair[0, 0:1] * carry[0] + pair[1, 0:1] * carry[1]
        last_lines = own[end] + pair[0, 1:2] * carry_end[0] + pair[1, 1:2] * carry_end[1]
        main = along_rows(lines, mat_ref[col], row_coef_ref[:, col])
        last = along_rows(last_lines, mat_ref[own_cols + col], row_coef_ref[:, own_cols + col])
        for b, (piece, extra) in enumerate(zip(main, last)):
            place = slice(b * BLOCK, (b + 1) * BLOCK)
            out_ref[col, 0 : subs - 8, place] = piece[0 : subs - 8]
            out_ref[col, end, place] = jnp.where(is_level[:, place], piece[end], extra)


def mixed(vert, static):
    return dot(vert, static.astype(BF16))


def rows_kernel(levels, scale, own_ref, coef_ref, mat_ref, row_coef_ref, part_ref, *refs):
    *last_refs, vert_ref, keep_ref, base_ref, filt = refs
    share = lax.axis_index("mem") & (CORES - 1)
    filter_share(levels, share, own_ref, coef_ref, mat_ref, row_coef_ref, part_ref, last_refs, filt)
    total = mixed(vert_ref[share], filt[...].reshape(vert_ref.shape[2], -1))
    base_ref[...] = total[: base_ref.shape[0]] + keep_ref[...] * scale


def rows_call(levels, scale, own, coef, mats, row_coef, shares, vert, keep):
    vmem = pl.BlockSpec(memory_space=pltpu.VMEM)
    args = [own, coef, mats, row_coef, *shares, vert, keep]
    return pl.pallas_call(
        functools.partial(rows_kernel, levels, scale),
        name="rows",
        in_specs=[vmem] * len(args),
        out_specs=vmem,
        out_shape=jax.ShapeDtypeStruct(keep.shape, F32),
        scratch_shapes=[pltpu.VMEM(own.shape, F32)],
        compiler_params=pltpu.CompilerParams(vmem_limit_bytes=VMEM),
        cost_estimate=taking(1.2),
    )(*args)


def join_kernel(
    levels, own_ref, coef_ref, mat_ref, row_coef_ref, part_ref, last_1_ref, last_2_ref, last_3_ref, vert_ref, base_ref,
    total_ref, filt
):
    other = 1 - (lax.axis_index("mem") & (CORES - 1))
    last_refs = last_1_ref, last_2_ref, last_3_ref
    filter_share(levels, other, own_ref, coef_ref, mat_ref, row_coef_ref, part_ref, last_refs, filt)
    total = mixed(vert_ref[other], filt[...].reshape(vert_ref.shape[2], -1))
    total_ref[...] = total[: base_ref.shape[0]] + base_ref[...]


def join_call(levels, own, coef, mats, row_coef, shares, vert, base):
    vmem = pl.BlockSpec(memory_space=pltpu.VMEM)
    args = [own, coef, mats, row_coef, *shares, vert, base]
    return pl.pallas_call(
        functools.partial(join_kernel, levels),
        name="join",
        in_specs=[vmem] * len(args),
        out_specs=vmem,
        out_shape=jax.ShapeDtypeStruct(base.shape, F32),
        scratch_shapes=[pltpu.VMEM(own.shape, F32)],
        compiler_params=pltpu.CompilerParams(vmem_limit_bytes=VMEM),
        cost_estimate=taking(0.8),
    )(*args)


def final_kernel(scale, total_ref, came_ref, out_hbm, out_ref, sent):
    count, own_cols, rows = out_ref.shape
    copies = []
    for piece, first in enumerate(range(0, count, SUB)):
        place = slice(first, min(first + SUB, count))
        wide = slice(place.start * own_cols, place.stop * own_cols)
        total = total_ref[wide] + came_ref[wide].astype(F32) * scale
        out_ref[place] = total.reshape(place.stop - place.start, own_cols, rows).astype(BF16)
        copies.append(pltpu.make_async_copy(out_ref.at[place], out_hbm.at[place], sent.at[piece]))
        copies[-1].start()
    for copy in copies:
        copy.wait()


def final_call(slab_count, own_cols, scale, total, came):
    rows = total.shape[1]
    vmem = pl.BlockSpec(memory_space=pltpu.VMEM)
    out_shape = (slab_count, own_cols, rows)
    return pl.pallas_call(
        functools.partial(final_kernel, scale),
        name="final",
        in_specs=[vmem] * 2,
        out_specs=pl.BlockSpec(memory_space=pl.ANY),
        out_shape=jax.ShapeDtypeStruct(out_shape, BF16),
        scratch_shapes=[pltpu.VMEM(out_shape, BF16), pltpu.SemaphoreType.DMA((-(-slab_count // SUB),))],
        compiler_params=pltpu.CompilerParams(vmem_limit_bytes=VMEM),
        cost_estimate=taking(0.8),
    )(total, came)


def merge_kernel(levels, steps, step, last, after_count, *refs):
    lines_ref, ends_ref = refs[:2]
    came_refs, outs = refs[2 : 2 + step], refs[2 + step + after_count :]
    _, subs, rows = ends_ref.shape
    tile, mem = lax.axis_index("tile"), lax.axis_index("mem")
    is_level = iota((subs, rows), 0) + (mem & (CORES - 1)) * subs < levels
    decay = jnp.where(is_level, lines_ref[1, 0:1], lines_ref[1, 1:2])
    behind = jnp.where(is_level, lines_ref[2, 0:1], lines_ref[2, 1:2])
    turned = behind * decay
    right, left = ends_ref[0].astype(F32), ends_ref[1].astype(F32)
    into_right, into_left, from_left, from_right = 0.0, behind * right, 1.0, 1.0
    for level, came_ref in enumerate(came_refs):
        second = ((tile >> level) & 1) == 1
        came_right, came_left = came_ref[0].astype(F32), came_ref[1].astype(F32)
        into_right = into_right + jnp.where(second, from_left * came_right, 0.0)
        into_left = into_left + jnp.where(second, 0.0, from_right * came_left)
        right = jnp.where(second, decay * came_right + right, decay * right + came_right)
        left = jnp.where(second, came_left + decay * left, left + decay * came_left)
        from_left = jnp.where(second, from_left * decay, from_left)
        from_right = jnp.where(second, from_right, from_right * decay)
        decay = decay * decay
    if last:
        quarter = tile >> (steps - 2)
        outs[0][...] = jnp.where((quarter & 1) == 1, left, right).astype(BF16)
        outs[1][...] = jnp.where(quarter >= 2, left, right).astype(BF16)
        outs[2][0] = into_right.astype(BF16)
        outs[2][1] = (into_left + turned * into_right).astype(BF16)
    else:
        outs[0][0] = right.astype(BF16)
        outs[0][1] = left.astype(BF16)


def merge_call(lines, ends, came, after, levels, steps):
    last = len(came) == steps - 2
    whole = jax.ShapeDtypeStruct(ends.shape, BF16)
    one = jax.ShapeDtypeStruct(ends.shape[1:], BF16)
    outs = [one, one, whole] if last else [whole]
    vmem = pl.BlockSpec(memory_space=pltpu.VMEM)
    held = [pl.BlockSpec(memory_space=pl.ANY)] * len(after)
    return pl.pallas_call(
        functools.partial(merge_kernel, levels, steps, len(came), last, len(after)),
        name="merge",
        in_specs=[vmem] * (2 + len(came)) + held,
        out_specs=[vmem] * len(outs) + held,
        out_shape=outs + [jax.ShapeDtypeStruct(array.shape, array.dtype) for array in after],
        input_output_aliases={2 + len(came) + k: len(outs) + k for k in range(len(after))},
        compiler_params=pltpu.CompilerParams(vmem_limit_bytes=VMEM),
        cost_estimate=taking(0.8),
    )(lines, ends, *came, *after)


def body(field, vert_filter, loc_filter, alpha_table, xscale_idx, yscale_idx, members):
    tile_count, mem_count = lax.axis_size("tile"), lax.axis_size("mem")
    slab_count, cols, rows = field.shape
    levels = vert_filter.shape[1]
    own_cols = cols // mem_count
    slabs = padded(slab_count)
    steps = tile_count.bit_length() - 1

    def swap(array, flip, axis="mem"):
        return lax.ppermute(array, axis, [(i, i ^ flip) for i in range(lax.axis_size(axis))])

    full_field = field.reshape(slab_count * cols, rows)
    flat_field = pltpu.with_memory_space_constraint(full_field, pltpu.HBM)
    mine = members.reshape(slab_count * cols, rows)
    other = swap(mine, 1)
    line_table = pltpu.with_memory_space_constraint(alpha_table, pltpu.HBM)
    line_entries = pltpu.with_memory_space_constraint(xscale_idx, pltpu.HBM)
    line_loc = pltpu.with_memory_space_constraint(loc_filter[0], pltpu.HBM)
    ends, states, lines, *matrices = ends_call(
        line_table, line_entries, line_loc, flat_field, levels, steps, cols, own_cols
    )
    blocks, came = [ends], []
    held = [*matrices, *mine_call(*matrices[:2], full_field, mine, ends, cols, own_cols)]
    send = send_call(held, other, cols)
    over = swap(send, 2)
    coef = coefs_call(lines, send, steps, cols)
    for level in range(steps - 2):
        came.append(swap(blocks[0], 1 << level, "tile"))
        *blocks, coef = merge_call(lines, ends, came, [coef], levels, steps)
    near, far, part = blocks
    last = {flip: swap(near if flip == 1 else far, flip << (steps - 2), "tile") for flip in ORDER}
    keep = keep_call(held, full_field, mine, other, near, cols)
    own_0, own_1 = local_call(lines, states, full_field, near, levels, cols, own_cols)
    mats, row_coef, vert = tables_call(alpha_table, yscale_idx, vert_filter[0], own_1, levels, own_cols, cols, slabs)
    shares = [part] + [last[flip] for flip in ORDER]
    others = [swap(share, 1) for share in shares]
    scale = 1.0 / (mem_count * members.shape[0] - 1)
    base = rows_call(levels, scale, own_0, coef, mats, row_coef, shares, vert, keep)
    total = join_call(levels, own_1, coef, mats, row_coef, others, vert, base)
    return final_call(slab_count, own_cols, scale, total, over)


def solution(mesh):
    return jax.shard_map(
        body,
        mesh=mesh,
        in_specs=(P(None, "tile", None), P(), P(), P(), P(), P(), P("mem", None, "tile", None)),
        out_specs=P(None, ("tile", "mem"), None),
        check_vma=False,
    )
```

```python
import functools

import jax
import jax.numpy as jnp
from jax import lax
from jax.experimental import pallas as pl
from jax.experimental.pallas import tpu as pltpu
from jax.sharding import PartitionSpec as P

F32, BF16 = jnp.float32, jnp.bfloat16
SUB = 16
CORES = 2
LANES = 256
ORDER = (1, 3, 2)
FETCHES = 1
BLOCK = 256
MIB = 1 << 20
VMEM = 32 * MIB


def iota(shape, dim):
    return lax.broadcasted_iota(jnp.int32, shape, dim)


def taking(microseconds):
    return pl.CostEstimate(flops=int(microseconds * 1.15e9), bytes_accessed=MIB // 4, transcendentals=0)


def split(number, size):
    assert size & (size - 1) == 0
    return number >> (size.bit_length() - 1), number & (size - 1)


def dot(left, right):
    return jnp.dot(left, right, preferred_element_type=F32)


def gain_of(alpha):
    rest = (1.0 - alpha) * (1.0 + alpha)
    return jnp.sqrt(rest) * rest / jnp.sqrt(1.0 + alpha * alpha)


def lookup(table_ref, entries):
    found = jnp.zeros(entries.shape, F32)
    for entry in range(table_ref.shape[0]):
        found = jnp.where(entries == entry, table_ref[entry], found)
    return found


def padded(slab_count):
    return -(-slab_count // (4 * SUB)) * 4 * SUB


def to_columns(perm, flat, out_ref, cols):
    total = flat.shape[0]
    wanted = out_ref.shape[0]
    step = SUB * cols
    for chunk in range(out_ref.shape[1] // SUB):
        depth = min(step, total - chunk * step)
        moved = dot(perm[:, :depth], flat[chunk * step : chunk * step + depth])
        out_ref[:, chunk * SUB : (chunk + 1) * SUB, :] = moved.reshape(wanted, SUB, -1).astype(out_ref.dtype)


def sweep(work, alpha):
    cols = work.shape[0]
    state = work[0]
    for col in range(1, cols):
        state = alpha * state + work[col]
        work[col] = state
    for col in range(cols - 2, -1, -1):
        state = alpha * state + work[col]
        work[col] = state


def transposer(cols):
    shape = (SUB * cols, SUB * cols)
    (out_col, out_slab), (in_slab, in_col) = split(iota(shape, 0), SUB), split(iota(shape, 1), cols)
    return ((out_slab == in_slab) & (out_col == in_col)).astype(BF16)


def share_rows(total, cols, subs, share):
    return slice(share * subs * cols, min((share + 1) * subs * cols, total))


def clear_rest(held_ref, rows):
    first = rows.stop - rows.start
    if first < held_ref.shape[0]:
        held_ref[first:, :] = jnp.zeros((held_ref.shape[0] - first, held_ref.shape[1]), BF16)


def sweep_share(levels, share, perm, alpha, held, work):
    cols, subs, lanes = work.shape
    to_columns(perm, held, work, cols)
    is_level = iota((subs, lanes), 0) + share * subs < levels
    alpha = jnp.where(is_level, alpha[0:1], alpha[1:2])
    sweep(work, alpha)
    return gain_of(alpha), is_level


def ends_kernel(
    levels, steps, slab_count, own_cols, table_hbm, entries_hbm, loc_hbm, field_hbm, ends_ref, work, lines_ref, perm_ref,
    local_ref, order_ref, table_ref, entries_ref, loc_ref, held_ref, small, arrived
):
    pieces, cols, subs, lanes = work.shape
    slabs, rows = CORES * subs, held_ref.shape[1]
    tile, mem = lax.axis_index("tile"), lax.axis_index("mem")
    chip, share = split(mem, CORES)
    parts = arrived.shape[0]

    def fetch(part, begin):
        width = rows // parts
        place = pl.ds(part * width, width)
        for core in range(CORES):
            held = share_rows(slab_count * cols, cols, subs, core)

            @pl.when(share == core)
            def _():
                copy = pltpu.make_async_copy(
                    field_hbm.at[held, place], held_ref.at[0 : held.stop - held.start, place], arrived.at[part]
                )
                if begin:
                    copy.start()
                    clear_rest(held_ref, held)
                else:
                    copy.wait()

    for part in range(parts):
        fetch(part, True)
    given = [
        pltpu.make_async_copy(source, target, small.at[k])
        for k, (source, target) in enumerate(
            ((table_hbm, table_ref), (entries_hbm, entries_ref), (loc_hbm, loc_ref))
        )
    ]
    for copy in given:
        copy.start()
    perm_ref[...] = selection(2 * (1 - chip) + share, perm_ref.shape, own_cols, cols)
    row, col = iota(local_ref.shape, 0), iota(local_ref.shape, 1)
    (row_col, row_slab), (col_col, col_slab) = split(row, slabs), split(col, slabs)
    order_slab, order_col = split(row, own_cols)
    order_ref[...] = ((order_slab == col_slab) & (order_col == col_col)).astype(BF16)
    perm = transposer(cols)
    for copy in given:
        copy.wait()
    local_ref[...] = spread(loc_ref[...], levels, row_slab, row_col, col_slab, col_col)
    pair = lookup(table_ref, entries_ref[...])
    decay, turn = line_coefs(pair, cols)
    behind = reflected(decay, turn, tile, steps)
    lines_ref[0], lines_ref[1], lines_ref[2] = pair, decay, behind
    for piece in range(pieces):
        if piece % (pieces // parts) == 0:
            fetch(piece // (pieces // parts), False)
        part = slice(piece * lanes, (piece + 1) * lanes)
        gain, is_level = sweep_share(levels, share, perm, pair[:, part], held_ref[:, part], work.at[piece])
        turned = (decay * behind)[:, part]
        turned = jnp.where(is_level, turned[0:1], turned[1:2])
        forward = gain * work[piece, cols - 1]
        ends_ref[0, :, part] = forward.astype(BF16)
        ends_ref[1, :, part] = (gain * work[piece, 0] + turned * forward).astype(BF16)


def ends_call(table, entries, loc, flat_field, levels, steps, cols, own_cols):
    total, rows = flat_field.shape
    subs = padded(total // cols) // CORES
    side = own_cols * CORES * subs
    vmem = pl.BlockSpec(memory_space=pltpu.VMEM)
    return pl.pallas_call(
        functools.partial(ends_kernel, levels, steps, total // cols, own_cols),
        name="ends",
        in_specs=[pl.BlockSpec(memory_space=pl.ANY)] * 4,
        out_specs=[vmem] * 6,
        out_shape=[
            jax.ShapeDtypeStruct((2, subs, rows), BF16),
            jax.ShapeDtypeStruct((rows // LANES, cols, subs, LANES), F32),
            jax.ShapeDtypeStruct((3, 2, rows), F32),
            jax.ShapeDtypeStruct((own_cols * SUB, cols * SUB), BF16),
            jax.ShapeDtypeStruct((side, side), BF16),
            jax.ShapeDtypeStruct((side, side), BF16),
        ],
        scratch_shapes=[
            pltpu.SMEM(table.shape, F32),
            pltpu.VMEM(entries.shape, jnp.int32),
            pltpu.VMEM(loc.shape, BF16),
            pltpu.VMEM((subs * cols, rows), BF16),
            pltpu.SemaphoreType.DMA((3,)),
            pltpu.SemaphoreType.DMA((FETCHES,)),
        ],
        compiler_params=pltpu.CompilerParams(vmem_limit_bytes=VMEM),
        cost_estimate=taking(2.1),
    )(table, entries, loc, flat_field)


def line_coefs(pair, cols):
    decay, turn = pair, pair
    while cols > 1:
        turn = turn * (1.0 + decay * decay)
        decay = decay * decay
        cols //= 2
    return decay, turn


def reflected(decay, turn, tile, steps):
    behind = (1 << steps) - 1 - tile
    total, power = jnp.zeros_like(turn), jnp.ones_like(turn)
    for level in range(steps):
        here = ((behind >> level) & 1) == 1
        total = jnp.where(here, total + power * power * turn, total)
        power = jnp.where(here, power * decay, power)
        turn = turn * (1.0 + decay * decay)
        decay = decay * decay
    return total


def local_kernel(levels, slab_count, lines_ref, states_ref, field_ref, after_ref, mine_ref, own_ref, held_ref, work):
    pieces, cols, subs, lanes = work.shape
    own_cols = own_ref.shape[0]
    mem = lax.axis_index("mem")
    share = (mem & (CORES - 1)) ^ 1
    for core in range(CORES):
        rows = share_rows(slab_count * cols, cols, subs, core)

        @pl.when(share == core)
        def _():
            held_ref[0 : rows.stop - rows.start, :] = field_ref[rows, :]
            clear_rest(held_ref, rows)

    pair, perm = lines_ref[0], transposer(cols)
    for piece in range(pieces):
        part = slice(piece * lanes, (piece + 1) * lanes)
        gain, _ = sweep_share(levels, share, perm, pair[:, part], held_ref[:, part], work.at[piece])
        wanted = pl.ds(mem * own_cols, own_cols)
        own_ref[:, :, part] = work[piece, wanted] * gain[None]
        is_level = iota((subs, lanes), 0) + (1 - share) * subs < levels
        gain = gain_of(jnp.where(is_level, pair[0:1, part], pair[1:2, part]))
        mine_ref[:, :, part] = states_ref[piece, wanted] * gain[None]


def local_call(lines, states, flat_field, after, levels, cols, own_cols):
    total, rows = flat_field.shape
    subs = padded(total // cols) // CORES
    vmem = pl.BlockSpec(memory_space=pltpu.VMEM)
    return pl.pallas_call(
        functools.partial(local_kernel, levels, total // cols),
        name="local",
        in_specs=[vmem] * 3 + [pl.BlockSpec(memory_space=pl.ANY)],
        out_specs=[vmem] * 2,
        out_shape=[jax.ShapeDtypeStruct((own_cols, subs, rows), F32)] * 2,
        scratch_shapes=[
            pltpu.VMEM((subs * cols, rows), BF16),
            pltpu.VMEM((rows // LANES, cols, subs, LANES), F32),
        ],
        compiler_params=pltpu.CompilerParams(vmem_limit_bytes=VMEM),
        cost_estimate=taking(0.5),
    )(lines, states, flat_field, after)


def coefs_kernel(steps, lines_ref, after_ref, coef_ref):
    cols = coef_ref.shape[1] - 3
    tile = lax.axis_index("tile")
    pair, decay, behind = lines_ref[0], lines_ref[1], lines_ref[2]
    square = pair * pair
    power, sums = jnp.ones_like(pair), jnp.zeros_like(pair)
    rights, geometric = [], []
    for _ in range(cols):
        power, sums = power * pair, sums * square + 1.0
        rights.append(power)
        geometric.append(sums)
    for col in range(cols):
        coef_ref[0, col] = rights[col] * geometric[cols - 1 - col]
        coef_ref[1, col] = rights[cols - 1 - col]
    turned = decay * behind
    from_left, from_right = jnp.ones_like(pair), jnp.ones_like(pair)
    for level in range(steps - 2):
        second = ((tile >> level) & 1) == 1
        from_left = jnp.where(second, from_left * decay, from_left)
        from_right = jnp.where(second, from_right, from_right * decay)
        decay = decay * decay
    quarter = tile >> (steps - 2)
    outer = (quarter == 0) | (quarter == 3)
    for flip, weight in ((1, 1.0), (2, decay), (3, jnp.where(outer, decay * decay, 1.0))):
        upper = (quarter ^ flip) < quarter
        coef_ref[0, cols + ORDER.index(flip)] = jnp.where(upper, from_left * weight, 0.0)
        coef_ref[1, cols + ORDER.index(flip)] = weight * jnp.where(upper, turned * from_left, from_right)


def coefs_call(lines, after, steps, cols):
    vmem = pl.BlockSpec(memory_space=pltpu.VMEM)
    return pl.pallas_call(
        functools.partial(coefs_kernel, steps),
        name="coefs",
        in_specs=[vmem, pl.BlockSpec(memory_space=pl.ANY)],
        out_specs=vmem,
        out_shape=jax.ShapeDtypeStruct((2, cols + 3, *lines.shape[1:]), F32),
        compiler_params=pltpu.CompilerParams(vmem_limit_bytes=VMEM),
        cost_estimate=taking(4.0),
    )(lines, after)


def spread(matrix, levels, row_slab, row_col, col_slab, col_col):
    rows, cols = row_slab.shape
    size = matrix.shape[0]
    left = (iota((rows, size), 1) == row_slab[:, :size]).astype(BF16)
    right = (iota((size, cols), 0) == col_slab[:size, :]).astype(BF16)
    inner = dot(left, matrix).astype(BF16)
    full = dot(inner, right)
    full = jnp.where((row_slab >= levels) & (row_slab == col_slab), 1.0, full)
    return jnp.where(row_col == col_col, full, 0.0).astype(BF16)


def selection(block, shape, own_cols, cols):
    (slot, out_slab), (in_slab, in_col) = split(iota(shape, 0), SUB), split(iota(shape, 1), cols)
    return ((out_slab == in_slab) & (block * own_cols + slot == in_col)).astype(BF16)


def member_term(local, member, field):
    scaled = (member * field.astype(F32)).astype(BF16).reshape(local.shape[0], -1)
    return member * dot(local, scaled).reshape(member.shape)


def send_kernel(
    cols, perm_ref, local_ref, order_ref, field_ref, mine_ref, other_ref, after_ref, send_ref, field_w, mine_w, other_w
):
    for ref, out in ((field_ref, field_w), (mine_ref, mine_w), (other_ref, other_w)):
        to_columns(perm_ref[...], ref, out, cols)
    field, local = field_w[...], local_ref[...]
    total = member_term(local, mine_w[...], field) + member_term(local, other_w[...], field)
    total = total.reshape(order_ref.shape[0], -1).astype(BF16)
    send_ref[...] = dot(order_ref[...], total)[: send_ref.shape[0]].astype(BF16)


def keep_kernel(cols, local_ref, order_ref, field_ref, mine_ref, other_ref, after_ref, keep_ref, field_w, mine_w, other_w):
    own_cols = field_w.shape[0]
    perm = selection(lax.axis_index("mem"), (own_cols * SUB, cols * SUB), own_cols, cols)
    for ref, out in ((field_ref, field_w), (mine_ref, mine_w), (other_ref, other_w)):
        to_columns(perm, ref, out, cols)
    field, local = field_w[...], local_ref[...]
    total = member_term(local, mine_w[...], field) + member_term(local, other_w[...], field)
    total = total.reshape(order_ref.shape[0], -1)
    high = total.astype(BF16)
    ordered = dot(order_ref[...], high) + dot(order_ref[...], (total - high.astype(F32)).astype(BF16))
    keep_ref[...] = ordered[: keep_ref.shape[0]]


def send_call(matrices, flat_field, mine, other, after, cols, own_cols):
    total, rows = other.shape
    work = pltpu.VMEM((own_cols, padded(total // cols), rows), F32)
    vmem = pl.BlockSpec(memory_space=pltpu.VMEM)
    return pl.pallas_call(
        functools.partial(send_kernel, cols),
        name="send",
        in_specs=[vmem] * 6 + [pl.BlockSpec(memory_space=pl.ANY)],
        out_specs=vmem,
        out_shape=jax.ShapeDtypeStruct((total // cols * own_cols, rows), BF16),
        scratch_shapes=[work] * 3,
        compiler_params=pltpu.CompilerParams(vmem_limit_bytes=VMEM),
        cost_estimate=taking(2.6),
    )(*matrices, flat_field, mine, other, after)


def keep_call(matrices, flat_field, mine, other, after, cols, own_cols):
    total, rows = other.shape
    work = pltpu.VMEM((own_cols, padded(total // cols), rows), F32)
    vmem = pl.BlockSpec(memory_space=pltpu.VMEM)
    return pl.pallas_call(
        functools.partial(keep_kernel, cols),
        name="keep",
        in_specs=[vmem] * 5 + [pl.BlockSpec(memory_space=pl.ANY)],
        out_specs=vmem,
        out_shape=jax.ShapeDtypeStruct((total // cols * own_cols, rows), F32),
        scratch_shapes=[work] * 3,
        compiler_params=pltpu.CompilerParams(vmem_limit_bytes=VMEM),
        cost_estimate=taking(0.6),
    )(*matrices[1:], flat_field, mine, other, after)


def tables_kernel(levels, own_cols, col_dev, slabs, table_ref, entries_ref, vert_ref, after_ref, mat_ref, coef_ref, vert_out):
    first = lax.axis_index("tile") * col_dev + lax.axis_index("mem") * own_cols
    count = 2 * own_cols
    by_row = jnp.zeros((count, 1), F32)
    every, found = entries_ref[...], jnp.zeros(entries_ref.shape, F32)
    for entry in range(table_ref.shape[1]):
        found = jnp.where(every == entry, table_ref[0:1, entry : entry + 1], found)
    for col in range(own_cols):
        here = iota(found.shape, 1) == first + col
        alphas = jnp.sum(jnp.where(here, found, 0.0), axis=1, keepdims=True)
        for var in range(2):
            by_row = jnp.where(iota((count, 1), 0) == var * own_cols + col, alphas[var : var + 1], by_row)

    def series(alpha, number):
        alpha = jnp.broadcast_to(alpha, number.shape)
        total, unit = jnp.zeros(number.shape, F32), jnp.ones(number.shape, F32)
        single, power, both = alpha, alpha * alpha, jnp.ones(number.shape, F32)
        for bit in range(BLOCK.bit_length()):
            here = ((number >> bit) & 1) == 1
            total = jnp.where(here, unit + power * total, total)
            both = jnp.where(here, both * single, both)
            unit, single, power = unit * (1.0 + power), single * single, power * power
        return total, both

    place = iota((count, BLOCK), 1)
    across, right = series(by_row, BLOCK - place)
    down = jnp.concatenate([across, jnp.zeros((128 - count, BLOCK), F32)], 0).T
    _, left = series(by_row, place + 1)
    coef_ref[0] = left * across
    coef_ref[1] = right
    coef_ref[2] = jnp.broadcast_to(right[:, 0:1], right.shape)
    coef_ref[3] = jnp.broadcast_to(left[:, 0:1] * across[:, 0:1], right.shape)
    far = jnp.abs(iota((BLOCK, BLOCK), 0) - iota((BLOCK, BLOCK), 1)).astype(F32)
    for k in range(count):
        alpha = by_row[k : k + 1]
        decay = jnp.exp(far * jnp.log(jnp.maximum(alpha, 1e-30)))
        reach = jnp.minimum(down[:, k : k + 1], across[k : k + 1])
        mat_ref[k] = (gain_of(alpha) * decay * reach).astype(BF16)
    shape = vert_out.shape[1:]
    (row_slab, row_col), (col_col, col_slab) = split(iota(shape, 0), own_cols), split(iota(shape, 1), slabs // CORES)
    for share in range(CORES):
        first = share * (slabs // CORES)
        vert_out[share] = spread(vert_ref[...], levels, row_slab, row_col, col_slab + first, col_col)


def tables_call(table, entries, vert, after, levels, own_cols, col_dev, slabs):
    count = 2 * own_cols
    return pl.pallas_call(
        functools.partial(tables_kernel, levels, own_cols, col_dev, slabs),
        name="tables",
        in_specs=[pl.BlockSpec(memory_space=pltpu.VMEM)] * 3 + [pl.BlockSpec(memory_space=pl.ANY)],
        out_specs=[pl.BlockSpec(memory_space=pltpu.VMEM)] * 3,
        out_shape=[
            jax.ShapeDtypeStruct((count, BLOCK, BLOCK), BF16),
            jax.ShapeDtypeStruct((4, count, BLOCK), F32),
            jax.ShapeDtypeStruct((CORES, own_cols * slabs, own_cols * slabs // CORES), BF16),
        ],
        compiler_params=pltpu.CompilerParams(vmem_limit_bytes=VMEM),
        cost_estimate=taking(0.4),
    )(table[None], entries, vert, after)


def along_rows(lines, matrix, coef):
    count, rows = lines.shape
    blocks = rows // BLOCK
    parts = jnp.concatenate([lines[:, b * BLOCK : (b + 1) * BLOCK] for b in range(blocks)], 0)
    local = dot(parts.astype(BF16), matrix)
    local = [local[b * count : (b + 1) * count] for b in range(blocks)]
    into, right, decay, turn = coef[0:1], coef[1:2], coef[2:3, 0:1], coef[3:4, 0:1]
    forward, state = [None], None
    for b in range(blocks - 1):
        end = local[b][:, BLOCK - 1 : BLOCK]
        state = end if state is None else decay * state + end
        forward.append(state)
    out, state = [None] * blocks, None
    for b in range(blocks - 1, -1, -1):
        piece = local[b]
        if forward[b] is not None:
            piece = piece + into * forward[b]
        if state is not None:
            piece = piece + right * state
        out[b] = piece
        if b:
            start = local[b][:, 0:1] + turn * forward[b]
            state = start if state is None else decay * state + start
    return out


def filter_share(levels, share, own_ref, coef_ref, mat_ref, row_coef_ref, part_ref, last_refs, out_ref):
    own_cols, subs, rows = own_ref.shape
    cols = coef_ref.shape[1] - 3
    mem = lax.axis_index("mem")
    end = slice(subs - 8, subs)
    is_level = iota((8, rows), 0) + share * subs + subs - 8 < levels
    lasts = [ref[...].astype(F32) for ref in last_refs]
    carry, carry_end = [], []
    for side in range(2):
        value = part_ref[side].astype(F32)
        other = value[end]
        for k, last in enumerate(lasts):
            value = value + coef_ref[side, cols + k, 0:1] * last
            other = other + coef_ref[side, cols + k, 1:2] * last[end]
        carry.append(value)
        carry_end.append(other)
    for col in range(own_cols):
        pair = coef_ref[:, mem * own_cols + col]
        own = own_ref[col]
        lines = own + pair[0, 0:1] * carry[0] + pair[1, 0:1] * carry[1]
        last_lines = own[end] + pair[0, 1:2] * carry_end[0] + pair[1, 1:2] * carry_end[1]
        main = along_rows(lines, mat_ref[col], row_coef_ref[:, col])
        last = along_rows(last_lines, mat_ref[own_cols + col], row_coef_ref[:, own_cols + col])
        for b, (piece, extra) in enumerate(zip(main, last)):
            place = slice(b * BLOCK, (b + 1) * BLOCK)
            out_ref[col, 0 : subs - 8, place] = piece[0 : subs - 8]
            out_ref[col, end, place] = jnp.where(is_level[:, place], piece[end], extra)


def mixed(vert, static):
    return dot(vert, static.astype(BF16))


def rows_kernel(levels, scale, own_ref, coef_ref, mat_ref, row_coef_ref, part_ref, *refs):
    *last_refs, vert_ref, keep_ref, base_ref, filt = refs
    share = lax.axis_index("mem") & (CORES - 1)
    filter_share(levels, share, own_ref, coef_ref, mat_ref, row_coef_ref, part_ref, last_refs, filt)
    total = mixed(vert_ref[share], filt[...].reshape(vert_ref.shape[2], -1))
    base_ref[...] = total[: base_ref.shape[0]] + keep_ref[...] * scale


def rows_call(levels, scale, own, coef, mats, row_coef, shares, vert, keep):
    vmem = pl.BlockSpec(memory_space=pltpu.VMEM)
    args = [own, coef, mats, row_coef, *shares, vert, keep]
    return pl.pallas_call(
        functools.partial(rows_kernel, levels, scale),
        name="rows",
        in_specs=[vmem] * len(args),
        out_specs=vmem,
        out_shape=jax.ShapeDtypeStruct(keep.shape, F32),
        scratch_shapes=[pltpu.VMEM(own.shape, F32)],
        compiler_params=pltpu.CompilerParams(vmem_limit_bytes=VMEM),
        cost_estimate=taking(1.2),
    )(*args)


def join_kernel(
    levels, own_ref, coef_ref, mat_ref, row_coef_ref, part_ref, last_1_ref, last_2_ref, last_3_ref, vert_ref, base_ref,
    total_ref, filt
):
    other = 1 - (lax.axis_index("mem") & (CORES - 1))
    last_refs = last_1_ref, last_2_ref, last_3_ref
    filter_share(levels, other, own_ref, coef_ref, mat_ref, row_coef_ref, part_ref, last_refs, filt)
    total = mixed(vert_ref[other], filt[...].reshape(vert_ref.shape[2], -1))
    total_ref[...] = total[: base_ref.shape[0]] + base_ref[...]


def join_call(levels, own, coef, mats, row_coef, shares, vert, base):
    vmem = pl.BlockSpec(memory_space=pltpu.VMEM)
    args = [own, coef, mats, row_coef, *shares, vert, base]
    return pl.pallas_call(
        functools.partial(join_kernel, levels),
        name="join",
        in_specs=[vmem] * len(args),
        out_specs=vmem,
        out_shape=jax.ShapeDtypeStruct(base.shape, F32),
        scratch_shapes=[pltpu.VMEM(own.shape, F32)],
        compiler_params=pltpu.CompilerParams(vmem_limit_bytes=VMEM),
        cost_estimate=taking(0.8),
    )(*args)


def final_kernel(scale, total_ref, came_ref, out_hbm, out_ref, sent):
    count, own_cols, rows = out_ref.shape
    copies = []
    for piece, first in enumerate(range(0, count, SUB)):
        place = slice(first, min(first + SUB, count))
        wide = slice(place.start * own_cols, place.stop * own_cols)
        total = total_ref[wide] + came_ref[wide].astype(F32) * scale
        out_ref[place] = total.reshape(place.stop - place.start, own_cols, rows).astype(BF16)
        copies.append(pltpu.make_async_copy(out_ref.at[place], out_hbm.at[place], sent.at[piece]))
        copies[-1].start()
    for copy in copies:
        copy.wait()


def final_call(slab_count, own_cols, scale, total, came):
    rows = total.shape[1]
    vmem = pl.BlockSpec(memory_space=pltpu.VMEM)
    out_shape = (slab_count, own_cols, rows)
    return pl.pallas_call(
        functools.partial(final_kernel, scale),
        name="final",
        in_specs=[vmem] * 2,
        out_specs=pl.BlockSpec(memory_space=pl.ANY),
        out_shape=jax.ShapeDtypeStruct(out_shape, BF16),
        scratch_shapes=[pltpu.VMEM(out_shape, BF16), pltpu.SemaphoreType.DMA((-(-slab_count // SUB),))],
        compiler_params=pltpu.CompilerParams(vmem_limit_bytes=VMEM),
        cost_estimate=taking(0.8),
    )(total, came)


def merge_kernel(levels, steps, step, last, after_count, *refs):
    lines_ref, ends_ref = refs[:2]
    came_refs, outs = refs[2 : 2 + step], refs[2 + step + after_count :]
    _, subs, rows = ends_ref.shape
    tile, mem = lax.axis_index("tile"), lax.axis_index("mem")
    is_level = iota((subs, rows), 0) + (mem & (CORES - 1)) * subs < levels
    decay = jnp.where(is_level, lines_ref[1, 0:1], lines_ref[1, 1:2])
    behind = jnp.where(is_level, lines_ref[2, 0:1], lines_ref[2, 1:2])
    turned = behind * decay
    right, left = ends_ref[0].astype(F32), ends_ref[1].astype(F32)
    into_right, into_left, from_left, from_right = 0.0, behind * right, 1.0, 1.0
    for level, came_ref in enumerate(came_refs):
        second = ((tile >> level) & 1) == 1
        came_right, came_left = came_ref[0].astype(F32), came_ref[1].astype(F32)
        into_right = into_right + jnp.where(second, from_left * came_right, 0.0)
        into_left = into_left + jnp.where(second, 0.0, from_right * came_left)
        right = jnp.where(second, decay * came_right + right, decay * right + came_right)
        left = jnp.where(second, came_left + decay * left, left + decay * came_left)
        from_left = jnp.where(second, from_left * decay, from_left)
        from_right = jnp.where(second, from_right, from_right * decay)
        decay = decay * decay
    if last:
        quarter = tile >> (steps - 2)
        outs[0][...] = jnp.where((quarter & 1) == 1, left, right).astype(BF16)
        outs[1][...] = jnp.where(quarter >= 2, left, right).astype(BF16)
        outs[2][0] = into_right.astype(BF16)
        outs[2][1] = (into_left + turned * into_right).astype(BF16)
    else:
        outs[0][0] = right.astype(BF16)
        outs[0][1] = left.astype(BF16)


def merge_call(lines, ends, came, after, levels, steps):
    last = len(came) == steps - 2
    whole = jax.ShapeDtypeStruct(ends.shape, BF16)
    one = jax.ShapeDtypeStruct(ends.shape[1:], BF16)
    outs = [one, one, whole] if last else [whole]
    vmem = pl.BlockSpec(memory_space=pltpu.VMEM)
    held = [pl.BlockSpec(memory_space=pl.ANY)] * len(after)
    return pl.pallas_call(
        functools.partial(merge_kernel, levels, steps, len(came), last, len(after)),
        name="merge",
        in_specs=[vmem] * (2 + len(came)) + held,
        out_specs=[vmem] * len(outs) + held,
        out_shape=outs + [jax.ShapeDtypeStruct(array.shape, array.dtype) for array in after],
        input_output_aliases={2 + len(came) + k: len(outs) + k for k in range(len(after))},
        compiler_params=pltpu.CompilerParams(vmem_limit_bytes=VMEM),
        cost_estimate=taking(0.8),
    )(lines, ends, *came, *after)


def body(field, vert_filter, loc_filter, alpha_table, xscale_idx, yscale_idx, members):
    tile_count, mem_count = lax.axis_size("tile"), lax.axis_size("mem")
    slab_count, cols, rows = field.shape
    levels = vert_filter.shape[1]
    own_cols = cols // mem_count
    slabs = padded(slab_count)
    steps = tile_count.bit_length() - 1

    def swap(array, flip, axis="mem"):
        return lax.ppermute(array, axis, [(i, i ^ flip) for i in range(lax.axis_size(axis))])

    full_field = field.reshape(slab_count * cols, rows)
    flat_field = pltpu.with_memory_space_constraint(full_field, pltpu.HBM)
    mine = members.reshape(slab_count * cols, rows)
    other = swap(mine, 1)
    line_table = pltpu.with_memory_space_constraint(alpha_table, pltpu.HBM)
    line_entries = pltpu.with_memory_space_constraint(xscale_idx, pltpu.HBM)
    line_loc = pltpu.with_memory_space_constraint(loc_filter[0], pltpu.HBM)
    ends, states, lines, *matrices = ends_call(
        line_table, line_entries, line_loc, flat_field, levels, steps, cols, own_cols
    )
    blocks, came = [ends], []
    send = send_call(matrices, full_field, mine, other, ends, cols, own_cols)
    over = swap(send, 2)
    coef = coefs_call(lines, send, steps, cols)
    for level in range(steps - 2):
        came.append(swap(blocks[0], 1 << level, "tile"))
        *blocks, coef = merge_call(lines, ends, came, [coef], levels, steps)
    near, far, part = blocks
    last = {flip: swap(near if flip == 1 else far, flip << (steps - 2), "tile") for flip in ORDER}
    keep = keep_call(matrices, full_field, mine, other, near, cols, own_cols)
    own_0, own_1 = local_call(lines, states, full_field, near, levels, cols, own_cols)
    mats, row_coef, vert = tables_call(alpha_table, yscale_idx, vert_filter[0], own_1, levels, own_cols, cols, slabs)
    shares = [part] + [last[flip] for flip in ORDER]
    others = [swap(share, 1) for share in shares]
    scale = 1.0 / (mem_count * members.shape[0] - 1)
    base = rows_call(levels, scale, own_0, coef, mats, row_coef, shares, vert, keep)
    total = join_call(levels, own_1, coef, mats, row_coef, others, vert, base)
    return final_call(slab_count, own_cols, scale, total, over)


def solution(mesh):
    return jax.shard_map(
        body,
        mesh=mesh,
        in_specs=(P(None, "tile", None), P(), P(), P(), P(), P(), P("mem", None, "tile", None)),
        out_specs=P(None, ("tile", "mem"), None),
        check_vma=False,
    )
```

```python
import functools

import jax
import jax.numpy as jnp
from jax import lax
from jax.experimental import pallas as pl
from jax.experimental.pallas import tpu as pltpu
from jax.sharding import PartitionSpec as P

F32, BF16 = jnp.float32, jnp.bfloat16
SUB = 16
CORES = 2
LANES = 256
ORDER = (1, 3, 2)
FETCHES = 1
BLOCK = 256
MIB = 1 << 20
VMEM = 32 * MIB


def iota(shape, dim):
    return lax.broadcasted_iota(jnp.int32, shape, dim)


def taking(microseconds):
    return pl.CostEstimate(flops=int(microseconds * 1.15e9), bytes_accessed=MIB // 4, transcendentals=0)


def split(number, size):
    assert size & (size - 1) == 0
    return number >> (size.bit_length() - 1), number & (size - 1)


def dot(left, right):
    return jnp.dot(left, right, preferred_element_type=F32)


def gain_of(alpha):
    rest = (1.0 - alpha) * (1.0 + alpha)
    return jnp.sqrt(rest) * rest / jnp.sqrt(1.0 + alpha * alpha)


def lookup(table_ref, entries):
    found = jnp.zeros(entries.shape, F32)
    for entry in range(table_ref.shape[0]):
        found = jnp.where(entries == entry, table_ref[entry], found)
    return found


def padded(slab_count):
    return -(-slab_count // (4 * SUB)) * 4 * SUB


def to_columns(perm, flat, out_ref, cols):
    total = flat.shape[0]
    wanted = out_ref.shape[0]
    step = SUB * cols
    for chunk in range(out_ref.shape[1] // SUB):
        depth = min(step, total - chunk * step)
        moved = dot(perm[:, :depth], flat[chunk * step : chunk * step + depth])
        out_ref[:, chunk * SUB : (chunk + 1) * SUB, :] = moved.reshape(wanted, SUB, -1).astype(out_ref.dtype)


def sweep(work, alpha):
    cols = work.shape[0]
    state = work[0]
    for col in range(1, cols):
        state = alpha * state + work[col]
        work[col] = state
    for col in range(cols - 2, -1, -1):
        state = alpha * state + work[col]
        work[col] = state


def transposer(cols):
    shape = (SUB * cols, SUB * cols)
    (out_col, out_slab), (in_slab, in_col) = split(iota(shape, 0), SUB), split(iota(shape, 1), cols)
    return ((out_slab == in_slab) & (out_col == in_col)).astype(BF16)


def share_rows(total, cols, subs, share):
    return slice(share * subs * cols, min((share + 1) * subs * cols, total))


def clear_rest(held_ref, rows):
    first = rows.stop - rows.start
    if first < held_ref.shape[0]:
        held_ref[first:, :] = jnp.zeros((held_ref.shape[0] - first, held_ref.shape[1]), BF16)


def sweep_share(levels, share, perm, alpha, held, work):
    cols, subs, lanes = work.shape
    to_columns(perm, held, work, cols)
    is_level = iota((subs, lanes), 0) + share * subs < levels
    alpha = jnp.where(is_level, alpha[0:1], alpha[1:2])
    sweep(work, alpha)
    return gain_of(alpha), is_level


def ends_kernel(
    levels, steps, slab_count, own_cols, table_hbm, entries_hbm, loc_hbm, field_hbm, ends_ref, work, lines_ref, perm_ref,
    local_ref, order_ref, table_ref, entries_ref, loc_ref, held_ref, small, arrived
):
    pieces, cols, subs, lanes = work.shape
    slabs, rows = CORES * subs, held_ref.shape[1]
    tile, mem = lax.axis_index("tile"), lax.axis_index("mem")
    chip, share = split(mem, CORES)
    parts = arrived.shape[0]

    def fetch(part, begin):
        width = rows // parts
        place = pl.ds(part * width, width)
        for core in range(CORES):
            held = share_rows(slab_count * cols, cols, subs, core)

            @pl.when(share == core)
            def _():
                copy = pltpu.make_async_copy(
                    field_hbm.at[held, place], held_ref.at[0 : held.stop - held.start, place], arrived.at[part]
                )
                if begin:
                    copy.start(priority=1)
                    clear_rest(held_ref, held)
                else:
                    copy.wait()

    for part in range(parts):
        fetch(part, True)
    given = [
        pltpu.make_async_copy(source, target, small.at[k])
        for k, (source, target) in enumerate(
            ((table_hbm, table_ref), (entries_hbm, entries_ref), (loc_hbm, loc_ref))
        )
    ]
    for copy in given:
        copy.start()
    perm_ref[...] = selection(2 * (1 - chip) + share, perm_ref.shape, own_cols, cols)
    row, col = iota(local_ref.shape, 0), iota(local_ref.shape, 1)
    (row_col, row_slab), (col_col, col_slab) = split(row, slabs), split(col, slabs)
    order_slab, order_col = split(row, own_cols)
    order_ref[...] = ((order_slab == col_slab) & (order_col == col_col)).astype(BF16)
    perm = transposer(cols)
    for copy in given:
        copy.wait()
    local_ref[...] = spread(loc_ref[...], levels, row_slab, row_col, col_slab, col_col)
    pair = lookup(table_ref, entries_ref[...])
    decay, turn = line_coefs(pair, cols)
    behind = reflected(decay, turn, tile, steps)
    lines_ref[0], lines_ref[1], lines_ref[2] = pair, decay, behind
    for piece in range(pieces):
        if piece % (pieces // parts) == 0:
            fetch(piece // (pieces // parts), False)
        part = slice(piece * lanes, (piece + 1) * lanes)
        gain, is_level = sweep_share(levels, share, perm, pair[:, part], held_ref[:, part], work.at[piece])
        turned = (decay * behind)[:, part]
        turned = jnp.where(is_level, turned[0:1], turned[1:2])
        forward = gain * work[piece, cols - 1]
        ends_ref[0, :, part] = forward.astype(BF16)
        ends_ref[1, :, part] = (gain * work[piece, 0] + turned * forward).astype(BF16)


def ends_call(table, entries, loc, flat_field, levels, steps, cols, own_cols):
    total, rows = flat_field.shape
    subs = padded(total // cols) // CORES
    side = own_cols * CORES * subs
    vmem = pl.BlockSpec(memory_space=pltpu.VMEM)
    return pl.pallas_call(
        functools.partial(ends_kernel, levels, steps, total // cols, own_cols),
        name="ends",
        in_specs=[pl.BlockSpec(memory_space=pl.ANY)] * 4,
        out_specs=[vmem] * 6,
        out_shape=[
            jax.ShapeDtypeStruct((2, subs, rows), BF16),
            jax.ShapeDtypeStruct((rows // LANES, cols, subs, LANES), F32),
            jax.ShapeDtypeStruct((3, 2, rows), F32),
            jax.ShapeDtypeStruct((own_cols * SUB, cols * SUB), BF16),
            jax.ShapeDtypeStruct((side, side), BF16),
            jax.ShapeDtypeStruct((side, side), BF16),
        ],
        scratch_shapes=[
            pltpu.SMEM(table.shape, F32),
            pltpu.VMEM(entries.shape, jnp.int32),
            pltpu.VMEM(loc.shape, BF16),
            pltpu.VMEM((subs * cols, rows), BF16),
            pltpu.SemaphoreType.DMA((3,)),
            pltpu.SemaphoreType.DMA((FETCHES,)),
        ],
        compiler_params=pltpu.CompilerParams(vmem_limit_bytes=VMEM),
        cost_estimate=taking(2.1),
    )(table, entries, loc, flat_field)


def line_coefs(pair, cols):
    decay, turn = pair, pair
    while cols > 1:
        turn = turn * (1.0 + decay * decay)
        decay = decay * decay
        cols //= 2
    return decay, turn


def reflected(decay, turn, tile, steps):
    behind = (1 << steps) - 1 - tile
    total, power = jnp.zeros_like(turn), jnp.ones_like(turn)
    for level in range(steps):
        here = ((behind >> level) & 1) == 1
        total = jnp.where(here, total + power * power * turn, total)
        power = jnp.where(here, power * decay, power)
        turn = turn * (1.0 + decay * decay)
        decay = decay * decay
    return total


def local_kernel(levels, slab_count, lines_ref, states_ref, field_ref, after_ref, mine_ref, own_ref, held_ref, work):
    pieces, cols, subs, lanes = work.shape
    own_cols = own_ref.shape[0]
    mem = lax.axis_index("mem")
    share = (mem & (CORES - 1)) ^ 1
    for core in range(CORES):
        rows = share_rows(slab_count * cols, cols, subs, core)

        @pl.when(share == core)
        def _():
            held_ref[0 : rows.stop - rows.start, :] = field_ref[rows, :]
            clear_rest(held_ref, rows)

    pair, perm = lines_ref[0], transposer(cols)
    for piece in range(pieces):
        part = slice(piece * lanes, (piece + 1) * lanes)
        gain, _ = sweep_share(levels, share, perm, pair[:, part], held_ref[:, part], work.at[piece])
        wanted = pl.ds(mem * own_cols, own_cols)
        own_ref[:, :, part] = work[piece, wanted] * gain[None]
        is_level = iota((subs, lanes), 0) + (1 - share) * subs < levels
        gain = gain_of(jnp.where(is_level, pair[0:1, part], pair[1:2, part]))
        mine_ref[:, :, part] = states_ref[piece, wanted] * gain[None]


def local_call(lines, states, flat_field, after, levels, cols, own_cols):
    total, rows = flat_field.shape
    subs = padded(total // cols) // CORES
    vmem = pl.BlockSpec(memory_space=pltpu.VMEM)
    return pl.pallas_call(
        functools.partial(local_kernel, levels, total // cols),
        name="local",
        in_specs=[vmem] * 3 + [pl.BlockSpec(memory_space=pl.ANY)],
        out_specs=[vmem] * 2,
        out_shape=[jax.ShapeDtypeStruct((own_cols, subs, rows), F32)] * 2,
        scratch_shapes=[
            pltpu.VMEM((subs * cols, rows), BF16),
            pltpu.VMEM((rows // LANES, cols, subs, LANES), F32),
        ],
        compiler_params=pltpu.CompilerParams(vmem_limit_bytes=VMEM),
        cost_estimate=taking(0.5),
    )(lines, states, flat_field, after)


def coefs_kernel(steps, lines_ref, after_ref, coef_ref):
    cols = coef_ref.shape[1] - 3
    tile = lax.axis_index("tile")
    pair, decay, behind = lines_ref[0], lines_ref[1], lines_ref[2]
    square = pair * pair
    power, sums = jnp.ones_like(pair), jnp.zeros_like(pair)
    rights, geometric = [], []
    for _ in range(cols):
        power, sums = power * pair, sums * square + 1.0
        rights.append(power)
        geometric.append(sums)
    for col in range(cols):
        coef_ref[0, col] = rights[col] * geometric[cols - 1 - col]
        coef_ref[1, col] = rights[cols - 1 - col]
    turned = decay * behind
    from_left, from_right = jnp.ones_like(pair), jnp.ones_like(pair)
    for level in range(steps - 2):
        second = ((tile >> level) & 1) == 1
        from_left = jnp.where(second, from_left * decay, from_left)
        from_right = jnp.where(second, from_right, from_right * decay)
        decay = decay * decay
    quarter = tile >> (steps - 2)
    outer = (quarter == 0) | (quarter == 3)
    for flip, weight in ((1, 1.0), (2, decay), (3, jnp.where(outer, decay * decay, 1.0))):
        upper = (quarter ^ flip) < quarter
        coef_ref[0, cols + ORDER.index(flip)] = jnp.where(upper, from_left * weight, 0.0)
        coef_ref[1, cols + ORDER.index(flip)] = weight * jnp.where(upper, turned * from_left, from_right)


def coefs_call(lines, after, steps, cols):
    vmem = pl.BlockSpec(memory_space=pltpu.VMEM)
    return pl.pallas_call(
        functools.partial(coefs_kernel, steps),
        name="coefs",
        in_specs=[vmem, pl.BlockSpec(memory_space=pl.ANY)],
        out_specs=vmem,
        out_shape=jax.ShapeDtypeStruct((2, cols + 3, *lines.shape[1:]), F32),
        compiler_params=pltpu.CompilerParams(vmem_limit_bytes=VMEM),
        cost_estimate=taking(4.0),
    )(lines, after)


def spread(matrix, levels, row_slab, row_col, col_slab, col_col):
    rows, cols = row_slab.shape
    size = matrix.shape[0]
    left = (iota((rows, size), 1) == row_slab[:, :size]).astype(BF16)
    right = (iota((size, cols), 0) == col_slab[:size, :]).astype(BF16)
    inner = dot(left, matrix).astype(BF16)
    full = dot(inner, right)
    full = jnp.where((row_slab >= levels) & (row_slab == col_slab), 1.0, full)
    return jnp.where(row_col == col_col, full, 0.0).astype(BF16)


def selection(block, shape, own_cols, cols):
    (slot, out_slab), (in_slab, in_col) = split(iota(shape, 0), SUB), split(iota(shape, 1), cols)
    return ((out_slab == in_slab) & (block * own_cols + slot == in_col)).astype(BF16)


def member_term(local, member, field):
    scaled = (member * field.astype(F32)).astype(BF16).reshape(local.shape[0], -1)
    return member * dot(local, scaled).reshape(member.shape)


def send_kernel(
    cols, perm_ref, local_ref, order_ref, field_ref, mine_ref, other_ref, after_ref, send_ref, field_w, mine_w, other_w
):
    for ref, out in ((field_ref, field_w), (mine_ref, mine_w), (other_ref, other_w)):
        to_columns(perm_ref[...], ref, out, cols)
    field, local = field_w[...], local_ref[...]
    total = member_term(local, mine_w[...], field) + member_term(local, other_w[...], field)
    total = total.reshape(order_ref.shape[0], -1).astype(BF16)
    send_ref[...] = dot(order_ref[...], total)[: send_ref.shape[0]].astype(BF16)


def keep_kernel(cols, local_ref, order_ref, field_ref, mine_ref, other_ref, after_ref, keep_ref, field_w, mine_w, other_w):
    own_cols = field_w.shape[0]
    perm = selection(lax.axis_index("mem"), (own_cols * SUB, cols * SUB), own_cols, cols)
    for ref, out in ((field_ref, field_w), (mine_ref, mine_w), (other_ref, other_w)):
        to_columns(perm, ref, out, cols)
    field, local = field_w[...], local_ref[...]
    total = member_term(local, mine_w[...], field) + member_term(local, other_w[...], field)
    total = total.reshape(order_ref.shape[0], -1)
    high = total.astype(BF16)
    ordered = dot(order_ref[...], high) + dot(order_ref[...], (total - high.astype(F32)).astype(BF16))
    keep_ref[...] = ordered[: keep_ref.shape[0]]


def send_call(matrices, flat_field, mine, other, after, cols, own_cols):
    total, rows = other.shape
    work = pltpu.VMEM((own_cols, padded(total // cols), rows), F32)
    vmem = pl.BlockSpec(memory_space=pltpu.VMEM)
    return pl.pallas_call(
        functools.partial(send_kernel, cols),
        name="send",
        in_specs=[vmem] * 6 + [pl.BlockSpec(memory_space=pl.ANY)],
        out_specs=vmem,
        out_shape=jax.ShapeDtypeStruct((total // cols * own_cols, rows), BF16),
        scratch_shapes=[work] * 3,
        compiler_params=pltpu.CompilerParams(vmem_limit_bytes=VMEM),
        cost_estimate=taking(2.6),
    )(*matrices, flat_field, mine, other, after)


def keep_call(matrices, flat_field, mine, other, after, cols, own_cols):
    total, rows = other.shape
    work = pltpu.VMEM((own_cols, padded(total // cols), rows), F32)
    vmem = pl.BlockSpec(memory_space=pltpu.VMEM)
    return pl.pallas_call(
        functools.partial(keep_kernel, cols),
        name="keep",
        in_specs=[vmem] * 5 + [pl.BlockSpec(memory_space=pl.ANY)],
        out_specs=vmem,
        out_shape=jax.ShapeDtypeStruct((total // cols * own_cols, rows), F32),
        scratch_shapes=[work] * 3,
        compiler_params=pltpu.CompilerParams(vmem_limit_bytes=VMEM),
        cost_estimate=taking(0.6),
    )(*matrices[1:], flat_field, mine, other, after)


def tables_kernel(levels, own_cols, col_dev, slabs, table_ref, entries_ref, vert_ref, after_ref, mat_ref, coef_ref, vert_out):
    first = lax.axis_index("tile") * col_dev + lax.axis_index("mem") * own_cols
    count = 2 * own_cols
    by_row = jnp.zeros((count, 1), F32)
    every, found = entries_ref[...], jnp.zeros(entries_ref.shape, F32)
    for entry in range(table_ref.shape[1]):
        found = jnp.where(every == entry, table_ref[0:1, entry : entry + 1], found)
    for col in range(own_cols):
        here = iota(found.shape, 1) == first + col
        alphas = jnp.sum(jnp.where(here, found, 0.0), axis=1, keepdims=True)
        for var in range(2):
            by_row = jnp.where(iota((count, 1), 0) == var * own_cols + col, alphas[var : var + 1], by_row)

    def series(alpha, number):
        alpha = jnp.broadcast_to(alpha, number.shape)
        total, unit = jnp.zeros(number.shape, F32), jnp.ones(number.shape, F32)
        single, power, both = alpha, alpha * alpha, jnp.ones(number.shape, F32)
        for bit in range(BLOCK.bit_length()):
            here = ((number >> bit) & 1) == 1
            total = jnp.where(here, unit + power * total, total)
            both = jnp.where(here, both * single, both)
            unit, single, power = unit * (1.0 + power), single * single, power * power
        return total, both

    place = iota((count, BLOCK), 1)
    across, right = series(by_row, BLOCK - place)
    down = jnp.concatenate([across, jnp.zeros((128 - count, BLOCK), F32)], 0).T
    _, left = series(by_row, place + 1)
    coef_ref[0] = left * across
    coef_ref[1] = right
    coef_ref[2] = jnp.broadcast_to(right[:, 0:1], right.shape)
    coef_ref[3] = jnp.broadcast_to(left[:, 0:1] * across[:, 0:1], right.shape)
    far = jnp.abs(iota((BLOCK, BLOCK), 0) - iota((BLOCK, BLOCK), 1)).astype(F32)
    for k in range(count):
        alpha = by_row[k : k + 1]
        decay = jnp.exp(far * jnp.log(jnp.maximum(alpha, 1e-30)))
        reach = jnp.minimum(down[:, k : k + 1], across[k : k + 1])
        mat_ref[k] = (gain_of(alpha) * decay * reach).astype(BF16)
    shape = vert_out.shape[1:]
    (row_slab, row_col), (col_col, col_slab) = split(iota(shape, 0), own_cols), split(iota(shape, 1), slabs // CORES)
    for share in range(CORES):
        first = share * (slabs // CORES)
        vert_out[share] = spread(vert_ref[...], levels, row_slab, row_col, col_slab + first, col_col)


def tables_call(table, entries, vert, after, levels, own_cols, col_dev, slabs):
    count = 2 * own_cols
    return pl.pallas_call(
        functools.partial(tables_kernel, levels, own_cols, col_dev, slabs),
        name="tables",
        in_specs=[pl.BlockSpec(memory_space=pltpu.VMEM)] * 3 + [pl.BlockSpec(memory_space=pl.ANY)],
        out_specs=[pl.BlockSpec(memory_space=pltpu.VMEM)] * 3,
        out_shape=[
            jax.ShapeDtypeStruct((count, BLOCK, BLOCK), BF16),
            jax.ShapeDtypeStruct((4, count, BLOCK), F32),
            jax.ShapeDtypeStruct((CORES, own_cols * slabs, own_cols * slabs // CORES), BF16),
        ],
        compiler_params=pltpu.CompilerParams(vmem_limit_bytes=VMEM),
        cost_estimate=taking(0.4),
    )(table[None], entries, vert, after)


def along_rows(lines, matrix, coef):
    count, rows = lines.shape
    blocks = rows // BLOCK
    parts = jnp.concatenate([lines[:, b * BLOCK : (b + 1) * BLOCK] for b in range(blocks)], 0)
    local = dot(parts.astype(BF16), matrix)
    local = [local[b * count : (b + 1) * count] for b in range(blocks)]
    into, right, decay, turn = coef[0:1], coef[1:2], coef[2:3, 0:1], coef[3:4, 0:1]
    forward, state = [None], None
    for b in range(blocks - 1):
        end = local[b][:, BLOCK - 1 : BLOCK]
        state = end if state is None else decay * state + end
        forward.append(state)
    out, state = [None] * blocks, None
    for b in range(blocks - 1, -1, -1):
        piece = local[b]
        if forward[b] is not None:
            piece = piece + into * forward[b]
        if state is not None:
            piece = piece + right * state
        out[b] = piece
        if b:
            start = local[b][:, 0:1] + turn * forward[b]
            state = start if state is None else decay * state + start
    return out


def filter_share(levels, share, own_ref, coef_ref, mat_ref, row_coef_ref, part_ref, last_refs, out_ref):
    own_cols, subs, rows = own_ref.shape
    cols = coef_ref.shape[1] - 3
    mem = lax.axis_index("mem")
    end = slice(subs - 8, subs)
    is_level = iota((8, rows), 0) + share * subs + subs - 8 < levels
    lasts = [ref[...].astype(F32) for ref in last_refs]
    carry, carry_end = [], []
    for side in range(2):
        value = part_ref[side].astype(F32)
        other = value[end]
        for k, last in enumerate(lasts):
            value = value + coef_ref[side, cols + k, 0:1] * last
            other = other + coef_ref[side, cols + k, 1:2] * last[end]
        carry.append(value)
        carry_end.append(other)
    for col in range(own_cols):
        pair = coef_ref[:, mem * own_cols + col]
        own = own_ref[col]
        lines = own + pair[0, 0:1] * carry[0] + pair[1, 0:1] * carry[1]
        last_lines = own[end] + pair[0, 1:2] * carry_end[0] + pair[1, 1:2] * carry_end[1]
        main = along_rows(lines, mat_ref[col], row_coef_ref[:, col])
        last = along_rows(last_lines, mat_ref[own_cols + col], row_coef_ref[:, own_cols + col])
        for b, (piece, extra) in enumerate(zip(main, last)):
            place = slice(b * BLOCK, (b + 1) * BLOCK)
            out_ref[col, 0 : subs - 8, place] = piece[0 : subs - 8]
            out_ref[col, end, place] = jnp.where(is_level[:, place], piece[end], extra)


def mixed(vert, static):
    return dot(vert, static.astype(BF16))


def rows_kernel(levels, scale, own_ref, coef_ref, mat_ref, row_coef_ref, part_ref, *refs):
    *last_refs, vert_ref, keep_ref, base_ref, filt = refs
    share = lax.axis_index("mem") & (CORES - 1)
    filter_share(levels, share, own_ref, coef_ref, mat_ref, row_coef_ref, part_ref, last_refs, filt)
    total = mixed(vert_ref[share], filt[...].reshape(vert_ref.shape[2], -1))
    base_ref[...] = total[: base_ref.shape[0]] + keep_ref[...] * scale


def rows_call(levels, scale, own, coef, mats, row_coef, shares, vert, keep):
    vmem = pl.BlockSpec(memory_space=pltpu.VMEM)
    args = [own, coef, mats, row_coef, *shares, vert, keep]
    return pl.pallas_call(
        functools.partial(rows_kernel, levels, scale),
        name="rows",
        in_specs=[vmem] * len(args),
        out_specs=vmem,
        out_shape=jax.ShapeDtypeStruct(keep.shape, F32),
        scratch_shapes=[pltpu.VMEM(own.shape, F32)],
        compiler_params=pltpu.CompilerParams(vmem_limit_bytes=VMEM),
        cost_estimate=taking(1.2),
    )(*args)


def join_kernel(
    levels, own_ref, coef_ref, mat_ref, row_coef_ref, part_ref, last_1_ref, last_2_ref, last_3_ref, vert_ref, base_ref,
    total_ref, filt
):
    other = 1 - (lax.axis_index("mem") & (CORES - 1))
    last_refs = last_1_ref, last_2_ref, last_3_ref
    filter_share(levels, other, own_ref, coef_ref, mat_ref, row_coef_ref, part_ref, last_refs, filt)
    total = mixed(vert_ref[other], filt[...].reshape(vert_ref.shape[2], -1))
    total_ref[...] = total[: base_ref.shape[0]] + base_ref[...]


def join_call(levels, own, coef, mats, row_coef, shares, vert, base):
    vmem = pl.BlockSpec(memory_space=pltpu.VMEM)
    args = [own, coef, mats, row_coef, *shares, vert, base]
    return pl.pallas_call(
        functools.partial(join_kernel, levels),
        name="join",
        in_specs=[vmem] * len(args),
        out_specs=vmem,
        out_shape=jax.ShapeDtypeStruct(base.shape, F32),
        scratch_shapes=[pltpu.VMEM(own.shape, F32)],
        compiler_params=pltpu.CompilerParams(vmem_limit_bytes=VMEM),
        cost_estimate=taking(0.8),
    )(*args)


def final_kernel(scale, total_ref, came_ref, out_hbm, out_ref, sent):
    count, own_cols, rows = out_ref.shape
    copies = []
    for piece, first in enumerate(range(0, count, SUB)):
        place = slice(first, min(first + SUB, count))
        wide = slice(place.start * own_cols, place.stop * own_cols)
        total = total_ref[wide] + came_ref[wide].astype(F32) * scale
        out_ref[place] = total.reshape(place.stop - place.start, own_cols, rows).astype(BF16)
        copies.append(pltpu.make_async_copy(out_ref.at[place], out_hbm.at[place], sent.at[piece]))
        copies[-1].start()
    for copy in copies:
        copy.wait()


def final_call(slab_count, own_cols, scale, total, came):
    rows = total.shape[1]
    vmem = pl.BlockSpec(memory_space=pltpu.VMEM)
    out_shape = (slab_count, own_cols, rows)
    return pl.pallas_call(
        functools.partial(final_kernel, scale),
        name="final",
        in_specs=[vmem] * 2,
        out_specs=pl.BlockSpec(memory_space=pl.ANY),
        out_shape=jax.ShapeDtypeStruct(out_shape, BF16),
        scratch_shapes=[pltpu.VMEM(out_shape, BF16), pltpu.SemaphoreType.DMA((-(-slab_count // SUB),))],
        compiler_params=pltpu.CompilerParams(vmem_limit_bytes=VMEM),
        cost_estimate=taking(0.8),
    )(total, came)


def merge_kernel(levels, steps, step, last, after_count, *refs):
    lines_ref, ends_ref = refs[:2]
    came_refs, outs = refs[2 : 2 + step], refs[2 + step + after_count :]
    _, subs, rows = ends_ref.shape
    tile, mem = lax.axis_index("tile"), lax.axis_index("mem")
    is_level = iota((subs, rows), 0) + (mem & (CORES - 1)) * subs < levels
    decay = jnp.where(is_level, lines_ref[1, 0:1], lines_ref[1, 1:2])
    behind = jnp.where(is_level, lines_ref[2, 0:1], lines_ref[2, 1:2])
    turned = behind * decay
    right, left = ends_ref[0].astype(F32), ends_ref[1].astype(F32)
    into_right, into_left, from_left, from_right = 0.0, behind * right, 1.0, 1.0
    for level, came_ref in enumerate(came_refs):
        second = ((tile >> level) & 1) == 1
        came_right, came_left = came_ref[0].astype(F32), came_ref[1].astype(F32)
        into_right = into_right + jnp.where(second, from_left * came_right, 0.0)
        into_left = into_left + jnp.where(second, 0.0, from_right * came_left)
        right = jnp.where(second, decay * came_right + right, decay * right + came_right)
        left = jnp.where(second, came_left + decay * left, left + decay * came_left)
        from_left = jnp.where(second, from_left * decay, from_left)
        from_right = jnp.where(second, from_right, from_right * decay)
        decay = decay * decay
    if last:
        quarter = tile >> (steps - 2)
        outs[0][...] = jnp.where((quarter & 1) == 1, left, right).astype(BF16)
        outs[1][...] = jnp.where(quarter >= 2, left, right).astype(BF16)
        outs[2][0] = into_right.astype(BF16)
        outs[2][1] = (into_left + turned * into_right).astype(BF16)
    else:
        outs[0][0] = right.astype(BF16)
        outs[0][1] = left.astype(BF16)


def merge_call(lines, ends, came, after, levels, steps):
    last = len(came) == steps - 2
    whole = jax.ShapeDtypeStruct(ends.shape, BF16)
    one = jax.ShapeDtypeStruct(ends.shape[1:], BF16)
    outs = [one, one, whole] if last else [whole]
    vmem = pl.BlockSpec(memory_space=pltpu.VMEM)
    held = [pl.BlockSpec(memory_space=pl.ANY)] * len(after)
    return pl.pallas_call(
        functools.partial(merge_kernel, levels, steps, len(came), last, len(after)),
        name="merge",
        in_specs=[vmem] * (2 + len(came)) + held,
        out_specs=[vmem] * len(outs) + held,
        out_shape=outs + [jax.ShapeDtypeStruct(array.shape, array.dtype) for array in after],
        input_output_aliases={2 + len(came) + k: len(outs) + k for k in range(len(after))},
        compiler_params=pltpu.CompilerParams(vmem_limit_bytes=VMEM),
        cost_estimate=taking(0.8),
    )(lines, ends, *came, *after)


def body(field, vert_filter, loc_filter, alpha_table, xscale_idx, yscale_idx, members):
    tile_count, mem_count = lax.axis_size("tile"), lax.axis_size("mem")
    slab_count, cols, rows = field.shape
    levels = vert_filter.shape[1]
    own_cols = cols // mem_count
    slabs = padded(slab_count)
    steps = tile_count.bit_length() - 1

    def swap(array, flip, axis="mem"):
        return lax.ppermute(array, axis, [(i, i ^ flip) for i in range(lax.axis_size(axis))])

    full_field = field.reshape(slab_count * cols, rows)
    flat_field = pltpu.with_memory_space_constraint(full_field, pltpu.HBM)
    mine = members.reshape(slab_count * cols, rows)
    other = swap(mine, 1)
    line_table = pltpu.with_memory_space_constraint(alpha_table, pltpu.HBM)
    line_entries = pltpu.with_memory_space_constraint(xscale_idx, pltpu.HBM)
    line_loc = pltpu.with_memory_space_constraint(loc_filter[0], pltpu.HBM)
    ends, states, lines, *matrices = ends_call(
        line_table, line_entries, line_loc, flat_field, levels, steps, cols, own_cols
    )
    blocks, came = [ends], []
    send = send_call(matrices, full_field, mine, other, ends, cols, own_cols)
    over = swap(send, 2)
    coef = coefs_call(lines, send, steps, cols)
    for level in range(steps - 2):
        came.append(swap(blocks[0], 1 << level, "tile"))
        *blocks, coef = merge_call(lines, ends, came, [coef], levels, steps)
    near, far, part = blocks
    last = {flip: swap(near if flip == 1 else far, flip << (steps - 2), "tile") for flip in ORDER}
    keep = keep_call(matrices, full_field, mine, other, near, cols, own_cols)
    own_0, own_1 = local_call(lines, states, full_field, near, levels, cols, own_cols)
    mats, row_coef, vert = tables_call(alpha_table, yscale_idx, vert_filter[0], own_1, levels, own_cols, cols, slabs)
    shares = [part] + [last[flip] for flip in ORDER]
    others = [swap(share, 1) for share in shares]
    scale = 1.0 / (mem_count * members.shape[0] - 1)
    base = rows_call(levels, scale, own_0, coef, mats, row_coef, shares, vert, keep)
    total = join_call(levels, own_1, coef, mats, row_coef, others, vert, base)
    return final_call(slab_count, own_cols, scale, total, over)


def solution(mesh):
    return jax.shard_map(
        body,
        mesh=mesh,
        in_specs=(P(None, "tile", None), P(), P(), P(), P(), P(), P("mem", None, "tile", None)),
        out_specs=P(None, ("tile", "mem"), None),
        check_vma=False,
    )
```

```python
import functools

import jax
import jax.numpy as jnp
from jax import lax
from jax.experimental import pallas as pl
from jax.experimental.pallas import tpu as pltpu
from jax.sharding import PartitionSpec as P

F32, BF16 = jnp.float32, jnp.bfloat16
SUB = 16
CORES = 2
LANES = 256
ORDER = (1, 3, 2)
FETCHES = 2
BLOCK = 256
MIB = 1 << 20
VMEM = 32 * MIB


def iota(shape, dim):
    return lax.broadcasted_iota(jnp.int32, shape, dim)


def taking(microseconds):
    return pl.CostEstimate(flops=int(microseconds * 1.15e9), bytes_accessed=MIB // 4, transcendentals=0)


def split(number, size):
    assert size & (size - 1) == 0
    return number >> (size.bit_length() - 1), number & (size - 1)


def dot(left, right):
    return jnp.dot(left, right, preferred_element_type=F32)


def gain_of(alpha):
    rest = (1.0 - alpha) * (1.0 + alpha)
    return jnp.sqrt(rest) * rest / jnp.sqrt(1.0 + alpha * alpha)


def lookup(table_ref, entries):
    found = jnp.zeros(entries.shape, F32)
    for entry in range(table_ref.shape[0]):
        found = jnp.where(entries == entry, table_ref[entry], found)
    return found


def padded(slab_count):
    return -(-slab_count // (4 * SUB)) * 4 * SUB


def to_columns(perm, flat, out_ref, cols):
    total = flat.shape[0]
    wanted = out_ref.shape[0]
    step = SUB * cols
    for chunk in range(out_ref.shape[1] // SUB):
        depth = min(step, total - chunk * step)
        moved = dot(perm[:, :depth], flat[chunk * step : chunk * step + depth])
        out_ref[:, chunk * SUB : (chunk + 1) * SUB, :] = moved.reshape(wanted, SUB, -1).astype(out_ref.dtype)


def sweep(work, alpha):
    cols = work.shape[0]
    state = work[0]
    for col in range(1, cols):
        state = alpha * state + work[col]
        work[col] = state
    for col in range(cols - 2, -1, -1):
        state = alpha * state + work[col]
        work[col] = state


def transposer(cols):
    shape = (SUB * cols, SUB * cols)
    (out_col, out_slab), (in_slab, in_col) = split(iota(shape, 0), SUB), split(iota(shape, 1), cols)
    return ((out_slab == in_slab) & (out_col == in_col)).astype(BF16)


def share_rows(total, cols, subs, share):
    return slice(share * subs * cols, min((share + 1) * subs * cols, total))


def clear_rest(held_ref, rows):
    first = rows.stop - rows.start
    if first < held_ref.shape[0]:
        held_ref[first:, :] = jnp.zeros((held_ref.shape[0] - first, held_ref.shape[1]), BF16)


def sweep_share(levels, share, perm, alpha, held, work):
    cols, subs, lanes = work.shape
    to_columns(perm, held, work, cols)
    is_level = iota((subs, lanes), 0) + share * subs < levels
    alpha = jnp.where(is_level, alpha[0:1], alpha[1:2])
    sweep(work, alpha)
    return gain_of(alpha), is_level


def ends_kernel(
    levels, steps, slab_count, own_cols, table_hbm, entries_hbm, loc_hbm, field_hbm, ends_ref, work, lines_ref, perm_ref,
    local_ref, order_ref, table_ref, entries_ref, loc_ref, held_ref, small, arrived
):
    pieces, cols, subs, lanes = work.shape
    slabs, rows = CORES * subs, held_ref.shape[1]
    tile, mem = lax.axis_index("tile"), lax.axis_index("mem")
    chip, share = split(mem, CORES)
    parts = arrived.shape[0]

    def fetch(part, begin):
        step = subs * cols // parts
        for core in range(CORES):
            held = share_rows(slab_count * cols, cols, subs, core)
            size = min(step, held.stop - held.start - part * step)

            @pl.when(share == core)
            def _():
                copy = pltpu.make_async_copy(
                    field_hbm.at[held.start + part * step : held.start + part * step + size],
                    held_ref.at[part * step : part * step + size],
                    arrived.at[part],
                )
                if begin:
                    copy.start(priority=1 - part % 2)
                    if part == parts - 1:
                        clear_rest(held_ref, held)
                else:
                    copy.wait()

    for part in range(parts):
        fetch(part, True)
    given = [
        pltpu.make_async_copy(source, target, small.at[k])
        for k, (source, target) in enumerate(
            ((table_hbm, table_ref), (entries_hbm, entries_ref), (loc_hbm, loc_ref))
        )
    ]
    for copy in given:
        copy.start()
    perm_ref[...] = selection(2 * (1 - chip) + share, perm_ref.shape, own_cols, cols)
    row, col = iota(local_ref.shape, 0), iota(local_ref.shape, 1)
    (row_col, row_slab), (col_col, col_slab) = split(row, slabs), split(col, slabs)
    order_slab, order_col = split(row, own_cols)
    order_ref[...] = ((order_slab == col_slab) & (order_col == col_col)).astype(BF16)
    perm = transposer(cols)
    for copy in given:
        copy.wait()
    local_ref[...] = spread(loc_ref[...], levels, row_slab, row_col, col_slab, col_col)
    pair = lookup(table_ref, entries_ref[...])
    decay, turn = line_coefs(pair, cols)
    behind = reflected(decay, turn, tile, steps)
    lines_ref[0], lines_ref[1], lines_ref[2] = pair, decay, behind
    for piece in range(pieces):
        if piece == 0:
            for k in range(parts):
                fetch(k, False)
        part = slice(piece * lanes, (piece + 1) * lanes)
        gain, is_level = sweep_share(levels, share, perm, pair[:, part], held_ref[:, part], work.at[piece])
        turned = (decay * behind)[:, part]
        turned = jnp.where(is_level, turned[0:1], turned[1:2])
        forward = gain * work[piece, cols - 1]
        ends_ref[0, :, part] = forward.astype(BF16)
        ends_ref[1, :, part] = (gain * work[piece, 0] + turned * forward).astype(BF16)


def ends_call(table, entries, loc, flat_field, levels, steps, cols, own_cols):
    total, rows = flat_field.shape
    subs = padded(total // cols) // CORES
    side = own_cols * CORES * subs
    vmem = pl.BlockSpec(memory_space=pltpu.VMEM)
    return pl.pallas_call(
        functools.partial(ends_kernel, levels, steps, total // cols, own_cols),
        name="ends",
        in_specs=[pl.BlockSpec(memory_space=pl.ANY)] * 4,
        out_specs=[vmem] * 6,
        out_shape=[
            jax.ShapeDtypeStruct((2, subs, rows), BF16),
            jax.ShapeDtypeStruct((rows // LANES, cols, subs, LANES), F32),
            jax.ShapeDtypeStruct((3, 2, rows), F32),
            jax.ShapeDtypeStruct((own_cols * SUB, cols * SUB), BF16),
            jax.ShapeDtypeStruct((side, side), BF16),
            jax.ShapeDtypeStruct((side, side), BF16),
        ],
        scratch_shapes=[
            pltpu.SMEM(table.shape, F32),
            pltpu.VMEM(entries.shape, jnp.int32),
            pltpu.VMEM(loc.shape, BF16),
            pltpu.VMEM((subs * cols, rows), BF16),
            pltpu.SemaphoreType.DMA((3,)),
            pltpu.SemaphoreType.DMA((FETCHES,)),
        ],
        compiler_params=pltpu.CompilerParams(vmem_limit_bytes=VMEM),
        cost_estimate=taking(2.1),
    )(table, entries, loc, flat_field)


def line_coefs(pair, cols):
    decay, turn = pair, pair
    while cols > 1:
        turn = turn * (1.0 + decay * decay)
        decay = decay * decay
        cols //= 2
    return decay, turn


def reflected(decay, turn, tile, steps):
    behind = (1 << steps) - 1 - tile
    total, power = jnp.zeros_like(turn), jnp.ones_like(turn)
    for level in range(steps):
        here = ((behind >> level) & 1) == 1
        total = jnp.where(here, total + power * power * turn, total)
        power = jnp.where(here, power * decay, power)
        turn = turn * (1.0 + decay * decay)
        decay = decay * decay
    return total


def local_kernel(levels, slab_count, lines_ref, states_ref, field_ref, after_ref, mine_ref, own_ref, held_ref, work):
    pieces, cols, subs, lanes = work.shape
    own_cols = own_ref.shape[0]
    mem = lax.axis_index("mem")
    share = (mem & (CORES - 1)) ^ 1
    for core in range(CORES):
        rows = share_rows(slab_count * cols, cols, subs, core)

        @pl.when(share == core)
        def _():
            held_ref[0 : rows.stop - rows.start, :] = field_ref[rows, :]
            clear_rest(held_ref, rows)

    pair, perm = lines_ref[0], transposer(cols)
    for piece in range(pieces):
        part = slice(piece * lanes, (piece + 1) * lanes)
        gain, _ = sweep_share(levels, share, perm, pair[:, part], held_ref[:, part], work.at[piece])
        wanted = pl.ds(mem * own_cols, own_cols)
        own_ref[:, :, part] = work[piece, wanted] * gain[None]
        is_level = iota((subs, lanes), 0) + (1 - share) * subs < levels
        gain = gain_of(jnp.where(is_level, pair[0:1, part], pair[1:2, part]))
        mine_ref[:, :, part] = states_ref[piece, wanted] * gain[None]


def local_call(lines, states, flat_field, after, levels, cols, own_cols):
    total, rows = flat_field.shape
    subs = padded(total // cols) // CORES
    vmem = pl.BlockSpec(memory_space=pltpu.VMEM)
    return pl.pallas_call(
        functools.partial(local_kernel, levels, total // cols),
        name="local",
        in_specs=[vmem] * 3 + [pl.BlockSpec(memory_space=pl.ANY)],
        out_specs=[vmem] * 2,
        out_shape=[jax.ShapeDtypeStruct((own_cols, subs, rows), F32)] * 2,
        scratch_shapes=[
            pltpu.VMEM((subs * cols, rows), BF16),
            pltpu.VMEM((rows // LANES, cols, subs, LANES), F32),
        ],
        compiler_params=pltpu.CompilerParams(vmem_limit_bytes=VMEM),
        cost_estimate=taking(0.5),
    )(lines, states, flat_field, after)


def coefs_kernel(steps, lines_ref, after_ref, coef_ref):
    cols = coef_ref.shape[1] - 3
    tile = lax.axis_index("tile")
    pair, decay, behind = lines_ref[0], lines_ref[1], lines_ref[2]
    square = pair * pair
    power, sums = jnp.ones_like(pair), jnp.zeros_like(pair)
    rights, geometric = [], []
    for _ in range(cols):
        power, sums = power * pair, sums * square + 1.0
        rights.append(power)
        geometric.append(sums)
    for col in range(cols):
        coef_ref[0, col] = rights[col] * geometric[cols - 1 - col]
        coef_ref[1, col] = rights[cols - 1 - col]
    turned = decay * behind
    from_left, from_right = jnp.ones_like(pair), jnp.ones_like(pair)
    for level in range(steps - 2):
        second = ((tile >> level) & 1) == 1
        from_left = jnp.where(second, from_left * decay, from_left)
        from_right = jnp.where(second, from_right, from_right * decay)
        decay = decay * decay
    quarter = tile >> (steps - 2)
    outer = (quarter == 0) | (quarter == 3)
    for flip, weight in ((1, 1.0), (2, decay), (3, jnp.where(outer, decay * decay, 1.0))):
        upper = (quarter ^ flip) < quarter
        coef_ref[0, cols + ORDER.index(flip)] = jnp.where(upper, from_left * weight, 0.0)
        coef_ref[1, cols + ORDER.index(flip)] = weight * jnp.where(upper, turned * from_left, from_right)


def coefs_call(lines, after, steps, cols):
    vmem = pl.BlockSpec(memory_space=pltpu.VMEM)
    return pl.pallas_call(
        functools.partial(coefs_kernel, steps),
        name="coefs",
        in_specs=[vmem, pl.BlockSpec(memory_space=pl.ANY)],
        out_specs=vmem,
        out_shape=jax.ShapeDtypeStruct((2, cols + 3, *lines.shape[1:]), F32),
        compiler_params=pltpu.CompilerParams(vmem_limit_bytes=VMEM),
        cost_estimate=taking(4.0),
    )(lines, after)


def spread(matrix, levels, row_slab, row_col, col_slab, col_col):
    rows, cols = row_slab.shape
    size = matrix.shape[0]
    left = (iota((rows, size), 1) == row_slab[:, :size]).astype(BF16)
    right = (iota((size, cols), 0) == col_slab[:size, :]).astype(BF16)
    inner = dot(left, matrix).astype(BF16)
    full = dot(inner, right)
    full = jnp.where((row_slab >= levels) & (row_slab == col_slab), 1.0, full)
    return jnp.where(row_col == col_col, full, 0.0).astype(BF16)


def selection(block, shape, own_cols, cols):
    (slot, out_slab), (in_slab, in_col) = split(iota(shape, 0), SUB), split(iota(shape, 1), cols)
    return ((out_slab == in_slab) & (block * own_cols + slot == in_col)).astype(BF16)


def member_term(local, member, field):
    scaled = (member * field.astype(F32)).astype(BF16).reshape(local.shape[0], -1)
    return member * dot(local, scaled).reshape(member.shape)


def send_kernel(
    cols, perm_ref, local_ref, order_ref, field_ref, mine_ref, other_ref, after_ref, send_ref, field_w, mine_w, other_w
):
    for ref, out in ((field_ref, field_w), (mine_ref, mine_w), (other_ref, other_w)):
        to_columns(perm_ref[...], ref, out, cols)
    field, local = field_w[...], local_ref[...]
    total = member_term(local, mine_w[...], field) + member_term(local, other_w[...], field)
    total = total.reshape(order_ref.shape[0], -1).astype(BF16)
    send_ref[...] = dot(order_ref[...], total)[: send_ref.shape[0]].astype(BF16)


def keep_kernel(cols, local_ref, order_ref, field_ref, mine_ref, other_ref, after_ref, keep_ref, field_w, mine_w, other_w):
    own_cols = field_w.shape[0]
    perm = selection(lax.axis_index("mem"), (own_cols * SUB, cols * SUB), own_cols, cols)
    for ref, out in ((field_ref, field_w), (mine_ref, mine_w), (other_ref, other_w)):
        to_columns(perm, ref, out, cols)
    field, local = field_w[...], local_ref[...]
    total = member_term(local, mine_w[...], field) + member_term(local, other_w[...], field)
    total = total.reshape(order_ref.shape[0], -1)
    high = total.astype(BF16)
    ordered = dot(order_ref[...], high) + dot(order_ref[...], (total - high.astype(F32)).astype(BF16))
    keep_ref[...] = ordered[: keep_ref.shape[0]]


def send_call(matrices, flat_field, mine, other, after, cols, own_cols):
    total, rows = other.shape
    work = pltpu.VMEM((own_cols, padded(total // cols), rows), F32)
    vmem = pl.BlockSpec(memory_space=pltpu.VMEM)
    return pl.pallas_call(
        functools.partial(send_kernel, cols),
        name="send",
        in_specs=[vmem] * 6 + [pl.BlockSpec(memory_space=pl.ANY)],
        out_specs=vmem,
        out_shape=jax.ShapeDtypeStruct((total // cols * own_cols, rows), BF16),
        scratch_shapes=[work] * 3,
        compiler_params=pltpu.CompilerParams(vmem_limit_bytes=VMEM),
        cost_estimate=taking(2.6),
    )(*matrices, flat_field, mine, other, after)


def keep_call(matrices, flat_field, mine, other, after, cols, own_cols):
    total, rows = other.shape
    work = pltpu.VMEM((own_cols, padded(total // cols), rows), F32)
    vmem = pl.BlockSpec(memory_space=pltpu.VMEM)
    return pl.pallas_call(
        functools.partial(keep_kernel, cols),
        name="keep",
        in_specs=[vmem] * 5 + [pl.BlockSpec(memory_space=pl.ANY)],
        out_specs=vmem,
        out_shape=jax.ShapeDtypeStruct((total // cols * own_cols, rows), F32),
        scratch_shapes=[work] * 3,
        compiler_params=pltpu.CompilerParams(vmem_limit_bytes=VMEM),
        cost_estimate=taking(0.6),
    )(*matrices[1:], flat_field, mine, other, after)


def tables_kernel(levels, own_cols, col_dev, slabs, table_ref, entries_ref, vert_ref, after_ref, mat_ref, coef_ref, vert_out):
    first = lax.axis_index("tile") * col_dev + lax.axis_index("mem") * own_cols
    count = 2 * own_cols
    by_row = jnp.zeros((count, 1), F32)
    every, found = entries_ref[...], jnp.zeros(entries_ref.shape, F32)
    for entry in range(table_ref.shape[1]):
        found = jnp.where(every == entry, table_ref[0:1, entry : entry + 1], found)
    for col in range(own_cols):
        here = iota(found.shape, 1) == first + col
        alphas = jnp.sum(jnp.where(here, found, 0.0), axis=1, keepdims=True)
        for var in range(2):
            by_row = jnp.where(iota((count, 1), 0) == var * own_cols + col, alphas[var : var + 1], by_row)

    def series(alpha, number):
        alpha = jnp.broadcast_to(alpha, number.shape)
        total, unit = jnp.zeros(number.shape, F32), jnp.ones(number.shape, F32)
        single, power, both = alpha, alpha * alpha, jnp.ones(number.shape, F32)
        for bit in range(BLOCK.bit_length()):
            here = ((number >> bit) & 1) == 1
            total = jnp.where(here, unit + power * total, total)
            both = jnp.where(here, both * single, both)
            unit, single, power = unit * (1.0 + power), single * single, power * power
        return total, both

    place = iota((count, BLOCK), 1)
    across, right = series(by_row, BLOCK - place)
    down = jnp.concatenate([across, jnp.zeros((128 - count, BLOCK), F32)], 0).T
    _, left = series(by_row, place + 1)
    coef_ref[0] = left * across
    coef_ref[1] = right
    coef_ref[2] = jnp.broadcast_to(right[:, 0:1], right.shape)
    coef_ref[3] = jnp.broadcast_to(left[:, 0:1] * across[:, 0:1], right.shape)
    far = jnp.abs(iota((BLOCK, BLOCK), 0) - iota((BLOCK, BLOCK), 1)).astype(F32)
    for k in range(count):
        alpha = by_row[k : k + 1]
        decay = jnp.exp(far * jnp.log(jnp.maximum(alpha, 1e-30)))
        reach = jnp.minimum(down[:, k : k + 1], across[k : k + 1])
        mat_ref[k] = (gain_of(alpha) * decay * reach).astype(BF16)
    shape = vert_out.shape[1:]
    (row_slab, row_col), (col_col, col_slab) = split(iota(shape, 0), own_cols), split(iota(shape, 1), slabs // CORES)
    for share in range(CORES):
        first = share * (slabs // CORES)
        vert_out[share] = spread(vert_ref[...], levels, row_slab, row_col, col_slab + first, col_col)


def tables_call(table, entries, vert, after, levels, own_cols, col_dev, slabs):
    count = 2 * own_cols
    return pl.pallas_call(
        functools.partial(tables_kernel, levels, own_cols, col_dev, slabs),
        name="tables",
        in_specs=[pl.BlockSpec(memory_space=pltpu.VMEM)] * 3 + [pl.BlockSpec(memory_space=pl.ANY)],
        out_specs=[pl.BlockSpec(memory_space=pltpu.VMEM)] * 3,
        out_shape=[
            jax.ShapeDtypeStruct((count, BLOCK, BLOCK), BF16),
            jax.ShapeDtypeStruct((4, count, BLOCK), F32),
            jax.ShapeDtypeStruct((CORES, own_cols * slabs, own_cols * slabs // CORES), BF16),
        ],
        compiler_params=pltpu.CompilerParams(vmem_limit_bytes=VMEM),
        cost_estimate=taking(0.4),
    )(table[None], entries, vert, after)


def along_rows(lines, matrix, coef):
    count, rows = lines.shape
    blocks = rows // BLOCK
    parts = jnp.concatenate([lines[:, b * BLOCK : (b + 1) * BLOCK] for b in range(blocks)], 0)
    local = dot(parts.astype(BF16), matrix)
    local = [local[b * count : (b + 1) * count] for b in range(blocks)]
    into, right, decay, turn = coef[0:1], coef[1:2], coef[2:3, 0:1], coef[3:4, 0:1]
    forward, state = [None], None
    for b in range(blocks - 1):
        end = local[b][:, BLOCK - 1 : BLOCK]
        state = end if state is None else decay * state + end
        forward.append(state)
    out, state = [None] * blocks, None
    for b in range(blocks - 1, -1, -1):
        piece = local[b]
        if forward[b] is not None:
            piece = piece + into * forward[b]
        if state is not None:
            piece = piece + right * state
        out[b] = piece
        if b:
            start = local[b][:, 0:1] + turn * forward[b]
            state = start if state is None else decay * state + start
    return out


def filter_share(levels, share, own_ref, coef_ref, mat_ref, row_coef_ref, part_ref, last_refs, out_ref):
    own_cols, subs, rows = own_ref.shape
    cols = coef_ref.shape[1] - 3
    mem = lax.axis_index("mem")
    end = slice(subs - 8, subs)
    is_level = iota((8, rows), 0) + share * subs + subs - 8 < levels
    lasts = [ref[...].astype(F32) for ref in last_refs]
    carry, carry_end = [], []
    for side in range(2):
        value = part_ref[side].astype(F32)
        other = value[end]
        for k, last in enumerate(lasts):
            value = value + coef_ref[side, cols + k, 0:1] * last
            other = other + coef_ref[side, cols + k, 1:2] * last[end]
        carry.append(value)
        carry_end.append(other)
    for col in range(own_cols):
        pair = coef_ref[:, mem * own_cols + col]
        own = own_ref[col]
        lines = own + pair[0, 0:1] * carry[0] + pair[1, 0:1] * carry[1]
        last_lines = own[end] + pair[0, 1:2] * carry_end[0] + pair[1, 1:2] * carry_end[1]
        main = along_rows(lines, mat_ref[col], row_coef_ref[:, col])
        last = along_rows(last_lines, mat_ref[own_cols + col], row_coef_ref[:, own_cols + col])
        for b, (piece, extra) in enumerate(zip(main, last)):
            place = slice(b * BLOCK, (b + 1) * BLOCK)
            out_ref[col, 0 : subs - 8, place] = piece[0 : subs - 8]
            out_ref[col, end, place] = jnp.where(is_level[:, place], piece[end], extra)


def mixed(vert, static):
    return dot(vert, static.astype(BF16))


def rows_kernel(levels, scale, own_ref, coef_ref, mat_ref, row_coef_ref, part_ref, *refs):
    *last_refs, vert_ref, keep_ref, base_ref, filt = refs
    share = lax.axis_index("mem") & (CORES - 1)
    filter_share(levels, share, own_ref, coef_ref, mat_ref, row_coef_ref, part_ref, last_refs, filt)
    total = mixed(vert_ref[share], filt[...].reshape(vert_ref.shape[2], -1))
    base_ref[...] = total[: base_ref.shape[0]] + keep_ref[...] * scale


def rows_call(levels, scale, own, coef, mats, row_coef, shares, vert, keep):
    vmem = pl.BlockSpec(memory_space=pltpu.VMEM)
    args = [own, coef, mats, row_coef, *shares, vert, keep]
    return pl.pallas_call(
        functools.partial(rows_kernel, levels, scale),
        name="rows",
        in_specs=[vmem] * len(args),
        out_specs=vmem,
        out_shape=jax.ShapeDtypeStruct(keep.shape, F32),
        scratch_shapes=[pltpu.VMEM(own.shape, F32)],
        compiler_params=pltpu.CompilerParams(vmem_limit_bytes=VMEM),
        cost_estimate=taking(1.2),
    )(*args)


def join_kernel(
    levels, own_ref, coef_ref, mat_ref, row_coef_ref, part_ref, last_1_ref, last_2_ref, last_3_ref, vert_ref, base_ref,
    total_ref, filt
):
    other = 1 - (lax.axis_index("mem") & (CORES - 1))
    last_refs = last_1_ref, last_2_ref, last_3_ref
    filter_share(levels, other, own_ref, coef_ref, mat_ref, row_coef_ref, part_ref, last_refs, filt)
    total = mixed(vert_ref[other], filt[...].reshape(vert_ref.shape[2], -1))
    total_ref[...] = total[: base_ref.shape[0]] + base_ref[...]


def join_call(levels, own, coef, mats, row_coef, shares, vert, base):
    vmem = pl.BlockSpec(memory_space=pltpu.VMEM)
    args = [own, coef, mats, row_coef, *shares, vert, base]
    return pl.pallas_call(
        functools.partial(join_kernel, levels),
        name="join",
        in_specs=[vmem] * len(args),
        out_specs=vmem,
        out_shape=jax.ShapeDtypeStruct(base.shape, F32),
        scratch_shapes=[pltpu.VMEM(own.shape, F32)],
        compiler_params=pltpu.CompilerParams(vmem_limit_bytes=VMEM),
        cost_estimate=taking(0.8),
    )(*args)


def final_kernel(scale, total_ref, came_ref, out_hbm, out_ref, sent):
    count, own_cols, rows = out_ref.shape
    copies = []
    for piece, first in enumerate(range(0, count, SUB)):
        place = slice(first, min(first + SUB, count))
        wide = slice(place.start * own_cols, place.stop * own_cols)
        total = total_ref[wide] + came_ref[wide].astype(F32) * scale
        out_ref[place] = total.reshape(place.stop - place.start, own_cols, rows).astype(BF16)
        copies.append(pltpu.make_async_copy(out_ref.at[place], out_hbm.at[place], sent.at[piece]))
        copies[-1].start()
    for copy in copies:
        copy.wait()


def final_call(slab_count, own_cols, scale, total, came):
    rows = total.shape[1]
    vmem = pl.BlockSpec(memory_space=pltpu.VMEM)
    out_shape = (slab_count, own_cols, rows)
    return pl.pallas_call(
        functools.partial(final_kernel, scale),
        name="final",
        in_specs=[vmem] * 2,
        out_specs=pl.BlockSpec(memory_space=pl.ANY),
        out_shape=jax.ShapeDtypeStruct(out_shape, BF16),
        scratch_shapes=[pltpu.VMEM(out_shape, BF16), pltpu.SemaphoreType.DMA((-(-slab_count // SUB),))],
        compiler_params=pltpu.CompilerParams(vmem_limit_bytes=VMEM),
        cost_estimate=taking(0.8),
    )(total, came)


def merge_kernel(levels, steps, step, last, after_count, *refs):
    lines_ref, ends_ref = refs[:2]
    came_refs, outs = refs[2 : 2 + step], refs[2 + step + after_count :]
    _, subs, rows = ends_ref.shape
    tile, mem = lax.axis_index("tile"), lax.axis_index("mem")
    is_level = iota((subs, rows), 0) + (mem & (CORES - 1)) * subs < levels
    decay = jnp.where(is_level, lines_ref[1, 0:1], lines_ref[1, 1:2])
    behind = jnp.where(is_level, lines_ref[2, 0:1], lines_ref[2, 1:2])
    turned = behind * decay
    right, left = ends_ref[0].astype(F32), ends_ref[1].astype(F32)
    into_right, into_left, from_left, from_right = 0.0, behind * right, 1.0, 1.0
    for level, came_ref in enumerate(came_refs):
        second = ((tile >> level) & 1) == 1
        came_right, came_left = came_ref[0].astype(F32), came_ref[1].astype(F32)
        into_right = into_right + jnp.where(second, from_left * came_right, 0.0)
        into_left = into_left + jnp.where(second, 0.0, from_right * came_left)
        right = jnp.where(second, decay * came_right + right, decay * right + came_right)
        left = jnp.where(second, came_left + decay * left, left + decay * came_left)
        from_left = jnp.where(second, from_left * decay, from_left)
        from_right = jnp.where(second, from_right, from_right * decay)
        decay = decay * decay
    if last:
        quarter = tile >> (steps - 2)
        outs[0][...] = jnp.where((quarter & 1) == 1, left, right).astype(BF16)
        outs[1][...] = jnp.where(quarter >= 2, left, right).astype(BF16)
        outs[2][0] = into_right.astype(BF16)
        outs[2][1] = (into_left + turned * into_right).astype(BF16)
    else:
        outs[0][0] = right.astype(BF16)
        outs[0][1] = left.astype(BF16)


def merge_call(lines, ends, came, after, levels, steps):
    last = len(came) == steps - 2
    whole = jax.ShapeDtypeStruct(ends.shape, BF16)
    one = jax.ShapeDtypeStruct(ends.shape[1:], BF16)
    outs = [one, one, whole] if last else [whole]
    vmem = pl.BlockSpec(memory_space=pltpu.VMEM)
    held = [pl.BlockSpec(memory_space=pl.ANY)] * len(after)
    return pl.pallas_call(
        functools.partial(merge_kernel, levels, steps, len(came), last, len(after)),
        name="merge",
        in_specs=[vmem] * (2 + len(came)) + held,
        out_specs=[vmem] * len(outs) + held,
        out_shape=outs + [jax.ShapeDtypeStruct(array.shape, array.dtype) for array in after],
        input_output_aliases={2 + len(came) + k: len(outs) + k for k in range(len(after))},
        compiler_params=pltpu.CompilerParams(vmem_limit_bytes=VMEM),
        cost_estimate=taking(0.8),
    )(lines, ends, *came, *after)


def body(field, vert_filter, loc_filter, alpha_table, xscale_idx, yscale_idx, members):
    tile_count, mem_count = lax.axis_size("tile"), lax.axis_size("mem")
    slab_count, cols, rows = field.shape
    levels = vert_filter.shape[1]
    own_cols = cols // mem_count
    slabs = padded(slab_count)
    steps = tile_count.bit_length() - 1

    def swap(array, flip, axis="mem"):
        return lax.ppermute(array, axis, [(i, i ^ flip) for i in range(lax.axis_size(axis))])

    full_field = field.reshape(slab_count * cols, rows)
    flat_field = pltpu.with_memory_space_constraint(full_field, pltpu.HBM)
    mine = members.reshape(slab_count * cols, rows)
    other = swap(mine, 1)
    line_table = pltpu.with_memory_space_constraint(alpha_table, pltpu.HBM)
    line_entries = pltpu.with_memory_space_constraint(xscale_idx, pltpu.HBM)
    line_loc = pltpu.with_memory_space_constraint(loc_filter[0], pltpu.HBM)
    ends, states, lines, *matrices = ends_call(
        line_table, line_entries, line_loc, flat_field, levels, steps, cols, own_cols
    )
    blocks, came = [ends], []
    send = send_call(matrices, full_field, mine, other, ends, cols, own_cols)
    over = swap(send, 2)
    coef = coefs_call(lines, send, steps, cols)
    for level in range(steps - 2):
        came.append(swap(blocks[0], 1 << level, "tile"))
        *blocks, coef = merge_call(lines, ends, came, [coef], levels, steps)
    near, far, part = blocks
    last = {flip: swap(near if flip == 1 else far, flip << (steps - 2), "tile") for flip in ORDER}
    keep = keep_call(matrices, full_field, mine, other, near, cols, own_cols)
    own_0, own_1 = local_call(lines, states, full_field, near, levels, cols, own_cols)
    mats, row_coef, vert = tables_call(alpha_table, yscale_idx, vert_filter[0], own_1, levels, own_cols, cols, slabs)
    shares = [part] + [last[flip] for flip in ORDER]
    others = [swap(share, 1) for share in shares]
    scale = 1.0 / (mem_count * members.shape[0] - 1)
    base = rows_call(levels, scale, own_0, coef, mats, row_coef, shares, vert, keep)
    total = join_call(levels, own_1, coef, mats, row_coef, others, vert, base)
    return final_call(slab_count, own_cols, scale, total, over)


def solution(mesh):
    return jax.shard_map(
        body,
        mesh=mesh,
        in_specs=(P(None, "tile", None), P(), P(), P(), P(), P(), P("mem", None, "tile", None)),
        out_specs=P(None, ("tile", "mem"), None),
        check_vma=False,
    )
```

```python
import functools

import jax
import jax.numpy as jnp
from jax import lax
from jax.experimental import pallas as pl
from jax.experimental.pallas import tpu as pltpu
from jax.sharding import PartitionSpec as P

F32, BF16 = jnp.float32, jnp.bfloat16
SUB = 16
CORES = 2
LANES = 256
ORDER = (3, 1, 2)
FETCHES = 1
BLOCK = 256
MIB = 1 << 20
VMEM = 32 * MIB


def iota(shape, dim):
    return lax.broadcasted_iota(jnp.int32, shape, dim)


def taking(microseconds):
    return pl.CostEstimate(flops=int(microseconds * 1.15e9), bytes_accessed=MIB // 4, transcendentals=0)


def split(number, size):
    assert size & (size - 1) == 0
    return number >> (size.bit_length() - 1), number & (size - 1)


def dot(left, right):
    return jnp.dot(left, right, preferred_element_type=F32)


def gain_of(alpha):
    rest = (1.0 - alpha) * (1.0 + alpha)
    return jnp.sqrt(rest) * rest / jnp.sqrt(1.0 + alpha * alpha)


def lookup(table_ref, entries):
    found = jnp.zeros(entries.shape, F32)
    for entry in range(table_ref.shape[0]):
        found = jnp.where(entries == entry, table_ref[entry], found)
    return found


def padded(slab_count):
    return -(-slab_count // (4 * SUB)) * 4 * SUB


def to_columns(perm, flat, out_ref, cols):
    total = flat.shape[0]
    wanted = out_ref.shape[0]
    step = SUB * cols
    for chunk in range(out_ref.shape[1] // SUB):
        depth = min(step, total - chunk * step)
        moved = dot(perm[:, :depth], flat[chunk * step : chunk * step + depth])
        out_ref[:, chunk * SUB : (chunk + 1) * SUB, :] = moved.reshape(wanted, SUB, -1).astype(out_ref.dtype)


def sweep(work, alpha):
    cols = work.shape[0]
    state = work[0]
    for col in range(1, cols):
        state = alpha * state + work[col]
        work[col] = state
    for col in range(cols - 2, -1, -1):
        state = alpha * state + work[col]
        work[col] = state


def transposer(cols):
    shape = (SUB * cols, SUB * cols)
    (out_col, out_slab), (in_slab, in_col) = split(iota(shape, 0), SUB), split(iota(shape, 1), cols)
    return ((out_slab == in_slab) & (out_col == in_col)).astype(BF16)


def share_rows(total, cols, subs, share):
    return slice(share * subs * cols, min((share + 1) * subs * cols, total))


def clear_rest(held_ref, rows):
    first = rows.stop - rows.start
    if first < held_ref.shape[0]:
        held_ref[first:, :] = jnp.zeros((held_ref.shape[0] - first, held_ref.shape[1]), BF16)


def sweep_share(levels, share, perm, alpha, held, work):
    cols, subs, lanes = work.shape
    to_columns(perm, held, work, cols)
    is_level = iota((subs, lanes), 0) + share * subs < levels
    alpha = jnp.where(is_level, alpha[0:1], alpha[1:2])
    sweep(work, alpha)
    return gain_of(alpha), is_level


def ends_kernel(
    levels, steps, slab_count, own_cols, table_hbm, entries_hbm, loc_hbm, field_hbm, ends_ref, work, lines_ref, perm_ref,
    local_ref, order_ref, table_ref, entries_ref, loc_ref, held_ref, small, arrived
):
    pieces, cols, subs, lanes = work.shape
    slabs, rows = CORES * subs, held_ref.shape[1]
    tile, mem = lax.axis_index("tile"), lax.axis_index("mem")
    chip, share = split(mem, CORES)
    parts = arrived.shape[0]

    def fetch(part, begin):
        width = rows // parts
        place = pl.ds(part * width, width)
        for core in range(CORES):
            held = share_rows(slab_count * cols, cols, subs, core)

            @pl.when(share == core)
            def _():
                copy = pltpu.make_async_copy(
                    field_hbm.at[held, place], held_ref.at[0 : held.stop - held.start, place], arrived.at[part]
                )
                if begin:
                    copy.start(priority=1)
                    clear_rest(held_ref, held)
                else:
                    copy.wait()

    for part in range(parts):
        fetch(part, True)
    given = [
        pltpu.make_async_copy(source, target, small.at[k])
        for k, (source, target) in enumerate(
            ((table_hbm, table_ref), (entries_hbm, entries_ref), (loc_hbm, loc_ref))
        )
    ]
    for copy in given:
        copy.start()
    perm_ref[...] = selection(2 * (1 - chip) + share, perm_ref.shape, own_cols, cols)
    row, col = iota(local_ref.shape, 0), iota(local_ref.shape, 1)
    (row_col, row_slab), (col_col, col_slab) = split(row, slabs), split(col, slabs)
    order_slab, order_col = split(row, own_cols)
    order_ref[...] = ((order_slab == col_slab) & (order_col == col_col)).astype(BF16)
    perm = transposer(cols)
    for copy in given:
        copy.wait()
    local_ref[...] = spread(loc_ref[...], levels, row_slab, row_col, col_slab, col_col)
    pair = lookup(table_ref, entries_ref[...])
    decay, turn = line_coefs(pair, cols)
    behind = reflected(decay, turn, tile, steps)
    lines_ref[0], lines_ref[1], lines_ref[2] = pair, decay, behind
    for piece in range(pieces):
        if piece % (pieces // parts) == 0:
            fetch(piece // (pieces // parts), False)
        part = slice(piece * lanes, (piece + 1) * lanes)
        gain, is_level = sweep_share(levels, share, perm, pair[:, part], held_ref[:, part], work.at[piece])
        turned = (decay * behind)[:, part]
        turned = jnp.where(is_level, turned[0:1], turned[1:2])
        forward = gain * work[piece, cols - 1]
        ends_ref[0, :, part] = forward.astype(BF16)
        ends_ref[1, :, part] = (gain * work[piece, 0] + turned * forward).astype(BF16)


def ends_call(table, entries, loc, flat_field, levels, steps, cols, own_cols):
    total, rows = flat_field.shape
    subs = padded(total // cols) // CORES
    side = own_cols * CORES * subs
    vmem = pl.BlockSpec(memory_space=pltpu.VMEM)
    return pl.pallas_call(
        functools.partial(ends_kernel, levels, steps, total // cols, own_cols),
        name="ends",
        in_specs=[pl.BlockSpec(memory_space=pl.ANY)] * 4,
        out_specs=[vmem] * 6,
        out_shape=[
            jax.ShapeDtypeStruct((2, subs, rows), BF16),
            jax.ShapeDtypeStruct((rows // LANES, cols, subs, LANES), F32),
            jax.ShapeDtypeStruct((3, 2, rows), F32),
            jax.ShapeDtypeStruct((own_cols * SUB, cols * SUB), BF16),
            jax.ShapeDtypeStruct((side, side), BF16),
            jax.ShapeDtypeStruct((side, side), BF16),
        ],
        scratch_shapes=[
            pltpu.SMEM(table.shape, F32),
            pltpu.VMEM(entries.shape, jnp.int32),
            pltpu.VMEM(loc.shape, BF16),
            pltpu.VMEM((subs * cols, rows), BF16),
            pltpu.SemaphoreType.DMA((3,)),
            pltpu.SemaphoreType.DMA((FETCHES,)),
        ],
        compiler_params=pltpu.CompilerParams(vmem_limit_bytes=VMEM),
        cost_estimate=taking(2.1),
    )(table, entries, loc, flat_field)


def line_coefs(pair, cols):
    decay, turn = pair, pair
    while cols > 1:
        turn = turn * (1.0 + decay * decay)
        decay = decay * decay
        cols //= 2
    return decay, turn


def reflected(decay, turn, tile, steps):
    behind = (1 << steps) - 1 - tile
    total, power = jnp.zeros_like(turn), jnp.ones_like(turn)
    for level in range(steps):
        here = ((behind >> level) & 1) == 1
        total = jnp.where(here, total + power * power * turn, total)
        power = jnp.where(here, power * decay, power)
        turn = turn * (1.0 + decay * decay)
        decay = decay * decay
    return total


def local_kernel(levels, slab_count, lines_ref, states_ref, field_ref, after_ref, mine_ref, own_ref, held_ref, work):
    pieces, cols, subs, lanes = work.shape
    own_cols = own_ref.shape[0]
    mem = lax.axis_index("mem")
    share = (mem & (CORES - 1)) ^ 1
    for core in range(CORES):
        rows = share_rows(slab_count * cols, cols, subs, core)

        @pl.when(share == core)
        def _():
            held_ref[0 : rows.stop - rows.start, :] = field_ref[rows, :]
            clear_rest(held_ref, rows)

    pair, perm = lines_ref[0], transposer(cols)
    for piece in range(pieces):
        part = slice(piece * lanes, (piece + 1) * lanes)
        gain, _ = sweep_share(levels, share, perm, pair[:, part], held_ref[:, part], work.at[piece])
        wanted = pl.ds(mem * own_cols, own_cols)
        own_ref[:, :, part] = work[piece, wanted] * gain[None]
        is_level = iota((subs, lanes), 0) + (1 - share) * subs < levels
        gain = gain_of(jnp.where(is_level, pair[0:1, part], pair[1:2, part]))
        mine_ref[:, :, part] = states_ref[piece, wanted] * gain[None]


def local_call(lines, states, flat_field, after, levels, cols, own_cols):
    total, rows = flat_field.shape
    subs = padded(total // cols) // CORES
    vmem = pl.BlockSpec(memory_space=pltpu.VMEM)
    return pl.pallas_call(
        functools.partial(local_kernel, levels, total // cols),
        name="local",
        in_specs=[vmem] * 3 + [pl.BlockSpec(memory_space=pl.ANY)],
        out_specs=[vmem] * 2,
        out_shape=[jax.ShapeDtypeStruct((own_cols, subs, rows), F32)] * 2,
        scratch_shapes=[
            pltpu.VMEM((subs * cols, rows), BF16),
            pltpu.VMEM((rows // LANES, cols, subs, LANES), F32),
        ],
        compiler_params=pltpu.CompilerParams(vmem_limit_bytes=VMEM),
        cost_estimate=taking(0.5),
    )(lines, states, flat_field, after)


def coefs_kernel(steps, lines_ref, after_ref, coef_ref):
    cols = coef_ref.shape[1] - 3
    tile = lax.axis_index("tile")
    pair, decay, behind = lines_ref[0], lines_ref[1], lines_ref[2]
    square = pair * pair
    power, sums = jnp.ones_like(pair), jnp.zeros_like(pair)
    rights, geometric = [], []
    for _ in range(cols):
        power, sums = power * pair, sums * square + 1.0
        rights.append(power)
        geometric.append(sums)
    for col in range(cols):
        coef_ref[0, col] = rights[col] * geometric[cols - 1 - col]
        coef_ref[1, col] = rights[cols - 1 - col]
    turned = decay * behind
    from_left, from_right = jnp.ones_like(pair), jnp.ones_like(pair)
    for level in range(steps - 2):
        second = ((tile >> level) & 1) == 1
        from_left = jnp.where(second, from_left * decay, from_left)
        from_right = jnp.where(second, from_right, from_right * decay)
        decay = decay * decay
    quarter = tile >> (steps - 2)
    outer = (quarter == 0) | (quarter == 3)
    for flip, weight in ((1, 1.0), (2, decay), (3, jnp.where(outer, decay * decay, 1.0))):
        upper = (quarter ^ flip) < quarter
        coef_ref[0, cols + ORDER.index(flip)] = jnp.where(upper, from_left * weight, 0.0)
        coef_ref[1, cols + ORDER.index(flip)] = weight * jnp.where(upper, turned * from_left, from_right)


def coefs_call(lines, after, steps, cols):
    vmem = pl.BlockSpec(memory_space=pltpu.VMEM)
    return pl.pallas_call(
        functools.partial(coefs_kernel, steps),
        name="coefs",
        in_specs=[vmem, pl.BlockSpec(memory_space=pl.ANY)],
        out_specs=vmem,
        out_shape=jax.ShapeDtypeStruct((2, cols + 3, *lines.shape[1:]), F32),
        compiler_params=pltpu.CompilerParams(vmem_limit_bytes=VMEM),
        cost_estimate=taking(4.0),
    )(lines, after)


def spread(matrix, levels, row_slab, row_col, col_slab, col_col):
    rows, cols = row_slab.shape
    size = matrix.shape[0]
    left = (iota((rows, size), 1) == row_slab[:, :size]).astype(BF16)
    right = (iota((size, cols), 0) == col_slab[:size, :]).astype(BF16)
    inner = dot(left, matrix).astype(BF16)
    full = dot(inner, right)
    full = jnp.where((row_slab >= levels) & (row_slab == col_slab), 1.0, full)
    return jnp.where(row_col == col_col, full, 0.0).astype(BF16)


def selection(block, shape, own_cols, cols):
    (slot, out_slab), (in_slab, in_col) = split(iota(shape, 0), SUB), split(iota(shape, 1), cols)
    return ((out_slab == in_slab) & (block * own_cols + slot == in_col)).astype(BF16)


def member_term(local, member, field):
    scaled = (member * field.astype(F32)).astype(BF16).reshape(local.shape[0], -1)
    return member * dot(local, scaled).reshape(member.shape)


def send_kernel(
    cols, perm_ref, local_ref, order_ref, field_ref, mine_ref, other_ref, after_ref, send_ref, field_w, mine_w, other_w
):
    for ref, out in ((field_ref, field_w), (mine_ref, mine_w), (other_ref, other_w)):
        to_columns(perm_ref[...], ref, out, cols)
    field, local = field_w[...], local_ref[...]
    total = member_term(local, mine_w[...], field) + member_term(local, other_w[...], field)
    total = total.reshape(order_ref.shape[0], -1).astype(BF16)
    send_ref[...] = dot(order_ref[...], total)[: send_ref.shape[0]].astype(BF16)


def keep_kernel(cols, local_ref, order_ref, field_ref, mine_ref, other_ref, after_ref, keep_ref, field_w, mine_w, other_w):
    own_cols = field_w.shape[0]
    perm = selection(lax.axis_index("mem"), (own_cols * SUB, cols * SUB), own_cols, cols)
    for ref, out in ((field_ref, field_w), (mine_ref, mine_w), (other_ref, other_w)):
        to_columns(perm, ref, out, cols)
    field, local = field_w[...], local_ref[...]
    total = member_term(local, mine_w[...], field) + member_term(local, other_w[...], field)
    total = total.reshape(order_ref.shape[0], -1)
    high = total.astype(BF16)
    ordered = dot(order_ref[...], high) + dot(order_ref[...], (total - high.astype(F32)).astype(BF16))
    keep_ref[...] = ordered[: keep_ref.shape[0]]


def send_call(matrices, flat_field, mine, other, after, cols, own_cols):
    total, rows = other.shape
    work = pltpu.VMEM((own_cols, padded(total // cols), rows), F32)
    vmem = pl.BlockSpec(memory_space=pltpu.VMEM)
    return pl.pallas_call(
        functools.partial(send_kernel, cols),
        name="send",
        in_specs=[vmem] * 6 + [pl.BlockSpec(memory_space=pl.ANY)],
        out_specs=vmem,
        out_shape=jax.ShapeDtypeStruct((total // cols * own_cols, rows), BF16),
        scratch_shapes=[work] * 3,
        compiler_params=pltpu.CompilerParams(vmem_limit_bytes=VMEM),
        cost_estimate=taking(2.6),
    )(*matrices, flat_field, mine, other, after)


def keep_call(matrices, flat_field, mine, other, after, cols, own_cols):
    total, rows = other.shape
    work = pltpu.VMEM((own_cols, padded(total // cols), rows), F32)
    vmem = pl.BlockSpec(memory_space=pltpu.VMEM)
    return pl.pallas_call(
        functools.partial(keep_kernel, cols),
        name="keep",
        in_specs=[vmem] * 5 + [pl.BlockSpec(memory_space=pl.ANY)],
        out_specs=vmem,
        out_shape=jax.ShapeDtypeStruct((total // cols * own_cols, rows), F32),
        scratch_shapes=[work] * 3,
        compiler_params=pltpu.CompilerParams(vmem_limit_bytes=VMEM),
        cost_estimate=taking(0.6),
    )(*matrices[1:], flat_field, mine, other, after)


def tables_kernel(levels, own_cols, col_dev, slabs, table_ref, entries_ref, vert_ref, after_ref, mat_ref, coef_ref, vert_out):
    first = lax.axis_index("tile") * col_dev + lax.axis_index("mem") * own_cols
    count = 2 * own_cols
    by_row = jnp.zeros((count, 1), F32)
    every, found = entries_ref[...], jnp.zeros(entries_ref.shape, F32)
    for entry in range(table_ref.shape[1]):
        found = jnp.where(every == entry, table_ref[0:1, entry : entry + 1], found)
    for col in range(own_cols):
        here = iota(found.shape, 1) == first + col
        alphas = jnp.sum(jnp.where(here, found, 0.0), axis=1, keepdims=True)
        for var in range(2):
            by_row = jnp.where(iota((count, 1), 0) == var * own_cols + col, alphas[var : var + 1], by_row)

    def series(alpha, number):
        alpha = jnp.broadcast_to(alpha, number.shape)
        total, unit = jnp.zeros(number.shape, F32), jnp.ones(number.shape, F32)
        single, power, both = alpha, alpha * alpha, jnp.ones(number.shape, F32)
        for bit in range(BLOCK.bit_length()):
            here = ((number >> bit) & 1) == 1
            total = jnp.where(here, unit + power * total, total)
            both = jnp.where(here, both * single, both)
            unit, single, power = unit * (1.0 + power), single * single, power * power
        return total, both

    place = iota((count, BLOCK), 1)
    across, right = series(by_row, BLOCK - place)
    down = jnp.concatenate([across, jnp.zeros((128 - count, BLOCK), F32)], 0).T
    _, left = series(by_row, place + 1)
    coef_ref[0] = left * across
    coef_ref[1] = right
    coef_ref[2] = jnp.broadcast_to(right[:, 0:1], right.shape)
    coef_ref[3] = jnp.broadcast_to(left[:, 0:1] * across[:, 0:1], right.shape)
    far = jnp.abs(iota((BLOCK, BLOCK), 0) - iota((BLOCK, BLOCK), 1)).astype(F32)
    for k in range(count):
        alpha = by_row[k : k + 1]
        decay = jnp.exp(far * jnp.log(jnp.maximum(alpha, 1e-30)))
        reach = jnp.minimum(down[:, k : k + 1], across[k : k + 1])
        mat_ref[k] = (gain_of(alpha) * decay * reach).astype(BF16)
    shape = vert_out.shape[1:]
    (row_slab, row_col), (col_col, col_slab) = split(iota(shape, 0), own_cols), split(iota(shape, 1), slabs // CORES)
    for share in range(CORES):
        first = share * (slabs // CORES)
        vert_out[share] = spread(vert_ref[...], levels, row_slab, row_col, col_slab + first, col_col)


def tables_call(table, entries, vert, after, levels, own_cols, col_dev, slabs):
    count = 2 * own_cols
    return pl.pallas_call(
        functools.partial(tables_kernel, levels, own_cols, col_dev, slabs),
        name="tables",
        in_specs=[pl.BlockSpec(memory_space=pltpu.VMEM)] * 3 + [pl.BlockSpec(memory_space=pl.ANY)],
        out_specs=[pl.BlockSpec(memory_space=pltpu.VMEM)] * 3,
        out_shape=[
            jax.ShapeDtypeStruct((count, BLOCK, BLOCK), BF16),
            jax.ShapeDtypeStruct((4, count, BLOCK), F32),
            jax.ShapeDtypeStruct((CORES, own_cols * slabs, own_cols * slabs // CORES), BF16),
        ],
        compiler_params=pltpu.CompilerParams(vmem_limit_bytes=VMEM),
        cost_estimate=taking(0.4),
    )(table[None], entries, vert, after)


def along_rows(lines, matrix, coef):
    count, rows = lines.shape
    blocks = rows // BLOCK
    parts = jnp.concatenate([lines[:, b * BLOCK : (b + 1) * BLOCK] for b in range(blocks)], 0)
    local = dot(parts.astype(BF16), matrix)
    local = [local[b * count : (b + 1) * count] for b in range(blocks)]
    into, right, decay, turn = coef[0:1], coef[1:2], coef[2:3, 0:1], coef[3:4, 0:1]
    forward, state = [None], None
    for b in range(blocks - 1):
        end = local[b][:, BLOCK - 1 : BLOCK]
        state = end if state is None else decay * state + end
        forward.append(state)
    out, state = [None] * blocks, None
    for b in range(blocks - 1, -1, -1):
        piece = local[b]
        if forward[b] is not None:
            piece = piece + into * forward[b]
        if state is not None:
            piece = piece + right * state
        out[b] = piece
        if b:
            start = local[b][:, 0:1] + turn * forward[b]
            state = start if state is None else decay * state + start
    return out


def filter_share(levels, share, own_ref, coef_ref, mat_ref, row_coef_ref, part_ref, last_refs, out_ref):
    own_cols, subs, rows = own_ref.shape
    cols = coef_ref.shape[1] - 3
    mem = lax.axis_index("mem")
    end = slice(subs - 8, subs)
    is_level = iota((8, rows), 0) + share * subs + subs - 8 < levels
    lasts = [ref[...].astype(F32) for ref in last_refs]
    carry, carry_end = [], []
    for side in range(2):
        value = part_ref[side].astype(F32)
        other = value[end]
        for k, last in enumerate(lasts):
            value = value + coef_ref[side, cols + k, 0:1] * last
            other = other + coef_ref[side, cols + k, 1:2] * last[end]
        carry.append(value)
        carry_end.append(other)
    for col in range(own_cols):
        pair = coef_ref[:, mem * own_cols + col]
        own = own_ref[col]
        lines = own + pair[0, 0:1] * carry[0] + pair[1, 0:1] * carry[1]
        last_lines = own[end] + pair[0, 1:2] * carry_end[0] + pair[1, 1:2] * carry_end[1]
        main = along_rows(lines, mat_ref[col], row_coef_ref[:, col])
        last = along_rows(last_lines, mat_ref[own_cols + col], row_coef_ref[:, own_cols + col])
        for b, (piece, extra) in enumerate(zip(main, last)):
            place = slice(b * BLOCK, (b + 1) * BLOCK)
            out_ref[col, 0 : subs - 8, place] = piece[0 : subs - 8]
            out_ref[col, end, place] = jnp.where(is_level[:, place], piece[end], extra)


def mixed(vert, static):
    return dot(vert, static.astype(BF16))


def rows_kernel(levels, scale, own_ref, coef_ref, mat_ref, row_coef_ref, part_ref, *refs):
    *last_refs, vert_ref, keep_ref, base_ref, filt = refs
    share = lax.axis_index("mem") & (CORES - 1)
    filter_share(levels, share, own_ref, coef_ref, mat_ref, row_coef_ref, part_ref, last_refs, filt)
    total = mixed(vert_ref[share], filt[...].reshape(vert_ref.shape[2], -1))
    base_ref[...] = total[: base_ref.shape[0]] + keep_ref[...] * scale


def rows_call(levels, scale, own, coef, mats, row_coef, shares, vert, keep):
    vmem = pl.BlockSpec(memory_space=pltpu.VMEM)
    args = [own, coef, mats, row_coef, *shares, vert, keep]
    return pl.pallas_call(
        functools.partial(rows_kernel, levels, scale),
        name="rows",
        in_specs=[vmem] * len(args),
        out_specs=vmem,
        out_shape=jax.ShapeDtypeStruct(keep.shape, F32),
        scratch_shapes=[pltpu.VMEM(own.shape, F32)],
        compiler_params=pltpu.CompilerParams(vmem_limit_bytes=VMEM),
        cost_estimate=taking(1.2),
    )(*args)


def join_kernel(
    levels, own_ref, coef_ref, mat_ref, row_coef_ref, part_ref, last_1_ref, last_2_ref, last_3_ref, vert_ref, base_ref,
    total_ref, filt
):
    other = 1 - (lax.axis_index("mem") & (CORES - 1))
    last_refs = last_1_ref, last_2_ref, last_3_ref
    filter_share(levels, other, own_ref, coef_ref, mat_ref, row_coef_ref, part_ref, last_refs, filt)
    total = mixed(vert_ref[other], filt[...].reshape(vert_ref.shape[2], -1))
    total_ref[...] = total[: base_ref.shape[0]] + base_ref[...]


def join_call(levels, own, coef, mats, row_coef, shares, vert, base):
    vmem = pl.BlockSpec(memory_space=pltpu.VMEM)
    args = [own, coef, mats, row_coef, *shares, vert, base]
    return pl.pallas_call(
        functools.partial(join_kernel, levels),
        name="join",
        in_specs=[vmem] * len(args),
        out_specs=vmem,
        out_shape=jax.ShapeDtypeStruct(base.shape, F32),
        scratch_shapes=[pltpu.VMEM(own.shape, F32)],
        compiler_params=pltpu.CompilerParams(vmem_limit_bytes=VMEM),
        cost_estimate=taking(0.8),
    )(*args)


def final_kernel(scale, total_ref, came_ref, out_hbm, out_ref, sent):
    count, own_cols, rows = out_ref.shape
    copies = []
    for piece, first in enumerate(range(0, count, SUB)):
        place = slice(first, min(first + SUB, count))
        wide = slice(place.start * own_cols, place.stop * own_cols)
        total = total_ref[wide] + came_ref[wide].astype(F32) * scale
        out_ref[place] = total.reshape(place.stop - place.start, own_cols, rows).astype(BF16)
        copies.append(pltpu.make_async_copy(out_ref.at[place], out_hbm.at[place], sent.at[piece]))
        copies[-1].start()
    for copy in copies:
        copy.wait()


def final_call(slab_count, own_cols, scale, total, came):
    rows = total.shape[1]
    vmem = pl.BlockSpec(memory_space=pltpu.VMEM)
    out_shape = (slab_count, own_cols, rows)
    return pl.pallas_call(
        functools.partial(final_kernel, scale),
        name="final",
        in_specs=[vmem] * 2,
        out_specs=pl.BlockSpec(memory_space=pl.ANY),
        out_shape=jax.ShapeDtypeStruct(out_shape, BF16),
        scratch_shapes=[pltpu.VMEM(out_shape, BF16), pltpu.SemaphoreType.DMA((-(-slab_count // SUB),))],
        compiler_params=pltpu.CompilerParams(vmem_limit_bytes=VMEM),
        cost_estimate=taking(0.8),
    )(total, came)


def merge_kernel(levels, steps, step, last, after_count, *refs):
    lines_ref, ends_ref = refs[:2]
    came_refs, outs = refs[2 : 2 + step], refs[2 + step + after_count :]
    _, subs, rows = ends_ref.shape
    tile, mem = lax.axis_index("tile"), lax.axis_index("mem")
    is_level = iota((subs, rows), 0) + (mem & (CORES - 1)) * subs < levels
    decay = jnp.where(is_level, lines_ref[1, 0:1], lines_ref[1, 1:2])
    behind = jnp.where(is_level, lines_ref[2, 0:1], lines_ref[2, 1:2])
    turned = behind * decay
    right, left = ends_ref[0].astype(F32), ends_ref[1].astype(F32)
    into_right, into_left, from_left, from_right = 0.0, behind * right, 1.0, 1.0
    for level, came_ref in enumerate(came_refs):
        second = ((tile >> level) & 1) == 1
        came_right, came_left = came_ref[0].astype(F32), came_ref[1].astype(F32)
        into_right = into_right + jnp.where(second, from_left * came_right, 0.0)
        into_left = into_left + jnp.where(second, 0.0, from_right * came_left)
        right = jnp.where(second, decay * came_right + right, decay * right + came_right)
        left = jnp.where(second, came_left + decay * left, left + decay * came_left)
        from_left = jnp.where(second, from_left * decay, from_left)
        from_right = jnp.where(second, from_right, from_right * decay)
        decay = decay * decay
    if last:
        quarter = tile >> (steps - 2)
        outs[0][...] = jnp.where((quarter & 1) == 1, left, right).astype(BF16)
        outs[1][...] = jnp.where(quarter >= 2, left, right).astype(BF16)
        outs[2][0] = into_right.astype(BF16)
        outs[2][1] = (into_left + turned * into_right).astype(BF16)
    else:
        outs[0][0] = right.astype(BF16)
        outs[0][1] = left.astype(BF16)


def merge_call(lines, ends, came, after, levels, steps):
    last = len(came) == steps - 2
    whole = jax.ShapeDtypeStruct(ends.shape, BF16)
    one = jax.ShapeDtypeStruct(ends.shape[1:], BF16)
    outs = [one, one, whole] if last else [whole]
    vmem = pl.BlockSpec(memory_space=pltpu.VMEM)
    held = [pl.BlockSpec(memory_space=pl.ANY)] * len(after)
    return pl.pallas_call(
        functools.partial(merge_kernel, levels, steps, len(came), last, len(after)),
        name="merge",
        in_specs=[vmem] * (2 + len(came)) + held,
        out_specs=[vmem] * len(outs) + held,
        out_shape=outs + [jax.ShapeDtypeStruct(array.shape, array.dtype) for array in after],
        input_output_aliases={2 + len(came) + k: len(outs) + k for k in range(len(after))},
        compiler_params=pltpu.CompilerParams(vmem_limit_bytes=VMEM),
        cost_estimate=taking(0.8),
    )(lines, ends, *came, *after)


def body(field, vert_filter, loc_filter, alpha_table, xscale_idx, yscale_idx, members):
    tile_count, mem_count = lax.axis_size("tile"), lax.axis_size("mem")
    slab_count, cols, rows = field.shape
    levels = vert_filter.shape[1]
    own_cols = cols // mem_count
    slabs = padded(slab_count)
    steps = tile_count.bit_length() - 1

    def swap(array, flip, axis="mem"):
        return lax.ppermute(array, axis, [(i, i ^ flip) for i in range(lax.axis_size(axis))])

    full_field = field.reshape(slab_count * cols, rows)
    flat_field = pltpu.with_memory_space_constraint(full_field, pltpu.HBM)
    mine = members.reshape(slab_count * cols, rows)
    other = swap(mine, 1)
    line_table = pltpu.with_memory_space_constraint(alpha_table, pltpu.HBM)
    line_entries = pltpu.with_memory_space_constraint(xscale_idx, pltpu.HBM)
    line_loc = pltpu.with_memory_space_constraint(loc_filter[0], pltpu.HBM)
    ends, states, lines, *matrices = ends_call(
        line_table, line_entries, line_loc, flat_field, levels, steps, cols, own_cols
    )
    blocks, came = [ends], []
    send = send_call(matrices, full_field, mine, other, ends, cols, own_cols)
    over = swap(send, 2)
    coef = coefs_call(lines, send, steps, cols)
    for level in range(steps - 2):
        came.append(swap(blocks[0], 1 << level, "tile"))
        *blocks, coef = merge_call(lines, ends, came, [coef], levels, steps)
    near, far, part = blocks
    last = {flip: swap(near if flip == 1 else far, flip << (steps - 2), "tile") for flip in ORDER}
    keep = keep_call(matrices, full_field, mine, other, near, cols, own_cols)
    own_0, own_1 = local_call(lines, states, full_field, near, levels, cols, own_cols)
    mats, row_coef, vert = tables_call(alpha_table, yscale_idx, vert_filter[0], own_1, levels, own_cols, cols, slabs)
    shares = [part] + [last[flip] for flip in ORDER]
    others = [swap(share, 1) for share in shares]
    scale = 1.0 / (mem_count * members.shape[0] - 1)
    base = rows_call(levels, scale, own_0, coef, mats, row_coef, shares, vert, keep)
    total = join_call(levels, own_1, coef, mats, row_coef, others, vert, base)
    return final_call(slab_count, own_cols, scale, total, over)


def solution(mesh):
    return jax.shard_map(
        body,
        mesh=mesh,
        in_specs=(P(None, "tile", None), P(), P(), P(), P(), P(), P("mem", None, "tile", None)),
        out_specs=P(None, ("tile", "mem"), None),
        check_vma=False,
    )
```
